32 devices in a mesh: seq: 16 (over z, y, x), ch: 2 (over core).
Axes of the slice: x: 2, y: 2, z: 4, core: 2. Of those that a mesh axis runs over, the one named last changes fastest.
Arguments:
- inputs: bfloat16 [8192, 1024], P('seq', 'ch'), may hold values from -6 to 6
- conv_weight: bfloat16 [3, 1024], P(None, 'ch'), may hold values from -3 to 3
- mixing: bfloat16 [6, 128, 64, 128], P(None, 'seq'), may hold values from -0.5 to 0.5
- pattern: int32 [2, 128], P(None, 'seq'), may hold values from 0 to 7, as said below
- w_in: bfloat16 [1024, 4096], P(None, 'ch'), may hold values from -0.1875 to 0.1875
- w_out: bfloat16 [4096, 1024], P('ch'), may hold values from -0.09375 to 0.09375
- cotangent: bfloat16 [8192, 1024], P('seq', 'ch'), may hold values from -6 to 6
Outputs:
- layer_out: bfloat16 [8192, 1024], P('seq', 'ch')
- convolved: bfloat16 [8192, 1024], P('seq', 'ch')
- grad_input: bfloat16 [8192, 1024], P('seq', 'ch')
The draws below stay inside these ranges and needn't reach their ends.
Inputs may be any that keep to these rules, and one draw needn't show every extreme that they name: `pattern`: for each of the 2 factors and each aligned run of 8 blocks (the blocks of one device), entry j of the run is a number k != j with entry k equal to j.
All inputs are finite; a program needn't handle non-finite values.
Results may differ from the reference program's by a relative error of at most 0.025.
Values may be sent and summed in bfloat16 or wider, within the bound.
No kernel may reach another device: no remote copies, remote signals or barrier semaphores. Data moves between devices by JAX's collectives and lax.ppermute only.
A program may use at most 64 MiB of HBM per device.

```python
import jax
import jax.numpy as jnp

D = 1024
HIDDEN_SIZE = 4096
BLOCK = 64
LOCAL = 2
BL = 8
NB = 128
TOKENS = 8192
LEVELS = 4
FACTORS = 6


def draw_pattern(key, part):
    count = LOCAL * (NB // BL)
    keys = jax.random.split(key, count)
    orders = jax.vmap(lambda sub_key: jax.random.permutation(sub_key, BL))(keys).astype(jnp.int32)
    spots = jnp.argsort(orders, axis=1, stable=True).astype(jnp.int32)
    mates = jnp.bitwise_xor(spots, 1)
    partner = jnp.take_along_axis(orders, mates, axis=1)
    return partner.reshape(LOCAL, NB).astype(jnp.int32)


def levels(own_key, dims, shards, low, largest):
    factor_of = 1.0
    for dim, blocks in shards:
        draws = jax.random.uniform(jax.random.fold_in(jax.random.fold_in(own_key, 6), dim), (blocks,), jnp.float32, low / len(shards), largest / len(shards))
        factor_of = factor_of * jnp.repeat(jnp.exp(draws), dims[dim] // blocks).reshape((-1,) + (1,) * (len(dims) - 1 - dim))
    return factor_of


def scatter_about(key, shape, deviation, reach, shards=(), kind=jnp.bfloat16):
    entries = jax.random.normal(key, shape, jnp.float32) * deviation
    if len(shards) > 0:
        entries = levels(key, shape, shards, -0.22, 0.18) * entries
    return jnp.clip(entries, min=-reach, max=reach).astype(kind)


def setup_inputs(seed: int = 0) -> dict:
    seeds = jax.random.split(jax.random.key(seed), 8)
    inputs = scatter_about(seeds[0], (TOKENS, D), 1.0, 6.0, ((0, 16), (1, 2)))
    conv_weight = scatter_about(seeds[1], (3, D), 0.6, 3.0, ((1, 2),))
    mixing = scatter_about(seeds[2], (FACTORS, NB, BLOCK, 2 * BLOCK), (2 * BLOCK) ** -0.5, 0.5, ((1, 16),))
    pattern = draw_pattern(jax.random.fold_in(seeds[7], 71), 0)
    w_in = scatter_about(seeds[4], (D, HIDDEN_SIZE), D ** -0.5, 0.1875, ((1, 2),))
    w_out = scatter_about(seeds[5], (HIDDEN_SIZE, D), HIDDEN_SIZE ** -0.5, 0.09375, ((0, 2),))
    cotangent = scatter_about(seeds[6], (TOKENS, D), 1.0, 6.0, ((0, 16), (1, 2)))
    return dict(inputs=inputs, conv_weight=conv_weight, mixing=mixing, pattern=pattern, w_in=w_in, w_out=w_out, cotangent=cotangent)


root_two_pi = 0.7978845608028654

def gelu_grad(hidden):
    inner_arg = root_two_pi * (hidden + 0.044715 * hidden * hidden * hidden)
    tanh_val = jnp.tanh(inner_arg)
    slope = root_two_pi * (1.0 + 3.0 * 0.044715 * hidden * hidden)
    return 0.5 * (1.0 + tanh_val) + 0.5 * hidden * (1.0 - tanh_val * tanh_val) * slope

def reference(inputs, conv_weight, mixing, pattern, w_in, w_out, cotangent):
    length = inputs.shape[0]
    taps = conv_weight.astype(jnp.float32)
    padded = jnp.pad(inputs.astype(jnp.float32), ((1, 1), (0, 0)))
    convolved = (taps[0] * padded[:-2] + taps[1] * padded[1:-1] + taps[2] * padded[2:]).astype(jnp.bfloat16)
    nblocks = length // BLOCK
    block_ids = jnp.arange(nblocks, dtype=jnp.int32)
    group_start = block_ids // BL * BL
    partners = []
    for factor in range(LOCAL):
        partners.append((group_start + pattern[factor]).astype(jnp.int32))
    for level in range(LEVELS):
        partners.append(jnp.bitwise_xor(block_ids, BL * 2 ** level).astype(jnp.int32))
    state = convolved.reshape(nblocks, BLOCK, D)
    for factor in range(FACTORS):
        weights = mixing[factor].astype(jnp.float32)
        current = state.astype(jnp.float32)
        mates = current[partners[factor]]
        updated = jnp.einsum('bij,bjd->bid', weights[:, :, :BLOCK], current) + jnp.einsum('bij,bjd->bid', weights[:, :, BLOCK:], mates)
        state = updated.astype(jnp.bfloat16)
    mixed = state.reshape(length, D)
    hidden = jnp.dot(mixed, w_in, preferred_element_type=jnp.float32)
    activation = jax.nn.gelu(hidden, approximate=True).astype(jnp.bfloat16)
    layer_out = (mixed.astype(jnp.float32) + jnp.dot(activation, w_out, preferred_element_type=jnp.float32)).astype(jnp.bfloat16)
    grad_act = jnp.dot(cotangent, w_out.T, preferred_element_type=jnp.float32)
    grad_hidden = (grad_act * gelu_grad(hidden)).astype(jnp.bfloat16)
    grad_mixed = (cotangent.astype(jnp.float32) + jnp.dot(grad_hidden, w_in.T, preferred_element_type=jnp.float32)).astype(jnp.bfloat16)
    grads = grad_mixed.reshape(nblocks, BLOCK, D)
    for factor in reversed(range(FACTORS)):
        weights = mixing[factor].astype(jnp.float32)
        current = grads.astype(jnp.float32)
        own_term = jnp.einsum('bji,bjd->bid', weights[:, :, :BLOCK], current)
        cross_term = jnp.einsum('bji,bjd->bid', weights[:, :, BLOCK:], current)
        grads = (own_term + cross_term[partners[factor]]).astype(jnp.bfloat16)
    grad_pad = jnp.pad(grads.reshape(length, D).astype(jnp.float32), ((1, 1), (0, 0)))
    grad_input = (taps[0] * grad_pad[2:] + taps[1] * grad_pad[1:-1] + taps[2] * grad_pad[:-2]).astype(jnp.bfloat16)
    return (layer_out, convolved, grad_input)
```

```python
import functools

import jax
import jax.numpy as jnp
from jax import lax
from jax.experimental import pallas as pl
from jax.experimental.pallas import tpu as pltpu
from jax.sharding import PartitionSpec as P

BLOCK = 64
LOCAL = 2
PIECES = 4
TILE = 512
VMEM_BYTES = 40 * 1024 * 1024

root_two_pi = 0.7978845608028654


def neighbours(first, last, axis):
    count = lax.axis_size(axis)
    ends = count - 1
    before = lax.ppermute(last, axis, [(i, (i + 1) % count) for i in range(ends)])
    after = lax.ppermute(first, axis, [((i + 1) % count, i) for i in range(ends)])
    return before, after


def from_partner(block, axis, bit):
    count = lax.axis_size(axis)
    route = []
    for low in range(count):
        high = low | 1 << bit
        if high != low and high < count:
            route += [(low, high), (high, low)]
    return lax.ppermute(block, axis, route)


def from_offset(block, axis, offset):
    count = lax.axis_size(axis)
    return lax.ppermute(block, axis, [((i + offset) % count, i) for i in range(count)])


def shifted(cells, before, after):
    rows = cells.shape[0]
    spot = lax.broadcasted_iota(jnp.int32, cells.shape, 0)
    up = jnp.where(spot == 0, before, pltpu.roll(cells, 1, 0))
    down = jnp.where(spot == rows - 1, after, pltpu.roll(cells, rows - 1, 0))
    return up, down


def entry_kernel(pattern, cells, before, after, taps, weights, conv_ref, *rest):
    pieces, (here, there) = rest[:-2], rest[-2:]
    blocks = here.shape[0]
    values = cells[...].astype(jnp.float32)
    scale = taps[...].astype(jnp.float32)
    up, down = shifted(
        values, before[...].astype(jnp.float32), after[...].astype(jnp.float32)
    )
    convolved = (scale[0:1] * up + scale[1:2] * values + scale[2:3] * down).astype(jnp.bfloat16)
    conv_ref[...] = convolved
    here[...] = convolved.reshape(here.shape)
    source, target = here, there
    per_piece = blocks // len(pieces)
    for factor in range(LOCAL):
        for block in range(blocks):
            pair = weights[factor, block]
            mixed = jnp.dot(
                pair[:, :BLOCK], source[block], preferred_element_type=jnp.float32
            ) + jnp.dot(
                pair[:, BLOCK:],
                source[pattern[factor, block]],
                preferred_element_type=jnp.float32,
            )
            mixed = mixed.astype(jnp.bfloat16)
            if factor == LOCAL - 1:
                pieces[block // per_piece][block % per_piece] = mixed
            else:
                target[block] = mixed
        source, target = target, source


def entry(pattern, cells, before, after, taps, weights, count):
    rows, chans = cells.shape
    blocks = rows // BLOCK
    whole = pl.BlockSpec(memory_space=pltpu.VMEM)
    return pl.pallas_call(
        entry_kernel,
        out_shape=[jax.ShapeDtypeStruct((rows, chans), jnp.bfloat16)]
        + [jax.ShapeDtypeStruct((blocks // count, BLOCK, chans), jnp.bfloat16)] * count,
        in_specs=[pl.BlockSpec(memory_space=pltpu.SMEM)] + [whole] * 5,
        out_specs=[whole] * (count + 1),
        scratch_shapes=[pltpu.VMEM((blocks, BLOCK, chans), jnp.bfloat16)] * 2,
        compiler_params=pltpu.CompilerParams(vmem_limit_bytes=VMEM_BYTES),
        name="conv_and_local_factors",
    )(pattern, cells, before, after, taps, weights)


def exit_kernel(pattern, *rest):
    pieces, (weights, out, here, cross) = rest[:-4], rest[-4:]
    blocks = here.shape[0]
    per_piece = blocks // len(pieces)
    for factor in reversed(range(LOCAL)):
        for block in range(blocks):
            if factor == LOCAL - 1:
                value = pieces[block // per_piece][block % per_piece]
            else:
                value = here[block]
            both = lax.dot_general(
                weights[factor, block],
                value,
                (((0,), (0,)), ((), ())),
                preferred_element_type=jnp.float32,
            )
            cross[0, block] = both[:BLOCK]
            cross[1, block] = both[BLOCK:]
        for block in range(blocks):
            combined = (cross[0, block] + cross[1, pattern[factor, block]]).astype(jnp.bfloat16)
            if factor == 0:
                out[block * BLOCK : (block + 1) * BLOCK] = combined
            else:
                here[block] = combined


def exit_factors(pattern, pieces, weights):
    per_piece, _, chans = pieces[0].shape
    blocks = per_piece * len(pieces)
    whole = pl.BlockSpec(memory_space=pltpu.VMEM)
    return pl.pallas_call(
        exit_kernel,
        out_shape=jax.ShapeDtypeStruct((blocks * BLOCK, chans), jnp.bfloat16),
        in_specs=[pl.BlockSpec(memory_space=pltpu.SMEM)] + [whole] * (len(pieces) + 1),
        out_specs=whole,
        scratch_shapes=[
            pltpu.VMEM((blocks, BLOCK, chans), jnp.bfloat16),
            pltpu.VMEM((2, blocks, BLOCK, chans), jnp.float32),
        ],
        compiler_params=pltpu.CompilerParams(vmem_limit_bytes=VMEM_BYTES),
        name="local_factors_back",
    )(pattern, *pieces, weights)


def mlp_kernel(count, place, *rest):
    mixed, cots = rest[:count], rest[count : 2 * count]
    w_in, w_out = rest[2 * count : 2 * count + 2]
    outs = rest[2 * count + 2 : 3 * count + 2]
    backs = rest[3 * count + 2 : 4 * count + 2]
    x_all, c_all, out_sum, back_sum = rest[4 * count + 2 :]
    rows, chans = mixed[0].shape
    step = pl.program_id(0)
    spots = [
        pl.ds(pl.multiple_of(lax.rem(place[0] + i, count) * chans, chans), chans)
        for i in range(count)
    ]

    @pl.when(step == 0)
    def _():
        for i in range(count):
            x_all[:, spots[i]] = mixed[i][...]
            c_all[:, spots[i]] = cots[i][...]
        out_sum[...] = jnp.zeros_like(out_sum)
        back_sum[...] = jnp.zeros_like(back_sum)

    across = (((1,), (1,)), ((), ()))
    hidden = jnp.dot(x_all[...], w_in[...], preferred_element_type=jnp.float32)
    grad_act = lax.dot_general(c_all[...], w_out[...], across, preferred_element_type=jnp.float32)
    square = hidden * hidden
    tanh_val = jnp.tanh(root_two_pi * (hidden + 0.044715 * square * hidden))
    half = 0.5 * (1.0 + tanh_val)
    activation = (hidden * half).astype(jnp.bfloat16)
    slope = root_two_pi * (1.0 + 3.0 * 0.044715 * square)
    derivative = half + 0.5 * hidden * (1.0 - tanh_val * tanh_val) * slope
    grad_hidden = (grad_act * derivative).astype(jnp.bfloat16)
    out_sum[...] += jnp.dot(activation, w_out[...], preferred_element_type=jnp.float32)
    back_sum[...] += lax.dot_general(
        grad_hidden, w_in[...], across, preferred_element_type=jnp.float32
    )

    @pl.when(step == pl.num_programs(0) - 1)
    def _():
        for i in range(count):
            outs[i][...] = out_sum[:, spots[i]].astype(outs[i].dtype)
            backs[i][...] = back_sum[:, spots[i]].astype(backs[i].dtype)


def mlp(place, mixed, cots, w_in, w_out):
    count = len(mixed)
    rows, chans = mixed[0].shape
    width, hidden = w_in.shape
    tile = min(TILE, hidden)
    part = pl.BlockSpec((rows, chans), lambda t, place: (0, 0))
    kinds = [jnp.float32] + [jnp.bfloat16] * (count - 1)
    shapes = [jax.ShapeDtypeStruct((rows, chans), kind) for kind in kinds]
    results = pl.pallas_call(
        functools.partial(mlp_kernel, count),
        out_shape=shapes * 2,
        grid_spec=pltpu.PrefetchScalarGridSpec(
            num_scalar_prefetch=1,
            grid=(hidden // tile,),
            in_specs=[part] * (2 * count)
            + [
                pl.BlockSpec((width, tile), lambda t, place: (0, t)),
                pl.BlockSpec((tile, width), lambda t, place: (t, 0)),
            ],
            out_specs=[part] * (2 * count),
            scratch_shapes=[
                pltpu.VMEM((rows, width), jnp.bfloat16),
                pltpu.VMEM((rows, width), jnp.bfloat16),
                pltpu.VMEM((rows, width), jnp.float32),
                pltpu.VMEM((rows, width), jnp.float32),
            ],
        ),
        compiler_params=pltpu.CompilerParams(vmem_limit_bytes=VMEM_BYTES),
        cost_estimate=pl.CostEstimate(
            flops=8 * rows * width * hidden,
            bytes_accessed=4 * width * hidden,
            transcendentals=rows * hidden,
        ),
        name="channel_mlp",
    )(place, *mixed, *cots, w_in, w_out)
    return results[:count], results[count:]


def on_device(inputs, conv_weight, mixing, pattern, w_in, w_out, cotangent):
    row_count, chan_count = inputs.shape
    blocks = row_count // BLOCK
    cores = lax.axis_size("ch")
    levels = lax.axis_size("seq").bit_length() - 1
    count = min(PIECES, blocks)
    per_piece = blocks // count
    piece_rows = per_piece * BLOCK
    place = lax.axis_index("ch").astype(jnp.int32).reshape(1)

    before, after = neighbours(inputs[:1], inputs[-1:], "seq")
    cots = [cotangent] + [from_offset(cotangent, "ch", i) for i in range(1, cores)]
    convolved, *states = entry(
        pattern, inputs, before, after, conv_weight, mixing[:LOCAL], count
    )
    outs, grads = [], []
    for piece in range(count):
        first = piece * per_piece
        state = states[piece]
        for factor in range(LOCAL, LOCAL + levels):
            weights = mixing[factor, first : first + per_piece]
            mates = from_partner(state, "seq", factor - LOCAL)
            updated = jnp.einsum(
                "bij,bjd->bid", weights[:, :, :BLOCK], state, preferred_element_type=jnp.float32
            )
            updated = updated + jnp.einsum(
                "bij,bjd->bid", weights[:, :, BLOCK:], mates, preferred_element_type=jnp.float32
            )
            state = updated.astype(jnp.bfloat16)
        mixed = state.reshape(piece_rows, chan_count)
        gathered = [mixed] + [from_offset(mixed, "ch", i) for i in range(1, cores)]
        start = piece * piece_rows
        piece_cots = [cot[start : start + piece_rows] for cot in cots]
        out_parts, back_parts = mlp(place, gathered, piece_cots, w_in, w_out)
        back = piece_cots[0].astype(jnp.float32) + back_parts[0]
        for i in range(1, cores):
            back = back + from_offset(back_parts[i], "ch", cores - i).astype(jnp.float32)
        out = mixed.astype(jnp.float32) + out_parts[0]
        for i in range(1, cores):
            out = out + from_offset(out_parts[i], "ch", cores - i).astype(jnp.float32)
        outs.append(out.astype(jnp.bfloat16))
        grad = back.astype(jnp.bfloat16).reshape(per_piece, BLOCK, chan_count)
        for factor in reversed(range(LOCAL, LOCAL + levels)):
            weights = mixing[factor, first : first + per_piece]
            cross = jnp.einsum(
                "bji,bjd->bid", weights[:, :, BLOCK:], grad, preferred_element_type=jnp.float32
            ).astype(jnp.bfloat16)
            cross = from_partner(cross, "seq", factor - LOCAL)
            own = jnp.einsum(
                "bji,bjd->bid", weights[:, :, :BLOCK], grad, preferred_element_type=jnp.float32
            )
            grad = (own + cross.astype(jnp.float32)).astype(jnp.bfloat16)
        grads.append(grad)
    layer_out = jnp.concatenate(outs, axis=0)
    grad_conv = exit_factors(pattern, grads, mixing[:LOCAL])
    before, after = neighbours(grad_conv[:1], grad_conv[-1:], "seq")
    taps = conv_weight.astype(jnp.float32)
    padded = jnp.concatenate([before, grad_conv, after], axis=0).astype(jnp.float32)
    grad_input = (taps[0] * padded[2:] + taps[1] * padded[1:-1] + taps[2] * padded[:-2]).astype(
        jnp.bfloat16
    )
    return (layer_out, convolved, grad_input)


def solution(mesh):
    return jax.shard_map(
        on_device,
        mesh=mesh,
        in_specs=(
            P("seq", "ch"),
            P(None, "ch"),
            P(None, "seq", None, None),
            P(None, "seq"),
            P(None, "ch"),
            P("ch", None),
            P("seq", "ch"),
        ),
        out_specs=(P("seq", "ch"), P("seq", "ch"), P("seq", "ch")),
        check_vma=False,
    )
```

```python
import functools

import jax
import jax.numpy as jnp
from jax import lax
from jax.experimental import pallas as pl
from jax.experimental.pallas import tpu as pltpu
from jax.sharding import PartitionSpec as P

BLOCK = 64
LOCAL = 2
QUARTERS = 4
TILE = 512
VMEM_BYTES = 40 * 1024 * 1024

root_two_pi = 0.7978845608028654

IN_SMEM = pl.BlockSpec(memory_space=pltpu.SMEM)
IN_VMEM = pl.BlockSpec(memory_space=pltpu.VMEM)
ANYWHERE = pl.BlockSpec(memory_space=pl.ANY)
ACROSS = (((1,), (1,)), ((), ()))
OVER_ROWS = (((0,), (0,)), ((), ()))


def times(weights, value):
    return jnp.dot(weights, value, preferred_element_type=jnp.float32)


def times_transposed(weights, value):
    return lax.dot_general(weights, value, OVER_ROWS, preferred_element_type=jnp.float32)


def neighbours(first, last, axis):
    count = lax.axis_size(axis)
    ends = count - 1
    before = lax.ppermute(last, axis, [(i, (i + 1) % count) for i in range(ends)])
    after = lax.ppermute(first, axis, [((i + 1) % count, i) for i in range(ends)])
    return before, after


def from_flipped(block, axis, mask):
    count = lax.axis_size(axis)
    return lax.ppermute(block, axis, [(i, i ^ mask) for i in range(count)])


def from_offset(block, axis, offset):
    count = lax.axis_size(axis)
    return lax.ppermute(block, axis, [((i + offset) % count, i) for i in range(count)])


def call(kernel, name, outs, scalars, arrays, scratch=(), order=(), flops=0):
    def body(*refs):
        kernel(*refs[: len(scalars) + len(arrays)], *refs[len(scalars) + len(arrays) + len(order) :])

    return pl.pallas_call(
        body,
        out_shape=[jax.ShapeDtypeStruct(shape, kind) for shape, kind in outs],
        in_specs=[IN_SMEM] * len(scalars) + [IN_VMEM] * len(arrays) + [ANYWHERE] * len(order),
        out_specs=[IN_VMEM] * len(outs),
        scratch_shapes=list(scratch),
        compiler_params=pltpu.CompilerParams(vmem_limit_bytes=VMEM_BYTES),
        name=name,
    )(*scalars, *arrays, *order)


def shifted(cells, before, after):
    rows = cells.shape[0]
    spot = lax.broadcasted_iota(jnp.int32, cells.shape, 0)
    up = jnp.where(spot == 0, before, pltpu.roll(cells, 1, 0))
    down = jnp.where(spot == rows - 1, after, pltpu.roll(cells, rows - 1, 0))
    return up, down


def entry_kernel(pattern, cells, before, after, taps, mixing, conv_ref, *rest):
    pieces, (here, there) = rest[:-2], rest[-2:]
    blocks = here.shape[0]
    values = cells[...].astype(jnp.float32)
    scale = taps[...].astype(jnp.float32)
    up, down = shifted(
        values, before[...].astype(jnp.float32), after[...].astype(jnp.float32)
    )
    convolved = (scale[0:1] * up + scale[1:2] * values + scale[2:3] * down).astype(jnp.bfloat16)
    conv_ref[...] = convolved
    here[...] = convolved.reshape(here.shape)
    source, target = here, there
    per_piece = blocks // len(pieces)
    for factor in range(LOCAL):
        for block in range(blocks):
            pair = mixing[factor, block]
            mixed = times(pair[:, :BLOCK], source[block]) + times(
                pair[:, BLOCK:], source[pattern[factor, block]]
            )
            mixed = mixed.astype(jnp.bfloat16)
            if factor == LOCAL - 1:
                pieces[block // per_piece][block % per_piece] = mixed
            else:
                target[block] = mixed
        source, target = target, source


def plain_kernel(factor, first, state, mates, mixing, out):
    for block in range(state.shape[0]):
        pair = mixing[factor, first + block]
        out[block] = (
            times(pair[:, :BLOCK], state[block]) + times(pair[:, BLOCK:], mates[block])
        ).astype(jnp.bfloat16)


def split_kernel(factor, first, place, state, mates, mixing, keep, send):
    for flip, out in enumerate((keep, send)):
        for late in range(2):
            spot = (place[1] ^ flip) * 2 + late
            pair = mixing[factor, first + spot]
            out[late] = (
                times(pair[:, :BLOCK], state[spot]) + times(pair[:, BLOCK:], mates[spot])
            ).astype(jnp.bfloat16)


def packed(message, pieces, number):
    across = message.shape[-1] // (2 * BLOCK)
    lanes = pl.ds(number % across * 2 * BLOCK, 2 * BLOCK)
    return message.at[pieces + number // across, :, lanes]


def pack_kernel(factor, pieces, place, cots, mixing, own, *messages):
    for piece in range(pieces):
        base = piece * QUARTERS
        own[piece] = cots[base + place[1] * 2 + place[2]]
        for flip, message in enumerate(messages, 1):
            early, late = flip & 1, flip >> 1
            spot = base + (place[1] ^ early) * 2 + (place[2] ^ late)
            message[piece] = cots[spot]
            for which in range(2):
                if flip == 1:
                    for other in range(2):
                        number = (which * pieces + piece) * 2 + other
                        spot = base + (place[1] ^ early) * 2 + (place[2] ^ other)
                        packed(message, pieces, number)[...] = mixing[factor + which, spot]
                else:
                    number = which * pieces + piece
                    packed(message, pieces, number)[...] = mixing[factor + which, spot]


def mixing_of(factor, which, pieces, piece, place, mixing, messages, quarter, other=0):
    if quarter == 0:
        spot = piece * QUARTERS + place[1] * 2 + (place[2] ^ other)
        return mixing[factor + which, spot]
    message = messages[quarter - 1]
    number = which * pieces + piece
    if quarter == 1:
        number = number * 2 + other
    return packed(message, pieces, number)[...]


def early_kernel(factor, pieces, piece, place, keep, recv, mixing, message, keep_out, send_out):
    weights = functools.partial(mixing_of, factor, 0, pieces, piece, place, mixing, [message])
    for other, out in enumerate((keep_out, send_out)):
        spot = place[2] ^ other
        mine, theirs = keep[spot], recv[spot]
        pair = weights(0, other)
        out[0] = (times(pair[:, :BLOCK], mine) + times(pair[:, BLOCK:], theirs)).astype(
            jnp.bfloat16
        )
        pair = weights(1, other)
        out[1] = (times(pair[:, :BLOCK], theirs) + times(pair[:, BLOCK:], mine)).astype(
            jnp.bfloat16
        )


def late_kernel(factor, pieces, piece, place, keep, recv, mixing, *rest):
    messages, out = rest[:-1], rest[-1]
    values = [keep[0], keep[1], recv[0], recv[1]]
    for quarter in range(QUARTERS):
        pair = mixing_of(factor, 1, pieces, piece, place, mixing, messages, quarter)
        out[quarter] = (
            times(pair[:, :BLOCK], values[quarter]) + times(pair[:, BLOCK:], values[quarter ^ 2])
        ).astype(jnp.bfloat16)


def back_kernel(factor, pieces, piece, cores, place, cots, total, *rest):
    parts, (mixing, message1, message2, message3, *outs) = rest[: cores - 1], rest[cores - 1 :]
    messages = (message1, message2, message3)
    grads = []
    for quarter in range(QUARTERS):
        rows = slice(quarter * BLOCK, (quarter + 1) * BLOCK)
        grad = cots[quarter].astype(jnp.float32) + total[rows]
        for part in parts:
            grad = grad + part[rows].astype(jnp.float32)
        grads.append(grad.astype(jnp.bfloat16))
    for which, flip in ((1, 2), (0, 1)):
        both = [
            times_transposed(
                mixing_of(factor, which, pieces, piece, place, mixing, messages, quarter),
                grads[quarter],
            )
            for quarter in range(QUARTERS)
        ]
        grads = [
            (both[quarter][:BLOCK] + both[quarter ^ flip][BLOCK:]).astype(jnp.bfloat16)
            for quarter in range(QUARTERS)
        ]
    for grad, out in zip(grads, outs):
        out[...] = grad


def regroup_kernel(factor, first, place, *rest):
    quarters, (mixing, own, cross) = rest[:QUARTERS], rest[QUARTERS:]
    for quarter in range(QUARTERS):
        early, late = quarter & 1, quarter >> 1
        spot = (place[1] ^ early) * 2 + (place[2] ^ late)
        both = times_transposed(mixing[factor, first + spot], quarters[quarter][...])
        own[spot] = both[:BLOCK]
        cross[spot] = both[BLOCK:].astype(jnp.bfloat16)


def plain_back_kernel(factor, first, mine, theirs, mixing, own, cross):
    for block in range(mine.shape[0]):
        grad = (mine[block] + theirs[block].astype(jnp.float32)).astype(jnp.bfloat16)
        both = times_transposed(mixing[factor, first + block], grad)
        own[block] = both[:BLOCK]
        cross[block] = both[BLOCK:].astype(jnp.bfloat16)


def exit_kernel(count, pattern, *rest):
    mine, theirs = rest[:count], rest[count : 2 * count]
    mixing, out, here, cross = rest[2 * count :]
    blocks = here.shape[0]
    per_piece = blocks // count
    for factor in reversed(range(LOCAL)):
        for block in range(blocks):
            if factor == LOCAL - 1:
                piece, spot = block // per_piece, block % per_piece
                value = mine[piece][spot] + theirs[piece][spot].astype(jnp.float32)
                value = value.astype(jnp.bfloat16)
            else:
                value = here[block]
            both = times_transposed(mixing[factor, block], value)
            cross[0, block] = both[:BLOCK]
            cross[1, block] = both[BLOCK:]
        for block in range(blocks):
            combined = (cross[0, block] + cross[1, pattern[factor, block]]).astype(jnp.bfloat16)
            if factor == 0:
                out[block * BLOCK : (block + 1) * BLOCK] = combined
            else:
                here[block] = combined


def conv_back_kernel(cells, before, after, taps, out):
    values = cells[...].astype(jnp.float32)
    scale = taps[...].astype(jnp.float32)
    up, down = shifted(
        values, before[...].astype(jnp.float32), after[...].astype(jnp.float32)
    )
    out[...] = (scale[0:1] * down + scale[1:2] * values + scale[2:3] * up).astype(jnp.bfloat16)


def channel_spots(place, count, chans):
    return [
        pl.ds(pl.multiple_of(lax.rem(place[0] + i, count) * chans, chans), chans)
        for i in range(count)
    ]


def tiled_call(kernel, name, outs, place, arrays, grid, scratch, cost):
    return pl.pallas_call(
        kernel,
        out_shape=[jax.ShapeDtypeStruct(shape, kind) for shape, kind, _, _ in outs],
        grid_spec=pltpu.PrefetchScalarGridSpec(
            num_scalar_prefetch=1,
            grid=(grid,),
            in_specs=[pl.BlockSpec(block, index) for _, block, index in arrays],
            out_specs=[pl.BlockSpec(block, index) for _, _, block, index in outs],
            scratch_shapes=scratch,
        ),
        compiler_params=pltpu.CompilerParams(vmem_limit_bytes=VMEM_BYTES),
        cost_estimate=pl.CostEstimate(
            flops=cost[0], bytes_accessed=cost[1], transcendentals=cost[2]
        ),
        name=name,
    )(place, *[array for array, _, _ in arrays])


def still(t, place):
    return (0, 0)


def grad_act_kernel(count, place, *rest):
    cots, (w_out, grad_act, c_all) = rest[:count], rest[count:]
    spots = channel_spots(place, count, cots[0].shape[1])

    @pl.when(pl.program_id(0) == 0)
    def _():
        for i in range(count):
            c_all[:, spots[i]] = cots[i][...]

    grad_act[...] = lax.dot_general(
        c_all[...], w_out[...], ACROSS, preferred_element_type=jnp.float32
    ).astype(grad_act.dtype)


def grad_act_of(place, cots, w_out):
    rows, chans = cots[0].shape
    hidden, width = w_out.shape
    tile = min(TILE, hidden)
    return tiled_call(
        functools.partial(grad_act_kernel, len(cots)),
        "grad_act",
        [((rows, hidden), jnp.bfloat16, (rows, tile), lambda t, place: (0, t))],
        place,
        [(cot, (rows, chans), still) for cot in cots]
        + [(w_out, (tile, width), lambda t, place: (t, 0))],
        hidden // tile,
        [pltpu.VMEM((rows, width), jnp.bfloat16)],
        (2 * rows * width * hidden, 2 * width * hidden, 0),
    )[0]


def hidden_kernel(count, place, *rest):
    mixed, (grad_act, w_in, activation, own) = rest[:count], rest[count : count + 4]
    backs, (x_all, back_sum) = rest[count + 4 : -2], rest[-2:]
    spots = channel_spots(place, count, mixed[0].shape[1])
    step = pl.program_id(0)

    @pl.when(step == 0)
    def _():
        for i in range(count):
            x_all[:, spots[i]] = mixed[i][...]
        back_sum[...] = jnp.zeros_like(back_sum)

    hidden = jnp.dot(x_all[...], w_in[...], preferred_element_type=jnp.float32)
    square = hidden * hidden
    tanh_val = jnp.tanh(root_two_pi * (hidden + 0.044715 * square * hidden))
    half = 0.5 * (1.0 + tanh_val)
    activation[...] = (hidden * half).astype(jnp.bfloat16)
    slope = root_two_pi * (1.0 + 3.0 * 0.044715 * square)
    derivative = half + 0.5 * hidden * (1.0 - tanh_val * tanh_val) * slope
    grad_hidden = (grad_act[...].astype(jnp.float32) * derivative).astype(jnp.bfloat16)
    back_sum[...] += lax.dot_general(
        grad_hidden, w_in[...], ACROSS, preferred_element_type=jnp.float32
    )

    @pl.when(step == pl.num_programs(0) - 1)
    def _():
        own[...] = back_sum[:, spots[0]]
        for i in range(1, count):
            backs[i - 1][...] = back_sum[:, spots[i]].astype(jnp.bfloat16)


def hidden_of(place, mixed, grad_act, w_in):
    count = len(mixed)
    rows, chans = mixed[0].shape
    width, hidden = w_in.shape
    tile = min(TILE, hidden)
    part = ((rows, chans), still)
    column = ((rows, tile), lambda t, place: (0, t))
    return tiled_call(
        functools.partial(hidden_kernel, count),
        "mlp_hidden_and_grad",
        [((rows, hidden), jnp.bfloat16, *column), ((rows, chans), jnp.float32, *part)]
        + [((rows, chans), jnp.bfloat16, *part)] * (count - 1),
        place,
        [(value, *part) for value in mixed]
        + [(grad_act, *column), (w_in, (width, tile), lambda t, place: (0, t))],
        hidden // tile,
        [pltpu.VMEM((rows, width), jnp.bfloat16), pltpu.VMEM((rows, width), jnp.float32)],
        (4 * rows * width * hidden, 2 * width * hidden, rows * hidden),
    )


def out_kernel(place, activation, w_out, own, others):
    step = pl.program_id(0)
    product = jnp.dot(activation[...], w_out[...], preferred_element_type=jnp.float32)

    @pl.when(step == 0)
    def _():
        own[...] = product

    @pl.when(step > 0)
    def _():
        others[0] = product.astype(jnp.bfloat16)


def out_of(place, activation, w_out, cores):
    rows, hidden = activation.shape
    width = w_out.shape[1]
    chans = width // cores
    return tiled_call(
        out_kernel,
        "mlp_out",
        [
            ((rows, chans), jnp.float32, (rows, chans), still),
            (
                (cores - 1, rows, chans),
                jnp.bfloat16,
                (1, rows, chans),
                lambda t, place: (jnp.maximum(t - 1, 0), 0, 0),
            ),
        ],
        place,
        [
            (activation, (rows, hidden), still),
            (w_out, (hidden, chans), lambda t, place: (0, lax.rem(place[0] + t, cores))),
        ],
        cores,
        [],
        (2 * rows * width * hidden, 2 * width * hidden, 0),
    )


def on_device(inputs, conv_weight, mixing, pattern, w_in, w_out, cotangent):
    row_count, chan_count = inputs.shape
    blocks = row_count // BLOCK
    pieces = blocks // QUARTERS
    cores = lax.axis_size("ch")
    levels = lax.axis_size("seq").bit_length() - 1
    plain = list(range(LOCAL, LOCAL + levels - 2))
    last = LOCAL + levels - 2
    early_bit, late_bit = 1 << (levels - 2), 1 << (levels - 1)
    masks = [(i & 1) * early_bit + (i >> 1) * late_bit for i in range(QUARTERS)]
    seat = lax.axis_index("seq")
    place = jnp.stack(
        [lax.axis_index("ch"), seat // early_bit % 2, seat // late_bit % 2]
    ).astype(jnp.int32)
    half = ((2, BLOCK, chan_count), jnp.bfloat16)
    full = ((QUARTERS, BLOCK, chan_count), jnp.bfloat16)
    wide = ((QUARTERS, BLOCK, chan_count), jnp.float32)

    before, after = neighbours(inputs[:1], inputs[-1:], "seq")
    convolved, *states = call(
        entry_kernel,
        "conv_and_local_factors",
        [((row_count, chan_count), jnp.bfloat16)] + [full] * pieces,
        [pattern],
        [inputs, before, after, conv_weight, mixing],
        [pltpu.VMEM((blocks, BLOCK, chan_count), jnp.bfloat16)] * 2,
    )
    per_block = chan_count // (2 * BLOCK)
    lengths = [pieces + -(-pieces * 2 * (1 + (flip == 1)) // per_block) for flip in (1, 2, 3)]
    own_cots, *messages = call(
        functools.partial(pack_kernel, last, pieces),
        "pack",
        [((pieces, BLOCK, chan_count), jnp.bfloat16)]
        + [((length, BLOCK, chan_count), jnp.bfloat16) for length in lengths],
        [place],
        [cotangent.reshape(blocks, BLOCK, chan_count), mixing],
    )
    messages = [from_flipped(m, "seq", mask) for m, mask in zip(messages, masks[1:])]
    stacked = jnp.stack([own_cots] + [m[:pieces] for m in messages], axis=1)
    all_cots = [stacked] + [from_offset(stacked, "ch", i) for i in range(1, cores)]
    piece_rows = QUARTERS * BLOCK
    grad_acts = [
        grad_act_of(place, [c[p].reshape(piece_rows, chan_count) for c in all_cots], w_out)
        for p in range(pieces)
    ]

    for factor in plain:
        for p in range(pieces):
            mates = from_flipped(states[p], "seq", 1 << (factor - LOCAL))
            if factor != plain[-1]:
                (states[p],) = call(
                    functools.partial(plain_kernel, factor, p * QUARTERS),
                    "factor",
                    [full],
                    [],
                    [states[p], mates, mixing],
                )
            else:
                states[p] = call(
                    functools.partial(split_kernel, factor, p * QUARTERS),
                    "factor_and_split",
                    [half, half],
                    [place],
                    [states[p], mates, mixing],
                )
    activations, mixeds, grads = [], [], []
    order = ()
    for p in range(pieces):
        keep, send = states[p]
        keep, send = call(
            functools.partial(early_kernel, last, pieces, p),
            "early_factor",
            [half, half],
            [place],
            [keep, from_flipped(send, "seq", early_bit), mixing, messages[0]],
        )
        (mixed,) = call(
            functools.partial(late_kernel, last, pieces, p),
            "late_factor",
            [full],
            [place],
            [keep, from_flipped(send, "seq", late_bit), mixing, *messages],
            order=order,
        )
        mixed = mixed.reshape(piece_rows, chan_count)
        gathered = [mixed] + [from_offset(mixed, "ch", i) for i in range(1, cores)]
        activation, own, *parts = hidden_of(place, gathered, grad_acts[p], w_in)
        order = (own,)
        parts = [from_offset(part, "ch", cores - i) for i, part in enumerate(parts, 1)]
        quarters = call(
            functools.partial(back_kernel, last, pieces, p, cores),
            "late_and_early_back",
            [((BLOCK, chan_count), jnp.bfloat16)] * QUARTERS,
            [place],
            [stacked[p], own, *parts, mixing, *messages],
        )
        quarters = [
            from_flipped(grad, "seq", mask) if mask else grad
            for grad, mask in zip(quarters, masks)
        ]
        grads.append(
            call(
                functools.partial(regroup_kernel, plain[-1], p * QUARTERS),
                "regroup_and_factor_back",
                [wide, full],
                [place],
                [*quarters, mixing],
            )
        )
        mixeds.append(mixed)
        activations.append(activation)
    for factor in reversed(plain):
        for p in range(pieces):
            mine, cross = grads[p]
            theirs = from_flipped(cross, "seq", 1 << (factor - LOCAL))
            if factor != plain[0]:
                grads[p] = call(
                    functools.partial(plain_back_kernel, factor - 1, p * QUARTERS),
                    "factor_back",
                    [wide, full],
                    [],
                    [mine, theirs, mixing],
                )
            else:
                grads[p] = (mine, theirs)
    (grad_conv,) = call(
        functools.partial(exit_kernel, pieces),
        "local_factors_back",
        [((row_count, chan_count), jnp.bfloat16)],
        [pattern],
        [g[0] for g in grads] + [g[1] for g in grads] + [mixing],
        [
            pltpu.VMEM((blocks, BLOCK, chan_count), jnp.bfloat16),
            pltpu.VMEM((2, blocks, BLOCK, chan_count), jnp.float32),
        ],
    )
    outs = []
    for p in range(pieces):
        own, others = out_of(place, activations[p], w_out, cores)
        out = mixeds[p].astype(jnp.float32) + own
        for i in range(1, cores):
            out = out + from_offset(others[i - 1], "ch", cores - i).astype(jnp.float32)
        outs.append(out.astype(jnp.bfloat16).reshape(QUARTERS, BLOCK, chan_count))
    outs = jnp.stack(outs, axis=1)
    arrived = jnp.stack(
        [from_flipped(outs[i], "seq", mask) if mask else outs[i] for i, mask in enumerate(masks)]
    )
    spots = jnp.arange(QUARTERS, dtype=jnp.int32) ^ (place[1] * 2 + place[2])
    swap = jnp.stack([spots // 2 % 2, spots % 2])
    layer_out = jnp.take(arrived, swap[0] + 2 * swap[1], axis=0)
    layer_out = layer_out.transpose(1, 0, 2, 3).reshape(row_count, chan_count)

    before, after = neighbours(grad_conv[:1], grad_conv[-1:], "seq")
    (grad_input,) = call(
        conv_back_kernel,
        "conv_back",
        [((row_count, chan_count), jnp.bfloat16)],
        [],
        [grad_conv, before, after, conv_weight],
    )
    return (layer_out, convolved, grad_input)


def solution(mesh):
    return jax.shard_map(
        on_device,
        mesh=mesh,
        in_specs=(
            P("seq", "ch"),
            P(None, "ch"),
            P(None, "seq", None, None),
            P(None, "seq"),
            P(None, "ch"),
            P("ch", None),
            P("seq", "ch"),
        ),
        out_specs=(P("seq", "ch"), P("seq", "ch"), P("seq", "ch")),
        check_vma=False,
    )
```

```python
import functools

import jax
import jax.numpy as jnp
from jax import lax
from jax.experimental import pallas as pl
from jax.experimental.pallas import tpu as pltpu
from jax.sharding import PartitionSpec as P

BLOCK = 64
LOCAL = 2
QUARTERS = 4
TILE = 512
SMALL = 8 * 1024 * 1024
LARGE = 20 * 1024 * 1024

root_two_pi = 0.7978845608028654

IN_SMEM = pl.BlockSpec(memory_space=pltpu.SMEM)
IN_VMEM = pl.BlockSpec(memory_space=pltpu.VMEM)
ANYWHERE = pl.BlockSpec(memory_space=pl.ANY)
ACROSS = (((1,), (1,)), ((), ()))
OVER_ROWS = (((0,), (0,)), ((), ()))


def times(weights, value):
    return jnp.dot(weights, value, preferred_element_type=jnp.float32)


def times_transposed(weights, value):
    return lax.dot_general(weights, value, OVER_ROWS, preferred_element_type=jnp.float32)


def neighbours(first, last, axis):
    count = lax.axis_size(axis)
    ends = count - 1
    before = lax.ppermute(last, axis, [(i, (i + 1) % count) for i in range(ends)])
    after = lax.ppermute(first, axis, [((i + 1) % count, i) for i in range(ends)])
    return before, after


def from_flipped(block, axis, mask):
    count = lax.axis_size(axis)
    return lax.ppermute(block, axis, [(i, i ^ mask) for i in range(count)])


def from_offset(block, axis, offset):
    count = lax.axis_size(axis)
    return lax.ppermute(block, axis, [((i + offset) % count, i) for i in range(count)])


def call(kernel, name, outs, arrays, scalars=(), scratch=(), order=(), limit=SMALL):
    count = len(scalars) + len(arrays)

    def body(*refs):
        kernel(*refs[:count], *refs[count + len(order) :])

    return pl.pallas_call(
        body,
        out_shape=[jax.ShapeDtypeStruct(shape, kind) for shape, kind in outs],
        in_specs=[IN_SMEM] * len(scalars) + [IN_VMEM] * len(arrays) + [ANYWHERE] * len(order),
        out_specs=[IN_VMEM] * len(outs),
        scratch_shapes=list(scratch),
        compiler_params=pltpu.CompilerParams(vmem_limit_bytes=limit),
        cost_estimate=pl.CostEstimate(flops=0, bytes_accessed=0, transcendentals=0),
        name=name,
    )(*scalars, *arrays, *order)


def own_bits():
    seat = lax.axis_index("seq")
    levels = lax.axis_size("seq").bit_length() - 1
    return (seat >> (levels - 2)) & 1, (seat >> (levels - 1)) & 1


def shifted(cells, before, after):
    rows = cells.shape[0]
    spot = lax.broadcasted_iota(jnp.int32, cells.shape, 0)
    up = jnp.where(spot == 0, before, pltpu.roll(cells, 1, 0))
    down = jnp.where(spot == rows - 1, after, pltpu.roll(cells, rows - 1, 0))
    return up, down


def chosen_blocks(sub):
    early, late = own_bits()
    first = sub // 2 * QUARTERS
    spot = early ^ (1 - sub % 2)
    return [first + spot * 2 + (late ^ other) for other in range(2)]


def local_factor(factor, pattern, source, mixing, target, chosen):
    for spot, block in enumerate(chosen):
        pair = mixing[factor, block]
        target[spot] = (
            times(pair[:, :BLOCK], source[block])
            + times(pair[:, BLOCK:], source[pattern[factor, block]])
        ).astype(jnp.bfloat16)


def entry_kernel(pattern, cells, before, after, taps, mixing, conv_ref, between, *rest):
    subs, first = rest[:-1], rest[-1]
    values = cells[...].astype(jnp.float32)
    scale = taps[...].astype(jnp.float32)
    up, down = shifted(
        values, before[...].astype(jnp.float32), after[...].astype(jnp.float32)
    )
    convolved = (scale[0:1] * up + scale[1:2] * values + scale[2:3] * down).astype(jnp.bfloat16)
    conv_ref[...] = convolved
    first[...] = convolved.reshape(first.shape)
    every = range(first.shape[0])
    refs = (first, between)
    for factor in range(LOCAL - 1):
        local_factor(factor, pattern, refs[factor % 2], mixing, refs[1 - factor % 2], every)
    if LOCAL % 2:
        between[...] = first[...]
    for number, sub in enumerate(subs):
        local_factor(LOCAL - 1, pattern, between, mixing, sub, chosen_blocks(number))


def entry_rest_kernel(number, pattern, between, mixing, sub):
    local_factor(LOCAL - 1, pattern, between, mixing, sub, chosen_blocks(number))


def plain_kernel(factor, number, state, mates, mixing, out):
    for spot, block in enumerate(chosen_blocks(number)):
        pair = mixing[factor, block]
        out[spot] = (
            times(pair[:, :BLOCK], state[spot]) + times(pair[:, BLOCK:], mates[spot])
        ).astype(jnp.bfloat16)


def packed(message, pieces, number):
    across = message.shape[-1] // (2 * BLOCK)
    lanes = pl.ds(number % across * 2 * BLOCK, 2 * BLOCK)
    return message.at[pieces + number // across, :, lanes]


def pack_kernel(factor, pieces, cots, mixing, own, *messages):
    my_early, my_late = own_bits()
    for piece in range(pieces):
        base = piece * QUARTERS
        own[piece] = cots[base + my_early * 2 + my_late]
        for flip, message in enumerate(messages, 1):
            early, late = my_early ^ (flip & 1), my_late ^ (flip >> 1)
            message[piece] = cots[base + early * 2 + late]
            for which in range(2):
                number = which * pieces + piece
                if flip == 1:
                    for other in range(2):
                        packed(message, pieces, number * 2 + other)[...] = mixing[
                            factor + which, base + early * 2 + (late ^ other)
                        ]
                else:
                    packed(message, pieces, number)[...] = mixing[
                        factor + which, base + early * 2 + late
                    ]


def stack_kernel(pieces, *rest):
    quarters, outs = rest[:QUARTERS], rest[QUARTERS:]
    for piece, out in enumerate(outs):
        for quarter, values in enumerate(quarters):
            out[quarter * BLOCK : (quarter + 1) * BLOCK] = values[piece]


def mixing_of(factor, which, pieces, piece, mixing, messages, quarter, other=0):
    if quarter == 0:
        early, late = own_bits()
        return mixing[factor + which, piece * QUARTERS + early * 2 + (late ^ other)]
    number = which * pieces + piece
    if quarter == 1:
        number = number * 2 + other
    return packed(messages[quarter - 1], pieces, number)[...]


def early_kernel(factor, pieces, piece, keep, recv, mixing, message, keep_out, send_out):
    weights = functools.partial(mixing_of, factor, 0, pieces, piece, mixing, [message])
    for other, out in enumerate((keep_out, send_out)):
        mine, theirs = keep[other], recv[other]
        pair = weights(0, other)
        out[0] = (times(pair[:, :BLOCK], mine) + times(pair[:, BLOCK:], theirs)).astype(
            jnp.bfloat16
        )
        pair = weights(1, other)
        out[1] = (times(pair[:, :BLOCK], theirs) + times(pair[:, BLOCK:], mine)).astype(
            jnp.bfloat16
        )


def late_kernel(factor, pieces, piece, keep, recv, mixing, *rest):
    messages, out = rest[:-1], rest[-1]
    values = [keep[0], keep[1], recv[0], recv[1]]
    for quarter in range(QUARTERS):
        pair = mixing_of(factor, 1, pieces, piece, mixing, messages, quarter)
        out[quarter] = (
            times(pair[:, :BLOCK], values[quarter]) + times(pair[:, BLOCK:], values[quarter ^ 2])
        ).astype(jnp.bfloat16)


def back_kernel(factor, pieces, piece, cores, cots, total, *rest):
    count = (cores - 1) * QUARTERS
    parts, (mixing, message1, message2, message3, *outs) = rest[:count], rest[count:]
    messages = (message1, message2, message3)
    grads = []
    for quarter in range(QUARTERS):
        rows = slice(quarter * BLOCK, (quarter + 1) * BLOCK)
        grad = cots[rows].astype(jnp.float32) + total[rows]
        for part in parts[quarter::QUARTERS]:
            grad = grad + part[...].astype(jnp.float32)
        grads.append(grad.astype(jnp.bfloat16))
    for which, flip in ((1, 2), (0, 1)):
        both = [
            times_transposed(
                mixing_of(factor, which, pieces, piece, mixing, messages, quarter),
                grads[quarter],
            )
            for quarter in range(QUARTERS)
        ]
        grads = [
            (both[quarter][:BLOCK] + both[quarter ^ flip][BLOCK:]).astype(jnp.bfloat16)
            for quarter in range(QUARTERS)
        ]
    for grad, out in zip(grads, outs):
        out[...] = grad


def regroup_kernel(factor, number, one, other, mixing, own, cross):
    for spot, block in enumerate(chosen_blocks(number)):
        both = times_transposed(mixing[factor, block], (one, other)[spot][...])
        own[spot] = both[:BLOCK]
        cross[spot] = both[BLOCK:].astype(jnp.bfloat16)


def plain_back_kernel(factor, number, mine, theirs, mixing, own, cross):
    for spot, block in enumerate(chosen_blocks(number)):
        grad = (mine[spot] + theirs[spot].astype(jnp.float32)).astype(jnp.bfloat16)
        both = times_transposed(mixing[factor, block], grad)
        own[spot] = both[:BLOCK]
        cross[spot] = both[BLOCK:].astype(cross.dtype)


def exit_kernel(count, pattern, *rest):
    mine, theirs = rest[:count], rest[count : 2 * count]
    mixing, out, own, cross = rest[2 * count :]
    blocks = own.shape[0]
    for number in range(count):
        for spot, block in enumerate(chosen_blocks(number)):
            own[block] = mine[number][spot]
            cross[block] = theirs[number][spot]
    for factor in reversed(range(LOCAL)):
        for block in range(blocks):
            own[block] += cross[pattern[factor, block]]
        for block in range(blocks):
            grad = own[block].astype(jnp.bfloat16)
            if factor == 0:
                out[block * BLOCK : (block + 1) * BLOCK] = grad
            else:
                both = times_transposed(mixing[factor - 1, block], grad)
                own[block] = both[:BLOCK]
                cross[block] = both[BLOCK:]


def conv_back_kernel(cells, before, after, taps, out):
    values = cells[...].astype(jnp.float32)
    scale = taps[...].astype(jnp.float32)
    up, down = shifted(
        values, before[...].astype(jnp.float32), after[...].astype(jnp.float32)
    )
    out[...] = (scale[0:1] * down + scale[1:2] * values + scale[2:3] * up).astype(jnp.bfloat16)


def channel_spots(count, chans):
    core = lax.axis_index("ch")
    return [
        pl.ds(pl.multiple_of(lax.rem(core + i, count) * chans, chans), chans)
        for i in range(count)
    ]


def grad_act_kernel(count, *rest):
    cots, (w_out, grad_act, c_all) = rest[:count], rest[count:]
    for spot, cot in zip(channel_spots(count, cots[0].shape[1]), cots):
        c_all[:, spot] = cot[...]
    hidden = w_out.shape[0]
    tile = min(TILE, hidden)
    for start in range(0, hidden, tile):
        grad_act[:, start : start + tile] = lax.dot_general(
            c_all[...], w_out[start : start + tile], ACROSS, preferred_element_type=jnp.float32
        ).astype(grad_act.dtype)


def hidden_kernel(count, *rest):
    mixed, (grad_act, w_in, activation, own) = rest[:count], rest[count : count + 4]
    backs, (x_all, back_sum) = rest[count + 4 : -2], rest[-2:]
    spots = channel_spots(count, mixed[0].shape[1])
    for spot, value in zip(spots, mixed):
        x_all[:, spot] = value[...]
    size = w_in.shape[1]
    tile = min(TILE, size)
    for start in range(0, size, tile):
        tiles = slice(start, start + tile)
        hidden = times(x_all[...], w_in[:, tiles])
        square = hidden * hidden
        tanh_val = jnp.tanh(hidden * (root_two_pi + root_two_pi * 0.044715 * square))
        half = 0.5 + 0.5 * tanh_val
        gelu = hidden * half
        activation[:, tiles] = gelu.astype(jnp.bfloat16)
        slope = 2.0 * root_two_pi + 6.0 * root_two_pi * 0.044715 * square
        derivative = half + gelu * (1.0 - half) * slope
        grad_hidden = (grad_act[:, tiles].astype(jnp.float32) * derivative).astype(jnp.bfloat16)
        back = lax.dot_general(
            grad_hidden, w_in[:, tiles], ACROSS, preferred_element_type=jnp.float32
        )
        if start == 0:
            back_sum[...] = back
        else:
            back_sum[...] += back
    own[...] = back_sum[:, spots[0]]
    for i, spot in enumerate(spots[1:]):
        for quarter in range(QUARTERS):
            rows = slice(quarter * BLOCK, (quarter + 1) * BLOCK)
            backs[i * QUARTERS + quarter][...] = back_sum[rows, spot].astype(jnp.bfloat16)


def out_kernel(count, pieces, *rest):
    activations, mixed = rest[:pieces], rest[pieces : 2 * pieces]
    w_out, own, *others = rest[2 * pieces :]
    rows, chans = mixed[0].shape
    for i, spot in enumerate(channel_spots(count, chans)):
        for piece in range(pieces):
            product = times(activations[piece][...], w_out[:, spot])
            if i == 0:
                part = slice(piece * rows, (piece + 1) * rows)
                own[part] = mixed[piece][...].astype(jnp.float32) + product
            else:
                others[(i - 1) * pieces + piece][...] = product.astype(jnp.bfloat16)


def combine_kernel(cores, pieces, own, *rest):
    parts, outs = rest[: (cores - 1) * pieces], rest[(cores - 1) * pieces :]
    for piece in range(pieces):
        for quarter, out in enumerate(outs):
            start = quarter * BLOCK
            total = own[pl.ds(piece * QUARTERS * BLOCK + start, BLOCK)]
            for part in parts[piece::pieces]:
                total = total + part[start : start + BLOCK].astype(jnp.float32)
            out[piece] = total.astype(jnp.bfloat16)


def assemble_kernel(pieces, *rest):
    quarters, out = rest[:-1], rest[-1]
    my_early, my_late = own_bits()
    for quarter, values in enumerate(quarters):
        spot = (my_early ^ (quarter & 1)) * 2 + (my_late ^ (quarter >> 1))
        for piece in range(pieces):
            start = pl.multiple_of((piece * QUARTERS + spot) * BLOCK, BLOCK)
            out[pl.ds(start, BLOCK)] = values[piece]


def on_device(inputs, conv_weight, mixing, pattern, w_in, w_out, cotangent):
    row_count, chan_count = inputs.shape
    blocks = row_count // BLOCK
    pieces = blocks // QUARTERS
    width, hidden = w_in.shape
    cores = lax.axis_size("ch")
    levels = lax.axis_size("seq").bit_length() - 1
    plain = list(range(LOCAL, LOCAL + levels - 2))
    last = LOCAL + levels - 2
    early_bit, late_bit = 1 << (levels - 2), 1 << (levels - 1)
    masks = [(i & 1) * early_bit + (i >> 1) * late_bit for i in range(QUARTERS)]
    half = ((2, BLOCK, chan_count), jnp.bfloat16)
    full = ((QUARTERS, BLOCK, chan_count), jnp.bfloat16)
    half_wide = ((2, BLOCK, chan_count), jnp.float32)
    whole = ((row_count, chan_count), jnp.bfloat16)
    piece_rows = QUARTERS * BLOCK
    flat = (piece_rows, chan_count)
    block = ((BLOCK, chan_count), jnp.bfloat16)
    flat_piece = (flat, jnp.bfloat16)
    flops = 2 * piece_rows * width * hidden

    latest = []

    def run(kernel, name, outs, arrays, *args, **kwargs):
        results = call(kernel, name, outs, arrays, *args, order=tuple(latest), **kwargs)
        latest[:] = results[:1]
        return results

    before, after = neighbours(inputs[:1], inputs[-1:], "seq")
    per_block = chan_count // (2 * BLOCK)
    lengths = [pieces + -(-pieces * 2 * (1 + (flip == 1)) // per_block) for flip in (1, 2, 3)]
    own_cots, *messages = run(
        functools.partial(pack_kernel, last, pieces),
        "pack",
        [((pieces, BLOCK, chan_count), jnp.bfloat16)]
        + [((length, BLOCK, chan_count), jnp.bfloat16) for length in lengths],
        [cotangent.reshape(blocks, BLOCK, chan_count), mixing],
    )
    messages = [from_flipped(m, "seq", mask) for m, mask in zip(messages, masks[1:])]
    convolved, between, *states = run(
        entry_kernel,
        "conv_and_local_factors",
        [whole, ((blocks, BLOCK, chan_count), jnp.bfloat16), half, half],
        [inputs, before, after, conv_weight, mixing],
        [pattern],
        [pltpu.VMEM((blocks, BLOCK, chan_count), jnp.bfloat16)],
    )
    subs = 2 * pieces
    states += [None] * (subs - 2)
    stacked = [None] * pieces
    all_cots = [None] * pieces
    grad_acts = [None] * pieces
    parts = [None] * pieces
    mixeds = [None] * pieces
    activations = [None] * pieces
    owns = [None] * pieces

    def entry_rest(s):
        (states[s],) = run(
            functools.partial(entry_rest_kernel, s),
            "local_factor",
            [half],
            [between, mixing],
            [pattern],
        )

    def stack():
        stacked[:] = run(
            functools.partial(stack_kernel, pieces),
            "stack",
            [flat_piece] * pieces,
            [own_cots, *messages],
        )
        for p, piece in enumerate(stacked):
            all_cots[p] = [piece] + [from_offset(piece, "ch", i) for i in range(1, cores)]

    def grad_act(p):
        (grad_acts[p],) = run(
            functools.partial(grad_act_kernel, cores),
            "grad_act",
            [((piece_rows, hidden), jnp.bfloat16)],
            [*all_cots[p], w_out],
            scratch=[pltpu.VMEM((piece_rows, width), jnp.bfloat16)],
            limit=LARGE,
        )

    def plain_factor(factor, s):
        mates = from_flipped(states[s], "seq", 1 << (factor - LOCAL))
        (states[s],) = run(
            functools.partial(plain_kernel, factor, s),
            "factor",
            [half],
            [states[s], mates, mixing],
        )

    def early_factor(p):
        send, keep = states[2 * p : 2 * p + 2]
        states[2 * p : 2 * p + 2] = run(
            functools.partial(early_kernel, last, pieces, p),
            "early_factor",
            [half, half],
            [keep, from_flipped(send, "seq", early_bit), mixing, messages[0]],
        )

    def late_factor(p):
        keep, send = states[2 * p : 2 * p + 2]
        (mixed,) = run(
            functools.partial(late_kernel, last, pieces, p),
            "late_factor",
            [full],
            [keep, from_flipped(send, "seq", late_bit), mixing, *messages],
        )
        mixeds[p] = mixed.reshape(flat)

    def hidden_and_grad(p):
        gathered = [mixeds[p]] + [from_offset(mixeds[p], "ch", i) for i in range(1, cores)]
        activations[p], owns[p], *backs = run(
            functools.partial(hidden_kernel, cores),
            "mlp_hidden_and_grad",
            [((piece_rows, hidden), jnp.bfloat16), (flat, jnp.float32)]
            + [block] * ((cores - 1) * QUARTERS),
            [*gathered, grad_acts[p], w_in],
            scratch=[
                pltpu.VMEM((piece_rows, width), jnp.bfloat16),
                pltpu.VMEM((piece_rows, width), jnp.float32),
            ],
            limit=LARGE,
        )
        parts[p] = [
            from_offset(back, "ch", cores - 1 - i // QUARTERS) for i, back in enumerate(backs)
        ]

    def transposed_back(p):
        quarters = run(
            functools.partial(back_kernel, last, pieces, p, cores),
            "late_and_early_back",
            [block] * QUARTERS,
            [stacked[p], owns[p], *parts[p], mixing, *messages],
        )
        quarters = [
            from_flipped(grad, "seq", mask) if mask else grad
            for grad, mask in zip(quarters, masks)
        ]
        states[2 * p : 2 * p + 2] = [quarters[1::2], quarters[0::2]]

    def regroup(s):
        states[s] = run(
            functools.partial(regroup_kernel, plain[-1], s),
            "regroup_and_factor_back",
            [half_wide, half],
            [*states[s], mixing],
        )

    def plain_back(factor, s):
        mine, cross = states[s]
        theirs = from_flipped(cross, "seq", 1 << (factor - LOCAL))
        states[s] = run(
            functools.partial(plain_back_kernel, factor - 1, s),
            "factor_back",
            [half_wide, half if factor != plain[0] else half_wide],
            [mine, theirs, mixing],
        )

    waves = sorted((s + 2 * i, -i, s) for i in range(len(plain)) for s in range(subs))
    for _, i, s in waves:
        if i == 0 and s + 2 < subs:
            entry_rest(s + 2)
        plain_factor(plain[-i], s)
        if plain[-i] == plain[-1] and s % 2:
            early_factor(s // 2)
        if i == 0 and s == 1:
            stack()
        if plain[-i] == plain[-1] and s == subs - 2:
            grad_act(0)
    late_factor(0)
    for p in range(pieces):
        hidden_and_grad(p)
        if p + 1 < pieces:
            grad_act(p + 1)
            late_factor(p + 1)
        if p == 1:
            regroup(1)
            regroup(0)
        transposed_back(p)
    own, *others = run(
        functools.partial(out_kernel, cores, pieces),
        "mlp_out",
        [((row_count, chan_count), jnp.float32)] + [flat_piece] * ((cores - 1) * pieces),
        [*activations, *mixeds, w_out],
        limit=LARGE,
    )
    others = [
        from_offset(other, "ch", cores - 1 - i // pieces) for i, other in enumerate(others)
    ]
    outs = None
    waves = []
    for s in range(subs):
        wave = s // 2 * 4 + 1 - s % 2
        waves += [(wave + 2 * i, i, s) for i in range(0 if s < 2 else -1, len(plain))]
    for wave, i, s in sorted(waves):
        if outs is None and wave > 5:
            outs = run(
                functools.partial(combine_kernel, cores, pieces),
                "combine",
                [((pieces, BLOCK, chan_count), jnp.bfloat16)] * QUARTERS,
                [own, *others],
            )
        if i < 0:
            regroup(s)
        else:
            plain_back(plain[-1 - i], s)
    arrived = [from_flipped(out, "seq", mask) if mask else out for out, mask in zip(outs, masks)]
    (grad_conv,) = run(
        functools.partial(exit_kernel, subs),
        "local_factors_back",
        [whole],
        [g[0] for g in states] + [g[1] for g in states] + [mixing],
        [pattern],
        [pltpu.VMEM((blocks, BLOCK, chan_count), jnp.float32)] * 2,
        limit=LARGE,
    )
    (layer_out,) = run(
        functools.partial(assemble_kernel, pieces), "assemble", [whole], arrived
    )
    before, after = neighbours(grad_conv[:1], grad_conv[-1:], "seq")
    (grad_input,) = run(
        conv_back_kernel, "conv_back", [whole], [grad_conv, before, after, conv_weight]
    )
    return (layer_out, convolved, grad_input)


def solution(mesh):
    return jax.shard_map(
        on_device,
        mesh=mesh,
        in_specs=(
            P("seq", "ch"),
            P(None, "ch"),
            P(None, "seq", None, None),
            P(None, "seq"),
            P(None, "ch"),
            P("ch", None),
            P("seq", "ch"),
        ),
        out_specs=(P("seq", "ch"), P("seq", "ch"), P("seq", "ch")),
        check_vma=False,
    )
```

```python
import functools

import jax
import jax.numpy as jnp
from jax import lax
from jax.experimental import pallas as pl
from jax.experimental.pallas import tpu as pltpu
from jax.sharding import PartitionSpec as P

BLOCK = 64
LOCAL = 2
QUARTERS = 4
TILE = 512
SMALL = 8 * 1024 * 1024
LARGE = 20 * 1024 * 1024
ALL = 44 * 1024 * 1024

root_two_pi = 0.7978845608028654

IN_HBM = pl.BlockSpec(memory_space=pltpu.HBM)
IN_VMEM = pl.BlockSpec(memory_space=pltpu.VMEM)
ANYWHERE = pl.BlockSpec(memory_space=pl.ANY)
ACROSS = (((1,), (1,)), ((), ()))
OVER_ROWS = (((0,), (0,)), ((), ()))


def times(weights, value):
    return jnp.dot(weights, value, preferred_element_type=jnp.float32)


def times_transposed(weights, value):
    return lax.dot_general(weights, value, OVER_ROWS, preferred_element_type=jnp.float32)


def neighbours(first, last, axis):
    count = lax.axis_size(axis)
    ends = count - 1
    before = lax.ppermute(last, axis, [(i, (i + 1) % count) for i in range(ends)])
    after = lax.ppermute(first, axis, [((i + 1) % count, i) for i in range(ends)])
    return before, after


def from_flipped(block, axis, mask):
    count = lax.axis_size(axis)
    return lax.ppermute(block, axis, [(i, i ^ mask) for i in range(count)])


def from_offset(block, axis, offset):
    count = lax.axis_size(axis)
    return lax.ppermute(block, axis, [((i + offset) % count, i) for i in range(count)])


def call(kernel, name, outs, arrays, distant=(), scratch=(), order=(), limit=SMALL):
    count = len(distant) + len(arrays)

    def body(*refs):
        kernel(*refs[:count], *refs[count + len(order) :])

    return pl.pallas_call(
        body,
        out_shape=[jax.ShapeDtypeStruct(shape, kind) for shape, kind in outs],
        in_specs=[IN_HBM] * len(distant) + [IN_VMEM] * len(arrays) + [ANYWHERE] * len(order),
        out_specs=[IN_VMEM] * len(outs),
        scratch_shapes=list(scratch),
        compiler_params=pltpu.CompilerParams(vmem_limit_bytes=limit),
        cost_estimate=pl.CostEstimate(flops=0, bytes_accessed=0, transcendentals=0),
        name=name,
    )(*distant, *arrays, *order)


def own_bits():
    seat = lax.axis_index("seq")
    levels = lax.axis_size("seq").bit_length() - 1
    return (seat >> (levels - 2)) & 1, (seat >> (levels - 1)) & 1


def shifted(cells, before, after):
    rows = cells.shape[0]
    spot = lax.broadcasted_iota(jnp.int32, cells.shape, 0)
    up = jnp.where(spot == 0, before, pltpu.roll(cells, 1, 0))
    down = jnp.where(spot == rows - 1, after, pltpu.roll(cells, rows - 1, 0))
    return up, down


def chosen_blocks(sub):
    early, late = own_bits()
    first = sub // 2 * QUARTERS
    spot = early ^ (1 - sub % 2)
    return [first + spot * 2 + (late ^ other) for other in range(2)]


def local_factor(factor, pattern, source, mixing, target, chosen):
    for spot, block in enumerate(chosen):
        pair = mixing[factor, block]
        target[spot] = (
            times(pair[:, :BLOCK], source[block])
            + times(pair[:, BLOCK:], source[pattern[factor, block]])
        ).astype(jnp.bfloat16)


def entry_kernel(pattern_far, cells, before, after, taps, mixing, conv_ref, *rest):
    subs, (first, between, pattern, arrival) = rest[:-4], rest[-4:]
    fetch = pltpu.make_async_copy(pattern_far, pattern, arrival)
    fetch.start()
    values = cells[...].astype(jnp.float32)
    scale = taps[...].astype(jnp.float32)
    up, down = shifted(
        values, before[...].astype(jnp.float32), after[...].astype(jnp.float32)
    )
    convolved = (scale[0:1] * up + scale[1:2] * values + scale[2:3] * down).astype(jnp.bfloat16)
    conv_ref[...] = convolved
    first[...] = convolved.reshape(first.shape)
    fetch.wait()
    every = range(first.shape[0])
    refs = (first, between)
    for factor in range(LOCAL - 1):
        local_factor(factor, pattern, refs[factor % 2], mixing, refs[1 - factor % 2], every)
    source = refs[(LOCAL - 1) % 2]
    for number, sub in enumerate(subs):
        local_factor(LOCAL - 1, pattern, source, mixing, sub, chosen_blocks(number))


def plain_kernel(factor, number, state, mates, mixing, out):
    for spot, block in enumerate(chosen_blocks(number)):
        pair = mixing[factor, block]
        out[spot] = (
            times(pair[:, :BLOCK], state[spot]) + times(pair[:, BLOCK:], mates[spot])
        ).astype(jnp.bfloat16)


def packed(message, pieces, number):
    across = message.shape[-1] // (2 * BLOCK)
    lanes = pl.ds(number % across * 2 * BLOCK, 2 * BLOCK)
    return message.at[pieces + number // across, :, lanes]


def load_kernel(factor, pieces, length, cots_far, mixing_far, cells_far, taps_far, *rest):
    own, message1, message2, mixing, cells, taps, cots, arrivals = rest
    fetches = [
        pltpu.make_async_copy(far, near, arrivals.at[i])
        for i, (far, near) in enumerate(
            ((mixing_far, mixing), (cots_far, cots), (cells_far, cells), (taps_far, taps))
        )
    ]
    for fetch in fetches:
        fetch.start()
    fetches[0].wait()
    fetches[1].wait()
    my_early, my_late = own_bits()
    for piece in range(pieces):
        base = piece * QUARTERS
        own[piece] = cots[base + my_early * 2 + my_late]
        for flip in (1, 2, 3):
            early, late = my_early ^ (flip & 1), my_late ^ (flip >> 1)
            message = message1 if flip == 1 else message2.at[pl.ds((flip - 2) * length, length)]
            message[piece] = cots[base + early * 2 + late]
            for which in range(2):
                number = which * pieces + piece
                if flip == 1:
                    for other in range(2):
                        packed(message, pieces, number * 2 + other)[...] = mixing[
                            factor + which, base + early * 2 + (late ^ other)
                        ]
                else:
                    packed(message, pieces, number)[...] = mixing[
                        factor + which, base + early * 2 + late
                    ]
    fetches[2].wait()
    fetches[3].wait()


def forward_kernel(message, out):
    length = out.shape[0]
    out[...] = message[length:]


def stack_kernel(pieces, *rest):
    quarters, outs = rest[:QUARTERS], rest[QUARTERS:]
    for piece, out in enumerate(outs):
        for quarter, values in enumerate(quarters):
            out[quarter * BLOCK : (quarter + 1) * BLOCK] = values[piece]


def mixing_of(factor, which, pieces, piece, mixing, messages, quarter, other=0):
    if quarter == 0:
        early, late = own_bits()
        return mixing[factor + which, piece * QUARTERS + early * 2 + (late ^ other)]
    number = which * pieces + piece
    if quarter == 1:
        number = number * 2 + other
    return packed(messages[quarter - 1], pieces, number)[...]


def early_kernel(factor, pieces, piece, keep, recv, mixing, message, keep_out, send_out):
    weights = functools.partial(mixing_of, factor, 0, pieces, piece, mixing, [message])
    for other, out in enumerate((keep_out, send_out)):
        mine, theirs = keep[other], recv[other]
        pair = weights(0, other)
        out[0] = (times(pair[:, :BLOCK], mine) + times(pair[:, BLOCK:], theirs)).astype(
            jnp.bfloat16
        )
        pair = weights(1, other)
        out[1] = (times(pair[:, :BLOCK], theirs) + times(pair[:, BLOCK:], mine)).astype(
            jnp.bfloat16
        )


def late_kernel(factor, pieces, piece, keep, recv, mixing, *rest):
    messages, out = rest[:-1], rest[-1]
    values = [keep[0], keep[1], recv[0], recv[1]]
    for quarter in range(QUARTERS):
        pair = mixing_of(factor, 1, pieces, piece, mixing, messages, quarter)
        out[quarter] = (
            times(pair[:, :BLOCK], values[quarter]) + times(pair[:, BLOCK:], values[quarter ^ 2])
        ).astype(jnp.bfloat16)


def back_kernel(factor, pieces, piece, cores, cots, total, *rest):
    count = (cores - 1) * QUARTERS
    parts, (mixing, message1, message2, message3, *outs) = rest[:count], rest[count:]
    messages = (message1, message2, message3)
    grads = []
    for quarter in range(QUARTERS):
        rows = slice(quarter * BLOCK, (quarter + 1) * BLOCK)
        grad = cots[rows].astype(jnp.float32) + total[rows]
        for part in parts[quarter::QUARTERS]:
            grad = grad + part[...].astype(jnp.float32)
        grads.append(grad.astype(jnp.bfloat16))
    for which, flip in ((1, 2), (0, 1)):
        both = [
            times_transposed(
                mixing_of(factor, which, pieces, piece, mixing, messages, quarter),
                grads[quarter],
            )
            for quarter in range(QUARTERS)
        ]
        grads = [
            (both[quarter][:BLOCK] + both[quarter ^ flip][BLOCK:]).astype(jnp.bfloat16)
            for quarter in range(QUARTERS)
        ]
    keep, send = outs
    for spot in range(2):
        keep[spot] = grads[spot]
        send[spot] = grads[2 + spot]


def regroup_kernel(factor, number, one, other, mixing, own, cross):
    for spot, block in enumerate(chosen_blocks(number)):
        both = times_transposed(mixing[factor, block], (one, other)[spot])
        own[spot] = both[:BLOCK]
        cross[spot] = both[BLOCK:].astype(jnp.bfloat16)


def keep_kernel(factor, number, kept, arrived, mixing, message, own, cross):
    message[0] = kept[1]
    message[1] = arrived[1]
    regroup_kernel(factor, number, kept[0], arrived[0], mixing, own, cross)


def handed_kernel(factor, number, arrived, mixing, own, cross):
    regroup_kernel(factor, number, arrived[0], arrived[1], mixing, own, cross)


def plain_back_kernel(factor, number, mine, theirs, mixing, own, cross):
    for spot, block in enumerate(chosen_blocks(number)):
        grad = (mine[spot] + theirs[spot].astype(jnp.float32)).astype(jnp.bfloat16)
        both = times_transposed(mixing[factor, block], grad)
        own[spot] = both[:BLOCK]
        cross[spot] = both[BLOCK:].astype(cross.dtype)


def exit_kernel(count, pattern_far, *rest):
    mine, theirs = rest[:count], rest[count : 2 * count]
    mixing, out, own, cross, pattern, arrival = rest[2 * count :]
    fetch = pltpu.make_async_copy(pattern_far, pattern, arrival)
    fetch.start()
    blocks = own.shape[0]
    for number in range(count):
        for spot, block in enumerate(chosen_blocks(number)):
            own[block] = mine[number][spot]
            cross[block] = theirs[number][spot]
    fetch.wait()
    for factor in reversed(range(LOCAL)):
        for block in range(blocks):
            own[block] += cross[pattern[factor, block]]
        for block in range(blocks):
            grad = own[block].astype(jnp.bfloat16)
            if factor == 0:
                out[block * BLOCK : (block + 1) * BLOCK] = grad
            else:
                both = times_transposed(mixing[factor - 1, block], grad)
                own[block] = both[:BLOCK]
                cross[block] = both[BLOCK:]


def conv_back_kernel(cells, before, after, taps, out):
    values = cells[...].astype(jnp.float32)
    scale = taps[...].astype(jnp.float32)
    up, down = shifted(
        values, before[...].astype(jnp.float32), after[...].astype(jnp.float32)
    )
    out[...] = (scale[0:1] * down + scale[1:2] * values + scale[2:3] * up).astype(jnp.bfloat16)


def channel_spots(count, chans):
    core = lax.axis_index("ch")
    return [
        pl.ds(pl.multiple_of(lax.rem(core + i, count) * chans, chans), chans)
        for i in range(count)
    ]


def grad_act_kernel(count, *rest):
    cots, (w_out, grad_act, c_all) = rest[:count], rest[count:]
    for spot, cot in zip(channel_spots(count, cots[0].shape[1]), cots):
        c_all[:, spot] = cot[...]
    hidden = w_out.shape[0]
    tile = min(TILE, hidden)
    for start in range(0, hidden, tile):
        grad_act[:, start : start + tile] = lax.dot_general(
            c_all[...], w_out[start : start + tile], ACROSS, preferred_element_type=jnp.float32
        ).astype(grad_act.dtype)


def hidden_kernel(count, *rest):
    mixed, (grad_act, w_in, activation, own) = rest[:count], rest[count : count + 4]
    backs, (x_all, back_sum) = rest[count + 4 : -2], rest[-2:]
    spots = channel_spots(count, mixed[0].shape[1])
    for spot, value in zip(spots, mixed):
        x_all[:, spot] = value[...]
    size = w_in.shape[1]
    tile = min(TILE, size)
    for start in range(0, size, tile):
        tiles = slice(start, start + tile)
        hidden = times(x_all[...], w_in[:, tiles])
        square = hidden * hidden
        tanh_val = jnp.tanh(hidden * (root_two_pi + root_two_pi * 0.044715 * square))
        half = 0.5 + 0.5 * tanh_val
        gelu = hidden * half
        activation[:, tiles] = gelu.astype(jnp.bfloat16)
        slope = 2.0 * root_two_pi + 6.0 * root_two_pi * 0.044715 * square
        derivative = half + gelu * (1.0 - half) * slope
        grad_hidden = (grad_act[:, tiles].astype(jnp.float32) * derivative).astype(jnp.bfloat16)
        back = lax.dot_general(
            grad_hidden, w_in[:, tiles], ACROSS, preferred_element_type=jnp.float32
        )
        if start == 0:
            back_sum[...] = back
        else:
            back_sum[...] += back
    own[...] = back_sum[:, spots[0]]
    for i, spot in enumerate(spots[1:]):
        for quarter in range(QUARTERS):
            rows = slice(quarter * BLOCK, (quarter + 1) * BLOCK)
            backs[i * QUARTERS + quarter][...] = back_sum[rows, spot].astype(jnp.bfloat16)


def out_kernel(count, activation, mixed, w_out, own, *others):
    for i, spot in enumerate(channel_spots(count, mixed.shape[1])):
        product = times(activation[...], w_out[:, spot])
        if i == 0:
            own[...] = mixed[...].astype(jnp.float32) + product
        else:
            others[i - 1][...] = product.astype(jnp.bfloat16)


def combine_kernel(cores, pieces, *rest):
    owns, parts, (keep, send) = rest[:pieces], rest[pieces:-2], rest[-2:]
    for piece in range(pieces):
        for quarter in range(QUARTERS):
            rows = slice(quarter * BLOCK, (quarter + 1) * BLOCK)
            total = owns[piece][rows]
            for part in parts[piece::pieces]:
                total = total + part[rows].astype(jnp.float32)
            (keep, send)[quarter // 2][piece, quarter % 2] = total.astype(jnp.bfloat16)


def relay_kernel(kept, arrived, message):
    message[:, 0] = kept[:, 1]
    message[:, 1] = arrived[:, 1]


def assemble_kernel(kept, arrived, handed, out):
    my_early, my_late = own_bits()
    for piece in range(kept.shape[0]):
        for early in range(2):
            for late in range(2):
                if early:
                    value = handed[piece, late]
                else:
                    value = (kept, arrived)[late][piece, 0]
                spot = (my_early ^ early) * 2 + (my_late ^ late)
                start = pl.multiple_of((piece * QUARTERS + spot) * BLOCK, BLOCK)
                out[pl.ds(start, BLOCK)] = value


def on_device(inputs, conv_weight, mixing, pattern, w_in, w_out, cotangent):
    row_count, chan_count = inputs.shape
    blocks = row_count // BLOCK
    pieces = blocks // QUARTERS
    width, hidden = w_in.shape
    cores = lax.axis_size("ch")
    levels = lax.axis_size("seq").bit_length() - 1
    plain = list(range(LOCAL, LOCAL + levels - 2))
    last = LOCAL + levels - 2
    early_bit, late_bit = 1 << (levels - 2), 1 << (levels - 1)
    half = ((2, BLOCK, chan_count), jnp.bfloat16)
    pair = ((pieces, 2, BLOCK, chan_count), jnp.bfloat16)
    full = ((QUARTERS, BLOCK, chan_count), jnp.bfloat16)
    half_wide = ((2, BLOCK, chan_count), jnp.float32)
    whole = ((row_count, chan_count), jnp.bfloat16)
    piece_rows = QUARTERS * BLOCK
    flat = (piece_rows, chan_count)
    block = ((BLOCK, chan_count), jnp.bfloat16)
    flat_piece = (flat, jnp.bfloat16)
    flops = 2 * piece_rows * width * hidden

    latest = []

    def run(kernel, name, outs, arrays, *args, **kwargs):
        results = call(kernel, name, outs, arrays, *args, order=tuple(latest), **kwargs)
        latest[:] = results[-1:]
        return results

    before, after = neighbours(inputs[:1], inputs[-1:], "seq")
    per_block = chan_count // (2 * BLOCK)
    lengths = [pieces + -(-pieces * 2 * (1 + (flip == 1)) // per_block) for flip in (1, 2, 3)]
    length = lengths[1]
    own_cots, *messages, mixing, cells, taps = run(
        functools.partial(load_kernel, last, pieces, length),
        "load_and_pack",
        [((pieces, BLOCK, chan_count), jnp.bfloat16)]
        + [((count, BLOCK, chan_count), jnp.bfloat16) for count in (lengths[0], 2 * length)]
        + [(array.shape, array.dtype) for array in (mixing, inputs, conv_weight)],
        [],
        [cotangent.reshape(blocks, BLOCK, chan_count), mixing, inputs, conv_weight],
        [pltpu.VMEM((blocks, BLOCK, chan_count), jnp.bfloat16), pltpu.SemaphoreType.DMA((4,))],
        limit=ALL,
    )
    messages = [
        from_flipped(messages[0], "seq", early_bit),
        from_flipped(messages[1], "seq", late_bit),
    ]
    subs = 2 * pieces
    convolved, *states = run(
        entry_kernel,
        "conv_and_local_factors",
        [whole] + [half] * subs,
        [cells, before, after, taps, mixing],
        [pattern],
        [pltpu.VMEM((blocks, BLOCK, chan_count), jnp.bfloat16)] * 2
        + [pltpu.SMEM(pattern.shape, jnp.int32), pltpu.SemaphoreType.DMA],
    )
    stacked = [None] * pieces
    all_cots = [None] * pieces
    grad_acts = [None] * pieces
    parts = [None] * pieces
    mixeds = [None] * pieces
    activations = [None] * pieces
    owns = [None] * pieces
    out_owns = [None] * pieces
    out_parts = [None] * (pieces * (cores - 1))

    def forward():
        (message,) = run(
            forward_kernel, "forward", [((length, BLOCK, chan_count), jnp.bfloat16)], [messages[1]]
        )
        messages.append(from_flipped(message, "seq", early_bit))

    def stack():
        stacked[:] = run(
            functools.partial(stack_kernel, pieces),
            "stack",
            [flat_piece] * pieces,
            [own_cots, *messages],
        )
        for p, piece in enumerate(stacked):
            all_cots[p] = [piece] + [from_offset(piece, "ch", i) for i in range(1, cores)]

    def grad_act(p):
        (grad_acts[p],) = run(
            functools.partial(grad_act_kernel, cores),
            "grad_act",
            [((piece_rows, hidden), jnp.bfloat16)],
            [*all_cots[p], w_out],
            scratch=[pltpu.VMEM((piece_rows, width), jnp.bfloat16)],
            limit=LARGE,
        )

    def plain_factor(factor, s):
        mates = from_flipped(states[s], "seq", 1 << (factor - LOCAL))
        (states[s],) = run(
            functools.partial(plain_kernel, factor, s),
            "factor",
            [half],
            [states[s], mates, mixing],
        )

    def early_factor(p):
        send, keep = states[2 * p : 2 * p + 2]
        states[2 * p : 2 * p + 2] = run(
            functools.partial(early_kernel, last, pieces, p),
            "early_factor",
            [half, half],
            [keep, from_flipped(send, "seq", early_bit), mixing, messages[0]],
        )

    def late_factor(p):
        keep, send = states[2 * p : 2 * p + 2]
        (mixed,) = run(
            functools.partial(late_kernel, last, pieces, p),
            "late_factor",
            [full],
            [keep, from_flipped(send, "seq", late_bit), mixing, *messages],
        )
        mixeds[p] = mixed.reshape(flat)

    def hidden_and_grad(p):
        gathered = [mixeds[p]] + [from_offset(mixeds[p], "ch", i) for i in range(1, cores)]
        activations[p], owns[p], *backs = run(
            functools.partial(hidden_kernel, cores),
            "mlp_hidden_and_grad",
            [((piece_rows, hidden), jnp.bfloat16), (flat, jnp.float32)]
            + [block] * ((cores - 1) * QUARTERS),
            [*gathered, grad_acts[p], w_in],
            scratch=[
                pltpu.VMEM((piece_rows, width), jnp.bfloat16),
                pltpu.VMEM((piece_rows, width), jnp.float32),
            ],
            limit=LARGE,
        )
        parts[p] = [
            from_offset(back, "ch", cores - 1 - i // QUARTERS) for i, back in enumerate(backs)
        ]

    def transposed_back(p):
        states[2 * p : 2 * p + 2] = run(
            functools.partial(back_kernel, last, pieces, p, cores),
            "late_and_early_back",
            [half, half],
            [stacked[p], owns[p], *parts[p], mixing, *messages],
        )

    def regroup(s):
        if s % 2:
            kept, sent = states[s - 1 : s + 1]
            message, *states[s] = run(
                functools.partial(keep_kernel, plain[-1], s),
                "regroup_and_factor_back",
                [half, half_wide, half],
                [kept, from_flipped(sent, "seq", late_bit), mixing],
            )
            states[s - 1] = from_flipped(message, "seq", early_bit)
        else:
            states[s] = run(
                functools.partial(handed_kernel, plain[-1], s),
                "handed_and_factor_back",
                [half_wide, half],
                [states[s], mixing],
            )

    def out_product(p):
        out_owns[p], *others = run(
            functools.partial(out_kernel, cores),
            "mlp_out",
            [(flat, jnp.float32)] + [flat_piece] * (cores - 1),
            [activations[p], mixeds[p], w_out],
            limit=LARGE,
        )
        for i, other in enumerate(others):
            out_parts[i * pieces + p] = from_offset(other, "ch", cores - 1 - i)

    def plain_back(factor, s):
        mine, cross = states[s]
        theirs = from_flipped(cross, "seq", 1 << (factor - LOCAL))
        states[s] = run(
            functools.partial(plain_back_kernel, factor - 1, s),
            "factor_back",
            [half_wide, half if factor != plain[0] else half_wide],
            [mine, theirs, mixing],
        )

    waves = sorted((s + 2 * i, -i, s) for i in range(len(plain)) for s in range(subs))
    for wave, i, s in waves:
        plain_factor(plain[-i], s)
        if wave == 2 and s == 2:
            forward()
        if plain[-i] == plain[-1] and s % 2:
            early_factor(s // 2)
            if s == 1:
                stack()
        if plain[-i] == plain[-1] and s == subs - 2:
            grad_act(0)
    late_factor(0)
    for p in range(pieces):
        hidden_and_grad(p)
        if p + 1 < pieces:
            grad_act(p + 1)
            out_product(p)
            late_factor(p + 1)
        if p == 1:
            regroup(1)
        transposed_back(p)
    waves = [(2, -2, 0), (5, -3, 0), (7, -4, 0)]
    for s in range(subs):
        wave = s // 2 * 4 + 1 - s % 2
        waves += [(wave + 2 * i, i, s) for i in range(-1, len(plain)) if i >= 0 or s != 1]
    for wave, i, s in sorted(waves):
        if i == -4:
            (message,) = run(relay_kernel, "relay", [pair], [kept, arrived])
            handed = from_flipped(message, "seq", early_bit)
        elif i == -3:
            kept, sent = run(
                functools.partial(combine_kernel, cores, pieces),
                "combine",
                [pair, pair],
                [*out_owns, *out_parts],
            )
            arrived = from_flipped(sent, "seq", late_bit)
        elif i == -2:
            out_product(pieces - 1)
        elif i < 0:
            regroup(s)
        else:
            plain_back(plain[-1 - i], s)
    (grad_conv,) = run(
        functools.partial(exit_kernel, subs),
        "local_factors_back",
        [whole],
        [g[0] for g in states] + [g[1] for g in states] + [mixing],
        [pattern],
        [pltpu.VMEM((blocks, BLOCK, chan_count), jnp.float32)] * 2
        + [pltpu.SMEM(pattern.shape, jnp.int32), pltpu.SemaphoreType.DMA],
        limit=LARGE,
    )
    (layer_out,) = call(assemble_kernel, "assemble", [whole], [kept, arrived, handed])
    before, after = neighbours(grad_conv[:1], grad_conv[-1:], "seq")
    (grad_input,) = run(
        conv_back_kernel, "conv_back", [whole], [grad_conv, before, after, taps]
    )
    return (layer_out, convolved, grad_input)


def solution(mesh):
    return jax.shard_map(
        on_device,
        mesh=mesh,
        in_specs=(
            P("seq", "ch"),
            P(None, "ch"),
            P(None, "seq", None, None),
            P(None, "seq"),
            P(None, "ch"),
            P("ch", None),
            P("seq", "ch"),
        ),
        out_specs=(P("seq", "ch"), P("seq", "ch"), P("seq", "ch")),
        check_vma=False,
    )
```

```python
import functools

import jax
import jax.numpy as jnp
from jax import lax
from jax.experimental import pallas as pl
from jax.experimental.pallas import tpu as pltpu
from jax.sharding import PartitionSpec as P

BLOCK = 64
LOCAL = 2
QUARTERS = 4
TILE = 512
SMALL = 8 * 1024 * 1024
LARGE = 20 * 1024 * 1024
ALL = 44 * 1024 * 1024

root_two_pi = 0.7978845608028654

IN_HBM = pl.BlockSpec(memory_space=pltpu.HBM)
IN_VMEM = pl.BlockSpec(memory_space=pltpu.VMEM)
ANYWHERE = pl.BlockSpec(memory_space=pl.ANY)
ACROSS = (((1,), (1,)), ((), ()))
OVER_ROWS = (((0,), (0,)), ((), ()))


def times(weights, value):
    return jnp.dot(weights, value, preferred_element_type=jnp.float32)


def times_transposed(weights, value):
    return lax.dot_general(weights, value, OVER_ROWS, preferred_element_type=jnp.float32)


def neighbours(first, last, axis):
    count = lax.axis_size(axis)
    ends = count - 1
    before = lax.ppermute(last, axis, [(i, (i + 1) % count) for i in range(ends)])
    after = lax.ppermute(first, axis, [((i + 1) % count, i) for i in range(ends)])
    return before, after


def from_flipped(block, axis, mask):
    count = lax.axis_size(axis)
    return lax.ppermute(block, axis, [(i, i ^ mask) for i in range(count)])


def from_offset(block, axis, offset):
    count = lax.axis_size(axis)
    return lax.ppermute(block, axis, [((i + offset) % count, i) for i in range(count)])


def call(kernel, name, outs, arrays, distant=(), scratch=(), order=(), limit=SMALL):
    count = len(distant) + len(arrays)

    def body(*refs):
        kernel(*refs[:count], *refs[count + len(order) :])

    return pl.pallas_call(
        body,
        out_shape=[jax.ShapeDtypeStruct(shape, kind) for shape, kind in outs],
        in_specs=[IN_HBM] * len(distant) + [IN_VMEM] * len(arrays) + [ANYWHERE] * len(order),
        out_specs=[IN_VMEM] * len(outs),
        scratch_shapes=list(scratch),
        compiler_params=pltpu.CompilerParams(vmem_limit_bytes=limit),
        cost_estimate=pl.CostEstimate(flops=0, bytes_accessed=0, transcendentals=0),
        name=name,
    )(*distant, *arrays, *order)


def own_bits():
    seat = lax.axis_index("seq")
    levels = lax.axis_size("seq").bit_length() - 1
    return (seat >> (levels - 2)) & 1, (seat >> (levels - 1)) & 1


def shifted(cells, before, after):
    rows = cells.shape[0]
    spot = lax.broadcasted_iota(jnp.int32, cells.shape, 0)
    up = jnp.where(spot == 0, before, pltpu.roll(cells, 1, 0))
    down = jnp.where(spot == rows - 1, after, pltpu.roll(cells, rows - 1, 0))
    return up, down


def chosen_blocks(sub):
    early, late = own_bits()
    first = sub // 2 * QUARTERS
    spot = early ^ (1 - sub % 2)
    return [first + spot * 2 + (late ^ other) for other in range(2)]


def local_factor(factor, pattern, source, mixing, target, chosen):
    for spot, block in enumerate(chosen):
        pair = mixing[factor, block]
        target[spot] = (
            times(pair[:, :BLOCK], source[block])
            + times(pair[:, BLOCK:], source[pattern[factor, block]])
        ).astype(jnp.bfloat16)


def entry_kernel(pattern_far, cells, before, after, taps, mixing, conv_ref, *rest):
    subs, (first, between, pattern, arrival) = rest[:-4], rest[-4:]
    fetch = pltpu.make_async_copy(pattern_far, pattern, arrival)
    fetch.start()
    values = cells[...].astype(jnp.float32)
    scale = taps[...].astype(jnp.float32)
    up, down = shifted(
        values, before[...].astype(jnp.float32), after[...].astype(jnp.float32)
    )
    convolved = (scale[0:1] * up + scale[1:2] * values + scale[2:3] * down).astype(jnp.bfloat16)
    conv_ref[...] = convolved
    first[...] = convolved.reshape(first.shape)
    fetch.wait()
    every = range(first.shape[0])
    refs = (first, between)
    for factor in range(LOCAL - 1):
        local_factor(factor, pattern, refs[factor % 2], mixing, refs[1 - factor % 2], every)
    source = refs[(LOCAL - 1) % 2]
    for number, sub in enumerate(subs, -1):
        chosen = chosen_blocks(max(number, 0))
        chosen = chosen if number > 0 else chosen[number + 1 : number + 2]
        local_factor(LOCAL - 1, pattern, source, mixing, sub, chosen)


def plain_kernel(factor, number, count, *rest):
    states, mates, (mixing, out) = rest[:count], rest[count : 2 * count], rest[2 * count :]
    for spot, block in enumerate(chosen_blocks(number)):
        pair = mixing[factor, block]
        part, place = spot * count // 2, spot % (2 // count)
        out[spot] = (
            times(pair[:, :BLOCK], states[part][place])
            + times(pair[:, BLOCK:], mates[part][place])
        ).astype(jnp.bfloat16)


def packed(message, pieces, number):
    across = message.shape[-1] // (2 * BLOCK)
    lanes = pl.ds(number % across * 2 * BLOCK, 2 * BLOCK)
    return message.at[pieces + number // across, :, lanes]


def load_kernel(factor, pieces, cots_far, mixing_far, cells_far, taps_far, *rest):
    own, *messages, mixing, cells, taps, cots, arrivals = rest
    fetches = [
        pltpu.make_async_copy(far, near, arrivals.at[i])
        for i, (far, near) in enumerate(
            ((mixing_far, mixing), (cots_far, cots), (cells_far, cells), (taps_far, taps))
        )
    ]
    for fetch in fetches:
        fetch.start()
    fetches[0].wait()
    fetches[1].wait()
    my_early, my_late = own_bits()
    for piece in range(pieces):
        base = piece * QUARTERS
        own[piece] = cots[base + my_early * 2 + my_late]
        for flip, message in enumerate(messages, 1):
            early, late = my_early ^ (flip & 1), my_late ^ (flip >> 1)
            message[piece] = cots[base + early * 2 + late]
            for which in range(2):
                number = which * pieces + piece
                if flip == 1:
                    for other in range(2):
                        packed(message, pieces, number * 2 + other)[...] = mixing[
                            factor + which, base + early * 2 + (late ^ other)
                        ]
                else:
                    packed(message, pieces, number)[...] = mixing[
                        factor + which, base + early * 2 + late
                    ]
    fetches[2].wait()
    fetches[3].wait()


def stack_kernel(pieces, *rest):
    quarters, outs = rest[:QUARTERS], rest[QUARTERS:]
    for piece, out in enumerate(outs):
        for quarter, values in enumerate(quarters):
            out[quarter * BLOCK : (quarter + 1) * BLOCK] = values[piece]


def mixing_of(factor, which, pieces, piece, mixing, messages, quarter, other=0):
    if quarter == 0:
        early, late = own_bits()
        return mixing[factor + which, piece * QUARTERS + early * 2 + (late ^ other)]
    number = which * pieces + piece
    if quarter == 1:
        number = number * 2 + other
    return packed(messages[quarter - 1], pieces, number)[...]


def early_kernel(factor, pieces, piece, keep, recv, mixing, message, keep_out, send_out):
    weights = functools.partial(mixing_of, factor, 0, pieces, piece, mixing, [message])
    for other, out in enumerate((keep_out, send_out)):
        mine, theirs = keep[other], recv[other]
        pair = weights(0, other)
        out[0] = (times(pair[:, :BLOCK], mine) + times(pair[:, BLOCK:], theirs)).astype(
            jnp.bfloat16
        )
        pair = weights(1, other)
        out[1] = (times(pair[:, :BLOCK], theirs) + times(pair[:, BLOCK:], mine)).astype(
            jnp.bfloat16
        )


def late_kernel(factor, pieces, piece, keep, recv, mixing, *rest):
    messages, outs = rest[:-2], rest[-2:]
    values = [keep[0], keep[1], recv[0], recv[1]]
    for quarter in range(QUARTERS):
        pair = mixing_of(factor, 1, pieces, piece, mixing, messages, quarter)
        rows = slice(quarter % 2 * BLOCK, (quarter % 2 + 1) * BLOCK)
        outs[quarter // 2][rows] = (
            times(pair[:, :BLOCK], values[quarter]) + times(pair[:, BLOCK:], values[quarter ^ 2])
        ).astype(jnp.bfloat16)


def back_kernel(factor, pieces, piece, cores, cots, total, *rest):
    count = (cores - 1) * QUARTERS
    parts, (mixing, message1, message2, message3, *outs) = rest[:count], rest[count:]
    messages = (message1, message2, message3)
    grads = []
    for quarter in range(QUARTERS):
        rows = slice(quarter * BLOCK, (quarter + 1) * BLOCK)
        grad = cots[rows].astype(jnp.float32) + total[rows]
        for part in parts[quarter::QUARTERS]:
            grad = grad + part[...].astype(jnp.float32)
        grads.append(grad.astype(jnp.bfloat16))
    for which, flip in ((1, 2), (0, 1)):
        both = [
            times_transposed(
                mixing_of(factor, which, pieces, piece, mixing, messages, quarter),
                grads[quarter],
            )
            for quarter in range(QUARTERS)
        ]
        grads = [
            (both[quarter][:BLOCK] + both[quarter ^ flip][BLOCK:]).astype(jnp.bfloat16)
            for quarter in range(QUARTERS)
        ]
    for grad, out in zip(grads, outs):
        out[...] = grad


def regroup_kernel(factor, number, one, other, mixing, own, cross):
    for spot, block in enumerate(chosen_blocks(number)):
        both = times_transposed(mixing[factor, block], (one, other)[spot][...])
        own[spot] = both[:BLOCK]
        cross[spot] = both[BLOCK:].astype(jnp.bfloat16)


def plain_back_kernel(factor, number, mine, theirs, mixing, own, cross):
    for spot, block in enumerate(chosen_blocks(number)):
        grad = (mine[spot] + theirs[spot].astype(jnp.float32)).astype(jnp.bfloat16)
        both = times_transposed(mixing[factor, block], grad)
        own[spot] = both[:BLOCK]
        cross[spot] = both[BLOCK:].astype(cross.dtype)


def exit_kernel(count, pattern_far, *rest):
    mine, theirs = rest[:count], rest[count : 2 * count]
    mixing, out, own, cross, pattern, arrival = rest[2 * count :]
    fetch = pltpu.make_async_copy(pattern_far, pattern, arrival)
    fetch.start()
    blocks = own.shape[0]
    for number in range(count):
        for spot, block in enumerate(chosen_blocks(number)):
            own[block] = mine[number][spot]
            cross[block] = theirs[number][spot]
    fetch.wait()
    for factor in reversed(range(LOCAL)):
        for block in range(blocks):
            own[block] += cross[pattern[factor, block]]
        for block in range(blocks):
            grad = own[block].astype(jnp.bfloat16)
            if factor == 0:
                out[block * BLOCK : (block + 1) * BLOCK] = grad
            else:
                both = times_transposed(mixing[factor - 1, block], grad)
                own[block] = both[:BLOCK]
                cross[block] = both[BLOCK:]


def conv_back_kernel(cells, before, after, taps, out):
    values = cells[...].astype(jnp.float32)
    scale = taps[...].astype(jnp.float32)
    up, down = shifted(
        values, before[...].astype(jnp.float32), after[...].astype(jnp.float32)
    )
    out[...] = (scale[0:1] * down + scale[1:2] * values + scale[2:3] * up).astype(jnp.bfloat16)


def channel_spots(count, chans):
    core = lax.axis_index("ch")
    return [
        pl.ds(pl.multiple_of(lax.rem(core + i, count) * chans, chans), chans)
        for i in range(count)
    ]


def grad_act_kernel(count, *rest):
    cots, (w_out, grad_act, c_all) = rest[:count], rest[count:]
    for spot, cot in zip(channel_spots(count, cots[0].shape[1]), cots):
        c_all[:, spot] = cot[...]
    hidden = w_out.shape[0]
    tile = min(TILE, hidden)
    for start in range(0, hidden, tile):
        grad_act[:, start : start + tile] = lax.dot_general(
            c_all[...], w_out[start : start + tile], ACROSS, preferred_element_type=jnp.float32
        ).astype(grad_act.dtype)


def hidden_kernel(count, *rest):
    mixed, (grad_act, w_in, activation, own) = rest[: 2 * count], rest[2 * count : 2 * count + 4]
    backs, (x_all, back_sum) = rest[2 * count + 4 : -2], rest[-2:]
    rows, chans = mixed[0].shape
    spots = channel_spots(count, chans)
    for i, spot in enumerate(spots):
        x_all[:rows, spot] = mixed[2 * i][...]
        x_all[rows:, spot] = mixed[2 * i + 1][...]
    size = w_in.shape[1]
    tile = min(TILE, size)
    for start in range(0, size, tile):
        tiles = slice(start, start + tile)
        hidden = times(x_all[...], w_in[:, tiles])
        square = hidden * hidden
        tanh_val = jnp.tanh(hidden * (root_two_pi + root_two_pi * 0.044715 * square))
        half = 0.5 + 0.5 * tanh_val
        gelu = hidden * half
        activation[:, tiles] = gelu.astype(jnp.bfloat16)
        slope = 2.0 * root_two_pi + 6.0 * root_two_pi * 0.044715 * square
        derivative = half + gelu * (1.0 - half) * slope
        grad_hidden = (grad_act[:, tiles].astype(jnp.float32) * derivative).astype(jnp.bfloat16)
        back = lax.dot_general(
            grad_hidden, w_in[:, tiles], ACROSS, preferred_element_type=jnp.float32
        )
        if start == 0:
            back_sum[...] = back
        else:
            back_sum[...] += back
    own[...] = back_sum[:, spots[0]]
    for i, spot in enumerate(spots[1:]):
        for quarter in range(QUARTERS):
            rows = slice(quarter * BLOCK, (quarter + 1) * BLOCK)
            backs[i * QUARTERS + quarter][...] = back_sum[rows, spot].astype(jnp.bfloat16)


def out_kernel(count, activation, top, bottom, w_out, own, *others):
    rows, chans = top.shape
    for i, spot in enumerate(channel_spots(count, chans)):
        product = times(activation[...], w_out[:, spot])
        if i == 0:
            own[:rows] = top[...].astype(jnp.float32) + product[:rows]
            own[rows:] = bottom[...].astype(jnp.float32) + product[rows:]
        else:
            others[i - 1][...] = product.astype(jnp.bfloat16)


def combine_kernel(cores, pieces, *rest):
    owns, parts, outs = rest[:pieces], rest[pieces:-QUARTERS], rest[-QUARTERS:]
    for piece in range(pieces):
        for quarter, out in enumerate(outs):
            rows = slice(quarter * BLOCK, (quarter + 1) * BLOCK)
            total = owns[piece][rows]
            for part in parts[piece::pieces]:
                total = total + part[rows].astype(jnp.float32)
            out[piece] = total.astype(jnp.bfloat16)


def assemble_kernel(*rest):
    quarters, out = rest[:-1], rest[-1]
    my_early, my_late = own_bits()
    for quarter, values in enumerate(quarters):
        spot = (my_early ^ (quarter & 1)) * 2 + (my_late ^ (quarter >> 1))
        for piece in range(values.shape[0]):
            start = pl.multiple_of((piece * QUARTERS + spot) * BLOCK, BLOCK)
            out[pl.ds(start, BLOCK)] = values[piece]


def on_device(inputs, conv_weight, mixing, pattern, w_in, w_out, cotangent):
    row_count, chan_count = inputs.shape
    blocks = row_count // BLOCK
    pieces = blocks // QUARTERS
    width, hidden = w_in.shape
    cores = lax.axis_size("ch")
    levels = lax.axis_size("seq").bit_length() - 1
    plain = list(range(LOCAL, LOCAL + levels - 2))
    last = LOCAL + levels - 2
    early_bit, late_bit = 1 << (levels - 2), 1 << (levels - 1)
    masks = [0, early_bit, late_bit, early_bit | late_bit]
    half = ((2, BLOCK, chan_count), jnp.bfloat16)
    half_wide = ((2, BLOCK, chan_count), jnp.float32)
    whole = ((row_count, chan_count), jnp.bfloat16)
    piece_rows = QUARTERS * BLOCK
    flat = (piece_rows, chan_count)
    block = ((BLOCK, chan_count), jnp.bfloat16)
    flat_piece = (flat, jnp.bfloat16)
    flops = 2 * piece_rows * width * hidden

    latest = []

    def run(kernel, name, outs, arrays, *args, **kwargs):
        results = call(kernel, name, outs, arrays, *args, order=tuple(latest), **kwargs)
        latest[:] = results[-1:]
        return results

    before, after = neighbours(inputs[:1], inputs[-1:], "seq")
    per_block = chan_count // (2 * BLOCK)
    lengths = [pieces + -(-pieces * 2 * (1 + (flip == 1)) // per_block) for flip in (1, 2, 3)]
    own_cots, *messages, mixing, cells, taps = run(
        functools.partial(load_kernel, last, pieces),
        "load_and_pack",
        [((pieces, BLOCK, chan_count), jnp.bfloat16)]
        + [((length, BLOCK, chan_count), jnp.bfloat16) for length in lengths]
        + [(array.shape, array.dtype) for array in (mixing, inputs, conv_weight)],
        [],
        [cotangent.reshape(blocks, BLOCK, chan_count), mixing, inputs, conv_weight],
        [pltpu.VMEM((blocks, BLOCK, chan_count), jnp.bfloat16), pltpu.SemaphoreType.DMA((4,))],
        limit=ALL,
    )
    messages = [from_flipped(m, "seq", mask) for m, mask in zip(messages, masks[1:])]
    subs = 2 * pieces
    convolved, *states = run(
        entry_kernel,
        "conv_and_local_factors",
        [whole] + [((1, BLOCK, chan_count), jnp.bfloat16)] * 2 + [half] * (subs - 1),
        [cells, before, after, taps, mixing],
        [pattern],
        [pltpu.VMEM((blocks, BLOCK, chan_count), jnp.bfloat16)] * 2
        + [pltpu.SMEM(pattern.shape, jnp.int32), pltpu.SemaphoreType.DMA],
    )
    states = [states[:2]] + [[state] for state in states[2:]]
    stacked = [None] * pieces
    all_cots = [None] * pieces
    grad_acts = [None] * pieces
    parts = [None] * pieces
    mixeds = [None] * pieces
    activations = [None] * pieces
    owns = [None] * pieces
    out_owns = [None] * pieces
    out_parts = [None] * (pieces * (cores - 1))

    def stack():
        stacked[:] = run(
            functools.partial(stack_kernel, pieces),
            "stack",
            [flat_piece] * pieces,
            [own_cots, *messages],
        )
        for p, piece in enumerate(stacked):
            all_cots[p] = [piece] + [from_offset(piece, "ch", i) for i in range(1, cores)]

    def grad_act(p):
        (grad_acts[p],) = run(
            functools.partial(grad_act_kernel, cores),
            "grad_act",
            [((piece_rows, hidden), jnp.bfloat16)],
            [*all_cots[p], w_out],
            scratch=[pltpu.VMEM((piece_rows, width), jnp.bfloat16)],
            limit=LARGE,
        )

    def plain_factor(factor, s):
        mates = [from_flipped(state, "seq", 1 << (factor - LOCAL)) for state in states[s]]
        states[s] = run(
            functools.partial(plain_kernel, factor, s, len(mates)),
            "factor",
            [half],
            [*states[s], *mates, mixing],
        )

    def early_factor(p):
        (send,), (keep,) = states[2 * p : 2 * p + 2]
        states[2 * p : 2 * p + 2] = run(
            functools.partial(early_kernel, last, pieces, p),
            "early_factor",
            [half, half],
            [keep, from_flipped(send, "seq", early_bit), mixing, messages[0]],
        )

    def late_factor(p):
        keep, send = states[2 * p : 2 * p + 2]
        mixeds[p] = run(
            functools.partial(late_kernel, last, pieces, p),
            "late_factor",
            [((2 * BLOCK, chan_count), jnp.bfloat16)] * 2,
            [keep, from_flipped(send, "seq", late_bit), mixing, *messages],
        )

    def hidden_and_grad(p):
        gathered = [
            from_offset(mixed, "ch", i) if i else mixed for i in range(cores) for mixed in mixeds[p]
        ]
        activations[p], owns[p], *backs = run(
            functools.partial(hidden_kernel, cores),
            "mlp_hidden_and_grad",
            [((piece_rows, hidden), jnp.bfloat16), (flat, jnp.float32)]
            + [block] * ((cores - 1) * QUARTERS),
            [*gathered, grad_acts[p], w_in],
            scratch=[
                pltpu.VMEM((piece_rows, width), jnp.bfloat16),
                pltpu.VMEM((piece_rows, width), jnp.float32),
            ],
            limit=LARGE,
        )
        parts[p] = [
            from_offset(back, "ch", cores - 1 - i // QUARTERS) for i, back in enumerate(backs)
        ]

    def transposed_back(p):
        quarters = run(
            functools.partial(back_kernel, last, pieces, p, cores),
            "late_and_early_back",
            [block] * QUARTERS,
            [stacked[p], owns[p], *parts[p], mixing, *messages],
        )
        quarters = [
            from_flipped(grad, "seq", mask) if mask else grad
            for grad, mask in zip(quarters, masks)
        ]
        states[2 * p : 2 * p + 2] = [quarters[1::2], quarters[0::2]]

    def regroup(s):
        states[s] = run(
            functools.partial(regroup_kernel, plain[-1], s),
            "regroup_and_factor_back",
            [half_wide, half],
            [*states[s], mixing],
        )

    def out_product(p):
        out_owns[p], *others = run(
            functools.partial(out_kernel, cores),
            "mlp_out",
            [(flat, jnp.float32)] + [flat_piece] * (cores - 1),
            [activations[p], *mixeds[p], w_out],
            limit=LARGE,
        )
        for i, other in enumerate(others):
            out_parts[i * pieces + p] = from_offset(other, "ch", cores - 1 - i)

    def plain_back(factor, s):
        mine, cross = states[s]
        theirs = from_flipped(cross, "seq", 1 << (factor - LOCAL))
        states[s] = run(
            functools.partial(plain_back_kernel, factor - 1, s),
            "factor_back",
            [half_wide, half if factor != plain[0] else half_wide],
            [mine, theirs, mixing],
        )

    waves = sorted((s + 2 * i, -i, s) for i in range(len(plain)) for s in range(subs))
    for _, i, s in waves:
        plain_factor(plain[-i], s)
        if i == 0 and s == 0:
            stack()
        if plain[-i] == plain[-1]:
            if s == subs - 1:
                late_factor(0)
            if s % 2:
                early_factor(s // 2)
    grad_act(0)
    for p in range(pieces):
        hidden_and_grad(p)
        if p + 1 < pieces:
            grad_act(p + 1)
            out_product(p)
            late_factor(p + 1)
        if p == 1:
            regroup(1)
            regroup(0)
        if p == pieces - 1:
            out_product(p)
        transposed_back(p)
    waves = [(5, -3, 0)]
    for s in range(subs):
        wave = s // 2 * 4 + 1 - s % 2
        waves += [(wave + 2 * i, i, s) for i in range(0 if s < 2 else -1, len(plain))]
    for wave, i, s in sorted(waves):
        if i == -3:
            outs = run(
                functools.partial(combine_kernel, cores, pieces),
                "combine",
                [((pieces, BLOCK, chan_count), jnp.bfloat16)] * QUARTERS,
                [*out_owns, *out_parts],
            )
            arrived = [
                from_flipped(out, "seq", mask) if mask else out for out, mask in zip(outs, masks)
            ]
        elif i < 0:
            regroup(s)
        else:
            plain_back(plain[-1 - i], s)
    (grad_conv,) = run(
        functools.partial(exit_kernel, subs),
        "local_factors_back",
        [whole],
        [g[0] for g in states] + [g[1] for g in states] + [mixing],
        [pattern],
        [pltpu.VMEM((blocks, BLOCK, chan_count), jnp.float32)] * 2
        + [pltpu.SMEM(pattern.shape, jnp.int32), pltpu.SemaphoreType.DMA],
        limit=LARGE,
    )
    (layer_out,) = call(assemble_kernel, "assemble", [whole], arrived)
    before, after = neighbours(grad_conv[:1], grad_conv[-1:], "seq")
    (grad_input,) = run(
        conv_back_kernel, "conv_back", [whole], [grad_conv, before, after, taps]
    )
    return (layer_out, convolved, grad_input)


def solution(mesh):
    return jax.shard_map(
        on_device,
        mesh=mesh,
        in_specs=(
            P("seq", "ch"),
            P(None, "ch"),
            P(None, "seq", None, None),
            P(None, "seq"),
            P(None, "ch"),
            P("ch", None),
            P("seq", "ch"),
        ),
        out_specs=(P("seq", "ch"), P("seq", "ch"), P("seq", "ch")),
        check_vma=False,
    )
```

```python
import functools

import jax
import jax.numpy as jnp
from jax import lax
from jax.experimental import pallas as pl
from jax.experimental.pallas import tpu as pltpu
from jax.sharding import PartitionSpec as P

BLOCK = 64
LOCAL = 2
QUARTERS = 4
TILE = 512
SMALL = 8 * 1024 * 1024
LARGE = 20 * 1024 * 1024
ALL = 44 * 1024 * 1024

root_two_pi = 0.7978845608028654

IN_HBM = pl.BlockSpec(memory_space=pltpu.HBM)
IN_VMEM = pl.BlockSpec(memory_space=pltpu.VMEM)
ANYWHERE = pl.BlockSpec(memory_space=pl.ANY)
ACROSS = (((1,), (1,)), ((), ()))
OVER_ROWS = (((0,), (0,)), ((), ()))


def times(weights, value):
    return jnp.dot(weights, value, preferred_element_type=jnp.float32)


def times_transposed(weights, value):
    return lax.dot_general(weights, value, OVER_ROWS, preferred_element_type=jnp.float32)


def neighbours(first, last, axis):
    count = lax.axis_size(axis)
    ends = count - 1
    before = lax.ppermute(last, axis, [(i, (i + 1) % count) for i in range(ends)])
    after = lax.ppermute(first, axis, [((i + 1) % count, i) for i in range(ends)])
    return before, after


def from_flipped(block, axis, mask):
    count = lax.axis_size(axis)
    return lax.ppermute(block, axis, [(i, i ^ mask) for i in range(count)])


def from_offset(block, axis, offset):
    count = lax.axis_size(axis)
    return lax.ppermute(block, axis, [((i + offset) % count, i) for i in range(count)])


def call(kernel, name, outs, arrays, distant=(), scratch=(), order=(), limit=SMALL):
    count = len(distant) + len(arrays)

    def body(*refs):
        kernel(*refs[:count], *refs[count + len(order) :])

    return pl.pallas_call(
        body,
        out_shape=[jax.ShapeDtypeStruct(shape, kind) for shape, kind in outs],
        in_specs=[IN_HBM] * len(distant) + [IN_VMEM] * len(arrays) + [ANYWHERE] * len(order),
        out_specs=[IN_VMEM] * len(outs),
        scratch_shapes=list(scratch),
        compiler_params=pltpu.CompilerParams(vmem_limit_bytes=limit),
        cost_estimate=pl.CostEstimate(flops=0, bytes_accessed=0, transcendentals=0),
        name=name,
    )(*distant, *arrays, *order)


def own_bits():
    seat = lax.axis_index("seq")
    levels = lax.axis_size("seq").bit_length() - 1
    return (seat >> (levels - 2)) & 1, (seat >> (levels - 1)) & 1


def shifted(cells, before, after):
    rows = cells.shape[0]
    spot = lax.broadcasted_iota(jnp.int32, cells.shape, 0)
    up = jnp.where(spot == 0, before, pltpu.roll(cells, 1, 0))
    down = jnp.where(spot == rows - 1, after, pltpu.roll(cells, rows - 1, 0))
    return up, down


def chosen_blocks(sub):
    early, late = own_bits()
    first = sub // 2 * QUARTERS
    spot = early ^ (1 - sub % 2)
    return [first + spot * 2 + (late ^ other) for other in range(2)]


def local_factor(factor, pattern, source, mixing, target, chosen):
    for spot, block in enumerate(chosen):
        pair = mixing[factor, block]
        target[spot] = (
            times(pair[:, :BLOCK], source[block])
            + times(pair[:, BLOCK:], source[pattern[factor, block]])
        ).astype(jnp.bfloat16)


def entry_kernel(pattern_far, cells, before, after, taps, mixing, conv_ref, *rest):
    subs, (first, between, pattern, arrival) = rest[:-4], rest[-4:]
    fetch = pltpu.make_async_copy(pattern_far, pattern, arrival)
    fetch.start()
    values = cells[...].astype(jnp.float32)
    scale = taps[...].astype(jnp.float32)
    up, down = shifted(
        values, before[...].astype(jnp.float32), after[...].astype(jnp.float32)
    )
    convolved = (scale[0:1] * up + scale[1:2] * values + scale[2:3] * down).astype(jnp.bfloat16)
    conv_ref[...] = convolved
    first[...] = convolved.reshape(first.shape)
    fetch.wait()
    every = range(first.shape[0])
    refs = (first, between)
    for factor in range(LOCAL - 1):
        local_factor(factor, pattern, refs[factor % 2], mixing, refs[1 - factor % 2], every)
    source = refs[(LOCAL - 1) % 2]
    for number, sub in enumerate(subs):
        local_factor(LOCAL - 1, pattern, source, mixing, sub, chosen_blocks(number))


def plain_kernel(factor, number, state, mates, mixing, out):
    for spot, block in enumerate(chosen_blocks(number)):
        pair = mixing[factor, block]
        out[spot] = (
            times(pair[:, :BLOCK], state[spot]) + times(pair[:, BLOCK:], mates[spot])
        ).astype(jnp.bfloat16)


def packed(message, pieces, number):
    across = message.shape[-1] // (2 * BLOCK)
    lanes = pl.ds(number % across * 2 * BLOCK, 2 * BLOCK)
    return message.at[pieces + number // across, :, lanes]


def load_kernel(factor, pieces, cots_far, mixing_far, cells_far, taps_far, *rest):
    own, *messages, mixing, cells, taps, cots, arrivals = rest
    fetches = [
        pltpu.make_async_copy(far, near, arrivals.at[i])
        for i, (far, near) in enumerate(
            ((mixing_far, mixing), (cots_far, cots), (cells_far, cells), (taps_far, taps))
        )
    ]
    for fetch in fetches:
        fetch.start()
    fetches[0].wait()
    fetches[1].wait()
    my_early, my_late = own_bits()
    for piece in range(pieces):
        base = piece * QUARTERS
        own[piece] = cots[base + my_early * 2 + my_late]
        for flip, message in enumerate(messages, 1):
            early, late = my_early ^ (flip & 1), my_late ^ (flip >> 1)
            message[piece] = cots[base + early * 2 + late]
            for which in range(2):
                number = which * pieces + piece
                if flip == 1:
                    for other in range(2):
                        packed(message, pieces, number * 2 + other)[...] = mixing[
                            factor + which, base + early * 2 + (late ^ other)
                        ]
                else:
                    packed(message, pieces, number)[...] = mixing[
                        factor + which, base + early * 2 + late
                    ]
    fetches[2].wait()
    fetches[3].wait()


def stack_kernel(pieces, *rest):
    quarters, outs = rest[:QUARTERS], rest[QUARTERS:]
    for piece, out in enumerate(outs):
        for quarter, values in enumerate(quarters):
            out[quarter * BLOCK : (quarter + 1) * BLOCK] = values[piece]


def mixing_of(factor, which, pieces, piece, mixing, messages, quarter, other=0):
    if quarter == 0:
        early, late = own_bits()
        return mixing[factor + which, piece * QUARTERS + early * 2 + (late ^ other)]
    number = which * pieces + piece
    if quarter == 1:
        number = number * 2 + other
    return packed(messages[quarter - 1], pieces, number)[...]


def early_kernel(factor, pieces, piece, keep, recv, mixing, message, keep_out, send_out):
    weights = functools.partial(mixing_of, factor, 0, pieces, piece, mixing, [message])
    for other, out in enumerate((keep_out, send_out)):
        mine, theirs = keep[other], recv[other]
        pair = weights(0, other)
        out[0] = (times(pair[:, :BLOCK], mine) + times(pair[:, BLOCK:], theirs)).astype(
            jnp.bfloat16
        )
        pair = weights(1, other)
        out[1] = (times(pair[:, :BLOCK], theirs) + times(pair[:, BLOCK:], mine)).astype(
            jnp.bfloat16
        )


def late_kernel(factor, pieces, piece, keep, recv, mixing, *rest):
    messages, outs = rest[:-2], rest[-2:]
    values = [keep[0], keep[1], recv[0], recv[1]]
    for quarter in range(QUARTERS):
        pair = mixing_of(factor, 1, pieces, piece, mixing, messages, quarter)
        rows = slice(quarter % 2 * BLOCK, (quarter % 2 + 1) * BLOCK)
        outs[quarter // 2][rows] = (
            times(pair[:, :BLOCK], values[quarter]) + times(pair[:, BLOCK:], values[quarter ^ 2])
        ).astype(jnp.bfloat16)


def back_kernel(factor, pieces, piece, cores, cots, total, *rest):
    count = (cores - 1) * QUARTERS
    parts, (mixing, message1, message2, message3, *outs) = rest[:count], rest[count:]
    messages = (message1, message2, message3)
    grads = []
    for quarter in range(QUARTERS):
        rows = slice(quarter * BLOCK, (quarter + 1) * BLOCK)
        grad = cots[rows].astype(jnp.float32) + total[rows]
        for part in parts[quarter::QUARTERS]:
            grad = grad + part[...].astype(jnp.float32)
        grads.append(grad.astype(jnp.bfloat16))
    for which, flip in ((1, 2), (0, 1)):
        both = [
            times_transposed(
                mixing_of(factor, which, pieces, piece, mixing, messages, quarter),
                grads[quarter],
            )
            for quarter in range(QUARTERS)
        ]
        grads = [
            (both[quarter][:BLOCK] + both[quarter ^ flip][BLOCK:]).astype(jnp.bfloat16)
            for quarter in range(QUARTERS)
        ]
    for grad, out in zip(grads, outs):
        out[...] = grad


def regroup_kernel(factor, number, one, other, mixing, own, cross):
    for spot, block in enumerate(chosen_blocks(number)):
        both = times_transposed(mixing[factor, block], (one, other)[spot][...])
        own[spot] = both[:BLOCK]
        cross[spot] = both[BLOCK:].astype(jnp.bfloat16)


def plain_back_kernel(factor, number, mine, theirs, mixing, own, cross):
    for spot, block in enumerate(chosen_blocks(number)):
        grad = (mine[spot] + theirs[spot].astype(jnp.float32)).astype(jnp.bfloat16)
        both = times_transposed(mixing[factor, block], grad)
        own[spot] = both[:BLOCK]
        cross[spot] = both[BLOCK:].astype(cross.dtype)


def exit_kernel(count, pattern_far, *rest):
    mine, theirs = rest[:count], rest[count : 2 * count]
    mixing, out, own, cross, pattern, arrival = rest[2 * count :]
    fetch = pltpu.make_async_copy(pattern_far, pattern, arrival)
    fetch.start()
    blocks = own.shape[0]
    for number in range(count):
        for spot, block in enumerate(chosen_blocks(number)):
            own[block] = mine[number][spot]
            cross[block] = theirs[number][spot]
    fetch.wait()
    for factor in reversed(range(LOCAL)):
        for block in range(blocks):
            own[block] += cross[pattern[factor, block]]
        for block in range(blocks):
            grad = own[block].astype(jnp.bfloat16)
            if factor == 0:
                out[block * BLOCK : (block + 1) * BLOCK] = grad
            else:
                both = times_transposed(mixing[factor - 1, block], grad)
                own[block] = both[:BLOCK]
                cross[block] = both[BLOCK:]


def conv_back_kernel(cells, before, after, taps, out):
    values = cells[...].astype(jnp.float32)
    scale = taps[...].astype(jnp.float32)
    up, down = shifted(
        values, before[...].astype(jnp.float32), after[...].astype(jnp.float32)
    )
    out[...] = (scale[0:1] * down + scale[1:2] * values + scale[2:3] * up).astype(jnp.bfloat16)


def channel_spots(count, chans):
    core = lax.axis_index("ch")
    return [
        pl.ds(pl.multiple_of(lax.rem(core + i, count) * chans, chans), chans)
        for i in range(count)
    ]


def grad_act_kernel(count, *rest):
    cots, (w_out, grad_act, c_all) = rest[:count], rest[count:]
    for spot, cot in zip(channel_spots(count, cots[0].shape[1]), cots):
        c_all[:, spot] = cot[...]
    hidden = w_out.shape[0]
    tile = min(TILE, hidden)
    for start in range(0, hidden, tile):
        grad_act[:, start : start + tile] = lax.dot_general(
            c_all[...], w_out[start : start + tile], ACROSS, preferred_element_type=jnp.float32
        ).astype(grad_act.dtype)


def hidden_kernel(count, *rest):
    mixed, (grad_act, w_in, activation, own) = rest[: 2 * count], rest[2 * count : 2 * count + 4]
    backs, (x_all, back_sum) = rest[2 * count + 4 : -2], rest[-2:]
    rows, chans = mixed[0].shape
    spots = channel_spots(count, chans)
    for i, spot in enumerate(spots):
        x_all[:rows, spot] = mixed[2 * i][...]
        x_all[rows:, spot] = mixed[2 * i + 1][...]
    size = w_in.shape[1]
    tile = min(TILE, size)
    for start in range(0, size, tile):
        tiles = slice(start, start + tile)
        hidden = times(x_all[...], w_in[:, tiles])
        square = hidden * hidden
        tanh_val = jnp.tanh(hidden * (root_two_pi + root_two_pi * 0.044715 * square))
        half = 0.5 + 0.5 * tanh_val
        gelu = hidden * half
        activation[:, tiles] = gelu.astype(jnp.bfloat16)
        slope = 2.0 * root_two_pi + 6.0 * root_two_pi * 0.044715 * square
        derivative = half + gelu * (1.0 - half) * slope
        grad_hidden = (grad_act[:, tiles].astype(jnp.float32) * derivative).astype(jnp.bfloat16)
        back = lax.dot_general(
            grad_hidden, w_in[:, tiles], ACROSS, preferred_element_type=jnp.float32
        )
        if start == 0:
            back_sum[...] = back
        else:
            back_sum[...] += back
    own[...] = back_sum[:, spots[0]]
    for i, spot in enumerate(spots[1:]):
        for quarter in range(QUARTERS):
            rows = slice(quarter * BLOCK, (quarter + 1) * BLOCK)
            backs[i * QUARTERS + quarter][...] = back_sum[rows, spot].astype(jnp.bfloat16)


def out_kernel(count, activation, top, bottom, w_out, own, *others):
    rows, chans = top.shape
    for i, spot in enumerate(channel_spots(count, chans)):
        product = times(activation[...], w_out[:, spot])
        if i == 0:
            own[:rows] = top[...].astype(jnp.float32) + product[:rows]
            own[rows:] = bottom[...].astype(jnp.float32) + product[rows:]
        else:
            others[i - 1][...] = product.astype(jnp.bfloat16)


def combine_kernel(cores, pieces, *rest):
    owns, parts, outs = rest[:pieces], rest[pieces:-QUARTERS], rest[-QUARTERS:]
    for piece in range(pieces):
        for quarter, out in enumerate(outs):
            rows = slice(quarter * BLOCK, (quarter + 1) * BLOCK)
            total = owns[piece][rows]
            for part in parts[piece::pieces]:
                total = total + part[rows].astype(jnp.float32)
            out[piece] = total.astype(jnp.bfloat16)


def assemble_kernel(*rest):
    quarters, out = rest[:-1], rest[-1]
    my_early, my_late = own_bits()
    for quarter, values in enumerate(quarters):
        spot = (my_early ^ (quarter & 1)) * 2 + (my_late ^ (quarter >> 1))
        for piece in range(values.shape[0]):
            start = pl.multiple_of((piece * QUARTERS + spot) * BLOCK, BLOCK)
            out[pl.ds(start, BLOCK)] = values[piece]


def on_device(inputs, conv_weight, mixing, pattern, w_in, w_out, cotangent):
    row_count, chan_count = inputs.shape
    blocks = row_count // BLOCK
    pieces = blocks // QUARTERS
    width, hidden = w_in.shape
    cores = lax.axis_size("ch")
    levels = lax.axis_size("seq").bit_length() - 1
    plain = list(range(LOCAL, LOCAL + levels - 2))
    last = LOCAL + levels - 2
    early_bit, late_bit = 1 << (levels - 2), 1 << (levels - 1)
    masks = [0, early_bit, late_bit, early_bit | late_bit]
    half = ((2, BLOCK, chan_count), jnp.bfloat16)
    half_wide = ((2, BLOCK, chan_count), jnp.float32)
    whole = ((row_count, chan_count), jnp.bfloat16)
    piece_rows = QUARTERS * BLOCK
    flat = (piece_rows, chan_count)
    block = ((BLOCK, chan_count), jnp.bfloat16)
    flat_piece = (flat, jnp.bfloat16)
    flops = 2 * piece_rows * width * hidden

    latest = []

    def run(kernel, name, outs, arrays, *args, **kwargs):
        results = call(kernel, name, outs, arrays, *args, order=tuple(latest), **kwargs)
        latest[:] = results[-1:]
        return results

    before, after = neighbours(inputs[:1], inputs[-1:], "seq")
    per_block = chan_count // (2 * BLOCK)
    lengths = [pieces + -(-pieces * 2 * (1 + (flip == 1)) // per_block) for flip in (1, 2, 3)]
    own_cots, *messages, mixing, cells, taps = run(
        functools.partial(load_kernel, last, pieces),
        "load_and_pack",
        [((pieces, BLOCK, chan_count), jnp.bfloat16)]
        + [((length, BLOCK, chan_count), jnp.bfloat16) for length in lengths]
        + [(array.shape, array.dtype) for array in (mixing, inputs, conv_weight)],
        [],
        [cotangent.reshape(blocks, BLOCK, chan_count), mixing, inputs, conv_weight],
        [pltpu.VMEM((blocks, BLOCK, chan_count), jnp.bfloat16), pltpu.SemaphoreType.DMA((4,))],
        limit=ALL,
    )
    messages = [from_flipped(m, "seq", mask) for m, mask in zip(messages, masks[1:])]
    subs = 2 * pieces
    convolved, *states = run(
        entry_kernel,
        "conv_and_local_factors",
        [whole] + [half] * subs,
        [cells, before, after, taps, mixing],
        [pattern],
        [pltpu.VMEM((blocks, BLOCK, chan_count), jnp.bfloat16)] * 2
        + [pltpu.SMEM(pattern.shape, jnp.int32), pltpu.SemaphoreType.DMA],
    )
    stacked = [None] * pieces
    all_cots = [None] * pieces
    grad_acts = [None] * pieces
    parts = [None] * pieces
    mixeds = [None] * pieces
    activations = [None] * pieces
    owns = [None] * pieces
    out_owns = [None] * pieces
    out_parts = [None] * (pieces * (cores - 1))

    def stack():
        stacked[:] = run(
            functools.partial(stack_kernel, pieces),
            "stack",
            [flat_piece] * pieces,
            [own_cots, *messages],
        )
        for p, piece in enumerate(stacked):
            all_cots[p] = [piece] + [from_offset(piece, "ch", i) for i in range(1, cores)]

    def grad_act(p):
        (grad_acts[p],) = run(
            functools.partial(grad_act_kernel, cores),
            "grad_act",
            [((piece_rows, hidden), jnp.bfloat16)],
            [*all_cots[p], w_out],
            scratch=[pltpu.VMEM((piece_rows, width), jnp.bfloat16)],
            limit=LARGE,
        )

    def plain_factor(factor, s):
        mates = from_flipped(states[s], "seq", 1 << (factor - LOCAL))
        (states[s],) = run(
            functools.partial(plain_kernel, factor, s),
            "factor",
            [half],
            [states[s], mates, mixing],
        )

    def early_factor(p):
        send, keep = states[2 * p : 2 * p + 2]
        states[2 * p : 2 * p + 2] = run(
            functools.partial(early_kernel, last, pieces, p),
            "early_factor",
            [half, half],
            [keep, from_flipped(send, "seq", early_bit), mixing, messages[0]],
        )

    def late_factor(p):
        keep, send = states[2 * p : 2 * p + 2]
        mixeds[p] = run(
            functools.partial(late_kernel, last, pieces, p),
            "late_factor",
            [((2 * BLOCK, chan_count), jnp.bfloat16)] * 2,
            [keep, from_flipped(send, "seq", late_bit), mixing, *messages],
        )

    def hidden_and_grad(p):
        gathered = [
            from_offset(mixed, "ch", i) if i else mixed for i in range(cores) for mixed in mixeds[p]
        ]
        activations[p], owns[p], *backs = run(
            functools.partial(hidden_kernel, cores),
            "mlp_hidden_and_grad",
            [((piece_rows, hidden), jnp.bfloat16), (flat, jnp.float32)]
            + [block] * ((cores - 1) * QUARTERS),
            [*gathered, grad_acts[p], w_in],
            scratch=[
                pltpu.VMEM((piece_rows, width), jnp.bfloat16),
                pltpu.VMEM((piece_rows, width), jnp.float32),
            ],
            limit=LARGE,
        )
        parts[p] = [
            from_offset(back, "ch", cores - 1 - i // QUARTERS) for i, back in enumerate(backs)
        ]

    def transposed_back(p):
        quarters = run(
            functools.partial(back_kernel, last, pieces, p, cores),
            "late_and_early_back",
            [block] * QUARTERS,
            [stacked[p], owns[p], *parts[p], mixing, *messages],
        )
        quarters = [
            from_flipped(grad, "seq", mask) if mask else grad
            for grad, mask in zip(quarters, masks)
        ]
        states[2 * p : 2 * p + 2] = [quarters[1::2], quarters[0::2]]

    def regroup(s):
        states[s] = run(
            functools.partial(regroup_kernel, plain[-1], s),
            "regroup_and_factor_back",
            [half_wide, half],
            [*states[s], mixing],
        )

    def out_product(p):
        out_owns[p], *others = run(
            functools.partial(out_kernel, cores),
            "mlp_out",
            [(flat, jnp.float32)] + [flat_piece] * (cores - 1),
            [activations[p], *mixeds[p], w_out],
            limit=LARGE,
        )
        for i, other in enumerate(others):
            out_parts[i * pieces + p] = from_offset(other, "ch", cores - 1 - i)

    def plain_back(factor, s):
        mine, cross = states[s]
        theirs = from_flipped(cross, "seq", 1 << (factor - LOCAL))
        states[s] = run(
            functools.partial(plain_back_kernel, factor - 1, s),
            "factor_back",
            [half_wide, half if factor != plain[0] else half_wide],
            [mine, theirs, mixing],
        )

    waves = sorted((s + 2 * i, -i, s) for i in range(len(plain)) for s in range(subs))
    for _, i, s in waves:
        plain_factor(plain[-i], s)
        if plain[-i] == plain[-1]:
            if s == 1:
                stack()
            if s == subs - 1:
                late_factor(0)
            if s % 2:
                early_factor(s // 2)
    grad_act(0)
    for p in range(pieces):
        hidden_and_grad(p)
        if p + 1 < pieces:
            grad_act(p + 1)
            out_product(p)
            late_factor(p + 1)
        if p == 1:
            regroup(1)
            regroup(0)
        if p == pieces - 1:
            out_product(p)
        transposed_back(p)
    waves = [(5, -3, 0)]
    for s in range(subs):
        wave = s // 2 * 4 + 1 - s % 2
        waves += [(wave + 2 * i, i, s) for i in range(0 if s < 2 else -1, len(plain))]
    for wave, i, s in sorted(waves):
        if i == -3:
            outs = run(
                functools.partial(combine_kernel, cores, pieces),
                "combine",
                [((pieces, BLOCK, chan_count), jnp.bfloat16)] * QUARTERS,
                [*out_owns, *out_parts],
            )
            arrived = [
                from_flipped(out, "seq", mask) if mask else out for out, mask in zip(outs, masks)
            ]
        elif i < 0:
            regroup(s)
        else:
            plain_back(plain[-1 - i], s)
    (grad_conv,) = run(
        functools.partial(exit_kernel, subs),
        "local_factors_back",
        [whole],
        [g[0] for g in states] + [g[1] for g in states] + [mixing],
        [pattern],
        [pltpu.VMEM((blocks, BLOCK, chan_count), jnp.float32)] * 2
        + [pltpu.SMEM(pattern.shape, jnp.int32), pltpu.SemaphoreType.DMA],
        limit=LARGE,
    )
    (layer_out,) = call(assemble_kernel, "assemble", [whole], arrived)
    before, after = neighbours(grad_conv[:1], grad_conv[-1:], "seq")
    (grad_input,) = run(
        conv_back_kernel, "conv_back", [whole], [grad_conv, before, after, taps]
    )
    return (layer_out, convolved, grad_input)


def solution(mesh):
    return jax.shard_map(
        on_device,
        mesh=mesh,
        in_specs=(
            P("seq", "ch"),
            P(None, "ch"),
            P(None, "seq", None, None),
            P(None, "seq"),
            P(None, "ch"),
            P("ch", None),
            P("seq", "ch"),
        ),
        out_specs=(P("seq", "ch"), P("seq", "ch"), P("seq", "ch")),
        check_vma=False,
    )
```

```python
import functools

import jax
import jax.numpy as jnp
from jax import lax
from jax.experimental import pallas as pl
from jax.experimental.pallas import tpu as pltpu
from jax.sharding import PartitionSpec as P

BLOCK = 64
LOCAL = 2
QUARTERS = 4
TILE = 512
SMALL = 8 * 1024 * 1024
LARGE = 24 * 1024 * 1024

root_two_pi = 0.7978845608028654

IN_HBM = pl.BlockSpec(memory_space=pltpu.HBM)
IN_VMEM = pl.BlockSpec(memory_space=pltpu.VMEM)
ANYWHERE = pl.BlockSpec(memory_space=pl.ANY)
ACROSS = (((1,), (1,)), ((), ()))
OVER_ROWS = (((0,), (0,)), ((), ()))


def times(weights, value):
    return jnp.dot(weights, value, preferred_element_type=jnp.float32)


def times_transposed(weights, value):
    return lax.dot_general(weights, value, OVER_ROWS, preferred_element_type=jnp.float32)


def neighbours(first, last, axis):
    count = lax.axis_size(axis)
    ends = count - 1
    before = lax.ppermute(last, axis, [(i, (i + 1) % count) for i in range(ends)])
    after = lax.ppermute(first, axis, [((i + 1) % count, i) for i in range(ends)])
    return before, after


def from_flipped(block, axis, mask):
    count = lax.axis_size(axis)
    return lax.ppermute(block, axis, [(i, i ^ mask) for i in range(count)])


def from_offset(block, axis, offset):
    count = lax.axis_size(axis)
    return lax.ppermute(block, axis, [((i + offset) % count, i) for i in range(count)])


def call(kernel, name, outs, arrays, distant=(), scratch=(), order=(), limit=SMALL):
    count = len(distant) + len(arrays)

    def body(*refs):
        kernel(*refs[:count], *refs[count + len(order) :])

    return pl.pallas_call(
        body,
        out_shape=[jax.ShapeDtypeStruct(shape, kind) for shape, kind in outs],
        in_specs=[IN_HBM] * len(distant) + [IN_VMEM] * len(arrays) + [ANYWHERE] * len(order),
        out_specs=[IN_VMEM] * len(outs),
        scratch_shapes=list(scratch),
        compiler_params=pltpu.CompilerParams(vmem_limit_bytes=limit),
        cost_estimate=pl.CostEstimate(flops=0, bytes_accessed=0, transcendentals=0),
        name=name,
    )(*distant, *arrays, *order)


def own_bits():
    seat = lax.axis_index("seq")
    levels = lax.axis_size("seq").bit_length() - 1
    return (seat >> (levels - 2)) & 1, (seat >> (levels - 1)) & 1


def shifted(cells, before, after):
    rows = cells.shape[0]
    spot = lax.broadcasted_iota(jnp.int32, cells.shape, 0)
    up = jnp.where(spot == 0, before, pltpu.roll(cells, 1, 0))
    down = jnp.where(spot == rows - 1, after, pltpu.roll(cells, rows - 1, 0))
    return up, down


def chosen_blocks(sub):
    early, late = own_bits()
    first = sub // 2 * QUARTERS
    spot = early ^ (1 - sub % 2)
    return [first + spot * 2 + (late ^ other) for other in range(2)]


def local_factor(factor, pattern, source, mixing, target, chosen):
    for spot, block in enumerate(chosen):
        pair = mixing[factor, block]
        target[spot] = (
            times(pair[:, :BLOCK], source[block])
            + times(pair[:, BLOCK:], source[pattern[factor, block]])
        ).astype(jnp.bfloat16)


def entry_kernel(pattern_far, cells, before, after, taps, mixing, conv_ref, *rest):
    subs, (mixing_out, first, between, pattern, arrivals) = rest[:-5], rest[-5:]
    fetch = pltpu.make_async_copy(pattern_far, pattern, arrivals.at[0])
    fetch.start()
    keep = pltpu.make_async_copy(mixing, mixing_out, arrivals.at[1])
    keep.start()
    values = cells[...].astype(jnp.float32)
    scale = taps[...].astype(jnp.float32)
    up, down = shifted(
        values, before[...].astype(jnp.float32), after[...].astype(jnp.float32)
    )
    convolved = (scale[0:1] * up + scale[1:2] * values + scale[2:3] * down).astype(jnp.bfloat16)
    conv_ref[...] = convolved
    first[...] = convolved.reshape(first.shape)
    fetch.wait()
    every = range(first.shape[0])
    refs = (first, between)
    for factor in range(LOCAL - 1):
        local_factor(factor, pattern, refs[factor % 2], mixing, refs[1 - factor % 2], every)
    source = refs[(LOCAL - 1) % 2]
    for number, sub in enumerate(subs):
        local_factor(LOCAL - 1, pattern, source, mixing, sub, chosen_blocks(number))
    keep.wait()


def plain_kernel(factor, number, state, mates, mixing, out):
    for spot, block in enumerate(chosen_blocks(number)):
        pair = mixing[factor, block]
        out[spot] = (
            times(pair[:, :BLOCK], state[spot]) + times(pair[:, BLOCK:], mates[spot])
        ).astype(jnp.bfloat16)


def packed(message, pieces, number):
    across = message.shape[-1] // (2 * BLOCK)
    lanes = pl.ds(number % across * 2 * BLOCK, 2 * BLOCK)
    return message.at[pieces + number // across, :, lanes]


def pack_kernel(factor, pieces, cots, mixing, own, *messages):
    my_early, my_late = own_bits()
    for piece in range(pieces):
        base = piece * QUARTERS
        own[piece] = cots[base + my_early * 2 + my_late]
        for flip, message in enumerate(messages, 1):
            early, late = my_early ^ (flip & 1), my_late ^ (flip >> 1)
            message[piece] = cots[base + early * 2 + late]
            for which in range(2):
                number = which * pieces + piece
                if flip == 1:
                    for other in range(2):
                        packed(message, pieces, number * 2 + other)[...] = mixing[
                            factor + which, base + early * 2 + (late ^ other)
                        ]
                else:
                    packed(message, pieces, number)[...] = mixing[
                        factor + which, base + early * 2 + late
                    ]


def stack_kernel(pieces, *rest):
    quarters, outs = rest[:QUARTERS], rest[QUARTERS:]
    for piece, out in enumerate(outs):
        for quarter, values in enumerate(quarters):
            out[quarter * BLOCK : (quarter + 1) * BLOCK] = values[piece]


def mixing_of(factor, which, pieces, piece, mixing, messages, quarter, other=0):
    if quarter == 0:
        early, late = own_bits()
        return mixing[factor + which, piece * QUARTERS + early * 2 + (late ^ other)]
    number = which * pieces + piece
    if quarter == 1:
        number = number * 2 + other
    return packed(messages[quarter - 1], pieces, number)[...]


def early_kernel(factor, pieces, piece, keep, recv, mixing, message, keep_out, send_out):
    weights = functools.partial(mixing_of, factor, 0, pieces, piece, mixing, [message])
    for other, out in enumerate((keep_out, send_out)):
        mine, theirs = keep[other], recv[other]
        pair = weights(0, other)
        out[0] = (times(pair[:, :BLOCK], mine) + times(pair[:, BLOCK:], theirs)).astype(
            jnp.bfloat16
        )
        pair = weights(1, other)
        out[1] = (times(pair[:, :BLOCK], theirs) + times(pair[:, BLOCK:], mine)).astype(
            jnp.bfloat16
        )


def late_kernel(factor, pieces, piece, keep, recv, mixing, *rest):
    messages, outs = rest[:-2], rest[-2:]
    values = [keep[0], keep[1], recv[0], recv[1]]
    for quarter in range(QUARTERS):
        pair = mixing_of(factor, 1, pieces, piece, mixing, messages, quarter)
        rows = slice(quarter % 2 * BLOCK, (quarter % 2 + 1) * BLOCK)
        outs[quarter // 2][rows] = (
            times(pair[:, :BLOCK], values[quarter]) + times(pair[:, BLOCK:], values[quarter ^ 2])
        ).astype(jnp.bfloat16)


def back_kernel(factor, pieces, piece, cores, cots, total, *rest):
    count = (cores - 1) * 2
    parts, (mixing, message1, message2, message3, *outs) = rest[:count], rest[count:]
    messages = (message1, message2, message3)
    grads = []
    for quarter in range(QUARTERS):
        rows = slice(quarter * BLOCK, (quarter + 1) * BLOCK)
        grad = cots[rows].astype(jnp.float32) + total[rows]
        inner = slice(quarter % 2 * BLOCK, (quarter % 2 + 1) * BLOCK)
        for part in parts[quarter // 2 :: 2]:
            grad = grad + part[inner].astype(jnp.float32)
        grads.append(grad.astype(jnp.bfloat16))
    for which, flip in ((1, 2), (0, 1)):
        both = [
            times_transposed(
                mixing_of(factor, which, pieces, piece, mixing, messages, quarter),
                grads[quarter],
            )
            for quarter in range(QUARTERS)
        ]
        grads = [
            (both[quarter][:BLOCK] + both[quarter ^ flip][BLOCK:]).astype(jnp.bfloat16)
            for quarter in range(QUARTERS)
        ]
    for grad, out in zip(grads, outs):
        out[...] = grad


def regroup_kernel(factor, piece, *rest):
    quarters, mixing, outs = rest[:QUARTERS], rest[QUARTERS], rest[QUARTERS + 1 :]
    for quarter, grad in enumerate(quarters):
        number = 2 * piece + 1 - quarter % 2
        own, cross = outs[:2] if number % 2 else outs[2:]
        spot = quarter // 2
        both = times_transposed(mixing[factor, chosen_blocks(number)[spot]], grad[...])
        own[spot] = both[:BLOCK]
        cross[spot] = both[BLOCK:].astype(jnp.bfloat16)


def plain_back_kernel(factor, number, mine, theirs, mixing, own, cross):
    for spot, block in enumerate(chosen_blocks(number)):
        grad = (mine[spot] + theirs[spot].astype(jnp.float32)).astype(jnp.bfloat16)
        both = times_transposed(mixing[factor, block], grad)
        own[spot] = both[:BLOCK]
        cross[spot] = both[BLOCK:].astype(cross.dtype)


def exit_kernel(count, pattern_far, *rest):
    mine, theirs = rest[:count], rest[count : 2 * count]
    mixing, out, own, cross, pattern, arrival = rest[2 * count :]
    fetch = pltpu.make_async_copy(pattern_far, pattern, arrival)
    fetch.start()
    blocks = own.shape[0]
    for number in range(count):
        for spot, block in enumerate(chosen_blocks(number)):
            own[block] = mine[number][spot]
            cross[block] = theirs[number][spot]
    fetch.wait()
    for factor in reversed(range(LOCAL)):
        for block in range(blocks):
            own[block] += cross[pattern[factor, block]]
        for block in range(blocks):
            grad = own[block].astype(jnp.bfloat16)
            if factor == 0:
                out[block * BLOCK : (block + 1) * BLOCK] = grad
            else:
                both = times_transposed(mixing[factor - 1, block], grad)
                own[block] = both[:BLOCK]
                cross[block] = both[BLOCK:]


def conv_back_kernel(cells, before, after, taps, out):
    values = cells[...].astype(jnp.float32)
    scale = taps[...].astype(jnp.float32)
    up, down = shifted(
        values, before[...].astype(jnp.float32), after[...].astype(jnp.float32)
    )
    out[...] = (scale[0:1] * down + scale[1:2] * values + scale[2:3] * up).astype(jnp.bfloat16)


def channel_spots(count, chans):
    core = lax.axis_index("ch")
    return [
        pl.ds(pl.multiple_of(lax.rem(core + i, count) * chans, chans), chans)
        for i in range(count)
    ]


def grad_act_kernel(count, *rest):
    cots, (w_out, grad_act, c_all) = rest[:count], rest[count:]
    for spot, cot in zip(channel_spots(count, cots[0].shape[1]), cots):
        c_all[:, spot] = cot[...]
    hidden = w_out.shape[0]
    tile = min(TILE, hidden)
    for start in range(0, hidden, tile):
        grad_act[:, start : start + tile] = lax.dot_general(
            c_all[...], w_out[start : start + tile], ACROSS, preferred_element_type=jnp.float32
        ).astype(grad_act.dtype)


def hidden_kernel(count, *rest):
    mixed, (grad_act, w_in, w_out) = rest[: 2 * count], rest[2 * count : 2 * count + 3]
    own, out_own = rest[2 * count + 3 : 2 * count + 5]
    sent, (x_all, back_sum, out_sum) = rest[2 * count + 5 : -3], rest[-3:]
    backs, outs = sent[: 2 * (count - 1)], sent[2 * (count - 1) :]
    rows, chans = mixed[0].shape
    spots = channel_spots(count, chans)
    for i, spot in enumerate(spots):
        x_all[:rows, spot] = mixed[2 * i][...]
        x_all[rows:, spot] = mixed[2 * i + 1][...]
    size = w_in.shape[1]
    tile = min(TILE, size)
    for start in range(0, size, tile):
        tiles = slice(start, start + tile)
        hidden = times(x_all[...], w_in[:, tiles])
        square = hidden * hidden
        tanh_val = jnp.tanh(hidden * (root_two_pi + root_two_pi * 0.044715 * square))
        half = 0.5 + 0.5 * tanh_val
        gelu = hidden * half
        slope = 2.0 * root_two_pi + 6.0 * root_two_pi * 0.044715 * square
        derivative = half + gelu * (1.0 - half) * slope
        grad_hidden = (grad_act[:, tiles].astype(jnp.float32) * derivative).astype(jnp.bfloat16)
        back = lax.dot_general(
            grad_hidden, w_in[:, tiles], ACROSS, preferred_element_type=jnp.float32
        )
        out = times(gelu.astype(jnp.bfloat16), w_out[tiles])
        if start == 0:
            back_sum[...] = back
            out_sum[...] = out
        else:
            back_sum[...] += back
            out_sum[...] += out
    own[...] = back_sum[:, spots[0]]
    out_own[:rows] = out_sum[:rows, spots[0]] + mixed[0][...].astype(jnp.float32)
    out_own[rows:] = out_sum[rows:, spots[0]] + mixed[1][...].astype(jnp.float32)
    for i, spot in enumerate(spots[1:]):
        backs[2 * i][...] = back_sum[:rows, spot].astype(jnp.bfloat16)
        backs[2 * i + 1][...] = back_sum[rows:, spot].astype(jnp.bfloat16)
        outs[2 * i][...] = out_sum[:rows, spot].astype(jnp.bfloat16)
        outs[2 * i + 1][...] = out_sum[rows:, spot].astype(jnp.bfloat16)


def sum_kernel(own, *rest):
    parts, out = rest[:-1], rest[-1]
    for side in range(2):
        rows = slice(side * 2 * BLOCK, (side + 1) * 2 * BLOCK)
        total = own[rows]
        for part in parts[side::2]:
            total = total + part[...].astype(jnp.float32)
        out[rows] = total.astype(jnp.bfloat16)


def combine_kernel(pieces, own, *rest):
    sums, parts, outs = rest[: pieces - 1], rest[pieces - 1 : -QUARTERS], rest[-QUARTERS:]
    for quarter, out in enumerate(outs):
        rows = slice(quarter * BLOCK, (quarter + 1) * BLOCK)
        for piece, done in enumerate(sums):
            out[piece] = done[rows]
        total = own[rows]
        inner = slice(quarter % 2 * BLOCK, (quarter % 2 + 1) * BLOCK)
        for part in parts[quarter // 2 :: 2]:
            total = total + part[inner].astype(jnp.float32)
        out[pieces - 1] = total.astype(jnp.bfloat16)


def assemble_kernel(*rest):
    quarters, (out, ready) = rest[:-2], rest[-2:]
    ready[...] = jnp.zeros_like(ready)
    my_early, my_late = own_bits()
    for quarter, values in enumerate(quarters):
        spot = (my_early ^ (quarter & 1)) * 2 + (my_late ^ (quarter >> 1))
        for piece in range(values.shape[0]):
            start = pl.multiple_of((piece * QUARTERS + spot) * BLOCK, BLOCK)
            out[pl.ds(start, BLOCK)] = values[piece]


def on_device(inputs, conv_weight, mixing, pattern, w_in, w_out, cotangent):
    row_count, chan_count = inputs.shape
    blocks = row_count // BLOCK
    pieces = blocks // QUARTERS
    width, hidden = w_in.shape
    cores = lax.axis_size("ch")
    levels = lax.axis_size("seq").bit_length() - 1
    plain = list(range(LOCAL, LOCAL + levels - 2))
    last = LOCAL + levels - 2
    early_bit, late_bit = 1 << (levels - 2), 1 << (levels - 1)
    masks = [0, early_bit, late_bit, early_bit | late_bit]
    half = ((2, BLOCK, chan_count), jnp.bfloat16)
    half_wide = ((2, BLOCK, chan_count), jnp.float32)
    whole = ((row_count, chan_count), jnp.bfloat16)
    piece_rows = QUARTERS * BLOCK
    flat = (piece_rows, chan_count)
    block = ((BLOCK, chan_count), jnp.bfloat16)
    half_flat = ((2 * BLOCK, chan_count), jnp.bfloat16)
    flat_piece = (flat, jnp.bfloat16)
    flops = 2 * piece_rows * width * hidden

    latest = []

    def run(kernel, name, outs, arrays, *args, **kwargs):
        results = call(kernel, name, outs, arrays, *args, order=tuple(latest), **kwargs)
        latest[:] = results[-1:]
        return results

    before, after = neighbours(inputs[:1], inputs[-1:], "seq")
    per_block = chan_count // (2 * BLOCK)
    lengths = [pieces + -(-pieces * 2 * (1 + (flip == 1)) // per_block) for flip in (1, 2, 3)]
    subs = 2 * pieces
    convolved, *states, mixing = run(
        entry_kernel,
        "conv_and_local_factors",
        [whole] + [half] * subs + [(mixing.shape, mixing.dtype)],
        [inputs, before, after, conv_weight, mixing],
        [pattern],
        [pltpu.VMEM((blocks, BLOCK, chan_count), jnp.bfloat16)] * 2
        + [pltpu.SMEM(pattern.shape, jnp.int32), pltpu.SemaphoreType.DMA((2,))],
    )
    own_cots, *messages = run(
        functools.partial(pack_kernel, last, pieces),
        "pack",
        [((pieces, BLOCK, chan_count), jnp.bfloat16)]
        + [((length, BLOCK, chan_count), jnp.bfloat16) for length in lengths],
        [cotangent.reshape(blocks, BLOCK, chan_count), mixing],
    )
    messages = [from_flipped(m, "seq", mask) for m, mask in zip(messages, masks[1:])]
    stacked = [None] * pieces
    all_cots = [None] * pieces
    grad_acts = [None] * pieces
    parts = [None] * pieces
    mixeds = [None] * pieces
    owns = [None] * pieces
    out_owns = [None] * pieces
    out_parts = [[] for _ in range(pieces)]
    out_sums = []

    def stack():
        stacked[:] = run(
            functools.partial(stack_kernel, pieces),
            "stack",
            [flat_piece] * pieces,
            [own_cots, *messages],
        )
        for p, piece in enumerate(stacked):
            all_cots[p] = [piece] + [from_offset(piece, "ch", i) for i in range(1, cores)]

    def grad_act(p):
        (grad_acts[p],) = run(
            functools.partial(grad_act_kernel, cores),
            "grad_act",
            [((piece_rows, hidden), jnp.bfloat16)],
            [*all_cots[p], w_out],
            scratch=[pltpu.VMEM((piece_rows, width), jnp.bfloat16)],
            limit=LARGE,
        )

    def plain_factor(factor, s):
        mates = from_flipped(states[s], "seq", 1 << (factor - LOCAL))
        (states[s],) = run(
            functools.partial(plain_kernel, factor, s),
            "factor",
            [half],
            [states[s], mates, mixing],
        )

    def early_factor(p):
        send, keep = states[2 * p : 2 * p + 2]
        states[2 * p : 2 * p + 2] = run(
            functools.partial(early_kernel, last, pieces, p),
            "early_factor",
            [half, half],
            [keep, from_flipped(send, "seq", early_bit), mixing, messages[0]],
        )

    def late_factor(p):
        keep, send = states[2 * p : 2 * p + 2]
        mixeds[p] = run(
            functools.partial(late_kernel, last, pieces, p),
            "late_factor",
            [half_flat] * 2,
            [keep, from_flipped(send, "seq", late_bit), mixing, *messages],
        )

    def hidden_and_grad(p):
        gathered = [
            from_offset(mixed, "ch", i) if i else mixed for i in range(cores) for mixed in mixeds[p]
        ]
        owns[p], out_owns[p], *sent = run(
            functools.partial(hidden_kernel, cores),
            "mlp_hidden_grad_and_out",
            [(flat, jnp.float32)] * 2
            + [half_flat] * ((cores - 1) * 4),
            [*gathered, grad_acts[p], w_in, w_out],
            scratch=[pltpu.VMEM((piece_rows, width), jnp.bfloat16)]
            + [pltpu.VMEM((piece_rows, width), jnp.float32)] * 2,
            limit=LARGE,
        )
        backs, outs = sent[: (cores - 1) * 2], sent[(cores - 1) * 2 :]
        parts[p] = [
            from_offset(back, "ch", cores - 1 - i // 2) for i, back in enumerate(backs)
        ]
        out_parts[p] = [
            from_offset(out, "ch", cores - 1 - i // 2) for i, out in enumerate(outs)
        ]

    def transposed_back(p):
        quarters = run(
            functools.partial(back_kernel, last, pieces, p, cores),
            "late_and_early_back",
            [block] * QUARTERS,
            [stacked[p], owns[p], *parts[p], mixing, *messages],
        )
        states[2 * p] = [
            from_flipped(grad, "seq", mask) if mask else grad
            for grad, mask in zip(quarters, masks)
        ]

    def regroup(p):
        results = run(
            functools.partial(regroup_kernel, plain[-1], p),
            "regroup_and_factor_back",
            [half_wide, half] * 2,
            [*states[2 * p], mixing],
        )
        states[2 * p : 2 * p + 2] = [results[2:], results[:2]]

    def plain_back(factor, s):
        mine, cross = states[s]
        theirs = from_flipped(cross, "seq", 1 << (factor - LOCAL))
        states[s] = run(
            functools.partial(plain_back_kernel, factor - 1, s),
            "factor_back",
            [half_wide, half if factor != plain[0] else half_wide],
            [mine, theirs, mixing],
        )

    waves = sorted((s + 2 * i, -i, s) for i in range(len(plain)) for s in range(subs))
    for wave, i, s in waves:
        plain_factor(plain[-i], s)
        if i == 0 and s == subs - 1:
            stack()
        if plain[-i] == plain[-1]:
            if s == subs - 1:
                late_factor(0)
            if s % 2:
                early_factor(s // 2)
    grad_act(0)
    for p in range(pieces):
        hidden_and_grad(p)
        if p + 1 < pieces:
            late_factor(p + 1)
            grad_act(p + 1)
        if p == 1:
            regroup(0)
        transposed_back(p)
        if p + 1 < pieces:
            out_sums += run(sum_kernel, "out_sum", [flat_piece], [out_owns[p], *out_parts[p]])
    waves = []
    for s in range(subs):
        wave = s // 2 * 4 + 1 - s % 2
        waves += [(wave + 2 * i, i, s) for i in range(len(plain))]
        if s % 2 and s > 1:
            waves.append((wave - 2.5, -1, s // 2))
    waves += [(3.5, -2, 0), (5.5, -3, 0)]
    for wave, i, s in sorted(waves):
        if i == -3:
            layer_out, _ = run(
                assemble_kernel, "assemble", [whole, ((8, 128), jnp.float32)], arrived
            )
        elif i == -2:
            outs = run(
                functools.partial(combine_kernel, pieces),
                "combine",
                [((pieces, BLOCK, chan_count), jnp.bfloat16)] * QUARTERS,
                [out_owns[-1], *out_sums, *out_parts[-1]],
            )
            arrived = [
                from_flipped(out, "seq", mask) if mask else out for out, mask in zip(outs, masks)
            ]
        elif i < 0:
            regroup(s)
        else:
            plain_back(plain[-1 - i], s)
    (grad_conv,) = run(
        functools.partial(exit_kernel, subs),
        "local_factors_back",
        [whole],
        [g[0] for g in states] + [g[1] for g in states] + [mixing],
        [pattern],
        [pltpu.VMEM((blocks, BLOCK, chan_count), jnp.float32)] * 2
        + [pltpu.SMEM(pattern.shape, jnp.int32), pltpu.SemaphoreType.DMA],
        limit=LARGE,
    )
    before, after = neighbours(grad_conv[:1], grad_conv[-1:], "seq")
    (grad_input,) = run(
        conv_back_kernel, "conv_back", [whole], [grad_conv, before, after, conv_weight]
    )
    return (layer_out, convolved, grad_input)


def solution(mesh):
    return jax.shard_map(
        on_device,
        mesh=mesh,
        in_specs=(
            P("seq", "ch"),
            P(None, "ch"),
            P(None, "seq", None, None),
            P(None, "seq"),
            P(None, "ch"),
            P("ch", None),
            P("seq", "ch"),
        ),
        out_specs=(P("seq", "ch"), P("seq", "ch"), P("seq", "ch")),
        check_vma=False,
    )
```

```python
import functools

import jax
import jax.numpy as jnp
from jax import lax
from jax.experimental import pallas as pl
from jax.experimental.pallas import tpu as pltpu
from jax.sharding import PartitionSpec as P

BLOCK = 64
LOCAL = 2
QUARTERS = 4
TILE = 512
SMALL = 8 * 1024 * 1024
LARGE = 20 * 1024 * 1024
ALL = 44 * 1024 * 1024

root_two_pi = 0.7978845608028654

IN_HBM = pl.BlockSpec(memory_space=pltpu.HBM)
IN_VMEM = pl.BlockSpec(memory_space=pltpu.VMEM)
ANYWHERE = pl.BlockSpec(memory_space=pl.ANY)
ACROSS = (((1,), (1,)), ((), ()))
OVER_ROWS = (((0,), (0,)), ((), ()))


def times(weights, value):
    return jnp.dot(weights, value, preferred_element_type=jnp.float32)


def times_transposed(weights, value):
    return lax.dot_general(weights, value, OVER_ROWS, preferred_element_type=jnp.float32)


def neighbours(first, last, axis):
    count = lax.axis_size(axis)
    ends = count - 1
    before = lax.ppermute(last, axis, [(i, (i + 1) % count) for i in range(ends)])
    after = lax.ppermute(first, axis, [((i + 1) % count, i) for i in range(ends)])
    return before, after


def from_flipped(block, axis, mask):
    count = lax.axis_size(axis)
    return lax.ppermute(block, axis, [(i, i ^ mask) for i in range(count)])


def from_offset(block, axis, offset):
    count = lax.axis_size(axis)
    return lax.ppermute(block, axis, [((i + offset) % count, i) for i in range(count)])


def call(kernel, name, outs, arrays, distant=(), scratch=(), order=(), limit=SMALL):
    count = len(distant) + len(arrays)

    def body(*refs):
        kernel(*refs[:count], *refs[count + len(order) :])

    return pl.pallas_call(
        body,
        out_shape=[jax.ShapeDtypeStruct(shape, kind) for shape, kind in outs],
        in_specs=[IN_HBM] * len(distant) + [IN_VMEM] * len(arrays) + [ANYWHERE] * len(order),
        out_specs=[IN_VMEM] * len(outs),
        scratch_shapes=list(scratch),
        compiler_params=pltpu.CompilerParams(vmem_limit_bytes=limit),
        cost_estimate=pl.CostEstimate(flops=0, bytes_accessed=0, transcendentals=0),
        name=name,
    )(*distant, *arrays, *order)


def own_bits():
    seat = lax.axis_index("seq")
    levels = lax.axis_size("seq").bit_length() - 1
    return (seat >> (levels - 2)) & 1, (seat >> (levels - 1)) & 1


def shifted(cells, before, after):
    rows = cells.shape[0]
    spot = lax.broadcasted_iota(jnp.int32, cells.shape, 0)
    up = jnp.where(spot == 0, before, pltpu.roll(cells, 1, 0))
    down = jnp.where(spot == rows - 1, after, pltpu.roll(cells, rows - 1, 0))
    return up, down


def chosen_blocks(subs):
    early, late = own_bits()
    return [
        sub // 2 * QUARTERS + (early ^ (1 - sub % 2)) * 2 + (late ^ other)
        for sub in subs
        for other in range(2)
    ]


def local_factor(factor, pattern, source, mixing, target, chosen):
    for spot, block in enumerate(chosen):
        pair = mixing[factor, block]
        target[spot] = (
            times(pair[:, :BLOCK], source[block])
            + times(pair[:, BLOCK:], source[pattern[factor, block]])
        ).astype(jnp.bfloat16)


def entry_kernel(units, pattern_far, cells, before, after, taps, mixing, conv_ref, *rest):
    outs, (first, between, pattern, arrival) = rest[:-4], rest[-4:]
    fetch = pltpu.make_async_copy(pattern_far, pattern, arrival)
    fetch.start()
    values = cells[...].astype(jnp.float32)
    scale = taps[...].astype(jnp.float32)
    up, down = shifted(
        values, before[...].astype(jnp.float32), after[...].astype(jnp.float32)
    )
    convolved = (scale[0:1] * up + scale[1:2] * values + scale[2:3] * down).astype(jnp.bfloat16)
    conv_ref[...] = convolved
    first[...] = convolved.reshape(first.shape)
    fetch.wait()
    every = range(first.shape[0])
    refs = (first, between)
    for factor in range(LOCAL - 1):
        local_factor(factor, pattern, refs[factor % 2], mixing, refs[1 - factor % 2], every)
    source = refs[(LOCAL - 1) % 2]
    for unit, out in zip(units, outs):
        local_factor(LOCAL - 1, pattern, source, mixing, out, chosen_blocks(unit))


def plain_kernel(factor, unit, state, mates, mixing, *outs):
    for spot, block in enumerate(chosen_blocks(unit)):
        pair = mixing[factor, block]
        per_out = state.shape[0] // len(outs)
        outs[spot // per_out][spot % per_out] = (
            times(pair[:, :BLOCK], state[spot]) + times(pair[:, BLOCK:], mates[spot])
        ).astype(jnp.bfloat16)


def packed(message, pieces, number):
    across = message.shape[-1] // (2 * BLOCK)
    lanes = pl.ds(number % across * 2 * BLOCK, 2 * BLOCK)
    return message.at[pieces + number // across, :, lanes]


def load_kernel(factor, pieces, cots_far, mixing_far, cells_far, taps_far, *rest):
    own, *messages, mixing, cells, taps, cots, arrivals = rest
    fetches = [
        pltpu.make_async_copy(far, near, arrivals.at[i])
        for i, (far, near) in enumerate(
            ((mixing_far, mixing), (cots_far, cots), (cells_far, cells), (taps_far, taps))
        )
    ]
    for fetch in fetches:
        fetch.start()
    fetches[0].wait()
    fetches[1].wait()
    my_early, my_late = own_bits()
    for piece in range(pieces):
        base = piece * QUARTERS
        own[piece] = cots[base + my_early * 2 + my_late]
        for flip, message in enumerate(messages, 1):
            early, late = my_early ^ (flip & 1), my_late ^ (flip >> 1)
            message[piece] = cots[base + early * 2 + late]
            for which in range(2):
                number = which * pieces + piece
                if flip == 1:
                    for other in range(2):
                        packed(message, pieces, number * 2 + other)[...] = mixing[
                            factor + which, base + early * 2 + (late ^ other)
                        ]
                else:
                    packed(message, pieces, number)[...] = mixing[
                        factor + which, base + early * 2 + late
                    ]
    fetches[2].wait()
    fetches[3].wait()


def stack_kernel(pieces, *rest):
    quarters, outs = rest[:QUARTERS], rest[QUARTERS:]
    for piece, out in enumerate(outs):
        for quarter, values in enumerate(quarters):
            out[quarter * BLOCK : (quarter + 1) * BLOCK] = values[piece]


def mixing_of(factor, which, pieces, piece, mixing, messages, quarter, other=0):
    if quarter == 0:
        early, late = own_bits()
        return mixing[factor + which, piece * QUARTERS + early * 2 + (late ^ other)]
    number = which * pieces + piece
    if quarter == 1:
        number = number * 2 + other
    return packed(messages[quarter - 1], pieces, number)[...]


def early_kernel(factor, pieces, piece, keep, recv, mixing, message, keep_out, send_out):
    weights = functools.partial(mixing_of, factor, 0, pieces, piece, mixing, [message])
    for other, out in enumerate((keep_out, send_out)):
        mine, theirs = keep[other], recv[other]
        pair = weights(0, other)
        out[0] = (times(pair[:, :BLOCK], mine) + times(pair[:, BLOCK:], theirs)).astype(
            jnp.bfloat16
        )
        pair = weights(1, other)
        out[1] = (times(pair[:, :BLOCK], theirs) + times(pair[:, BLOCK:], mine)).astype(
            jnp.bfloat16
        )


def late_kernel(factor, pieces, piece, keep, recv, mixing, *rest):
    messages, outs = rest[:-2], rest[-2:]
    values = [keep[0], keep[1], recv[0], recv[1]]
    for quarter in range(QUARTERS):
        pair = mixing_of(factor, 1, pieces, piece, mixing, messages, quarter)
        rows = slice(quarter % 2 * BLOCK, (quarter % 2 + 1) * BLOCK)
        outs[quarter // 2][rows] = (
            times(pair[:, :BLOCK], values[quarter]) + times(pair[:, BLOCK:], values[quarter ^ 2])
        ).astype(jnp.bfloat16)


def back_kernel(factor, pieces, piece, cores, cots, total, *rest):
    count = (cores - 1) * 2
    parts, (mixing, message1, message2, message3, *outs) = rest[:count], rest[count:]
    messages = (message1, message2, message3)
    grads = []
    for quarter in range(QUARTERS):
        rows = slice(quarter * BLOCK, (quarter + 1) * BLOCK)
        grad = cots[rows].astype(jnp.float32) + total[rows]
        inner = slice(quarter % 2 * BLOCK, (quarter % 2 + 1) * BLOCK)
        for part in parts[quarter // 2 :: 2]:
            grad = grad + part[inner].astype(jnp.float32)
        grads.append(grad.astype(jnp.bfloat16))
    for which, flip in ((1, 2), (0, 1)):
        both = [
            times_transposed(
                mixing_of(factor, which, pieces, piece, mixing, messages, quarter),
                grads[quarter],
            )
            for quarter in range(QUARTERS)
        ]
        grads = [
            (both[quarter][:BLOCK] + both[quarter ^ flip][BLOCK:]).astype(jnp.bfloat16)
            for quarter in range(QUARTERS)
        ]
    for grad, out in zip(grads, outs):
        out[...] = grad


def regroup_kernel(factor, units, *rest):
    quarters, mixing, outs = rest[:QUARTERS], rest[QUARTERS], rest[QUARTERS + 1 :]
    for number, unit in enumerate(units):
        own, cross = outs[2 * number : 2 * number + 2]
        for spot, block in enumerate(chosen_blocks(unit)):
            grad = quarters[1 - unit[spot // 2] % 2 + spot % 2 * 2][...]
            both = times_transposed(mixing[factor, block], grad)
            own[spot] = both[:BLOCK]
            cross[spot] = both[BLOCK:].astype(jnp.bfloat16)


def plain_back_kernel(factor, unit, mine, theirs, mixing, own, cross):
    for spot, block in enumerate(chosen_blocks(unit)):
        grad = (mine[spot] + theirs[spot].astype(jnp.float32)).astype(jnp.bfloat16)
        both = times_transposed(mixing[factor, block], grad)
        own[spot] = both[:BLOCK]
        cross[spot] = both[BLOCK:].astype(cross.dtype)


def exit_kernel(units, pattern_far, *rest):
    count = len(units)
    mine, theirs = rest[:count], rest[count : 2 * count]
    mixing, out, own, cross, pattern, arrival = rest[2 * count :]
    fetch = pltpu.make_async_copy(pattern_far, pattern, arrival)
    fetch.start()
    blocks = own.shape[0]
    for number, unit in enumerate(units):
        for spot, block in enumerate(chosen_blocks(unit)):
            own[block] = mine[number][spot]
            cross[block] = theirs[number][spot]
    fetch.wait()
    for factor in reversed(range(LOCAL)):
        for block in range(blocks):
            own[block] += cross[pattern[factor, block]]
        for block in range(blocks):
            grad = own[block].astype(jnp.bfloat16)
            if factor == 0:
                out[block * BLOCK : (block + 1) * BLOCK] = grad
            else:
                both = times_transposed(mixing[factor - 1, block], grad)
                own[block] = both[:BLOCK]
                cross[block] = both[BLOCK:]


def conv_back_kernel(cells, before, after, taps, out):
    values = cells[...].astype(jnp.float32)
    scale = taps[...].astype(jnp.float32)
    up, down = shifted(
        values, before[...].astype(jnp.float32), after[...].astype(jnp.float32)
    )
    out[...] = (scale[0:1] * down + scale[1:2] * values + scale[2:3] * up).astype(jnp.bfloat16)


def channel_spots(count, chans):
    core = lax.axis_index("ch")
    return [
        pl.ds(pl.multiple_of(lax.rem(core + i, count) * chans, chans), chans)
        for i in range(count)
    ]


def grad_act_kernel(count, *rest):
    cots, (w_out, grad_act, c_all) = rest[:count], rest[count:]
    for spot, cot in zip(channel_spots(count, cots[0].shape[1]), cots):
        c_all[:, spot] = cot[...]
    hidden = w_out.shape[0]
    tile = min(TILE, hidden)
    for start in range(0, hidden, tile):
        grad_act[:, start : start + tile] = lax.dot_general(
            c_all[...], w_out[start : start + tile], ACROSS, preferred_element_type=jnp.float32
        ).astype(grad_act.dtype)


def hidden_kernel(count, *rest):
    mixed, (grad_act, w_in, activation, own) = rest[: 2 * count], rest[2 * count : 2 * count + 4]
    backs, (x_all, back_sum) = rest[2 * count + 4 : -2], rest[-2:]
    rows, chans = mixed[0].shape
    spots = channel_spots(count, chans)
    for i, spot in enumerate(spots):
        x_all[:rows, spot] = mixed[2 * i][...]
        x_all[rows:, spot] = mixed[2 * i + 1][...]
    size = w_in.shape[1]
    tile = min(TILE, size)
    for start in range(0, size, tile):
        tiles = slice(start, start + tile)
        hidden = times(x_all[...], w_in[:, tiles])
        square = hidden * hidden
        tanh_val = jnp.tanh(hidden * (root_two_pi + root_two_pi * 0.044715 * square))
        half = 0.5 + 0.5 * tanh_val
        gelu = hidden * half
        activation[:, tiles] = gelu.astype(jnp.bfloat16)
        slope = 2.0 * root_two_pi + 6.0 * root_two_pi * 0.044715 * square
        derivative = half + gelu * (1.0 - half) * slope
        grad_hidden = (grad_act[:, tiles].astype(jnp.float32) * derivative).astype(jnp.bfloat16)
        back = lax.dot_general(
            grad_hidden, w_in[:, tiles], ACROSS, preferred_element_type=jnp.float32
        )
        if start == 0:
            back_sum[...] = back
        else:
            back_sum[...] += back
    own[...] = back_sum[:, spots[0]]
    for i, spot in enumerate(spots[1:]):
        backs[2 * i][...] = back_sum[:rows, spot].astype(jnp.bfloat16)
        backs[2 * i + 1][...] = back_sum[rows:, spot].astype(jnp.bfloat16)


def out_kernel(count, activation, top, bottom, w_out, own, *others):
    rows, chans = top.shape
    for i, spot in enumerate(channel_spots(count, chans)):
        product = times(activation[...], w_out[:, spot])
        if i == 0:
            own[:rows] = top[...].astype(jnp.float32) + product[:rows]
            own[rows:] = bottom[...].astype(jnp.float32) + product[rows:]
        else:
            cuts = len(others) // (count - 1)
            for cut in range(cuts):
                size = 2 * rows // cuts
                part = product[cut * size : (cut + 1) * size]
                others[(i - 1) * cuts + cut][...] = part.astype(jnp.bfloat16)


def combine_kernel(pieces, counts, *rest):
    owns, parts, outs = rest[:pieces], rest[pieces:-QUARTERS], rest[-QUARTERS:]
    for piece in range(pieces):
        per_piece = counts[piece]
        mine, parts = parts[:per_piece], parts[per_piece:]
        for quarter, out in enumerate(outs):
            total = owns[piece][quarter * BLOCK : (quarter + 1) * BLOCK]
            cuts = total.shape[0] * QUARTERS // mine[0].shape[0]
            start = quarter * BLOCK % mine[0].shape[0]
            for part in mine[quarter * cuts // QUARTERS :: cuts]:
                total = total + part[start : start + BLOCK].astype(jnp.float32)
            out[piece] = total.astype(jnp.bfloat16)


def assemble_kernel(*rest):
    quarters, out = rest[:-1], rest[-1]
    my_early, my_late = own_bits()
    for quarter, values in enumerate(quarters):
        spot = (my_early ^ (quarter & 1)) * 2 + (my_late ^ (quarter >> 1))
        for piece in range(values.shape[0]):
            start = pl.multiple_of((piece * QUARTERS + spot) * BLOCK, BLOCK)
            out[pl.ds(start, BLOCK)] = values[piece]


def on_device(inputs, conv_weight, mixing, pattern, w_in, w_out, cotangent):
    row_count, chan_count = inputs.shape
    blocks = row_count // BLOCK
    pieces = blocks // QUARTERS
    width, hidden = w_in.shape
    cores = lax.axis_size("ch")
    levels = lax.axis_size("seq").bit_length() - 1
    plain = list(range(LOCAL, LOCAL + levels - 2))
    last = LOCAL + levels - 2
    early_bit, late_bit = 1 << (levels - 2), 1 << (levels - 1)
    masks = [0, early_bit, late_bit, early_bit | late_bit]

    def blocks_of(size, kind=jnp.bfloat16):
        return ((size, BLOCK, chan_count), kind)

    half = blocks_of(2)
    whole = ((row_count, chan_count), jnp.bfloat16)
    piece_rows = QUARTERS * BLOCK
    flat = (piece_rows, chan_count)
    block = ((BLOCK, chan_count), jnp.bfloat16)
    half_flat = ((2 * BLOCK, chan_count), jnp.bfloat16)
    flat_piece = (flat, jnp.bfloat16)
    flops = 2 * piece_rows * width * hidden

    latest = []

    def run(kernel, name, outs, arrays, *args, **kwargs):
        results = call(kernel, name, outs, arrays, *args, order=tuple(latest), **kwargs)
        latest[:] = results[-1:]
        return results

    before, after = neighbours(inputs[:1], inputs[-1:], "seq")
    per_block = chan_count // (2 * BLOCK)
    lengths = [pieces + -(-pieces * 2 * (1 + (flip == 1)) // per_block) for flip in (1, 2, 3)]
    own_cots, *messages, mixing, cells, taps = run(
        functools.partial(load_kernel, last, pieces),
        "load_and_pack",
        [((pieces, BLOCK, chan_count), jnp.bfloat16)]
        + [((length, BLOCK, chan_count), jnp.bfloat16) for length in lengths]
        + [(array.shape, array.dtype) for array in (mixing, inputs, conv_weight)],
        [],
        [cotangent.reshape(blocks, BLOCK, chan_count), mixing, inputs, conv_weight],
        [pltpu.VMEM((blocks, BLOCK, chan_count), jnp.bfloat16), pltpu.SemaphoreType.DMA((4,))],
        limit=ALL,
    )
    messages = [from_flipped(m, "seq", mask) for m, mask in zip(messages, masks[1:])]
    units = [(s,) for s in range(2 * pieces)]
    convolved, *states = run(
        functools.partial(entry_kernel, units),
        "conv_and_local_factors",
        [whole] + [blocks_of(2 * len(unit)) for unit in units],
        [cells, before, after, taps, mixing],
        [pattern],
        [pltpu.VMEM((blocks, BLOCK, chan_count), jnp.bfloat16)] * 2
        + [pltpu.SMEM(pattern.shape, jnp.int32), pltpu.SemaphoreType.DMA],
    )
    all_cots = []
    halves = {}
    transposed = [None] * pieces
    grad_acts = [None] * pieces
    parts = [None] * pieces
    mixeds = [None] * pieces
    activations = [None] * pieces
    owns = [None] * pieces
    out_owns = [None] * pieces
    out_parts = [None] * pieces

    def stack():
        stacked = run(
            functools.partial(stack_kernel, pieces),
            "stack",
            [flat_piece] * pieces,
            [own_cots, *messages],
        )
        for piece in stacked:
            all_cots.append([piece] + [from_offset(piece, "ch", i) for i in range(1, cores)])

    def grad_act(p):
        (grad_acts[p],) = run(
            functools.partial(grad_act_kernel, cores),
            "grad_act",
            [((piece_rows, hidden), jnp.bfloat16)],
            [*all_cots[p], w_out],
            scratch=[pltpu.VMEM((piece_rows, width), jnp.bfloat16)],
            limit=LARGE,
        )

    def plain_factor(factor, u):
        unit = units[u]
        mates = from_flipped(states[u], "seq", 1 << (factor - LOCAL))
        split = factor == plain[-1] and len(unit) == 2
        results = run(
            functools.partial(plain_kernel, factor, unit),
            "factor",
            [half, half] if split else [blocks_of(2 * len(unit))],
            [states[u], mates, mixing],
        )
        if factor == plain[-1]:
            halves.update(zip(unit, results))
        else:
            states[u] = results[0]

    def early_factor(p):
        send, keep = halves[2 * p], halves[2 * p + 1]
        transposed[p] = run(
            functools.partial(early_kernel, last, pieces, p),
            "early_factor",
            [half, half],
            [keep, from_flipped(send, "seq", early_bit), mixing, messages[0]],
        )

    def late_factor(p):
        keep, send = transposed[p]
        mixeds[p] = run(
            functools.partial(late_kernel, last, pieces, p),
            "late_factor",
            [half_flat] * 2,
            [keep, from_flipped(send, "seq", late_bit), mixing, *messages],
        )

    def hidden_and_grad(p):
        gathered = [
            from_offset(mixed, "ch", i) if i else mixed for i in range(cores) for mixed in mixeds[p]
        ]
        activations[p], owns[p], *backs = run(
            functools.partial(hidden_kernel, cores),
            "mlp_hidden_and_grad",
            [((piece_rows, hidden), jnp.bfloat16), (flat, jnp.float32)]
            + [half_flat] * ((cores - 1) * 2),
            [*gathered, grad_acts[p], w_in],
            scratch=[
                pltpu.VMEM((piece_rows, width), jnp.bfloat16),
                pltpu.VMEM((piece_rows, width), jnp.float32),
            ],
            limit=LARGE,
        )
        parts[p] = [
            from_offset(back, "ch", cores - 1 - i // 2) for i, back in enumerate(backs)
        ]

    def transposed_back(p):
        quarters = run(
            functools.partial(back_kernel, last, pieces, p, cores),
            "late_and_early_back",
            [block] * QUARTERS,
            [all_cots[p][0], owns[p], *parts[p], mixing, *messages],
        )
        transposed[p] = [
            from_flipped(grad, "seq", mask) if mask else grad
            for grad, mask in zip(quarters, masks)
        ]

    def regroup(p):
        chosen = [u for u, unit in enumerate(back_units) if unit[0] // 2 == p]
        sizes = [2 * len(back_units[u]) for u in chosen]
        results = run(
            functools.partial(regroup_kernel, plain[-1], [back_units[u] for u in chosen]),
            "regroup_and_factor_back",
            [blocks_of(size, kind) for size in sizes for kind in (jnp.float32, jnp.bfloat16)],
            [*transposed[p], mixing],
        )
        for number, u in enumerate(chosen):
            states[u] = results[2 * number : 2 * number + 2]

    def out_product(p):
        cuts = 1 if p + 1 < pieces else 2
        out_owns[p], *others = run(
            functools.partial(out_kernel, cores),
            "mlp_out",
            [(flat, jnp.float32)] + [flat_piece if cuts == 1 else half_flat] * (cuts * (cores - 1)),
            [activations[p], *mixeds[p], w_out],
            limit=LARGE,
        )
        out_parts[p] = [
            from_offset(other, "ch", cores - 1 - i // cuts) for i, other in enumerate(others)
        ]

    def plain_back(factor, u):
        mine, cross = states[u]
        theirs = from_flipped(cross, "seq", 1 << (factor - LOCAL))
        kind = jnp.bfloat16 if factor != plain[0] else jnp.float32
        size = 2 * len(back_units[u])
        states[u] = run(
            functools.partial(plain_back_kernel, factor - 1, back_units[u]),
            "factor_back",
            [blocks_of(size, jnp.float32), blocks_of(size, kind)],
            [mine, theirs, mixing],
        )

    waves = sorted((u + 2 * i, -i, u) for i in range(len(plain)) for u in range(len(units)))
    for _, i, u in waves:
        plain_factor(plain[-i], u)
        if plain[-i] == plain[-1] and u == 1:
            early_factor(0)
        if i == 0 and u == len(units) - 1:
            stack()
    late_factor(0)
    for p in range(1, pieces):
        early_factor(p)
    grad_act(0)
    back_units = [(2 * p, 2 * p + 1) for p in range(pieces - 1)]
    back_units += [(2 * pieces - 1,), (2 * pieces - 2,)]
    states = [None] * len(back_units)
    for p in range(pieces):
        hidden_and_grad(p)
        if p + 1 < pieces:
            grad_act(p + 1)
            out_product(p)
            late_factor(p + 1)
        if p > 0:
            regroup(p - 1)
        if p == pieces - 1:
            out_product(p)
        transposed_back(p)
    early_units = range(pieces - 1)
    late_units = range(pieces - 1, pieces + 1)
    def combine():
        return run(
            functools.partial(combine_kernel, pieces, [len(piece) for piece in out_parts]),
            "combine",
            [((pieces, BLOCK, chan_count), jnp.bfloat16)] * QUARTERS,
            [*out_owns, *[part for piece in out_parts for part in piece]],
        )

    outs = combine()
    regroup(pieces - 1)
    for factor in reversed(plain):
        for u in (*early_units, *late_units):
            plain_back(factor, u)
    arrived = [from_flipped(out, "seq", mask) if mask else out for out, mask in zip(outs, masks)]
    (grad_conv,) = run(
        functools.partial(exit_kernel, back_units),
        "local_factors_back",
        [whole],
        [g[0] for g in states] + [g[1] for g in states] + [mixing],
        [pattern],
        [pltpu.VMEM((blocks, BLOCK, chan_count), jnp.float32)] * 2
        + [pltpu.SMEM(pattern.shape, jnp.int32), pltpu.SemaphoreType.DMA],
        limit=LARGE,
    )
    (layer_out,) = call(assemble_kernel, "assemble", [whole], arrived)
    before, after = neighbours(grad_conv[:1], grad_conv[-1:], "seq")
    (grad_input,) = run(
        conv_back_kernel, "conv_back", [whole], [grad_conv, before, after, taps]
    )
    return (layer_out, convolved, grad_input)


def solution(mesh):
    return jax.shard_map(
        on_device,
        mesh=mesh,
        in_specs=(
            P("seq", "ch"),
            P(None, "ch"),
            P(None, "seq", None, None),
            P(None, "seq"),
            P(None, "ch"),
            P("ch", None),
            P("seq", "ch"),
        ),
        out_specs=(P("seq", "ch"), P("seq", "ch"), P("seq", "ch")),
        check_vma=False,
    )
```

```python
import functools

import jax
import jax.numpy as jnp
from jax import lax
from jax.experimental import pallas as pl
from jax.experimental.pallas import tpu as pltpu
from jax.sharding import PartitionSpec as P

BLOCK = 64
LOCAL = 2
QUARTERS = 4
TILE = 512
SMALL = 8 * 1024 * 1024
LARGE = 20 * 1024 * 1024
ALL = 44 * 1024 * 1024

root_two_pi = 0.7978845608028654

IN_HBM = pl.BlockSpec(memory_space=pltpu.HBM)
IN_VMEM = pl.BlockSpec(memory_space=pltpu.VMEM)
ANYWHERE = pl.BlockSpec(memory_space=pl.ANY)
ACROSS = (((1,), (1,)), ((), ()))
OVER_ROWS = (((0,), (0,)), ((), ()))


def times(weights, value):
    return jnp.dot(weights, value, preferred_element_type=jnp.float32)


def times_transposed(weights, value):
    return lax.dot_general(weights, value, OVER_ROWS, preferred_element_type=jnp.float32)


def neighbours(edges, axis):
    count = lax.axis_size(axis)
    near = lax.ppermute(edges, axis, [(i, i ^ 1) for i in range(count)])
    route = []
    for low in range(1, count - 1, 2):
        route += [(low, low + 1), (low + 1, low)]
    return near, lax.ppermute(edges[:2], axis, route)


def from_flipped(block, axis, mask):
    count = lax.axis_size(axis)
    return lax.ppermute(block, axis, [(i, i ^ mask) for i in range(count)])


def from_offset(block, axis, offset):
    count = lax.axis_size(axis)
    return lax.ppermute(block, axis, [((i + offset) % count, i) for i in range(count)])


def call(kernel, name, outs, arrays, distant=(), scratch=(), order=(), limit=SMALL):
    count = len(distant) + len(arrays)

    def body(*refs):
        kernel(*refs[:count], *refs[count + len(order) :])

    return pl.pallas_call(
        body,
        out_shape=[jax.ShapeDtypeStruct(shape, kind) for shape, kind in outs],
        in_specs=[IN_HBM] * len(distant) + [IN_VMEM] * len(arrays) + [ANYWHERE] * len(order),
        out_specs=[IN_VMEM] * len(outs),
        scratch_shapes=list(scratch),
        compiler_params=pltpu.CompilerParams(vmem_limit_bytes=limit),
        cost_estimate=pl.CostEstimate(flops=0, bytes_accessed=0, transcendentals=0),
        name=name,
    )(*distant, *arrays, *order)


def own_bits():
    seat = lax.axis_index("seq")
    levels = lax.axis_size("seq").bit_length() - 1
    return (seat >> (levels - 2)) & 1, (seat >> (levels - 1)) & 1


def shifted(cells, near, far):
    rows = cells.shape[0]
    even = lax.axis_index("seq") % 2 == 0
    near, far = near.astype(jnp.float32), far.astype(jnp.float32)
    before = jnp.where(even, far[1:2], near[1:2])
    after = jnp.where(even, near[0:1], far[0:1])
    spot = lax.broadcasted_iota(jnp.int32, cells.shape, 0)
    up = jnp.where(spot == 0, before, pltpu.roll(cells, 1, 0))
    down = jnp.where(spot == rows - 1, after, pltpu.roll(cells, rows - 1, 0))
    return up, down


def chosen_blocks(subs):
    early, late = own_bits()
    return [
        sub // 2 * QUARTERS + (early ^ (1 - sub % 2)) * 2 + (late ^ other)
        for sub in subs
        for other in range(2)
    ]


def local_factor(factor, pattern, source, mixing, target, chosen):
    for spot, block in enumerate(chosen):
        pair = mixing[factor, block]
        target[spot] = (
            times(pair[:, :BLOCK], source[block])
            + times(pair[:, BLOCK:], source[pattern[factor, block]])
        ).astype(jnp.bfloat16)


def entry_kernel(units, pattern_far, cells, near, far, mixing, conv_ref, *rest):
    outs, (first, between, pattern, arrival) = rest[:-4], rest[-4:]
    fetch = pltpu.make_async_copy(pattern_far, pattern, arrival)
    fetch.start()
    values = cells[...].astype(jnp.float32)
    scale = near[2:5].astype(jnp.float32)
    up, down = shifted(values, near[...], far[...])
    convolved = (scale[0:1] * up + scale[1:2] * values + scale[2:3] * down).astype(jnp.bfloat16)
    conv_ref[...] = convolved
    first[...] = convolved.reshape(first.shape)
    fetch.wait()
    every = range(first.shape[0])
    refs = (first, between)
    for factor in range(LOCAL - 1):
        local_factor(factor, pattern, refs[factor % 2], mixing, refs[1 - factor % 2], every)
    source = refs[(LOCAL - 1) % 2]
    for unit, out in zip(units, outs):
        local_factor(LOCAL - 1, pattern, source, mixing, out, chosen_blocks(unit))


def plain_kernel(factor, unit, state, mates, mixing, *outs):
    for spot, block in enumerate(chosen_blocks(unit)):
        pair = mixing[factor, block]
        per_out = state.shape[0] // len(outs)
        outs[spot // per_out][spot % per_out] = (
            times(pair[:, :BLOCK], state[spot]) + times(pair[:, BLOCK:], mates[spot])
        ).astype(jnp.bfloat16)


def packed(message, pieces, number):
    across = message.shape[-1] // (2 * BLOCK)
    lanes = pl.ds(number % across * 2 * BLOCK, 2 * BLOCK)
    return message.at[pieces + number // across, :, lanes]


def load_kernel(mixing_far, cells_far, mixing, cells, arrivals):
    fetches = [
        pltpu.make_async_copy(far, near, arrivals.at[i])
        for i, (far, near) in enumerate(((mixing_far, mixing), (cells_far, cells)))
    ]
    for fetch in fetches:
        fetch.start()
    for fetch in fetches:
        fetch.wait()


def pack_kernel(factor, pieces, cots, mixing, own, *messages):
    my_early, my_late = own_bits()
    for piece in range(pieces):
        base = piece * QUARTERS
        own[piece] = cots[base + my_early * 2 + my_late]
        for flip, message in enumerate(messages, 1):
            early, late = my_early ^ (flip & 1), my_late ^ (flip >> 1)
            message[piece] = cots[base + early * 2 + late]
            for which in range(2):
                number = which * pieces + piece
                if flip == 1:
                    for other in range(2):
                        packed(message, pieces, number * 2 + other)[...] = mixing[
                            factor + which, base + early * 2 + (late ^ other)
                        ]
                else:
                    packed(message, pieces, number)[...] = mixing[
                        factor + which, base + early * 2 + late
                    ]


def stack_kernel(pieces, *rest):
    quarters, outs = rest[:QUARTERS], rest[QUARTERS:]
    for piece, out in enumerate(outs):
        for quarter, values in enumerate(quarters):
            out[quarter * BLOCK : (quarter + 1) * BLOCK] = values[piece]


def mixing_of(factor, which, pieces, piece, mixing, messages, quarter, other=0):
    if quarter == 0:
        early, late = own_bits()
        return mixing[factor + which, piece * QUARTERS + early * 2 + (late ^ other)]
    number = which * pieces + piece
    if quarter == 1:
        number = number * 2 + other
    return packed(messages[quarter - 1], pieces, number)[...]


def early_kernel(factor, pieces, piece, keep, recv, mixing, message, keep_out, send_out):
    weights = functools.partial(mixing_of, factor, 0, pieces, piece, mixing, [message])
    for other, out in enumerate((keep_out, send_out)):
        mine, theirs = keep[other], recv[other]
        pair = weights(0, other)
        out[0] = (times(pair[:, :BLOCK], mine) + times(pair[:, BLOCK:], theirs)).astype(
            jnp.bfloat16
        )
        pair = weights(1, other)
        out[1] = (times(pair[:, :BLOCK], theirs) + times(pair[:, BLOCK:], mine)).astype(
            jnp.bfloat16
        )


def late_kernel(factor, pieces, piece, keep, recv, mixing, *rest):
    messages, outs = rest[:-2], rest[-2:]
    values = [keep[0], keep[1], recv[0], recv[1]]
    for quarter in range(QUARTERS):
        pair = mixing_of(factor, 1, pieces, piece, mixing, messages, quarter)
        rows = slice(quarter % 2 * BLOCK, (quarter % 2 + 1) * BLOCK)
        outs[quarter // 2][rows] = (
            times(pair[:, :BLOCK], values[quarter]) + times(pair[:, BLOCK:], values[quarter ^ 2])
        ).astype(jnp.bfloat16)


def back_kernel(factor, pieces, piece, cores, cots, total, *rest):
    count = (cores - 1) * 2
    parts, (mixing, message1, message2, message3, *outs) = rest[:count], rest[count:]
    messages = (message1, message2, message3)
    grads = []
    for quarter in range(QUARTERS):
        rows = slice(quarter * BLOCK, (quarter + 1) * BLOCK)
        grad = cots[rows].astype(jnp.float32) + total[rows]
        inner = slice(quarter % 2 * BLOCK, (quarter % 2 + 1) * BLOCK)
        for part in parts[quarter // 2 :: 2]:
            grad = grad + part[inner].astype(jnp.float32)
        grads.append(grad.astype(jnp.bfloat16))
    for which, flip in ((1, 2), (0, 1)):
        both = [
            times_transposed(
                mixing_of(factor, which, pieces, piece, mixing, messages, quarter),
                grads[quarter],
            )
            for quarter in range(QUARTERS)
        ]
        grads = [
            (both[quarter][:BLOCK] + both[quarter ^ flip][BLOCK:]).astype(jnp.bfloat16)
            for quarter in range(QUARTERS)
        ]
    for grad, out in zip(grads, outs):
        out[...] = grad


def regroup_kernel(factor, units, *rest):
    quarters, mixing, outs = rest[:QUARTERS], rest[QUARTERS], rest[QUARTERS + 1 :]
    for number, unit in enumerate(units):
        own, cross = outs[2 * number : 2 * number + 2]
        for spot, block in enumerate(chosen_blocks(unit)):
            grad = quarters[1 - unit[spot // 2] % 2 + spot % 2 * 2][...]
            both = times_transposed(mixing[factor, block], grad)
            own[spot] = both[:BLOCK]
            cross[spot] = both[BLOCK:].astype(jnp.bfloat16)


def plain_back_kernel(factor, unit, mine, theirs, mixing, own, cross):
    for spot, block in enumerate(chosen_blocks(unit)):
        grad = (mine[spot] + theirs[spot].astype(jnp.float32)).astype(jnp.bfloat16)
        both = times_transposed(mixing[factor, block], grad)
        own[spot] = both[:BLOCK]
        cross[spot] = both[BLOCK:].astype(cross.dtype)


def exit_kernel(units, pattern_far, *rest):
    count = len(units)
    mine, theirs = rest[:count], rest[count : 2 * count]
    mixing, out, edges, own, cross, pattern, arrival = rest[2 * count :]
    fetch = pltpu.make_async_copy(pattern_far, pattern, arrival)
    fetch.start()
    blocks = own.shape[0]
    for number, unit in enumerate(units):
        for spot, block in enumerate(chosen_blocks(unit)):
            own[block] = mine[number][spot]
            cross[block] = theirs[number][spot]
    fetch.wait()
    for factor in reversed(range(LOCAL)):
        for block in range(blocks):
            own[block] += cross[pattern[factor, block]]
        for block in range(blocks):
            grad = own[block].astype(jnp.bfloat16)
            if factor == 0:
                out[block * BLOCK : (block + 1) * BLOCK] = grad
                if block == 0:
                    edges[0:1] = grad[:1]
                if block == blocks - 1:
                    edges[1:2] = grad[-1:]
            else:
                both = times_transposed(mixing[factor - 1, block], grad)
                own[block] = both[:BLOCK]
                cross[block] = both[BLOCK:]


def conv_back_kernel(cells, near, far, taps, out):
    values = cells[...].astype(jnp.float32)
    scale = taps[2:5].astype(jnp.float32)
    up, down = shifted(values, near[...], far[...])
    out[...] = (scale[0:1] * down + scale[1:2] * values + scale[2:3] * up).astype(jnp.bfloat16)


def channel_spots(count, chans):
    core = lax.axis_index("ch")
    return [
        pl.ds(pl.multiple_of(lax.rem(core + i, count) * chans, chans), chans)
        for i in range(count)
    ]


def grad_act_kernel(count, *rest):
    cots, (w_out, grad_act, c_all) = rest[:count], rest[count:]
    for spot, cot in zip(channel_spots(count, cots[0].shape[1]), cots):
        c_all[:, spot] = cot[...]
    hidden = w_out.shape[0]
    tile = min(TILE, hidden)
    for start in range(0, hidden, tile):
        grad_act[:, start : start + tile] = lax.dot_general(
            c_all[...], w_out[start : start + tile], ACROSS, preferred_element_type=jnp.float32
        ).astype(grad_act.dtype)


def hidden_kernel(count, *rest):
    mixed, (grad_act, w_in, activation, own) = rest[: 2 * count], rest[2 * count : 2 * count + 4]
    backs, (x_all, back_sum) = rest[2 * count + 4 : -2], rest[-2:]
    rows, chans = mixed[0].shape
    spots = channel_spots(count, chans)
    for i, spot in enumerate(spots):
        x_all[:rows, spot] = mixed[2 * i][...]
        x_all[rows:, spot] = mixed[2 * i + 1][...]
    size = w_in.shape[1]
    tile = min(TILE, size)
    for start in range(0, size, tile):
        tiles = slice(start, start + tile)
        hidden = times(x_all[...], w_in[:, tiles])
        square = hidden * hidden
        tanh_val = jnp.tanh(hidden * (root_two_pi + root_two_pi * 0.044715 * square))
        half = 0.5 + 0.5 * tanh_val
        gelu = hidden * half
        activation[:, tiles] = gelu.astype(jnp.bfloat16)
        slope = 2.0 * root_two_pi + 6.0 * root_two_pi * 0.044715 * square
        derivative = half + gelu * (1.0 - half) * slope
        grad_hidden = (grad_act[:, tiles].astype(jnp.float32) * derivative).astype(jnp.bfloat16)
        back = lax.dot_general(
            grad_hidden, w_in[:, tiles], ACROSS, preferred_element_type=jnp.float32
        )
        if start == 0:
            back_sum[...] = back
        else:
            back_sum[...] += back
    own[...] = back_sum[:, spots[0]]
    for i, spot in enumerate(spots[1:]):
        backs[2 * i][...] = back_sum[:rows, spot].astype(jnp.bfloat16)
        backs[2 * i + 1][...] = back_sum[rows:, spot].astype(jnp.bfloat16)


def out_kernel(count, activation, top, bottom, w_out, own, *others):
    rows, chans = top.shape
    for i, spot in enumerate(channel_spots(count, chans)):
        product = times(activation[...], w_out[:, spot])
        if i == 0:
            own[:rows] = top[...].astype(jnp.float32) + product[:rows]
            own[rows:] = bottom[...].astype(jnp.float32) + product[rows:]
        else:
            cuts = len(others) // (count - 1)
            for cut in range(cuts):
                size = 2 * rows // cuts
                part = product[cut * size : (cut + 1) * size]
                others[(i - 1) * cuts + cut][...] = part.astype(jnp.bfloat16)


def combine_kernel(pieces, counts, *rest):
    owns, parts, outs = rest[:pieces], rest[pieces:-QUARTERS], rest[-QUARTERS:]
    for piece in range(pieces):
        per_piece = counts[piece]
        mine, parts = parts[:per_piece], parts[per_piece:]
        for quarter, out in enumerate(outs):
            total = owns[piece][quarter * BLOCK : (quarter + 1) * BLOCK]
            cuts = total.shape[0] * QUARTERS // mine[0].shape[0]
            start = quarter * BLOCK % mine[0].shape[0]
            for part in mine[quarter * cuts // QUARTERS :: cuts]:
                total = total + part[start : start + BLOCK].astype(jnp.float32)
            out[piece] = total.astype(jnp.bfloat16)


def assemble_kernel(*rest):
    quarters, out = rest[:-1], rest[-1]
    my_early, my_late = own_bits()
    for quarter, values in enumerate(quarters):
        spot = (my_early ^ (quarter & 1)) * 2 + (my_late ^ (quarter >> 1))
        for piece in range(values.shape[0]):
            start = pl.multiple_of((piece * QUARTERS + spot) * BLOCK, BLOCK)
            out[pl.ds(start, BLOCK)] = values[piece]


def on_device(inputs, conv_weight, mixing, pattern, w_in, w_out, cotangent):
    row_count, chan_count = inputs.shape
    blocks = row_count // BLOCK
    pieces = blocks // QUARTERS
    width, hidden = w_in.shape
    cores = lax.axis_size("ch")
    levels = lax.axis_size("seq").bit_length() - 1
    plain = list(range(LOCAL, LOCAL + levels - 2))
    last = LOCAL + levels - 2
    early_bit, late_bit = 1 << (levels - 2), 1 << (levels - 1)
    masks = [0, early_bit, late_bit, early_bit | late_bit]

    def blocks_of(size, kind=jnp.bfloat16):
        return ((size, BLOCK, chan_count), kind)

    half = blocks_of(2)
    whole = ((row_count, chan_count), jnp.bfloat16)
    piece_rows = QUARTERS * BLOCK
    flat = (piece_rows, chan_count)
    block = ((BLOCK, chan_count), jnp.bfloat16)
    half_flat = ((2 * BLOCK, chan_count), jnp.bfloat16)
    flat_piece = (flat, jnp.bfloat16)
    flops = 2 * piece_rows * width * hidden

    latest = []

    def run(kernel, name, outs, arrays, *args, **kwargs):
        results = call(kernel, name, outs, arrays, *args, order=tuple(latest), **kwargs)
        latest[:] = results[-1:]
        return results

    near, far = neighbours(jnp.concatenate([inputs[:1], inputs[-1:], conv_weight]), "seq")
    per_block = chan_count // (2 * BLOCK)
    lengths = [pieces + -(-pieces * 2 * (1 + (flip == 1)) // per_block) for flip in (1, 2, 3)]
    mixing, cells = run(
        load_kernel,
        "load",
        [(array.shape, array.dtype) for array in (mixing, inputs)],
        [],
        [mixing, inputs],
        [pltpu.SemaphoreType.DMA((2,))],
        limit=ALL,
    )
    units = [(s,) for s in range(2 * pieces)]
    convolved, *states = run(
        functools.partial(entry_kernel, units),
        "conv_and_local_factors",
        [whole] + [blocks_of(2 * len(unit)) for unit in units],
        [cells, near, far, mixing],
        [pattern],
        [pltpu.VMEM((blocks, BLOCK, chan_count), jnp.bfloat16)] * 2
        + [pltpu.SMEM(pattern.shape, jnp.int32), pltpu.SemaphoreType.DMA],
    )
    own_cots, *messages = run(
        functools.partial(pack_kernel, last, pieces),
        "pack",
        [((pieces, BLOCK, chan_count), jnp.bfloat16)]
        + [((length, BLOCK, chan_count), jnp.bfloat16) for length in lengths],
        [cotangent.reshape(blocks, BLOCK, chan_count), mixing],
    )
    messages = [from_flipped(m, "seq", mask) for m, mask in zip(messages, masks[1:])]
    all_cots = []
    halves = {}
    transposed = [None] * pieces
    grad_acts = [None] * pieces
    parts = [None] * pieces
    mixeds = [None] * pieces
    activations = [None] * pieces
    owns = [None] * pieces
    out_owns = [None] * pieces
    out_parts = [None] * pieces

    def stack():
        stacked = run(
            functools.partial(stack_kernel, pieces),
            "stack",
            [flat_piece] * pieces,
            [own_cots, *messages],
        )
        for piece in stacked:
            all_cots.append([piece] + [from_offset(piece, "ch", i) for i in range(1, cores)])

    def grad_act(p):
        (grad_acts[p],) = run(
            functools.partial(grad_act_kernel, cores),
            "grad_act",
            [((piece_rows, hidden), jnp.bfloat16)],
            [*all_cots[p], w_out],
            scratch=[pltpu.VMEM((piece_rows, width), jnp.bfloat16)],
            limit=LARGE,
        )

    def plain_factor(factor, u):
        unit = units[u]
        mates = from_flipped(states[u], "seq", 1 << (factor - LOCAL))
        split = factor == plain[-1] and len(unit) == 2
        results = run(
            functools.partial(plain_kernel, factor, unit),
            "factor",
            [half, half] if split else [blocks_of(2 * len(unit))],
            [states[u], mates, mixing],
        )
        if factor == plain[-1]:
            halves.update(zip(unit, results))
        else:
            states[u] = results[0]

    def early_factor(p):
        send, keep = halves[2 * p], halves[2 * p + 1]
        transposed[p] = run(
            functools.partial(early_kernel, last, pieces, p),
            "early_factor",
            [half, half],
            [keep, from_flipped(send, "seq", early_bit), mixing, messages[0]],
        )

    def late_factor(p):
        keep, send = transposed[p]
        mixeds[p] = run(
            functools.partial(late_kernel, last, pieces, p),
            "late_factor",
            [half_flat] * 2,
            [keep, from_flipped(send, "seq", late_bit), mixing, *messages],
        )

    def hidden_and_grad(p):
        gathered = [
            from_offset(mixed, "ch", i) if i else mixed for i in range(cores) for mixed in mixeds[p]
        ]
        activations[p], owns[p], *backs = run(
            functools.partial(hidden_kernel, cores),
            "mlp_hidden_and_grad",
            [((piece_rows, hidden), jnp.bfloat16), (flat, jnp.float32)]
            + [half_flat] * ((cores - 1) * 2),
            [*gathered, grad_acts[p], w_in],
            scratch=[
                pltpu.VMEM((piece_rows, width), jnp.bfloat16),
                pltpu.VMEM((piece_rows, width), jnp.float32),
            ],
            limit=LARGE,
        )
        parts[p] = [
            from_offset(back, "ch", cores - 1 - i // 2) for i, back in enumerate(backs)
        ]

    def transposed_back(p):
        quarters = run(
            functools.partial(back_kernel, last, pieces, p, cores),
            "late_and_early_back",
            [block] * QUARTERS,
            [all_cots[p][0], owns[p], *parts[p], mixing, *messages],
        )
        transposed[p] = [
            from_flipped(grad, "seq", mask) if mask else grad
            for grad, mask in zip(quarters, masks)
        ]

    def regroup(p):
        chosen = [u for u, unit in enumerate(back_units) if unit[0] // 2 == p]
        sizes = [2 * len(back_units[u]) for u in chosen]
        results = run(
            functools.partial(regroup_kernel, plain[-1], [back_units[u] for u in chosen]),
            "regroup_and_factor_back",
            [blocks_of(size, kind) for size in sizes for kind in (jnp.float32, jnp.bfloat16)],
            [*transposed[p], mixing],
        )
        for number, u in enumerate(chosen):
            states[u] = results[2 * number : 2 * number + 2]

    def out_product(p):
        cuts = 1 if p + 1 < pieces else 2
        out_owns[p], *others = run(
            functools.partial(out_kernel, cores),
            "mlp_out",
            [(flat, jnp.float32)] + [flat_piece if cuts == 1 else half_flat] * (cuts * (cores - 1)),
            [activations[p], *mixeds[p], w_out],
            limit=LARGE,
        )
        out_parts[p] = [
            from_offset(other, "ch", cores - 1 - i // cuts) for i, other in enumerate(others)
        ]

    def plain_back(factor, u):
        mine, cross = states[u]
        theirs = from_flipped(cross, "seq", 1 << (factor - LOCAL))
        kind = jnp.bfloat16 if factor != plain[0] else jnp.float32
        size = 2 * len(back_units[u])
        states[u] = run(
            functools.partial(plain_back_kernel, factor - 1, back_units[u]),
            "factor_back",
            [blocks_of(size, jnp.float32), blocks_of(size, kind)],
            [mine, theirs, mixing],
        )

    waves = sorted((u + 2 * i, -i, u) for i in range(len(plain)) for u in range(len(units)))
    for _, i, u in waves:
        plain_factor(plain[-i], u)
        if plain[-i] == plain[-1] and u == 1:
            early_factor(0)
    late_factor(0)
    for p in range(1, pieces):
        early_factor(p)
    stack()
    grad_act(0)
    back_units = [(2 * p, 2 * p + 1) for p in range(pieces - 1)]
    back_units += [(2 * pieces - 1,), (2 * pieces - 2,)]
    states = [None] * len(back_units)
    for p in range(pieces):
        hidden_and_grad(p)
        if p + 1 < pieces:
            grad_act(p + 1)
            out_product(p)
            late_factor(p + 1)
        if p > 0:
            regroup(p - 1)
        if p == pieces - 1:
            out_product(p)
        transposed_back(p)
    early_units = range(pieces - 1)
    late_units = range(pieces - 1, pieces + 1)
    def combine():
        return run(
            functools.partial(combine_kernel, pieces, [len(piece) for piece in out_parts]),
            "combine",
            [((pieces, BLOCK, chan_count), jnp.bfloat16)] * QUARTERS,
            [*out_owns, *[part for piece in out_parts for part in piece]],
        )

    outs = combine()
    regroup(pieces - 1)
    for factor in reversed(plain):
        for u in (*early_units, *late_units):
            plain_back(factor, u)
    arrived = [from_flipped(out, "seq", mask) if mask else out for out, mask in zip(outs, masks)]
    grad_conv, edges = run(
        functools.partial(exit_kernel, back_units),
        "local_factors_back",
        [whole, ((2, chan_count), jnp.bfloat16)],
        [g[0] for g in states] + [g[1] for g in states] + [mixing],
        [pattern],
        [pltpu.VMEM((blocks, BLOCK, chan_count), jnp.float32)] * 2
        + [pltpu.SMEM(pattern.shape, jnp.int32), pltpu.SemaphoreType.DMA],
        limit=LARGE,
    )
    (layer_out,) = call(assemble_kernel, "assemble", [whole], arrived)
    near_grad, far_grad = neighbours(edges, "seq")
    (grad_input,) = run(
        conv_back_kernel, "conv_back", [whole], [grad_conv, near_grad, far_grad, near]
    )
    return (layer_out, convolved, grad_input)


def solution(mesh):
    return jax.shard_map(
        on_device,
        mesh=mesh,
        in_specs=(
            P("seq", "ch"),
            P(None, "ch"),
            P(None, "seq", None, None),
            P(None, "seq"),
            P(None, "ch"),
            P("ch", None),
            P("seq", "ch"),
        ),
        out_specs=(P("seq", "ch"), P("seq", "ch"), P("seq", "ch")),
        check_vma=False,
    )
```

```python
import functools

import jax
import jax.numpy as jnp
from jax import lax
from jax.experimental import pallas as pl
from jax.experimental.pallas import tpu as pltpu
from jax.sharding import PartitionSpec as P

BLOCK = 64
LOCAL = 2
QUARTERS = 4
TILE = 512
SMALL = 8 * 1024 * 1024
LARGE = 20 * 1024 * 1024
ALL = 44 * 1024 * 1024

root_two_pi = 0.7978845608028654

IN_HBM = pl.BlockSpec(memory_space=pltpu.HBM)
IN_VMEM = pl.BlockSpec(memory_space=pltpu.VMEM)
ANYWHERE = pl.BlockSpec(memory_space=pl.ANY)
ACROSS = (((1,), (1,)), ((), ()))
OVER_ROWS = (((0,), (0,)), ((), ()))


def times(weights, value):
    return jnp.dot(weights, value, preferred_element_type=jnp.float32)


def times_transposed(weights, value):
    return lax.dot_general(weights, value, OVER_ROWS, preferred_element_type=jnp.float32)


def neighbours(edges, axis):
    count = lax.axis_size(axis)
    near = lax.ppermute(edges, axis, [(i, i ^ 1) for i in range(count)])
    route = []
    for low in range(1, count - 1, 2):
        route += [(low, low + 1), (low + 1, low)]
    return near, lax.ppermute(edges[:2], axis, route)


def from_flipped(block, axis, mask):
    count = lax.axis_size(axis)
    return lax.ppermute(block, axis, [(i, i ^ mask) for i in range(count)])


def from_offset(block, axis, offset):
    count = lax.axis_size(axis)
    return lax.ppermute(block, axis, [((i + offset) % count, i) for i in range(count)])


def call(kernel, name, outs, arrays, distant=(), scratch=(), order=(), limit=SMALL):
    count = len(distant) + len(arrays)

    def body(*refs):
        kernel(*refs[:count], *refs[count + len(order) :])

    return pl.pallas_call(
        body,
        out_shape=[jax.ShapeDtypeStruct(shape, kind) for shape, kind in outs],
        in_specs=[IN_HBM] * len(distant) + [IN_VMEM] * len(arrays) + [ANYWHERE] * len(order),
        out_specs=[IN_VMEM] * len(outs),
        scratch_shapes=list(scratch),
        compiler_params=pltpu.CompilerParams(vmem_limit_bytes=limit),
        cost_estimate=pl.CostEstimate(flops=0, bytes_accessed=0, transcendentals=0),
        name=name,
    )(*distant, *arrays, *order)


def own_bits():
    seat = lax.axis_index("seq")
    levels = lax.axis_size("seq").bit_length() - 1
    return (seat >> (levels - 2)) & 1, (seat >> (levels - 1)) & 1


def shifted(cells, near, far):
    rows = cells.shape[0]
    even = lax.axis_index("seq") % 2 == 0
    near, far = near.astype(jnp.float32), far.astype(jnp.float32)
    before = jnp.where(even, far[1:2], near[1:2])
    after = jnp.where(even, near[0:1], far[0:1])
    spot = lax.broadcasted_iota(jnp.int32, cells.shape, 0)
    up = jnp.where(spot == 0, before, pltpu.roll(cells, 1, 0))
    down = jnp.where(spot == rows - 1, after, pltpu.roll(cells, rows - 1, 0))
    return up, down


def chosen_blocks(subs):
    early, late = own_bits()
    return [
        sub // 2 * QUARTERS + (early ^ (1 - sub % 2)) * 2 + (late ^ other)
        for sub in subs
        for other in range(2)
    ]


def local_factor(factor, pattern, source, mixing, target, chosen):
    for spot, block in enumerate(chosen):
        pair = mixing[factor, block]
        target[spot] = (
            times(pair[:, :BLOCK], source[block])
            + times(pair[:, BLOCK:], source[pattern[factor, block]])
        ).astype(jnp.bfloat16)


def entry_kernel(units, pattern_far, cells, near, far, mixing, conv_ref, *rest):
    outs, (first, between, pattern, arrival) = rest[:-4], rest[-4:]
    fetch = pltpu.make_async_copy(pattern_far, pattern, arrival)
    fetch.start()
    values = cells[...].astype(jnp.float32)
    scale = near[2:5].astype(jnp.float32)
    up, down = shifted(values, near[...], far[...])
    convolved = (scale[0:1] * up + scale[1:2] * values + scale[2:3] * down).astype(jnp.bfloat16)
    conv_ref[...] = convolved
    first[...] = convolved.reshape(first.shape)
    fetch.wait()
    every = range(first.shape[0])
    refs = (first, between)
    for factor in range(LOCAL - 1):
        local_factor(factor, pattern, refs[factor % 2], mixing, refs[1 - factor % 2], every)
    source = refs[(LOCAL - 1) % 2]
    for unit, out in zip(units, outs):
        local_factor(LOCAL - 1, pattern, source, mixing, out, chosen_blocks(unit))


def plain_kernel(factor, unit, state, mates, mixing, *outs):
    for spot, block in enumerate(chosen_blocks(unit)):
        pair = mixing[factor, block]
        per_out = state.shape[0] // len(outs)
        outs[spot // per_out][spot % per_out] = (
            times(pair[:, :BLOCK], state[spot]) + times(pair[:, BLOCK:], mates[spot])
        ).astype(jnp.bfloat16)


def packed(message, pieces, number):
    across = message.shape[-1] // (2 * BLOCK)
    lanes = pl.ds(number % across * 2 * BLOCK, 2 * BLOCK)
    return message.at[pieces + number // across, :, lanes]


def load_kernel(mixing_far, cells_far, mixing, cells, arrivals):
    fetches = [
        pltpu.make_async_copy(far, near, arrivals.at[i])
        for i, (far, near) in enumerate(((mixing_far, mixing), (cells_far, cells)))
    ]
    for fetch in fetches:
        fetch.start()
    for fetch in fetches:
        fetch.wait()


def pack_kernel(factor, pieces, length, cots, mixing, own, near, across):
    messages = (near, across.at[pl.ds(0, length)], across.at[pl.ds(length, length)])
    my_early, my_late = own_bits()
    for piece in range(pieces):
        base = piece * QUARTERS
        own[piece] = cots[base + my_early * 2 + my_late]
        for flip, message in enumerate(messages, 1):
            early, late = my_early ^ (flip & 1), my_late ^ (flip >> 1)
            message[piece] = cots[base + early * 2 + late]
            for which in range(2):
                number = which * pieces + piece
                if flip == 1:
                    for other in range(2):
                        packed(message, pieces, number * 2 + other)[...] = mixing[
                            factor + which, base + early * 2 + (late ^ other)
                        ]
                else:
                    packed(message, pieces, number)[...] = mixing[
                        factor + which, base + early * 2 + late
                    ]


def forward_kernel(message, out):
    out[...] = message[out.shape[0] :]


def stack_kernel(pieces, *rest):
    quarters, outs = rest[:QUARTERS], rest[QUARTERS:]
    for piece, out in enumerate(outs):
        for quarter, values in enumerate(quarters):
            out[quarter * BLOCK : (quarter + 1) * BLOCK] = values[piece]


def mixing_of(factor, which, pieces, piece, mixing, messages, quarter, other=0):
    if quarter == 0:
        early, late = own_bits()
        return mixing[factor + which, piece * QUARTERS + early * 2 + (late ^ other)]
    number = which * pieces + piece
    if quarter == 1:
        number = number * 2 + other
    return packed(messages[quarter - 1], pieces, number)[...]


def early_kernel(factor, pieces, piece, keep, recv, mixing, message, keep_out, send_out):
    weights = functools.partial(mixing_of, factor, 0, pieces, piece, mixing, [message])
    for other, out in enumerate((keep_out, send_out)):
        mine, theirs = keep[other], recv[other]
        pair = weights(0, other)
        out[0] = (times(pair[:, :BLOCK], mine) + times(pair[:, BLOCK:], theirs)).astype(
            jnp.bfloat16
        )
        pair = weights(1, other)
        out[1] = (times(pair[:, :BLOCK], theirs) + times(pair[:, BLOCK:], mine)).astype(
            jnp.bfloat16
        )


def late_kernel(factor, pieces, piece, keep, recv, mixing, *rest):
    messages, outs = rest[:-2], rest[-2:]
    values = [keep[0], keep[1], recv[0], recv[1]]
    for quarter in range(QUARTERS):
        pair = mixing_of(factor, 1, pieces, piece, mixing, messages, quarter)
        rows = slice(quarter % 2 * BLOCK, (quarter % 2 + 1) * BLOCK)
        outs[quarter // 2][rows] = (
            times(pair[:, :BLOCK], values[quarter]) + times(pair[:, BLOCK:], values[quarter ^ 2])
        ).astype(jnp.bfloat16)


def back_kernel(factor, pieces, piece, cores, cots, total, *rest):
    count = (cores - 1) * 2
    parts, (mixing, message1, message2, message3, *outs) = rest[:count], rest[count:]
    messages = (message1, message2, message3)
    grads = []
    for quarter in range(QUARTERS):
        rows = slice(quarter * BLOCK, (quarter + 1) * BLOCK)
        grad = cots[rows].astype(jnp.float32) + total[rows]
        inner = slice(quarter % 2 * BLOCK, (quarter % 2 + 1) * BLOCK)
        for part in parts[quarter // 2 :: 2]:
            grad = grad + part[inner].astype(jnp.float32)
        grads.append(grad.astype(jnp.bfloat16))
    for which, flip in ((1, 2), (0, 1)):
        both = [
            times_transposed(
                mixing_of(factor, which, pieces, piece, mixing, messages, quarter),
                grads[quarter],
            )
            for quarter in range(QUARTERS)
        ]
        grads = [
            (both[quarter][:BLOCK] + both[quarter ^ flip][BLOCK:]).astype(jnp.bfloat16)
            for quarter in range(QUARTERS)
        ]
    for grad, out in zip(grads, outs):
        out[...] = grad


def regroup_kernel(factor, units, *rest):
    quarters, mixing, outs = rest[:QUARTERS], rest[QUARTERS], rest[QUARTERS + 1 :]
    for number, unit in enumerate(units):
        own, cross = outs[2 * number : 2 * number + 2]
        for spot, block in enumerate(chosen_blocks(unit)):
            grad = quarters[1 - unit[spot // 2] % 2 + spot % 2 * 2][...]
            both = times_transposed(mixing[factor, block], grad)
            own[spot] = both[:BLOCK]
            cross[spot] = both[BLOCK:].astype(jnp.bfloat16)


def plain_back_kernel(factor, unit, mine, theirs, mixing, own, cross):
    for spot, block in enumerate(chosen_blocks(unit)):
        grad = (mine[spot] + theirs[spot].astype(jnp.float32)).astype(jnp.bfloat16)
        both = times_transposed(mixing[factor, block], grad)
        own[spot] = both[:BLOCK]
        cross[spot] = both[BLOCK:].astype(cross.dtype)


def exit_kernel(units, pattern_far, *rest):
    count = len(units)
    mine, theirs = rest[:count], rest[count : 2 * count]
    mixing, out, edges, own, cross, pattern, arrival = rest[2 * count :]
    fetch = pltpu.make_async_copy(pattern_far, pattern, arrival)
    fetch.start()
    blocks = own.shape[0]
    for number, unit in enumerate(units):
        for spot, block in enumerate(chosen_blocks(unit)):
            own[block] = mine[number][spot]
            cross[block] = theirs[number][spot]
    fetch.wait()
    for factor in reversed(range(LOCAL)):
        for block in range(blocks):
            own[block] += cross[pattern[factor, block]]
        for block in range(blocks):
            grad = own[block].astype(jnp.bfloat16)
            if factor == 0:
                out[block * BLOCK : (block + 1) * BLOCK] = grad
                if block == 0:
                    edges[0:1] = grad[:1]
                if block == blocks - 1:
                    edges[1:2] = grad[-1:]
            else:
                both = times_transposed(mixing[factor - 1, block], grad)
                own[block] = both[:BLOCK]
                cross[block] = both[BLOCK:]


def conv_back_kernel(cells, near, far, taps, out):
    values = cells[...].astype(jnp.float32)
    scale = taps[2:5].astype(jnp.float32)
    up, down = shifted(values, near[...], far[...])
    out[...] = (scale[0:1] * down + scale[1:2] * values + scale[2:3] * up).astype(jnp.bfloat16)


def channel_spots(count, chans):
    core = lax.axis_index("ch")
    return [
        pl.ds(pl.multiple_of(lax.rem(core + i, count) * chans, chans), chans)
        for i in range(count)
    ]


def grad_act_kernel(count, *rest):
    cots, (w_out, grad_act, c_all) = rest[:count], rest[count:]
    for spot, cot in zip(channel_spots(count, cots[0].shape[1]), cots):
        c_all[:, spot] = cot[...]
    hidden = w_out.shape[0]
    tile = min(TILE, hidden)
    for start in range(0, hidden, tile):
        grad_act[:, start : start + tile] = lax.dot_general(
            c_all[...], w_out[start : start + tile], ACROSS, preferred_element_type=jnp.float32
        ).astype(grad_act.dtype)


def hidden_kernel(count, *rest):
    mixed, (grad_act, w_in, activation, own) = rest[: 2 * count], rest[2 * count : 2 * count + 4]
    backs, (x_all, back_sum) = rest[2 * count + 4 : -2], rest[-2:]
    rows, chans = mixed[0].shape
    spots = channel_spots(count, chans)
    for i, spot in enumerate(spots):
        x_all[:rows, spot] = mixed[2 * i][...]
        x_all[rows:, spot] = mixed[2 * i + 1][...]
    size = w_in.shape[1]
    tile = min(TILE, size)
    for start in range(0, size, tile):
        tiles = slice(start, start + tile)
        hidden = times(x_all[...], w_in[:, tiles])
        square = hidden * hidden
        tanh_val = jnp.tanh(hidden * (root_two_pi + root_two_pi * 0.044715 * square))
        half = 0.5 + 0.5 * tanh_val
        gelu = hidden * half
        activation[:, tiles] = gelu.astype(jnp.bfloat16)
        slope = 2.0 * root_two_pi + 6.0 * root_two_pi * 0.044715 * square
        derivative = half + gelu * (1.0 - half) * slope
        grad_hidden = (grad_act[:, tiles].astype(jnp.float32) * derivative).astype(jnp.bfloat16)
        back = lax.dot_general(
            grad_hidden, w_in[:, tiles], ACROSS, preferred_element_type=jnp.float32
        )
        if start == 0:
            back_sum[...] = back
        else:
            back_sum[...] += back
    own[...] = back_sum[:, spots[0]]
    for i, spot in enumerate(spots[1:]):
        backs[2 * i][...] = back_sum[:rows, spot].astype(jnp.bfloat16)
        backs[2 * i + 1][...] = back_sum[rows:, spot].astype(jnp.bfloat16)


def out_kernel(count, activation, top, bottom, w_out, own, *others):
    rows, chans = top.shape
    for i, spot in enumerate(channel_spots(count, chans)):
        product = times(activation[...], w_out[:, spot])
        if i == 0:
            own[:rows] = top[...].astype(jnp.float32) + product[:rows]
            own[rows:] = bottom[...].astype(jnp.float32) + product[rows:]
        else:
            cuts = len(others) // (count - 1)
            for cut in range(cuts):
                size = 2 * rows // cuts
                part = product[cut * size : (cut + 1) * size]
                others[(i - 1) * cuts + cut][...] = part.astype(jnp.bfloat16)


def combine_kernel(pieces, counts, *rest):
    owns, parts, outs = rest[:pieces], rest[pieces:-QUARTERS], rest[-QUARTERS:]
    for piece in range(pieces):
        per_piece = counts[piece]
        mine, parts = parts[:per_piece], parts[per_piece:]
        for quarter, out in enumerate(outs):
            total = owns[piece][quarter * BLOCK : (quarter + 1) * BLOCK]
            cuts = total.shape[0] * QUARTERS // mine[0].shape[0]
            start = quarter * BLOCK % mine[0].shape[0]
            for part in mine[quarter * cuts // QUARTERS :: cuts]:
                total = total + part[start : start + BLOCK].astype(jnp.float32)
            out[piece] = total.astype(jnp.bfloat16)


def assemble_kernel(*rest):
    quarters, out = rest[:-1], rest[-1]
    my_early, my_late = own_bits()
    for quarter, values in enumerate(quarters):
        spot = (my_early ^ (quarter & 1)) * 2 + (my_late ^ (quarter >> 1))
        for piece in range(values.shape[0]):
            start = pl.multiple_of((piece * QUARTERS + spot) * BLOCK, BLOCK)
            out[pl.ds(start, BLOCK)] = values[piece]


def on_device(inputs, conv_weight, mixing, pattern, w_in, w_out, cotangent):
    row_count, chan_count = inputs.shape
    blocks = row_count // BLOCK
    pieces = blocks // QUARTERS
    width, hidden = w_in.shape
    cores = lax.axis_size("ch")
    levels = lax.axis_size("seq").bit_length() - 1
    plain = list(range(LOCAL, LOCAL + levels - 2))
    last = LOCAL + levels - 2
    early_bit, late_bit = 1 << (levels - 2), 1 << (levels - 1)
    masks = [0, early_bit, late_bit, early_bit | late_bit]

    def blocks_of(size, kind=jnp.bfloat16):
        return ((size, BLOCK, chan_count), kind)

    half = blocks_of(2)
    whole = ((row_count, chan_count), jnp.bfloat16)
    piece_rows = QUARTERS * BLOCK
    flat = (piece_rows, chan_count)
    block = ((BLOCK, chan_count), jnp.bfloat16)
    half_flat = ((2 * BLOCK, chan_count), jnp.bfloat16)
    flat_piece = (flat, jnp.bfloat16)
    flops = 2 * piece_rows * width * hidden

    latest = []

    def run(kernel, name, outs, arrays, *args, **kwargs):
        results = call(kernel, name, outs, arrays, *args, order=tuple(latest), **kwargs)
        latest[:] = results[-1:]
        return results

    near, far = neighbours(jnp.concatenate([inputs[:1], inputs[-1:], conv_weight]), "seq")
    per_block = chan_count // (2 * BLOCK)
    lengths = [pieces + -(-pieces * 2 * (1 + (flip == 1)) // per_block) for flip in (1, 2, 3)]
    length = lengths[1]
    mixing, cells = run(
        load_kernel,
        "load",
        [(array.shape, array.dtype) for array in (mixing, inputs)],
        [],
        [mixing, inputs],
        [pltpu.SemaphoreType.DMA((2,))],
        limit=ALL,
    )
    units = [(s,) for s in range(2 * pieces)]
    convolved, *states = run(
        functools.partial(entry_kernel, units),
        "conv_and_local_factors",
        [whole] + [blocks_of(2 * len(unit)) for unit in units],
        [cells, near, far, mixing],
        [pattern],
        [pltpu.VMEM((blocks, BLOCK, chan_count), jnp.bfloat16)] * 2
        + [pltpu.SMEM(pattern.shape, jnp.int32), pltpu.SemaphoreType.DMA],
    )
    own_cots, *messages = run(
        functools.partial(pack_kernel, last, pieces, length),
        "pack",
        [((pieces, BLOCK, chan_count), jnp.bfloat16)]
        + [blocks_of(lengths[0]), blocks_of(2 * length)],
        [cotangent.reshape(blocks, BLOCK, chan_count), mixing],
    )
    messages = [from_flipped(m, "seq", mask) for m, mask in zip(messages, masks[1:])]

    def forward():
        (message,) = run(forward_kernel, "forward", [blocks_of(length)], [messages[1]])
        messages.append(from_flipped(message, "seq", early_bit))

    all_cots = []
    halves = {}
    transposed = [None] * pieces
    grad_acts = [None] * pieces
    parts = [None] * pieces
    mixeds = [None] * pieces
    activations = [None] * pieces
    owns = [None] * pieces
    out_owns = [None] * pieces
    out_parts = [None] * pieces

    def stack():
        stacked = run(
            functools.partial(stack_kernel, pieces),
            "stack",
            [flat_piece] * pieces,
            [own_cots, *messages],
        )
        for piece in stacked:
            all_cots.append([piece] + [from_offset(piece, "ch", i) for i in range(1, cores)])

    def grad_act(p):
        (grad_acts[p],) = run(
            functools.partial(grad_act_kernel, cores),
            "grad_act",
            [((piece_rows, hidden), jnp.bfloat16)],
            [*all_cots[p], w_out],
            scratch=[pltpu.VMEM((piece_rows, width), jnp.bfloat16)],
            limit=LARGE,
        )

    def plain_factor(factor, u):
        unit = units[u]
        mates = from_flipped(states[u], "seq", 1 << (factor - LOCAL))
        split = factor == plain[-1] and len(unit) == 2
        results = run(
            functools.partial(plain_kernel, factor, unit),
            "factor",
            [half, half] if split else [blocks_of(2 * len(unit))],
            [states[u], mates, mixing],
        )
        if factor == plain[-1]:
            halves.update(zip(unit, results))
        else:
            states[u] = results[0]

    def early_factor(p):
        send, keep = halves[2 * p], halves[2 * p + 1]
        transposed[p] = run(
            functools.partial(early_kernel, last, pieces, p),
            "early_factor",
            [half, half],
            [keep, from_flipped(send, "seq", early_bit), mixing, messages[0]],
        )

    def late_factor(p):
        keep, send = transposed[p]
        mixeds[p] = run(
            functools.partial(late_kernel, last, pieces, p),
            "late_factor",
            [half_flat] * 2,
            [keep, from_flipped(send, "seq", late_bit), mixing, *messages],
        )

    def hidden_and_grad(p):
        gathered = [
            from_offset(mixed, "ch", i) if i else mixed for i in range(cores) for mixed in mixeds[p]
        ]
        activations[p], owns[p], *backs = run(
            functools.partial(hidden_kernel, cores),
            "mlp_hidden_and_grad",
            [((piece_rows, hidden), jnp.bfloat16), (flat, jnp.float32)]
            + [half_flat] * ((cores - 1) * 2),
            [*gathered, grad_acts[p], w_in],
            scratch=[
                pltpu.VMEM((piece_rows, width), jnp.bfloat16),
                pltpu.VMEM((piece_rows, width), jnp.float32),
            ],
            limit=LARGE,
        )
        parts[p] = [
            from_offset(back, "ch", cores - 1 - i // 2) for i, back in enumerate(backs)
        ]

    def transposed_back(p):
        quarters = run(
            functools.partial(back_kernel, last, pieces, p, cores),
            "late_and_early_back",
            [block] * QUARTERS,
            [all_cots[p][0], owns[p], *parts[p], mixing, *messages],
        )
        transposed[p] = [
            from_flipped(grad, "seq", mask) if mask else grad
            for grad, mask in zip(quarters, masks)
        ]

    def regroup(p):
        chosen = [u for u, unit in enumerate(back_units) if unit[0] // 2 == p]
        sizes = [2 * len(back_units[u]) for u in chosen]
        results = run(
            functools.partial(regroup_kernel, plain[-1], [back_units[u] for u in chosen]),
            "regroup_and_factor_back",
            [blocks_of(size, kind) for size in sizes for kind in (jnp.float32, jnp.bfloat16)],
            [*transposed[p], mixing],
        )
        for number, u in enumerate(chosen):
            states[u] = results[2 * number : 2 * number + 2]

    def out_product(p):
        cuts = 1 if p + 1 < pieces else 2
        out_owns[p], *others = run(
            functools.partial(out_kernel, cores),
            "mlp_out",
            [(flat, jnp.float32)] + [flat_piece if cuts == 1 else half_flat] * (cuts * (cores - 1)),
            [activations[p], *mixeds[p], w_out],
            limit=LARGE,
        )
        out_parts[p] = [
            from_offset(other, "ch", cores - 1 - i // cuts) for i, other in enumerate(others)
        ]

    def plain_back(factor, u):
        mine, cross = states[u]
        theirs = from_flipped(cross, "seq", 1 << (factor - LOCAL))
        kind = jnp.bfloat16 if factor != plain[0] else jnp.float32
        size = 2 * len(back_units[u])
        states[u] = run(
            functools.partial(plain_back_kernel, factor - 1, back_units[u]),
            "factor_back",
            [blocks_of(size, jnp.float32), blocks_of(size, kind)],
            [mine, theirs, mixing],
        )

    waves = sorted((u + 2 * i, -i, u) for i in range(len(plain)) for u in range(len(units)))
    for _, i, u in waves:
        plain_factor(plain[-i], u)
        if plain[-i] == plain[-1] and u == 1:
            early_factor(0)
            forward()
    late_factor(0)
    for p in range(1, pieces):
        early_factor(p)
    stack()
    grad_act(0)
    back_units = [(2 * p, 2 * p + 1) for p in range(pieces - 1)]
    back_units += [(2 * pieces - 1,), (2 * pieces - 2,)]
    states = [None] * len(back_units)
    for p in range(pieces):
        hidden_and_grad(p)
        if p + 1 < pieces:
            grad_act(p + 1)
            out_product(p)
            late_factor(p + 1)
        if p > 0:
            regroup(p - 1)
        if p == pieces - 1:
            out_product(p)
        transposed_back(p)
    early_units = range(pieces - 1)
    late_units = range(pieces - 1, pieces + 1)
    def combine():
        return run(
            functools.partial(combine_kernel, pieces, [len(piece) for piece in out_parts]),
            "combine",
            [((pieces, BLOCK, chan_count), jnp.bfloat16)] * QUARTERS,
            [*out_owns, *[part for piece in out_parts for part in piece]],
        )

    outs = combine()
    regroup(pieces - 1)
    for factor in reversed(plain):
        for u in (*early_units, *late_units):
            plain_back(factor, u)
    arrived = [from_flipped(out, "seq", mask) if mask else out for out, mask in zip(outs, masks)]
    grad_conv, edges = run(
        functools.partial(exit_kernel, back_units),
        "local_factors_back",
        [whole, ((2, chan_count), jnp.bfloat16)],
        [g[0] for g in states] + [g[1] for g in states] + [mixing],
        [pattern],
        [pltpu.VMEM((blocks, BLOCK, chan_count), jnp.float32)] * 2
        + [pltpu.SMEM(pattern.shape, jnp.int32), pltpu.SemaphoreType.DMA],
        limit=LARGE,
    )
    (layer_out,) = call(assemble_kernel, "assemble", [whole], arrived)
    near_grad, far_grad = neighbours(edges, "seq")
    (grad_input,) = run(
        conv_back_kernel, "conv_back", [whole], [grad_conv, near_grad, far_grad, near]
    )
    return (layer_out, convolved, grad_input)


def solution(mesh):
    return jax.shard_map(
        on_device,
        mesh=mesh,
        in_specs=(
            P("seq", "ch"),
            P(None, "ch"),
            P(None, "seq", None, None),
            P(None, "seq"),
            P(None, "ch"),
            P("ch", None),
            P("seq", "ch"),
        ),
        out_specs=(P("seq", "ch"), P("seq", "ch"), P("seq", "ch")),
        check_vma=False,
    )
```

```python
import functools

import jax
import jax.numpy as jnp
from jax import lax
from jax.experimental import pallas as pl
from jax.experimental.pallas import tpu as pltpu
from jax.sharding import PartitionSpec as P

BLOCK = 64
LOCAL = 2
QUARTERS = 4
TILE = 512
SMALL = 8 * 1024 * 1024
LARGE = 20 * 1024 * 1024
ALL = 44 * 1024 * 1024

root_two_pi = 0.7978845608028654

IN_HBM = pl.BlockSpec(memory_space=pltpu.HBM)
IN_VMEM = pl.BlockSpec(memory_space=pltpu.VMEM)
ANYWHERE = pl.BlockSpec(memory_space=pl.ANY)
ACROSS = (((1,), (1,)), ((), ()))
OVER_ROWS = (((0,), (0,)), ((), ()))


def times(weights, value):
    return jnp.dot(weights, value, preferred_element_type=jnp.float32)


def times_transposed(weights, value):
    return lax.dot_general(weights, value, OVER_ROWS, preferred_element_type=jnp.float32)


def neighbours(edges, axis):
    count = lax.axis_size(axis)
    near = lax.ppermute(edges, axis, [(i, i ^ 1) for i in range(count)])
    route = []
    for low in range(1, count - 1, 2):
        route += [(low, low + 1), (low + 1, low)]
    return near, lax.ppermute(edges[:2], axis, route)


def from_flipped(block, axis, mask):
    count = lax.axis_size(axis)
    return lax.ppermute(block, axis, [(i, i ^ mask) for i in range(count)])


def from_offset(block, axis, offset):
    count = lax.axis_size(axis)
    return lax.ppermute(block, axis, [((i + offset) % count, i) for i in range(count)])


def call(kernel, name, outs, arrays, distant=(), scratch=(), order=(), limit=SMALL):
    count = len(distant) + len(arrays)

    def body(*refs):
        kernel(*refs[:count], *refs[count + len(order) :])

    return pl.pallas_call(
        body,
        out_shape=[jax.ShapeDtypeStruct(shape, kind) for shape, kind in outs],
        in_specs=[IN_HBM] * len(distant) + [IN_VMEM] * len(arrays) + [ANYWHERE] * len(order),
        out_specs=[IN_VMEM] * len(outs),
        scratch_shapes=list(scratch),
        compiler_params=pltpu.CompilerParams(vmem_limit_bytes=limit),
        cost_estimate=pl.CostEstimate(flops=0, bytes_accessed=0, transcendentals=0),
        name=name,
    )(*distant, *arrays, *order)


def own_bits():
    seat = lax.axis_index("seq")
    levels = lax.axis_size("seq").bit_length() - 1
    return (seat >> (levels - 2)) & 1, (seat >> (levels - 1)) & 1


def shifted(cells, near, far):
    rows = cells.shape[0]
    even = lax.axis_index("seq") % 2 == 0
    near, far = near.astype(jnp.float32), far.astype(jnp.float32)
    before = jnp.where(even, far[1:2], near[1:2])
    after = jnp.where(even, near[0:1], far[0:1])
    spot = lax.broadcasted_iota(jnp.int32, cells.shape, 0)
    up = jnp.where(spot == 0, before, pltpu.roll(cells, 1, 0))
    down = jnp.where(spot == rows - 1, after, pltpu.roll(cells, rows - 1, 0))
    return up, down


def chosen_blocks(subs):
    early, late = own_bits()
    return [
        sub // 2 * QUARTERS + (early ^ (1 - sub % 2)) * 2 + (late ^ other)
        for sub in subs
        for other in range(2)
    ]


def local_factor(factor, pattern, source, mixing, target, chosen):
    for spot, block in enumerate(chosen):
        pair = mixing[factor, block]
        target[spot] = (
            times(pair[:, :BLOCK], source[block])
            + times(pair[:, BLOCK:], source[pattern[factor, block]])
        ).astype(jnp.bfloat16)


def entry_kernel(units, pattern_far, cells, near, far, mixing, conv_ref, *rest):
    outs, (first, between, pattern, arrival) = rest[:-4], rest[-4:]
    fetch = pltpu.make_async_copy(pattern_far, pattern, arrival)
    fetch.start()
    values = cells[...].astype(jnp.float32)
    scale = near[2:5].astype(jnp.float32)
    up, down = shifted(values, near[...], far[...])
    convolved = (scale[0:1] * up + scale[1:2] * values + scale[2:3] * down).astype(jnp.bfloat16)
    conv_ref[...] = convolved
    first[...] = convolved.reshape(first.shape)
    fetch.wait()
    every = range(first.shape[0])
    refs = (first, between)
    for factor in range(LOCAL - 1):
        local_factor(factor, pattern, refs[factor % 2], mixing, refs[1 - factor % 2], every)
    source = refs[(LOCAL - 1) % 2]
    for unit, out in zip(units, outs):
        local_factor(LOCAL - 1, pattern, source, mixing, out, chosen_blocks(unit))


def plain_kernel(factor, unit, state, mates, mixing, *outs):
    for spot, block in enumerate(chosen_blocks(unit)):
        pair = mixing[factor, block]
        per_out = state.shape[0] // len(outs)
        outs[spot // per_out][spot % per_out] = (
            times(pair[:, :BLOCK], state[spot]) + times(pair[:, BLOCK:], mates[spot])
        ).astype(jnp.bfloat16)


def packed(message, pieces, number):
    across = message.shape[-1] // (2 * BLOCK)
    lanes = pl.ds(number % across * 2 * BLOCK, 2 * BLOCK)
    return message.at[pieces + number // across, :, lanes]


def load_kernel(mixing_far, cells_far, mixing, cells, arrivals):
    fetches = [
        pltpu.make_async_copy(far, near, arrivals.at[i])
        for i, (far, near) in enumerate(((mixing_far, mixing), (cells_far, cells)))
    ]
    for fetch in fetches:
        fetch.start()
    for fetch in fetches:
        fetch.wait()


def pack_kernel(factor, pieces, cots, mixing, own, soon, near, across):
    my_early, my_late = own_bits()
    half = across.shape[0] // 2
    for piece in range(pieces):
        base = piece * QUARTERS
        for quarter, (message, first) in enumerate(((own, 0), (near, 0), (across, 0), (across, half))):
            early, late = my_early ^ (quarter & 1), my_late ^ (quarter >> 1)
            block = base + early * 2 + late
            message[first + piece] = cots[block]
            if quarter == 1:
                packed(near, pieces, piece)[...] = mixing[factor + 1, block]
                for other in range(2):
                    packed(soon, 0, piece * 2 + other)[...] = mixing[
                        factor, base + early * 2 + (late ^ other)
                    ]
            elif quarter > 1:
                for which in range(2):
                    packed(across, first + pieces, which * pieces + piece)[...] = mixing[
                        factor + which, block
                    ]


def forward_kernel(near, across, out):
    length, half = near.shape[0], across.shape[0] // 2
    out[:length] = near[...]
    out[length:] = across[half:]


def stack_kernel(pieces, own, across, handed, *outs):
    first = handed.shape[0] - across.shape[0] // 2
    for piece, out in enumerate(outs):
        for quarter, values in enumerate(
            (own[piece], handed[piece], across[piece], handed[first + piece])
        ):
            out[quarter * BLOCK : (quarter + 1) * BLOCK] = values


def mixing_of(factor, which, pieces, piece, mixing, messages, quarter, other=0):
    if quarter == 0:
        early, late = own_bits()
        return mixing[factor + which, piece * QUARTERS + early * 2 + (late ^ other)]
    if quarter == 1 and which == 0:
        return packed(messages[0], 0, piece * 2 + other)[...]
    across, handed = messages[1:]
    if quarter == 1:
        return packed(handed, pieces, piece)[...]
    number = which * pieces + piece
    if quarter == 2:
        return packed(across, pieces, number)[...]
    first = handed.shape[0] - across.shape[0] // 2
    return packed(handed, first + pieces, number)[...]


def early_kernel(factor, pieces, piece, keep, recv, mixing, message, keep_out, send_out):
    weights = functools.partial(mixing_of, factor, 0, pieces, piece, mixing, [message])
    for other, out in enumerate((keep_out, send_out)):
        mine, theirs = keep[other], recv[other]
        pair = weights(0, other)
        out[0] = (times(pair[:, :BLOCK], mine) + times(pair[:, BLOCK:], theirs)).astype(
            jnp.bfloat16
        )
        pair = weights(1, other)
        out[1] = (times(pair[:, :BLOCK], theirs) + times(pair[:, BLOCK:], mine)).astype(
            jnp.bfloat16
        )


def late_kernel(factor, pieces, piece, keep, recv, mixing, *rest):
    messages, outs = rest[:-2], rest[-2:]
    values = [keep[0], keep[1], recv[0], recv[1]]
    for quarter in range(QUARTERS):
        pair = mixing_of(factor, 1, pieces, piece, mixing, messages, quarter)
        rows = slice(quarter % 2 * BLOCK, (quarter % 2 + 1) * BLOCK)
        outs[quarter // 2][rows] = (
            times(pair[:, :BLOCK], values[quarter]) + times(pair[:, BLOCK:], values[quarter ^ 2])
        ).astype(jnp.bfloat16)


def back_kernel(factor, pieces, piece, cores, cots, total, *rest):
    count = (cores - 1) * 2
    parts, (mixing, message1, message2, message3, *outs) = rest[:count], rest[count:]
    messages = (message1, message2, message3)
    grads = []
    for quarter in range(QUARTERS):
        rows = slice(quarter * BLOCK, (quarter + 1) * BLOCK)
        grad = cots[rows].astype(jnp.float32) + total[rows]
        inner = slice(quarter % 2 * BLOCK, (quarter % 2 + 1) * BLOCK)
        for part in parts[quarter // 2 :: 2]:
            grad = grad + part[inner].astype(jnp.float32)
        grads.append(grad.astype(jnp.bfloat16))
    for which, flip in ((1, 2), (0, 1)):
        both = [
            times_transposed(
                mixing_of(factor, which, pieces, piece, mixing, messages, quarter),
                grads[quarter],
            )
            for quarter in range(QUARTERS)
        ]
        grads = [
            (both[quarter][:BLOCK] + both[quarter ^ flip][BLOCK:]).astype(jnp.bfloat16)
            for quarter in range(QUARTERS)
        ]
    for grad, out in zip(grads, outs):
        out[...] = grad


def regroup_kernel(factor, units, *rest):
    quarters, mixing, outs = rest[:QUARTERS], rest[QUARTERS], rest[QUARTERS + 1 :]
    for number, unit in enumerate(units):
        own, cross = outs[2 * number : 2 * number + 2]
        for spot, block in enumerate(chosen_blocks(unit)):
            grad = quarters[1 - unit[spot // 2] % 2 + spot % 2 * 2][...]
            both = times_transposed(mixing[factor, block], grad)
            own[spot] = both[:BLOCK]
            cross[spot] = both[BLOCK:].astype(jnp.bfloat16)


def plain_back_kernel(factor, unit, mine, theirs, mixing, own, cross):
    for spot, block in enumerate(chosen_blocks(unit)):
        grad = (mine[spot] + theirs[spot].astype(jnp.float32)).astype(jnp.bfloat16)
        both = times_transposed(mixing[factor, block], grad)
        own[spot] = both[:BLOCK]
        cross[spot] = both[BLOCK:].astype(cross.dtype)


def exit_kernel(units, pattern_far, *rest):
    count = len(units)
    mine, theirs = rest[:count], rest[count : 2 * count]
    mixing, out, edges, own, cross, pattern, arrival = rest[2 * count :]
    fetch = pltpu.make_async_copy(pattern_far, pattern, arrival)
    fetch.start()
    blocks = own.shape[0]
    for number, unit in enumerate(units):
        for spot, block in enumerate(chosen_blocks(unit)):
            own[block] = mine[number][spot]
            cross[block] = theirs[number][spot]
    fetch.wait()
    for factor in reversed(range(LOCAL)):
        for block in range(blocks):
            own[block] += cross[pattern[factor, block]]
        for block in range(blocks):
            grad = own[block].astype(jnp.bfloat16)
            if factor == 0:
                out[block * BLOCK : (block + 1) * BLOCK] = grad
                if block == 0:
                    edges[0:1] = grad[:1]
                if block == blocks - 1:
                    edges[1:2] = grad[-1:]
            else:
                both = times_transposed(mixing[factor - 1, block], grad)
                own[block] = both[:BLOCK]
                cross[block] = both[BLOCK:]


def conv_back_kernel(cells, near, far, taps, out):
    values = cells[...].astype(jnp.float32)
    scale = taps[2:5].astype(jnp.float32)
    up, down = shifted(values, near[...], far[...])
    out[...] = (scale[0:1] * down + scale[1:2] * values + scale[2:3] * up).astype(jnp.bfloat16)


def channel_spots(count, chans):
    core = lax.axis_index("ch")
    return [
        pl.ds(pl.multiple_of(lax.rem(core + i, count) * chans, chans), chans)
        for i in range(count)
    ]


def grad_act_kernel(count, *rest):
    cots, (w_out, grad_act, c_all) = rest[:count], rest[count:]
    for spot, cot in zip(channel_spots(count, cots[0].shape[1]), cots):
        c_all[:, spot] = cot[...]
    hidden = w_out.shape[0]
    tile = min(TILE, hidden)
    for start in range(0, hidden, tile):
        grad_act[:, start : start + tile] = lax.dot_general(
            c_all[...], w_out[start : start + tile], ACROSS, preferred_element_type=jnp.float32
        ).astype(grad_act.dtype)


def hidden_kernel(count, *rest):
    mixed, (grad_act, w_in, activation, own) = rest[: 2 * count], rest[2 * count : 2 * count + 4]
    backs, (x_all, back_sum) = rest[2 * count + 4 : -2], rest[-2:]
    rows, chans = mixed[0].shape
    spots = channel_spots(count, chans)
    for i, spot in enumerate(spots):
        x_all[:rows, spot] = mixed[2 * i][...]
        x_all[rows:, spot] = mixed[2 * i + 1][...]
    size = w_in.shape[1]
    tile = min(TILE, size)
    for start in range(0, size, tile):
        tiles = slice(start, start + tile)
        hidden = times(x_all[...], w_in[:, tiles])
        square = hidden * hidden
        tanh_val = jnp.tanh(hidden * (root_two_pi + root_two_pi * 0.044715 * square))
        half = 0.5 + 0.5 * tanh_val
        gelu = hidden * half
        activation[:, tiles] = gelu.astype(jnp.bfloat16)
        slope = 2.0 * root_two_pi + 6.0 * root_two_pi * 0.044715 * square
        derivative = half + gelu * (1.0 - half) * slope
        grad_hidden = (grad_act[:, tiles].astype(jnp.float32) * derivative).astype(jnp.bfloat16)
        back = lax.dot_general(
            grad_hidden, w_in[:, tiles], ACROSS, preferred_element_type=jnp.float32
        )
        if start == 0:
            back_sum[...] = back
        else:
            back_sum[...] += back
    own[...] = back_sum[:, spots[0]]
    for i, spot in enumerate(spots[1:]):
        backs[2 * i][...] = back_sum[:rows, spot].astype(jnp.bfloat16)
        backs[2 * i + 1][...] = back_sum[rows:, spot].astype(jnp.bfloat16)


def out_kernel(count, activation, top, bottom, w_out, own, *others):
    rows, chans = top.shape
    for i, spot in enumerate(channel_spots(count, chans)):
        product = times(activation[...], w_out[:, spot])
        if i == 0:
            own[:rows] = top[...].astype(jnp.float32) + product[:rows]
            own[rows:] = bottom[...].astype(jnp.float32) + product[rows:]
        else:
            cuts = len(others) // (count - 1)
            for cut in range(cuts):
                size = 2 * rows // cuts
                part = product[cut * size : (cut + 1) * size]
                others[(i - 1) * cuts + cut][...] = part.astype(jnp.bfloat16)


def combine_kernel(pieces, counts, *rest):
    owns, parts, outs = rest[:pieces], rest[pieces:-QUARTERS], rest[-QUARTERS:]
    for piece in range(pieces):
        per_piece = counts[piece]
        mine, parts = parts[:per_piece], parts[per_piece:]
        for quarter, out in enumerate(outs):
            total = owns[piece][quarter * BLOCK : (quarter + 1) * BLOCK]
            cuts = total.shape[0] * QUARTERS // mine[0].shape[0]
            start = quarter * BLOCK % mine[0].shape[0]
            for part in mine[quarter * cuts // QUARTERS :: cuts]:
                total = total + part[start : start + BLOCK].astype(jnp.float32)
            out[piece] = total.astype(jnp.bfloat16)


def assemble_kernel(*rest):
    quarters, out = rest[:-1], rest[-1]
    my_early, my_late = own_bits()
    for quarter, values in enumerate(quarters):
        spot = (my_early ^ (quarter & 1)) * 2 + (my_late ^ (quarter >> 1))
        for piece in range(values.shape[0]):
            start = pl.multiple_of((piece * QUARTERS + spot) * BLOCK, BLOCK)
            out[pl.ds(start, BLOCK)] = values[piece]


def on_device(inputs, conv_weight, mixing, pattern, w_in, w_out, cotangent):
    row_count, chan_count = inputs.shape
    blocks = row_count // BLOCK
    pieces = blocks // QUARTERS
    width, hidden = w_in.shape
    cores = lax.axis_size("ch")
    levels = lax.axis_size("seq").bit_length() - 1
    plain = list(range(LOCAL, LOCAL + levels - 2))
    last = LOCAL + levels - 2
    early_bit, late_bit = 1 << (levels - 2), 1 << (levels - 1)
    masks = [0, early_bit, late_bit, early_bit | late_bit]

    def blocks_of(size, kind=jnp.bfloat16):
        return ((size, BLOCK, chan_count), kind)

    half = blocks_of(2)
    whole = ((row_count, chan_count), jnp.bfloat16)
    piece_rows = QUARTERS * BLOCK
    flat = (piece_rows, chan_count)
    block = ((BLOCK, chan_count), jnp.bfloat16)
    half_flat = ((2 * BLOCK, chan_count), jnp.bfloat16)
    flat_piece = (flat, jnp.bfloat16)
    flops = 2 * piece_rows * width * hidden

    latest = []

    def run(kernel, name, outs, arrays, *args, **kwargs):
        results = call(kernel, name, outs, arrays, *args, order=tuple(latest), **kwargs)
        latest[:] = results[-1:]
        return results

    near, far = neighbours(jnp.concatenate([inputs[:1], inputs[-1:], conv_weight]), "seq")
    per_block = chan_count // (2 * BLOCK)
    short, middle, length = (
        first + -(-pieces * count // per_block)
        for first, count in ((0, 2), (pieces, 1), (pieces, 2))
    )
    mixing, cells = run(
        load_kernel,
        "load",
        [(array.shape, array.dtype) for array in (mixing, inputs)],
        [],
        [mixing, inputs],
        [pltpu.SemaphoreType.DMA((2,))],
        limit=ALL,
    )
    units = [(s,) for s in range(2 * pieces)]
    convolved, *states = run(
        functools.partial(entry_kernel, units),
        "conv_and_local_factors",
        [whole] + [blocks_of(2 * len(unit)) for unit in units],
        [cells, near, far, mixing],
        [pattern],
        [pltpu.VMEM((blocks, BLOCK, chan_count), jnp.bfloat16)] * 2
        + [pltpu.SMEM(pattern.shape, jnp.int32), pltpu.SemaphoreType.DMA],
    )
    own_cots, soon, near_cots, across = run(
        functools.partial(pack_kernel, last, pieces),
        "pack",
        [blocks_of(pieces), blocks_of(short), blocks_of(middle), blocks_of(2 * length)],
        [cotangent.reshape(blocks, BLOCK, chan_count), mixing],
    )
    messages = [from_flipped(soon, "seq", early_bit), from_flipped(across, "seq", late_bit)]

    def forward():
        (message,) = run(
            forward_kernel, "forward", [blocks_of(middle + length)], [near_cots, messages[1]]
        )
        messages.append(from_flipped(message, "seq", early_bit))

    all_cots = []
    halves = {}
    transposed = [None] * pieces
    grad_acts = [None] * pieces
    parts = [None] * pieces
    mixeds = [None] * pieces
    activations = [None] * pieces
    owns = [None] * pieces
    out_owns = [None] * pieces
    out_parts = [None] * pieces

    def stack():
        stacked = run(
            functools.partial(stack_kernel, pieces),
            "stack",
            [flat_piece] * pieces,
            [own_cots, *messages[1:]],
        )
        for piece in stacked:
            all_cots.append([piece] + [from_offset(piece, "ch", i) for i in range(1, cores)])

    def grad_act(p):
        (grad_acts[p],) = run(
            functools.partial(grad_act_kernel, cores),
            "grad_act",
            [((piece_rows, hidden), jnp.bfloat16)],
            [*all_cots[p], w_out],
            scratch=[pltpu.VMEM((piece_rows, width), jnp.bfloat16)],
            limit=LARGE,
        )

    def plain_factor(factor, u):
        unit = units[u]
        mates = from_flipped(states[u], "seq", 1 << (factor - LOCAL))
        split = factor == plain[-1] and len(unit) == 2
        results = run(
            functools.partial(plain_kernel, factor, unit),
            "factor",
            [half, half] if split else [blocks_of(2 * len(unit))],
            [states[u], mates, mixing],
        )
        if factor == plain[-1]:
            halves.update(zip(unit, results))
        else:
            states[u] = results[0]

    def early_factor(p):
        send, keep = halves[2 * p], halves[2 * p + 1]
        transposed[p] = run(
            functools.partial(early_kernel, last, pieces, p),
            "early_factor",
            [half, half],
            [keep, from_flipped(send, "seq", early_bit), mixing, messages[0]],
        )

    def late_factor(p):
        keep, send = transposed[p]
        mixeds[p] = run(
            functools.partial(late_kernel, last, pieces, p),
            "late_factor",
            [half_flat] * 2,
            [keep, from_flipped(send, "seq", late_bit), mixing, *messages],
        )

    def hidden_and_grad(p):
        gathered = [
            from_offset(mixed, "ch", i) if i else mixed for i in range(cores) for mixed in mixeds[p]
        ]
        activations[p], owns[p], *backs = run(
            functools.partial(hidden_kernel, cores),
            "mlp_hidden_and_grad",
            [((piece_rows, hidden), jnp.bfloat16), (flat, jnp.float32)]
            + [half_flat] * ((cores - 1) * 2),
            [*gathered, grad_acts[p], w_in],
            scratch=[
                pltpu.VMEM((piece_rows, width), jnp.bfloat16),
                pltpu.VMEM((piece_rows, width), jnp.float32),
            ],
            limit=LARGE,
        )
        parts[p] = [
            from_offset(back, "ch", cores - 1 - i // 2) for i, back in enumerate(backs)
        ]

    def transposed_back(p):
        quarters = run(
            functools.partial(back_kernel, last, pieces, p, cores),
            "late_and_early_back",
            [block] * QUARTERS,
            [all_cots[p][0], owns[p], *parts[p], mixing, *messages],
        )
        transposed[p] = [
            from_flipped(grad, "seq", mask) if mask else grad
            for grad, mask in zip(quarters, masks)
        ]

    def regroup(p):
        chosen = [u for u, unit in enumerate(back_units) if unit[0] // 2 == p]
        sizes = [2 * len(back_units[u]) for u in chosen]
        results = run(
            functools.partial(regroup_kernel, plain[-1], [back_units[u] for u in chosen]),
            "regroup_and_factor_back",
            [blocks_of(size, kind) for size in sizes for kind in (jnp.float32, jnp.bfloat16)],
            [*transposed[p], mixing],
        )
        for number, u in enumerate(chosen):
            states[u] = results[2 * number : 2 * number + 2]

    def out_product(p):
        cuts = 1 if p + 1 < pieces else 2
        out_owns[p], *others = run(
            functools.partial(out_kernel, cores),
            "mlp_out",
            [(flat, jnp.float32)] + [flat_piece if cuts == 1 else half_flat] * (cuts * (cores - 1)),
            [activations[p], *mixeds[p], w_out],
            limit=LARGE,
        )
        out_parts[p] = [
            from_offset(other, "ch", cores - 1 - i // cuts) for i, other in enumerate(others)
        ]

    def plain_back(factor, u):
        mine, cross = states[u]
        theirs = from_flipped(cross, "seq", 1 << (factor - LOCAL))
        kind = jnp.bfloat16 if factor != plain[0] else jnp.float32
        size = 2 * len(back_units[u])
        states[u] = run(
            functools.partial(plain_back_kernel, factor - 1, back_units[u]),
            "factor_back",
            [blocks_of(size, jnp.float32), blocks_of(size, kind)],
            [mine, theirs, mixing],
        )

    waves = sorted((u + 2 * i, -i, u) for i in range(len(plain)) for u in range(len(units)))
    for _, i, u in waves:
        plain_factor(plain[-i], u)
        if plain[-i] == plain[-1] and u == 1:
            early_factor(0)
            forward()
    for p in range(1, pieces):
        early_factor(p)
    stack()
    late_factor(0)
    grad_act(0)
    back_units = [(2 * p, 2 * p + 1) for p in range(pieces - 1)]
    back_units += [(2 * pieces - 1,), (2 * pieces - 2,)]
    states = [None] * len(back_units)
    for p in range(pieces):
        hidden_and_grad(p)
        if p + 1 < pieces:
            grad_act(p + 1)
            out_product(p)
            late_factor(p + 1)
        if p > 0:
            regroup(p - 1)
        if p == pieces - 1:
            out_product(p)
        transposed_back(p)
    early_units = range(pieces - 1)
    late_units = range(pieces - 1, pieces + 1)
    def combine():
        return run(
            functools.partial(combine_kernel, pieces, [len(piece) for piece in out_parts]),
            "combine",
            [((pieces, BLOCK, chan_count), jnp.bfloat16)] * QUARTERS,
            [*out_owns, *[part for piece in out_parts for part in piece]],
        )

    outs = combine()
    regroup(pieces - 1)
    for factor in reversed(plain):
        for u in (*early_units, *late_units):
            plain_back(factor, u)
    arrived = [from_flipped(out, "seq", mask) if mask else out for out, mask in zip(outs, masks)]
    grad_conv, edges = run(
        functools.partial(exit_kernel, back_units),
        "local_factors_back",
        [whole, ((2, chan_count), jnp.bfloat16)],
        [g[0] for g in states] + [g[1] for g in states] + [mixing],
        [pattern],
        [pltpu.VMEM((blocks, BLOCK, chan_count), jnp.float32)] * 2
        + [pltpu.SMEM(pattern.shape, jnp.int32), pltpu.SemaphoreType.DMA],
        limit=LARGE,
    )
    (layer_out,) = call(assemble_kernel, "assemble", [whole], arrived)
    near_grad, far_grad = neighbours(edges, "seq")
    (grad_input,) = run(
        conv_back_kernel, "conv_back", [whole], [grad_conv, near_grad, far_grad, near]
    )
    return (layer_out, convolved, grad_input)


def solution(mesh):
    return jax.shard_map(
        on_device,
        mesh=mesh,
        in_specs=(
            P("seq", "ch"),
            P(None, "ch"),
            P(None, "seq", None, None),
            P(None, "seq"),
            P(None, "ch"),
            P("ch", None),
            P("seq", "ch"),
        ),
        out_specs=(P("seq", "ch"), P("seq", "ch"), P("seq", "ch")),
        check_vma=False,
    )
```

```python
import functools

import jax
import jax.numpy as jnp
from jax import lax
from jax.experimental import pallas as pl
from jax.experimental.pallas import tpu as pltpu
from jax.sharding import PartitionSpec as P

BLOCK = 64
LOCAL = 2
QUARTERS = 4
TILE = 512
SMALL = 8 * 1024 * 1024
LARGE = 20 * 1024 * 1024
ALL = 44 * 1024 * 1024

root_two_pi = 0.7978845608028654

IN_HBM = pl.BlockSpec(memory_space=pltpu.HBM)
IN_VMEM = pl.BlockSpec(memory_space=pltpu.VMEM)
ANYWHERE = pl.BlockSpec(memory_space=pl.ANY)
ACROSS = (((1,), (1,)), ((), ()))
OVER_ROWS = (((0,), (0,)), ((), ()))


def times(weights, value):
    return jnp.dot(weights, value, preferred_element_type=jnp.float32)


def times_transposed(weights, value):
    return lax.dot_general(weights, value, OVER_ROWS, preferred_element_type=jnp.float32)


def neighbours(edges, axis):
    count = lax.axis_size(axis)
    near = lax.ppermute(edges, axis, [(i, i ^ 1) for i in range(count)])
    route = []
    for low in range(1, count - 1, 2):
        route += [(low, low + 1), (low + 1, low)]
    return near, lax.ppermute(edges[:2], axis, route)


def from_flipped(block, axis, mask):
    count = lax.axis_size(axis)
    return lax.ppermute(block, axis, [(i, i ^ mask) for i in range(count)])


def from_offset(block, axis, offset):
    count = lax.axis_size(axis)
    return lax.ppermute(block, axis, [((i + offset) % count, i) for i in range(count)])


def call(kernel, name, outs, arrays, distant=(), scratch=(), order=(), limit=SMALL):
    count = len(distant) + len(arrays)

    def body(*refs):
        kernel(*refs[:count], *refs[count + len(order) :])

    return pl.pallas_call(
        body,
        out_shape=[jax.ShapeDtypeStruct(shape, kind) for shape, kind in outs],
        in_specs=[IN_HBM] * len(distant) + [IN_VMEM] * len(arrays) + [ANYWHERE] * len(order),
        out_specs=[IN_VMEM] * len(outs),
        scratch_shapes=list(scratch),
        compiler_params=pltpu.CompilerParams(vmem_limit_bytes=limit),
        cost_estimate=pl.CostEstimate(flops=0, bytes_accessed=0, transcendentals=0),
        name=name,
    )(*distant, *arrays, *order)


def own_bits():
    seat = lax.axis_index("seq")
    levels = lax.axis_size("seq").bit_length() - 1
    return (seat >> (levels - 2)) & 1, (seat >> (levels - 1)) & 1


def shifted(cells, near, far):
    rows = cells.shape[0]
    even = lax.axis_index("seq") % 2 == 0
    near, far = near.astype(jnp.float32), far.astype(jnp.float32)
    before = jnp.where(even, far[1:2], near[1:2])
    after = jnp.where(even, near[0:1], far[0:1])
    spot = lax.broadcasted_iota(jnp.int32, cells.shape, 0)
    up = jnp.where(spot == 0, before, pltpu.roll(cells, 1, 0))
    down = jnp.where(spot == rows - 1, after, pltpu.roll(cells, rows - 1, 0))
    return up, down


def chosen_blocks(subs):
    early, late = own_bits()
    return [
        sub // 2 * QUARTERS + (early ^ (1 - sub % 2)) * 2 + (late ^ other)
        for sub in subs
        for other in range(2)
    ]


def local_factor(factor, pattern, source, mixing, target, chosen):
    for spot, block in enumerate(chosen):
        pair = mixing[factor, block]
        target[spot] = (
            times(pair[:, :BLOCK], source[block])
            + times(pair[:, BLOCK:], source[pattern[factor, block]])
        ).astype(jnp.bfloat16)


def entry_kernel(units, pattern_far, cells, near, far, mixing, conv_ref, *rest):
    outs, (first, between, pattern, arrival) = rest[:-4], rest[-4:]
    fetch = pltpu.make_async_copy(pattern_far, pattern, arrival)
    fetch.start()
    values = cells[...].astype(jnp.float32)
    scale = near[2:5].astype(jnp.float32)
    up, down = shifted(values, near[...], far[...])
    convolved = (scale[0:1] * up + scale[1:2] * values + scale[2:3] * down).astype(jnp.bfloat16)
    conv_ref[...] = convolved
    first[...] = convolved.reshape(first.shape)
    fetch.wait()
    every = range(first.shape[0])
    refs = (first, between)
    for factor in range(LOCAL - 1):
        local_factor(factor, pattern, refs[factor % 2], mixing, refs[1 - factor % 2], every)
    source = refs[(LOCAL - 1) % 2]
    for unit, out in zip(units, outs):
        local_factor(LOCAL - 1, pattern, source, mixing, out, chosen_blocks(unit))


def plain_kernel(factor, unit, state, mates, mixing, *outs):
    for spot, block in enumerate(chosen_blocks(unit)):
        pair = mixing[factor, block]
        per_out = state.shape[0] // len(outs)
        outs[spot // per_out][spot % per_out] = (
            times(pair[:, :BLOCK], state[spot]) + times(pair[:, BLOCK:], mates[spot])
        ).astype(jnp.bfloat16)


def packed(message, pieces, number):
    across = message.shape[-1] // (2 * BLOCK)
    lanes = pl.ds(number % across * 2 * BLOCK, 2 * BLOCK)
    return message.at[pieces + number // across, :, lanes]


def load_kernel(mixing_far, cells_far, mixing, cells, arrivals):
    fetches = [
        pltpu.make_async_copy(far, near, arrivals.at[i])
        for i, (far, near) in enumerate(((mixing_far, mixing), (cells_far, cells)))
    ]
    for fetch in fetches:
        fetch.start()
    for fetch in fetches:
        fetch.wait()


def pack_kernel(factor, pieces, length, cots, mixing, own, near, across):
    messages = (near, across.at[pl.ds(0, length)], across.at[pl.ds(length, length)])
    my_early, my_late = own_bits()
    for piece in range(pieces):
        base = piece * QUARTERS
        own[piece] = cots[base + my_early * 2 + my_late]
        for flip, message in enumerate(messages, 1):
            early, late = my_early ^ (flip & 1), my_late ^ (flip >> 1)
            message[piece] = cots[base + early * 2 + late]
            for which in range(2):
                number = which * pieces + piece
                if flip == 1:
                    for other in range(2):
                        packed(message, pieces, number * 2 + other)[...] = mixing[
                            factor + which, base + early * 2 + (late ^ other)
                        ]
                else:
                    packed(message, pieces, number)[...] = mixing[
                        factor + which, base + early * 2 + late
                    ]


def forward_kernel(message, out):
    out[...] = message[out.shape[0] :]


def stack_kernel(pieces, *rest):
    quarters, outs = rest[:QUARTERS], rest[QUARTERS:]
    for piece, out in enumerate(outs):
        for quarter, values in enumerate(quarters):
            out[quarter * BLOCK : (quarter + 1) * BLOCK] = values[piece]


def mixing_of(factor, which, pieces, piece, mixing, messages, quarter, other=0):
    if quarter == 0:
        early, late = own_bits()
        return mixing[factor + which, piece * QUARTERS + early * 2 + (late ^ other)]
    number = which * pieces + piece
    if quarter == 1:
        number = number * 2 + other
    return packed(messages[quarter - 1], pieces, number)[...]


def early_kernel(factor, pieces, piece, keep, recv, mixing, message, keep_out, send_out):
    weights = functools.partial(mixing_of, factor, 0, pieces, piece, mixing, [message])
    for other, out in enumerate((keep_out, send_out)):
        mine, theirs = keep[other], recv[other]
        pair = weights(0, other)
        out[0] = (times(pair[:, :BLOCK], mine) + times(pair[:, BLOCK:], theirs)).astype(
            jnp.bfloat16
        )
        pair = weights(1, other)
        out[1] = (times(pair[:, :BLOCK], theirs) + times(pair[:, BLOCK:], mine)).astype(
            jnp.bfloat16
        )


def hold_kernel(received, out):
    out[...] = received[...]


def late_kernel(factor, pieces, piece, keep, recv, mixing, *rest):
    messages, outs = rest[:-2], rest[-2:]
    values = [keep[0], keep[1], recv[0], recv[1]]
    for quarter in range(QUARTERS):
        pair = mixing_of(factor, 1, pieces, piece, mixing, messages, quarter)
        rows = slice(quarter % 2 * BLOCK, (quarter % 2 + 1) * BLOCK)
        outs[quarter // 2][rows] = (
            times(pair[:, :BLOCK], values[quarter]) + times(pair[:, BLOCK:], values[quarter ^ 2])
        ).astype(jnp.bfloat16)


def back_kernel(factor, pieces, piece, cores, cots, total, *rest):
    count = (cores - 1) * 2
    parts, (mixing, message1, message2, message3, *outs) = rest[:count], rest[count:]
    messages = (message1, message2, message3)
    grads = []
    for quarter in range(QUARTERS):
        rows = slice(quarter * BLOCK, (quarter + 1) * BLOCK)
        grad = cots[rows].astype(jnp.float32) + total[rows]
        inner = slice(quarter % 2 * BLOCK, (quarter % 2 + 1) * BLOCK)
        for part in parts[quarter // 2 :: 2]:
            grad = grad + part[inner].astype(jnp.float32)
        grads.append(grad.astype(jnp.bfloat16))
    for which, flip in ((1, 2), (0, 1)):
        both = [
            times_transposed(
                mixing_of(factor, which, pieces, piece, mixing, messages, quarter),
                grads[quarter],
            )
            for quarter in range(QUARTERS)
        ]
        grads = [
            (both[quarter][:BLOCK] + both[quarter ^ flip][BLOCK:]).astype(jnp.bfloat16)
            for quarter in range(QUARTERS)
        ]
    for grad, out in zip(grads, outs):
        out[...] = grad


def regroup_kernel(factor, units, *rest):
    quarters, mixing, outs = rest[:QUARTERS], rest[QUARTERS], rest[QUARTERS + 1 :]
    for number, unit in enumerate(units):
        own, cross = outs[2 * number : 2 * number + 2]
        for spot, block in enumerate(chosen_blocks(unit)):
            grad = quarters[1 - unit[spot // 2] % 2 + spot % 2 * 2][...]
            both = times_transposed(mixing[factor, block], grad)
            own[spot] = both[:BLOCK]
            cross[spot] = both[BLOCK:].astype(jnp.bfloat16)


def plain_back_kernel(factor, unit, mine, theirs, mixing, own, cross):
    for spot, block in enumerate(chosen_blocks(unit)):
        grad = (mine[spot] + theirs[spot].astype(jnp.float32)).astype(jnp.bfloat16)
        both = times_transposed(mixing[factor, block], grad)
        own[spot] = both[:BLOCK]
        cross[spot] = both[BLOCK:].astype(cross.dtype)


def exit_kernel(units, pattern_far, *rest):
    count = len(units)
    mine, theirs = rest[:count], rest[count : 2 * count]
    mixing, out, edges, own, cross, pattern, arrival = rest[2 * count :]
    fetch = pltpu.make_async_copy(pattern_far, pattern, arrival)
    fetch.start()
    blocks = own.shape[0]
    for number, unit in enumerate(units):
        for spot, block in enumerate(chosen_blocks(unit)):
            own[block] = mine[number][spot]
            cross[block] = theirs[number][spot]
    fetch.wait()
    for factor in reversed(range(LOCAL)):
        for block in range(blocks):
            own[block] += cross[pattern[factor, block]]
        for block in range(blocks):
            grad = own[block].astype(jnp.bfloat16)
            if factor == 0:
                out[block * BLOCK : (block + 1) * BLOCK] = grad
                if block == 0:
                    edges[0:1] = grad[:1]
                if block == blocks - 1:
                    edges[1:2] = grad[-1:]
            else:
                both = times_transposed(mixing[factor - 1, block], grad)
                own[block] = both[:BLOCK]
                cross[block] = both[BLOCK:]


def conv_back_kernel(cells, near, far, taps, out, ready):
    ready[...] = jnp.zeros_like(ready)
    values = cells[...].astype(jnp.float32)
    scale = taps[2:5].astype(jnp.float32)
    up, down = shifted(values, near[...], far[...])
    out[...] = (scale[0:1] * down + scale[1:2] * values + scale[2:3] * up).astype(jnp.bfloat16)


def channel_spots(count, chans):
    core = lax.axis_index("ch")
    return [
        pl.ds(pl.multiple_of(lax.rem(core + i, count) * chans, chans), chans)
        for i in range(count)
    ]


def grad_act_kernel(count, *rest):
    cots, (w_out, grad_act, c_all) = rest[:count], rest[count:]
    for spot, cot in zip(channel_spots(count, cots[0].shape[1]), cots):
        c_all[:, spot] = cot[...]
    hidden = w_out.shape[0]
    tile = min(TILE, hidden)
    for start in range(0, hidden, tile):
        grad_act[:, start : start + tile] = lax.dot_general(
            c_all[...], w_out[start : start + tile], ACROSS, preferred_element_type=jnp.float32
        ).astype(grad_act.dtype)


def hidden_kernel(count, *rest):
    mixed, (grad_act, w_in, activation, own) = rest[: 2 * count], rest[2 * count : 2 * count + 4]
    backs, (x_all, back_sum) = rest[2 * count + 4 : -2], rest[-2:]
    rows, chans = mixed[0].shape
    spots = channel_spots(count, chans)
    for i, spot in enumerate(spots):
        x_all[:rows, spot] = mixed[2 * i][...]
        x_all[rows:, spot] = mixed[2 * i + 1][...]
    size = w_in.shape[1]
    tile = min(TILE, size)
    for start in range(0, size, tile):
        tiles = slice(start, start + tile)
        hidden = times(x_all[...], w_in[:, tiles])
        square = hidden * hidden
        tanh_val = jnp.tanh(hidden * (root_two_pi + root_two_pi * 0.044715 * square))
        half = 0.5 + 0.5 * tanh_val
        gelu = hidden * half
        activation[:, tiles] = gelu.astype(jnp.bfloat16)
        slope = 2.0 * root_two_pi + 6.0 * root_two_pi * 0.044715 * square
        derivative = half + gelu * (1.0 - half) * slope
        grad_hidden = (grad_act[:, tiles].astype(jnp.float32) * derivative).astype(jnp.bfloat16)
        back = lax.dot_general(
            grad_hidden, w_in[:, tiles], ACROSS, preferred_element_type=jnp.float32
        )
        if start == 0:
            back_sum[...] = back
        else:
            back_sum[...] += back
    own[...] = back_sum[:, spots[0]]
    for i, spot in enumerate(spots[1:]):
        backs[2 * i][...] = back_sum[:rows, spot].astype(jnp.bfloat16)
        backs[2 * i + 1][...] = back_sum[rows:, spot].astype(jnp.bfloat16)


def out_kernel(count, activation, top, bottom, w_out, own, *others):
    rows, chans = top.shape
    for i, spot in enumerate(channel_spots(count, chans)):
        product = times(activation[...], w_out[:, spot])
        if i == 0:
            own[:rows] = top[...].astype(jnp.float32) + product[:rows]
            own[rows:] = bottom[...].astype(jnp.float32) + product[rows:]
        else:
            cuts = len(others) // (count - 1)
            for cut in range(cuts):
                size = 2 * rows // cuts
                part = product[cut * size : (cut + 1) * size]
                others[(i - 1) * cuts + cut][...] = part.astype(jnp.bfloat16)


def combine_kernel(pieces, counts, *rest):
    owns, parts, outs = rest[:pieces], rest[pieces:-QUARTERS], rest[-QUARTERS:]
    for piece in range(pieces):
        per_piece = counts[piece]
        mine, parts = parts[:per_piece], parts[per_piece:]
        for quarter, out in enumerate(outs):
            total = owns[piece][quarter * BLOCK : (quarter + 1) * BLOCK]
            cuts = total.shape[0] * QUARTERS // mine[0].shape[0]
            start = quarter * BLOCK % mine[0].shape[0]
            for part in mine[quarter * cuts // QUARTERS :: cuts]:
                total = total + part[start : start + BLOCK].astype(jnp.float32)
            out[piece] = total.astype(jnp.bfloat16)


def assemble_kernel(*rest):
    quarters, out = rest[:-1], rest[-1]
    my_early, my_late = own_bits()
    for quarter, values in enumerate(quarters):
        spot = (my_early ^ (quarter & 1)) * 2 + (my_late ^ (quarter >> 1))
        for piece in range(values.shape[0]):
            start = pl.multiple_of((piece * QUARTERS + spot) * BLOCK, BLOCK)
            out[pl.ds(start, BLOCK)] = values[piece]


def on_device(inputs, conv_weight, mixing, pattern, w_in, w_out, cotangent):
    row_count, chan_count = inputs.shape
    blocks = row_count // BLOCK
    pieces = blocks // QUARTERS
    width, hidden = w_in.shape
    cores = lax.axis_size("ch")
    levels = lax.axis_size("seq").bit_length() - 1
    plain = list(range(LOCAL, LOCAL + levels - 2))
    last = LOCAL + levels - 2
    early_bit, late_bit = 1 << (levels - 2), 1 << (levels - 1)
    masks = [0, early_bit, late_bit, early_bit | late_bit]

    def blocks_of(size, kind=jnp.bfloat16):
        return ((size, BLOCK, chan_count), kind)

    half = blocks_of(2)
    whole = ((row_count, chan_count), jnp.bfloat16)
    piece_rows = QUARTERS * BLOCK
    flat = (piece_rows, chan_count)
    block = ((BLOCK, chan_count), jnp.bfloat16)
    half_flat = ((2 * BLOCK, chan_count), jnp.bfloat16)
    flat_piece = (flat, jnp.bfloat16)
    flops = 2 * piece_rows * width * hidden

    latest = []

    def run(kernel, name, outs, arrays, *args, **kwargs):
        results = call(kernel, name, outs, arrays, *args, order=tuple(latest), **kwargs)
        latest[:] = results[-1:]
        return results

    near, far = neighbours(jnp.concatenate([inputs[:1], inputs[-1:], conv_weight]), "seq")
    per_block = chan_count // (2 * BLOCK)
    lengths = [pieces + -(-pieces * 2 * (1 + (flip == 1)) // per_block) for flip in (1, 2, 3)]
    length = lengths[1]
    mixing, cells = run(
        load_kernel,
        "load",
        [(array.shape, array.dtype) for array in (mixing, inputs)],
        [],
        [mixing, inputs],
        [pltpu.SemaphoreType.DMA((2,))],
        limit=ALL,
    )
    units = [(s,) for s in range(2 * pieces)]
    convolved, *states = run(
        functools.partial(entry_kernel, units),
        "conv_and_local_factors",
        [whole] + [blocks_of(2 * len(unit)) for unit in units],
        [cells, near, far, mixing],
        [pattern],
        [pltpu.VMEM((blocks, BLOCK, chan_count), jnp.bfloat16)] * 2
        + [pltpu.SMEM(pattern.shape, jnp.int32), pltpu.SemaphoreType.DMA],
    )
    own_cots, *messages = run(
        functools.partial(pack_kernel, last, pieces, length),
        "pack",
        [((pieces, BLOCK, chan_count), jnp.bfloat16)]
        + [blocks_of(lengths[0]), blocks_of(2 * length)],
        [cotangent.reshape(blocks, BLOCK, chan_count), mixing],
    )
    messages = [from_flipped(m, "seq", mask) for m, mask in zip(messages, masks[1:])]

    def forward():
        (message,) = run(forward_kernel, "forward", [blocks_of(length)], [messages[1]])
        messages.append(from_flipped(message, "seq", early_bit))

    all_cots = []
    halves = {}
    transposed = [None] * pieces
    grad_acts = [None] * pieces
    parts = [None] * pieces
    mixeds = [None] * pieces
    activations = [None] * pieces
    owns = [None] * pieces
    out_owns = [None] * pieces
    out_parts = [None] * pieces

    def stack():
        stacked = run(
            functools.partial(stack_kernel, pieces),
            "stack",
            [flat_piece] * pieces,
            [own_cots, *messages],
        )
        for piece in stacked:
            all_cots.append([piece] + [from_offset(piece, "ch", i) for i in range(1, cores)])

    def grad_act(p):
        (grad_acts[p],) = run(
            functools.partial(grad_act_kernel, cores),
            "grad_act",
            [((piece_rows, hidden), jnp.bfloat16)],
            [*all_cots[p], w_out],
            scratch=[pltpu.VMEM((piece_rows, width), jnp.bfloat16)],
            limit=LARGE,
        )

    def plain_factor(factor, u):
        unit = units[u]
        mates = from_flipped(states[u], "seq", 1 << (factor - LOCAL))
        split = factor == plain[-1] and len(unit) == 2
        results = run(
            functools.partial(plain_kernel, factor, unit),
            "factor",
            [half, half] if split else [blocks_of(2 * len(unit))],
            [states[u], mates, mixing],
        )
        if factor == plain[-1]:
            halves.update(zip(unit, results))
        else:
            states[u] = results[0]

    def early_factor(p):
        send, keep = halves[2 * p], halves[2 * p + 1]
        transposed[p] = run(
            functools.partial(early_kernel, last, pieces, p),
            "early_factor",
            [half, half],
            [keep, from_flipped(send, "seq", early_bit), mixing, messages[0]],
        )

    def arrive(p):
        keep, send = transposed[p]
        (received,) = run(hold_kernel, "hold", [half], [from_flipped(send, "seq", late_bit)])
        transposed[p] = keep, received

    def late_factor(p):
        keep, received = transposed[p]
        if p > 0:
            received = from_flipped(received, "seq", late_bit)
        mixeds[p] = run(
            functools.partial(late_kernel, last, pieces, p),
            "late_factor",
            [half_flat] * 2,
            [keep, received, mixing, *messages],
        )

    def hidden_and_grad(p):
        gathered = [
            from_offset(mixed, "ch", i) if i else mixed for i in range(cores) for mixed in mixeds[p]
        ]
        activations[p], owns[p], *backs = run(
            functools.partial(hidden_kernel, cores),
            "mlp_hidden_and_grad",
            [((piece_rows, hidden), jnp.bfloat16), (flat, jnp.float32)]
            + [half_flat] * ((cores - 1) * 2),
            [*gathered, grad_acts[p], w_in],
            scratch=[
                pltpu.VMEM((piece_rows, width), jnp.bfloat16),
                pltpu.VMEM((piece_rows, width), jnp.float32),
            ],
            limit=LARGE,
        )
        parts[p] = [
            from_offset(back, "ch", cores - 1 - i // 2) for i, back in enumerate(backs)
        ]

    def transposed_back(p):
        quarters = run(
            functools.partial(back_kernel, last, pieces, p, cores),
            "late_and_early_back",
            [block] * QUARTERS,
            [all_cots[p][0], owns[p], *parts[p], mixing, *messages],
        )
        transposed[p] = [
            from_flipped(grad, "seq", mask) if mask else grad
            for grad, mask in zip(quarters, masks)
        ]

    def regroup(p):
        chosen = [u for u, unit in enumerate(back_units) if unit[0] // 2 == p]
        sizes = [2 * len(back_units[u]) for u in chosen]
        results = run(
            functools.partial(regroup_kernel, plain[-1], [back_units[u] for u in chosen]),
            "regroup_and_factor_back",
            [blocks_of(size, kind) for size in sizes for kind in (jnp.float32, jnp.bfloat16)],
            [*transposed[p], mixing],
        )
        for number, u in enumerate(chosen):
            states[u] = results[2 * number : 2 * number + 2]

    def out_product(p):
        cuts = 1 if p + 1 < pieces else 2
        out_owns[p], *others = run(
            functools.partial(out_kernel, cores),
            "mlp_out",
            [(flat, jnp.float32)] + [flat_piece if cuts == 1 else half_flat] * (cuts * (cores - 1)),
            [activations[p], *mixeds[p], w_out],
            limit=LARGE,
        )
        out_parts[p] = [
            from_offset(other, "ch", cores - 1 - i // cuts) for i, other in enumerate(others)
        ]

    def plain_back(factor, u):
        mine, cross = states[u]
        theirs = from_flipped(cross, "seq", 1 << (factor - LOCAL))
        kind = jnp.bfloat16 if factor != plain[0] else jnp.float32
        size = 2 * len(back_units[u])
        states[u] = run(
            functools.partial(plain_back_kernel, factor - 1, back_units[u]),
            "factor_back",
            [blocks_of(size, jnp.float32), blocks_of(size, kind)],
            [mine, theirs, mixing],
        )

    waves = sorted((u + 2 * i, -i, u) for i in range(len(plain)) for u in range(len(units)))
    for _, i, u in waves:
        plain_factor(plain[-i], u)
        if plain[-i] == plain[-1] and u == len(units) - 2:
            arrive(0)
        if plain[-i] == plain[-1] and u == 1:
            early_factor(0)
            forward()
    late_factor(0)
    for p in range(1, pieces):
        early_factor(p)
    stack()
    grad_act(0)
    back_units = [(2 * p, 2 * p + 1) for p in range(pieces - 1)]
    back_units += [(2 * pieces - 1,), (2 * pieces - 2,)]
    states = [None] * len(back_units)
    for p in range(pieces):
        hidden_and_grad(p)
        if p + 1 < pieces:
            grad_act(p + 1)
            out_product(p)
            late_factor(p + 1)
        if p > 0:
            regroup(p - 1)
        if p == pieces - 1:
            out_product(p)
        transposed_back(p)
    early_units = range(pieces - 1)
    late_units = range(pieces - 1, pieces + 1)
    def combine():
        return run(
            functools.partial(combine_kernel, pieces, [len(piece) for piece in out_parts]),
            "combine",
            [((pieces, BLOCK, chan_count), jnp.bfloat16)] * QUARTERS,
            [*out_owns, *[part for piece in out_parts for part in piece]],
        )

    outs = combine()
    regroup(pieces - 1)
    for factor in reversed(plain):
        for u in (*early_units, *late_units):
            plain_back(factor, u)
    arrived = [from_flipped(out, "seq", mask) if mask else out for out, mask in zip(outs, masks)]
    grad_conv, edges = run(
        functools.partial(exit_kernel, back_units),
        "local_factors_back",
        [whole, ((2, chan_count), jnp.bfloat16)],
        [g[0] for g in states] + [g[1] for g in states] + [mixing],
        [pattern],
        [pltpu.VMEM((blocks, BLOCK, chan_count), jnp.float32)] * 2
        + [pltpu.SMEM(pattern.shape, jnp.int32), pltpu.SemaphoreType.DMA],
        limit=LARGE,
    )
    near_grad, far_grad = neighbours(edges, "seq")
    grad_input, _ = run(
        conv_back_kernel,
        "conv_back",
        [whole, ((8, 128), jnp.float32)],
        [grad_conv, near_grad, far_grad, near],
    )
    (layer_out,) = run(assemble_kernel, "assemble", [whole], arrived)
    return (layer_out, convolved, grad_input)


def solution(mesh):
    return jax.shard_map(
        on_device,
        mesh=mesh,
        in_specs=(
            P("seq", "ch"),
            P(None, "ch"),
            P(None, "seq", None, None),
            P(None, "seq"),
            P(None, "ch"),
            P("ch", None),
            P("seq", "ch"),
        ),
        out_specs=(P("seq", "ch"), P("seq", "ch"), P("seq", "ch")),
        check_vma=False,
    )
```

```python
import functools

import jax
import jax.numpy as jnp
from jax import lax
from jax.experimental import pallas as pl
from jax.experimental.pallas import tpu as pltpu
from jax.sharding import PartitionSpec as P

BLOCK = 64
LOCAL = 2
QUARTERS = 4
TILE = 512
SMALL = 8 * 1024 * 1024
LARGE = 20 * 1024 * 1024
ALL = 44 * 1024 * 1024

root_two_pi = 0.7978845608028654

IN_HBM = pl.BlockSpec(memory_space=pltpu.HBM)
IN_VMEM = pl.BlockSpec(memory_space=pltpu.VMEM)
ANYWHERE = pl.BlockSpec(memory_space=pl.ANY)
ACROSS = (((1,), (1,)), ((), ()))
OVER_ROWS = (((0,), (0,)), ((), ()))


def times(weights, value):
    return jnp.dot(weights, value, preferred_element_type=jnp.float32)


def times_transposed(weights, value):
    return lax.dot_general(weights, value, OVER_ROWS, preferred_element_type=jnp.float32)


def neighbours(edges, axis):
    count = lax.axis_size(axis)
    near = lax.ppermute(edges, axis, [(i, i ^ 1) for i in range(count)])
    route = []
    for low in range(1, count - 1, 2):
        route += [(low, low + 1), (low + 1, low)]
    return near, lax.ppermute(edges, axis, route)


def from_flipped(block, axis, mask):
    count = lax.axis_size(axis)
    return lax.ppermute(block, axis, [(i, i ^ mask) for i in range(count)])


def from_offset(block, axis, offset):
    count = lax.axis_size(axis)
    return lax.ppermute(block, axis, [((i + offset) % count, i) for i in range(count)])


def call(kernel, name, outs, arrays, distant=(), scratch=(), order=(), limit=SMALL):
    count = len(distant) + len(arrays)

    def body(*refs):
        kernel(*refs[:count], *refs[count + len(order) :])

    return pl.pallas_call(
        body,
        out_shape=[jax.ShapeDtypeStruct(shape, kind) for shape, kind in outs],
        in_specs=[ANYWHERE] * len(distant) + [IN_VMEM] * len(arrays) + [ANYWHERE] * len(order),
        out_specs=[IN_VMEM] * len(outs),
        scratch_shapes=list(scratch),
        compiler_params=pltpu.CompilerParams(vmem_limit_bytes=limit),
        cost_estimate=pl.CostEstimate(flops=0, bytes_accessed=0, transcendentals=0),
        name=name,
    )(*distant, *arrays, *order)


def own_bits():
    seat = lax.axis_index("seq")
    levels = lax.axis_size("seq").bit_length() - 1
    return (seat >> (levels - 2)) & 1, (seat >> (levels - 1)) & 1


def shifted(cells, near, far):
    rows = cells.shape[0]
    even = lax.axis_index("seq") % 2 == 0
    near, far = near.astype(jnp.float32), far.astype(jnp.float32)
    before = jnp.where(even, far[1:2], near[1:2])
    after = jnp.where(even, near[0:1], far[0:1])
    spot = lax.broadcasted_iota(jnp.int32, cells.shape, 0)
    up = jnp.where(spot == 0, before, pltpu.roll(cells, 1, 0))
    down = jnp.where(spot == rows - 1, after, pltpu.roll(cells, rows - 1, 0))
    return up, down


def chosen_blocks(subs):
    early, late = own_bits()
    return [
        sub // 2 * QUARTERS + (early ^ (1 - sub % 2)) * 2 + (late ^ other)
        for sub in subs
        for other in range(2)
    ]


def local_factor(factor, pattern, source, mixing, target, chosen):
    for spot, block in enumerate(chosen):
        pair = mixing[factor, block]
        target[spot] = (
            times(pair[:, :BLOCK], source[block])
            + times(pair[:, BLOCK:], source[pattern[factor, block]])
        ).astype(jnp.bfloat16)


def entry_kernel(units, pattern_far, cells, far, near, mixing, conv_ref, *rest):
    outs, (first, between, pattern, arrival) = rest[:-4], rest[-4:]
    fetch = pltpu.make_async_copy(pattern_far, pattern, arrival)
    fetch.start()
    values = cells[...].astype(jnp.float32)
    scale = near[2:5].astype(jnp.float32)
    up, down = shifted(values, near[...], far[...])
    convolved = (scale[0:1] * up + scale[1:2] * values + scale[2:3] * down).astype(jnp.bfloat16)
    conv_ref[...] = convolved
    first[...] = convolved.reshape(first.shape)
    fetch.wait()
    every = range(first.shape[0])
    refs = (first, between)
    for factor in range(LOCAL - 1):
        local_factor(factor, pattern, refs[factor % 2], mixing, refs[1 - factor % 2], every)
    source = refs[(LOCAL - 1) % 2]
    for unit, out in zip(units, outs):
        local_factor(LOCAL - 1, pattern, source, mixing, out, chosen_blocks(unit))


def plain_kernel(factor, unit, state, mates, mixing, *outs):
    for spot, block in enumerate(chosen_blocks(unit)):
        pair = mixing[factor, block]
        per_out = state.shape[0] // len(outs)
        outs[spot // per_out][spot % per_out] = (
            times(pair[:, :BLOCK], state[spot]) + times(pair[:, BLOCK:], mates[spot])
        ).astype(jnp.bfloat16)


def packed(message, pieces, number):
    across = message.shape[-1] // (2 * BLOCK)
    lanes = pl.ds(number % across * 2 * BLOCK, 2 * BLOCK)
    return message.at[pieces + number // across, :, lanes]


def load_kernel(mixing_far, cells_far, pattern_far, mixing, cells, pattern, arrivals):
    pairs = ((mixing_far, mixing), (cells_far, cells), (pattern_far, pattern))
    fetches = [
        pltpu.make_async_copy(far, near, arrivals.at[i]) for i, (far, near) in enumerate(pairs)
    ]
    for fetch in fetches:
        fetch.start()
    for fetch in fetches:
        fetch.wait()


def pack_kernel(factor, pieces, length, cots, mixing, own, near, across):
    messages = (near, across.at[pl.ds(0, length)], across.at[pl.ds(length, length)])
    my_early, my_late = own_bits()
    for piece in range(pieces):
        base = piece * QUARTERS
        own[piece] = cots[base + my_early * 2 + my_late]
        for flip, message in enumerate(messages, 1):
            early, late = my_early ^ (flip & 1), my_late ^ (flip >> 1)
            message[piece] = cots[base + early * 2 + late]
            for which in range(2):
                number = which * pieces + piece
                if flip == 1:
                    for other in range(2):
                        packed(message, pieces, number * 2 + other)[...] = mixing[
                            factor + which, base + early * 2 + (late ^ other)
                        ]
                else:
                    packed(message, pieces, number)[...] = mixing[
                        factor + which, base + early * 2 + late
                    ]


def forward_kernel(message, out):
    out[...] = message[out.shape[0] :]


def stack_kernel(pieces, *rest):
    quarters, outs = rest[:QUARTERS], rest[QUARTERS:]
    for piece, out in enumerate(outs):
        for quarter, values in enumerate(quarters):
            out[quarter * BLOCK : (quarter + 1) * BLOCK] = values[piece]


def mixing_of(factor, which, pieces, piece, mixing, messages, quarter, other=0):
    if quarter == 0:
        early, late = own_bits()
        return mixing[factor + which, piece * QUARTERS + early * 2 + (late ^ other)]
    number = which * pieces + piece
    if quarter == 1:
        number = number * 2 + other
    return packed(messages[quarter - 1], pieces, number)[...]


def early_kernel(factor, pieces, piece, keep, recv, mixing, message, keep_out, send_out):
    weights = functools.partial(mixing_of, factor, 0, pieces, piece, mixing, [message])
    for other, out in enumerate((keep_out, send_out)):
        mine, theirs = keep[other], recv[other]
        pair = weights(0, other)
        out[0] = (times(pair[:, :BLOCK], mine) + times(pair[:, BLOCK:], theirs)).astype(
            jnp.bfloat16
        )
        pair = weights(1, other)
        out[1] = (times(pair[:, :BLOCK], theirs) + times(pair[:, BLOCK:], mine)).astype(
            jnp.bfloat16
        )


def hold_kernel(received, out):
    out[...] = received[...]


def late_kernel(factor, pieces, piece, keep, recv, mixing, *rest):
    messages, outs = rest[:-2], rest[-2:]
    values = [keep[0], keep[1], recv[0], recv[1]]
    for quarter in range(QUARTERS):
        pair = mixing_of(factor, 1, pieces, piece, mixing, messages, quarter)
        rows = slice(quarter % 2 * BLOCK, (quarter % 2 + 1) * BLOCK)
        outs[quarter // 2][rows] = (
            times(pair[:, :BLOCK], values[quarter]) + times(pair[:, BLOCK:], values[quarter ^ 2])
        ).astype(jnp.bfloat16)


def back_kernel(factor, pieces, piece, cores, cots, total, *rest):
    count = (cores - 1) * 2
    parts, (mixing, message1, message2, message3, *outs) = rest[:count], rest[count:]
    messages = (message1, message2, message3)
    grads = []
    for quarter in range(QUARTERS):
        rows = slice(quarter * BLOCK, (quarter + 1) * BLOCK)
        grad = cots[rows].astype(jnp.float32) + total[rows]
        inner = slice(quarter % 2 * BLOCK, (quarter % 2 + 1) * BLOCK)
        for part in parts[quarter // 2 :: 2]:
            grad = grad + part[inner].astype(jnp.float32)
        grads.append(grad.astype(jnp.bfloat16))
    for which, flip in ((1, 2), (0, 1)):
        both = [
            times_transposed(
                mixing_of(factor, which, pieces, piece, mixing, messages, quarter),
                grads[quarter],
            )
            for quarter in range(QUARTERS)
        ]
        grads = [
            (both[quarter][:BLOCK] + both[quarter ^ flip][BLOCK:]).astype(jnp.bfloat16)
            for quarter in range(QUARTERS)
        ]
    for grad, out in zip(grads, outs):
        out[...] = grad


def regroup_kernel(factor, units, *rest):
    quarters, mixing, outs = rest[:QUARTERS], rest[QUARTERS], rest[QUARTERS + 1 :]
    for number, unit in enumerate(units):
        own, cross = outs[2 * number : 2 * number + 2]
        for spot, block in enumerate(chosen_blocks(unit)):
            grad = quarters[1 - unit[spot // 2] % 2 + spot % 2 * 2][...]
            both = times_transposed(mixing[factor, block], grad)
            own[spot] = both[:BLOCK]
            cross[spot] = both[BLOCK:].astype(jnp.bfloat16)


def plain_back_kernel(factor, unit, mine, theirs, mixing, own, cross):
    for spot, block in enumerate(chosen_blocks(unit)):
        grad = (mine[spot] + theirs[spot].astype(jnp.float32)).astype(jnp.bfloat16)
        both = times_transposed(mixing[factor, block], grad)
        own[spot] = both[:BLOCK]
        cross[spot] = both[BLOCK:].astype(cross.dtype)


def exit_kernel(units, pattern_far, *rest):
    count = len(units)
    mine, theirs = rest[:count], rest[count : 2 * count]
    mixing, out, edges, own, cross, pattern, arrival = rest[2 * count :]
    fetch = pltpu.make_async_copy(pattern_far, pattern, arrival)
    fetch.start()
    blocks = own.shape[0]
    for number, unit in enumerate(units):
        for spot, block in enumerate(chosen_blocks(unit)):
            own[block] = mine[number][spot]
            cross[block] = theirs[number][spot]
    fetch.wait()
    for factor in reversed(range(LOCAL)):
        for block in range(blocks):
            own[block] += cross[pattern[factor, block]]
        for block in range(blocks):
            grad = own[block].astype(jnp.bfloat16)
            if factor == 0:
                out[block * BLOCK : (block + 1) * BLOCK] = grad
                if block == 0:
                    edges[0:1] = grad[:1]
                if block == blocks - 1:
                    edges[1:2] = grad[-1:]
            else:
                both = times_transposed(mixing[factor - 1, block], grad)
                own[block] = both[:BLOCK]
                cross[block] = both[BLOCK:]


def conv_back_kernel(cells, far, near, taps, out, ready):
    ready[...] = jnp.zeros_like(ready)
    values = cells[...].astype(jnp.float32)
    scale = taps[2:5].astype(jnp.float32)
    up, down = shifted(values, near[...], far[...])
    out[...] = (scale[0:1] * down + scale[1:2] * values + scale[2:3] * up).astype(jnp.bfloat16)


def channel_spots(count, chans):
    core = lax.axis_index("ch")
    return [
        pl.ds(pl.multiple_of(lax.rem(core + i, count) * chans, chans), chans)
        for i in range(count)
    ]


def grad_act_kernel(count, *rest):
    cots, (w_out, grad_act, c_all) = rest[:count], rest[count:]
    for spot, cot in zip(channel_spots(count, cots[0].shape[1]), cots):
        c_all[:, spot] = cot[...]
    hidden = w_out.shape[0]
    tile = min(TILE, hidden)
    for start in range(0, hidden, tile):
        grad_act[:, start : start + tile] = lax.dot_general(
            c_all[...], w_out[start : start + tile], ACROSS, preferred_element_type=jnp.float32
        ).astype(grad_act.dtype)


def hidden_kernel(count, *rest):
    mixed, (grad_act, w_in, activation, own) = rest[: 2 * count], rest[2 * count : 2 * count + 4]
    backs, (x_all, back_sum) = rest[2 * count + 4 : -2], rest[-2:]
    rows, chans = mixed[0].shape
    spots = channel_spots(count, chans)
    for i, spot in enumerate(spots):
        x_all[:rows, spot] = mixed[2 * i][...]
        x_all[rows:, spot] = mixed[2 * i + 1][...]
    size = w_in.shape[1]
    tile = min(TILE, size)
    for start in range(0, size, tile):
        tiles = slice(start, start + tile)
        hidden = times(x_all[...], w_in[:, tiles])
        square = hidden * hidden
        tanh_val = jnp.tanh(hidden * (root_two_pi + root_two_pi * 0.044715 * square))
        half = 0.5 + 0.5 * tanh_val
        gelu = hidden * half
        activation[:, tiles] = gelu.astype(jnp.bfloat16)
        slope = 2.0 * root_two_pi + 6.0 * root_two_pi * 0.044715 * square
        derivative = half + gelu * (1.0 - half) * slope
        grad_hidden = (grad_act[:, tiles].astype(jnp.float32) * derivative).astype(jnp.bfloat16)
        back = lax.dot_general(
            grad_hidden, w_in[:, tiles], ACROSS, preferred_element_type=jnp.float32
        )
        if start == 0:
            back_sum[...] = back
        else:
            back_sum[...] += back
    own[...] = back_sum[:, spots[0]]
    for i, spot in enumerate(spots[1:]):
        backs[2 * i][...] = back_sum[:rows, spot].astype(jnp.bfloat16)
        backs[2 * i + 1][...] = back_sum[rows:, spot].astype(jnp.bfloat16)


def out_kernel(count, activation, top, bottom, w_out, own, *others):
    rows, chans = top.shape
    for i, spot in enumerate(channel_spots(count, chans)):
        product = times(activation[...], w_out[:, spot])
        if i == 0:
            own[:rows] = top[...].astype(jnp.float32) + product[:rows]
            own[rows:] = bottom[...].astype(jnp.float32) + product[rows:]
        else:
            cuts = len(others) // (count - 1)
            for cut in range(cuts):
                size = 2 * rows // cuts
                part = product[cut * size : (cut + 1) * size]
                others[(i - 1) * cuts + cut][...] = part.astype(jnp.bfloat16)


def combine_kernel(pieces, counts, *rest):
    owns, parts, outs = rest[:pieces], rest[pieces:-QUARTERS], rest[-QUARTERS:]
    for piece in range(pieces):
        per_piece = counts[piece]
        mine, parts = parts[:per_piece], parts[per_piece:]
        for quarter, out in enumerate(outs):
            total = owns[piece][quarter * BLOCK : (quarter + 1) * BLOCK]
            cuts = total.shape[0] * QUARTERS // mine[0].shape[0]
            start = quarter * BLOCK % mine[0].shape[0]
            for part in mine[quarter * cuts // QUARTERS :: cuts]:
                total = total + part[start : start + BLOCK].astype(jnp.float32)
            out[piece] = total.astype(jnp.bfloat16)


def assemble_kernel(*rest):
    quarters, out = rest[:-1], rest[-1]
    my_early, my_late = own_bits()
    for quarter, values in enumerate(quarters):
        spot = (my_early ^ (quarter & 1)) * 2 + (my_late ^ (quarter >> 1))
        for piece in range(values.shape[0]):
            start = pl.multiple_of((piece * QUARTERS + spot) * BLOCK, BLOCK)
            out[pl.ds(start, BLOCK)] = values[piece]


def on_device(inputs, conv_weight, mixing, pattern, w_in, w_out, cotangent):
    row_count, chan_count = inputs.shape
    blocks = row_count // BLOCK
    pieces = blocks // QUARTERS
    width, hidden = w_in.shape
    cores = lax.axis_size("ch")
    levels = lax.axis_size("seq").bit_length() - 1
    plain = list(range(LOCAL, LOCAL + levels - 2))
    last = LOCAL + levels - 2
    early_bit, late_bit = 1 << (levels - 2), 1 << (levels - 1)
    masks = [0, early_bit, late_bit, early_bit | late_bit]

    def blocks_of(size, kind=jnp.bfloat16):
        return ((size, BLOCK, chan_count), kind)

    half = blocks_of(2)
    whole = ((row_count, chan_count), jnp.bfloat16)
    piece_rows = QUARTERS * BLOCK
    flat = (piece_rows, chan_count)
    block = ((BLOCK, chan_count), jnp.bfloat16)
    half_flat = ((2 * BLOCK, chan_count), jnp.bfloat16)
    flat_piece = (flat, jnp.bfloat16)
    flops = 2 * piece_rows * width * hidden

    latest = []

    def run(kernel, name, outs, arrays, *args, **kwargs):
        results = call(kernel, name, outs, arrays, *args, order=tuple(latest), **kwargs)
        latest[:] = results[-1:]
        return results

    near, far = neighbours(jnp.concatenate([inputs[:1], inputs[-1:], conv_weight]), "seq")
    per_block = chan_count // (2 * BLOCK)
    lengths = [pieces + -(-pieces * 2 * (1 + (flip == 1)) // per_block) for flip in (1, 2, 3)]
    length = lengths[1]
    mixing, cells, pattern = run(
        load_kernel,
        "load",
        [(array.shape, array.dtype) for array in (mixing, inputs, pattern)],
        [],
        [mixing, inputs, pattern],
        [pltpu.SemaphoreType.DMA((3,))],
        limit=ALL,
    )
    units = [(s,) for s in range(2 * pieces)]
    convolved, *states = run(
        functools.partial(entry_kernel, units),
        "conv_and_local_factors",
        [whole] + [blocks_of(2 * len(unit)) for unit in units],
        [cells, far, near, mixing],
        [pattern],
        [pltpu.VMEM((blocks, BLOCK, chan_count), jnp.bfloat16)] * 2
        + [pltpu.SMEM(pattern.shape, jnp.int32), pltpu.SemaphoreType.DMA],
    )
    own_cots, *messages = run(
        functools.partial(pack_kernel, last, pieces, length),
        "pack",
        [((pieces, BLOCK, chan_count), jnp.bfloat16)]
        + [blocks_of(lengths[0]), blocks_of(2 * length)],
        [cotangent.reshape(blocks, BLOCK, chan_count), mixing],
    )
    messages = [from_flipped(m, "seq", mask) for m, mask in zip(messages, masks[1:])]

    def forward():
        (message,) = run(forward_kernel, "forward", [blocks_of(length)], [messages[1]])
        messages.append(from_flipped(message, "seq", early_bit))

    all_cots = []
    halves = {}
    transposed = [None] * pieces
    grad_acts = [None] * pieces
    parts = [None] * pieces
    mixeds = [None] * pieces
    activations = [None] * pieces
    owns = [None] * pieces
    out_owns = [None] * pieces
    out_parts = [None] * pieces

    def stack():
        stacked = run(
            functools.partial(stack_kernel, pieces),
            "stack",
            [flat_piece] * pieces,
            [own_cots, *messages],
        )
        for piece in stacked:
            all_cots.append([piece] + [from_offset(piece, "ch", i) for i in range(1, cores)])

    def grad_act(p):
        (grad_acts[p],) = run(
            functools.partial(grad_act_kernel, cores),
            "grad_act",
            [((piece_rows, hidden), jnp.bfloat16)],
            [*all_cots[p], w_out],
            scratch=[pltpu.VMEM((piece_rows, width), jnp.bfloat16)],
            limit=LARGE,
        )

    def plain_factor(factor, u):
        unit = units[u]
        mates = from_flipped(states[u], "seq", 1 << (factor - LOCAL))
        split = factor == plain[-1] and len(unit) == 2
        results = run(
            functools.partial(plain_kernel, factor, unit),
            "factor",
            [half, half] if split else [blocks_of(2 * len(unit))],
            [states[u], mates, mixing],
        )
        if factor == plain[-1]:
            halves.update(zip(unit, results))
        else:
            states[u] = results[0]

    def early_factor(p):
        send, keep = halves[2 * p], halves[2 * p + 1]
        transposed[p] = run(
            functools.partial(early_kernel, last, pieces, p),
            "early_factor",
            [half, half],
            [keep, from_flipped(send, "seq", early_bit), mixing, messages[0]],
        )

    def arrive(p):
        keep, send = transposed[p]
        (received,) = run(hold_kernel, "hold", [half], [from_flipped(send, "seq", late_bit)])
        transposed[p] = keep, received

    def late_factor(p):
        keep, received = transposed[p]
        if p > 0:
            received = from_flipped(received, "seq", late_bit)
        mixeds[p] = run(
            functools.partial(late_kernel, last, pieces, p),
            "late_factor",
            [half_flat] * 2,
            [keep, received, mixing, *messages],
        )

    def hidden_and_grad(p):
        gathered = [
            from_offset(mixed, "ch", i) if i else mixed for i in range(cores) for mixed in mixeds[p]
        ]
        activations[p], owns[p], *backs = run(
            functools.partial(hidden_kernel, cores),
            "mlp_hidden_and_grad",
            [((piece_rows, hidden), jnp.bfloat16), (flat, jnp.float32)]
            + [half_flat] * ((cores - 1) * 2),
            [*gathered, grad_acts[p], w_in],
            scratch=[
                pltpu.VMEM((piece_rows, width), jnp.bfloat16),
                pltpu.VMEM((piece_rows, width), jnp.float32),
            ],
            limit=LARGE,
        )
        parts[p] = [
            from_offset(back, "ch", cores - 1 - i // 2) for i, back in enumerate(backs)
        ]

    def transposed_back(p):
        quarters = run(
            functools.partial(back_kernel, last, pieces, p, cores),
            "late_and_early_back",
            [block] * QUARTERS,
            [all_cots[p][0], owns[p], *parts[p], mixing, *messages],
        )
        transposed[p] = [
            from_flipped(grad, "seq", mask) if mask else grad
            for grad, mask in zip(quarters, masks)
        ]

    def regroup(p):
        chosen = [u for u, unit in enumerate(back_units) if unit[0] // 2 == p]
        sizes = [2 * len(back_units[u]) for u in chosen]
        results = run(
            functools.partial(regroup_kernel, plain[-1], [back_units[u] for u in chosen]),
            "regroup_and_factor_back",
            [blocks_of(size, kind) for size in sizes for kind in (jnp.float32, jnp.bfloat16)],
            [*transposed[p], mixing],
        )
        for number, u in enumerate(chosen):
            states[u] = results[2 * number : 2 * number + 2]

    def out_product(p):
        cuts = 1 if p + 1 < pieces else 2
        out_owns[p], *others = run(
            functools.partial(out_kernel, cores),
            "mlp_out",
            [(flat, jnp.float32)] + [flat_piece if cuts == 1 else half_flat] * (cuts * (cores - 1)),
            [activations[p], *mixeds[p], w_out],
            limit=LARGE,
        )
        out_parts[p] = [
            from_offset(other, "ch", cores - 1 - i // cuts) for i, other in enumerate(others)
        ]

    def plain_back(factor, u):
        mine, cross = states[u]
        theirs = from_flipped(cross, "seq", 1 << (factor - LOCAL))
        kind = jnp.bfloat16 if factor != plain[0] else jnp.float32
        size = 2 * len(back_units[u])
        states[u] = run(
            functools.partial(plain_back_kernel, factor - 1, back_units[u]),
            "factor_back",
            [blocks_of(size, jnp.float32), blocks_of(size, kind)],
            [mine, theirs, mixing],
        )

    waves = sorted((u + 2 * i, -i, u) for i in range(len(plain)) for u in range(len(units)))
    for _, i, u in waves:
        plain_factor(plain[-i], u)
        if plain[-i] == plain[-1] and u == len(units) - 2:
            arrive(0)
        if plain[-i] == plain[-1] and u == 1:
            early_factor(0)
            forward()
    late_factor(0)
    for p in range(1, pieces):
        early_factor(p)
    stack()
    grad_act(0)
    back_units = [(2 * p, 2 * p + 1) for p in range(pieces - 1)]
    back_units.append((2 * pieces - 1, 2 * pieces - 2))
    states = [None] * len(back_units)
    for p in range(pieces):
        hidden_and_grad(p)
        if p + 1 < pieces:
            grad_act(p + 1)
            out_product(p)
            late_factor(p + 1)
        if p > 0:
            regroup(p - 1)
        if p == pieces - 1:
            out_product(p)
        transposed_back(p)
    early_units = range(pieces - 1)
    late_units = range(pieces - 1, pieces)
    def combine():
        return run(
            functools.partial(combine_kernel, pieces, [len(piece) for piece in out_parts]),
            "combine",
            [((pieces, BLOCK, chan_count), jnp.bfloat16)] * QUARTERS,
            [*out_owns, *[part for piece in out_parts for part in piece]],
        )

    outs = combine()
    regroup(pieces - 1)
    for factor in reversed(plain):
        for u in (*early_units, *late_units):
            plain_back(factor, u)
    arrived = [from_flipped(out, "seq", mask) if mask else out for out, mask in zip(outs, masks)]
    grad_conv, edges = run(
        functools.partial(exit_kernel, back_units),
        "local_factors_back",
        [whole, ((2, chan_count), jnp.bfloat16)],
        [g[0] for g in states] + [g[1] for g in states] + [mixing],
        [pattern],
        [pltpu.VMEM((blocks, BLOCK, chan_count), jnp.float32)] * 2
        + [pltpu.SMEM(pattern.shape, jnp.int32), pltpu.SemaphoreType.DMA],
        limit=LARGE,
    )
    near_grad, far_grad = neighbours(edges, "seq")
    grad_input, _ = run(
        conv_back_kernel,
        "conv_back",
        [whole, ((8, 128), jnp.float32)],
        [grad_conv, far_grad, near_grad, near],
    )
    (layer_out,) = run(assemble_kernel, "assemble", [whole], arrived)
    return (layer_out, convolved, grad_input)


def solution(mesh):
    return jax.shard_map(
        on_device,
        mesh=mesh,
        in_specs=(
            P("seq", "ch"),
            P(None, "ch"),
            P(None, "seq", None, None),
            P(None, "seq"),
            P(None, "ch"),
            P("ch", None),
            P("seq", "ch"),
        ),
        out_specs=(P("seq", "ch"), P("seq", "ch"), P("seq", "ch")),
        check_vma=False,
    )
```

```python
import functools

import jax
import jax.numpy as jnp
from jax import lax
from jax.experimental import pallas as pl
from jax.experimental.pallas import tpu as pltpu
from jax.sharding import PartitionSpec as P

BLOCK = 64
LOCAL = 2
QUARTERS = 4
TILE = 512
SMALL = 8 * 1024 * 1024
LARGE = 20 * 1024 * 1024
ALL = 44 * 1024 * 1024

root_two_pi = 0.7978845608028654

IN_HBM = pl.BlockSpec(memory_space=pltpu.HBM)
IN_VMEM = pl.BlockSpec(memory_space=pltpu.VMEM)
ANYWHERE = pl.BlockSpec(memory_space=pl.ANY)
ACROSS = (((1,), (1,)), ((), ()))
OVER_ROWS = (((0,), (0,)), ((), ()))


def times(weights, value):
    return jnp.dot(weights, value, preferred_element_type=jnp.float32)


def times_transposed(weights, value):
    return lax.dot_general(weights, value, OVER_ROWS, preferred_element_type=jnp.float32)


def neighbours(edges, axis):
    count = lax.axis_size(axis)
    near = lax.ppermute(edges, axis, [(i, i ^ 1) for i in range(count)])
    route = []
    for low in range(1, count - 1, 2):
        route += [(low, low + 1), (low + 1, low)]
    return near, lax.ppermute(edges, axis, route)


def from_flipped(block, axis, mask):
    count = lax.axis_size(axis)
    return lax.ppermute(block, axis, [(i, i ^ mask) for i in range(count)])


def from_offset(block, axis, offset):
    count = lax.axis_size(axis)
    return lax.ppermute(block, axis, [((i + offset) % count, i) for i in range(count)])


def call(kernel, name, outs, arrays, distant=(), scratch=(), order=(), limit=SMALL):
    count = len(distant) + len(arrays)

    def body(*refs):
        kernel(*refs[:count], *refs[count + len(order) :])

    return pl.pallas_call(
        body,
        out_shape=[jax.ShapeDtypeStruct(shape, kind) for shape, kind in outs],
        in_specs=[ANYWHERE] * len(distant) + [IN_VMEM] * len(arrays) + [ANYWHERE] * len(order),
        out_specs=[IN_VMEM] * len(outs),
        scratch_shapes=list(scratch),
        compiler_params=pltpu.CompilerParams(vmem_limit_bytes=limit),
        cost_estimate=pl.CostEstimate(flops=0, bytes_accessed=0, transcendentals=0),
        name=name,
    )(*distant, *arrays, *order)


def own_bits():
    seat = lax.axis_index("seq")
    levels = lax.axis_size("seq").bit_length() - 1
    return (seat >> (levels - 2)) & 1, (seat >> (levels - 1)) & 1


def shifted(cells, near, far):
    rows = cells.shape[0]
    even = lax.axis_index("seq") % 2 == 0
    near, far = near.astype(jnp.float32), far.astype(jnp.float32)
    before = jnp.where(even, far[1:2], near[1:2])
    after = jnp.where(even, near[0:1], far[0:1])
    spot = lax.broadcasted_iota(jnp.int32, cells.shape, 0)
    up = jnp.where(spot == 0, before, pltpu.roll(cells, 1, 0))
    down = jnp.where(spot == rows - 1, after, pltpu.roll(cells, rows - 1, 0))
    return up, down


def chosen_blocks(subs):
    early, late = own_bits()
    return [
        sub // 2 * QUARTERS + (early ^ (1 - sub % 2)) * 2 + (late ^ other)
        for sub in subs
        for other in range(2)
    ]


def local_factor(factor, pattern, source, mixing, target, chosen):
    for spot, block in enumerate(chosen):
        pair = mixing[factor, block]
        target[spot] = (
            times(pair[:, :BLOCK], source[block])
            + times(pair[:, BLOCK:], source[pattern[factor, block]])
        ).astype(jnp.bfloat16)


def entry_kernel(units, pattern_far, cells, far, near, mixing, conv_ref, *rest):
    outs, (first, between, pattern, arrival) = rest[:-4], rest[-4:]
    fetch = pltpu.make_async_copy(pattern_far, pattern, arrival)
    fetch.start()
    values = cells[...].astype(jnp.float32)
    scale = near[2:5].astype(jnp.float32)
    up, down = shifted(values, near[...], far[...])
    convolved = (scale[0:1] * up + scale[1:2] * values + scale[2:3] * down).astype(jnp.bfloat16)
    conv_ref[...] = convolved
    first[...] = convolved.reshape(first.shape)
    fetch.wait()
    every = range(first.shape[0])
    refs = (first, between)
    for factor in range(LOCAL - 1):
        local_factor(factor, pattern, refs[factor % 2], mixing, refs[1 - factor % 2], every)
    source = refs[(LOCAL - 1) % 2]
    for unit, out in zip(units, outs):
        local_factor(LOCAL - 1, pattern, source, mixing, out, chosen_blocks(unit))


def plain_kernel(factor, unit, state, mates, mixing, *outs):
    for spot, block in enumerate(chosen_blocks(unit)):
        pair = mixing[factor, block]
        per_out = state.shape[0] // len(outs)
        outs[spot // per_out][spot % per_out] = (
            times(pair[:, :BLOCK], state[spot]) + times(pair[:, BLOCK:], mates[spot])
        ).astype(jnp.bfloat16)


def packed(message, pieces, number):
    across = message.shape[-1] // (2 * BLOCK)
    lanes = pl.ds(number % across * 2 * BLOCK, 2 * BLOCK)
    return message.at[pieces + number // across, :, lanes]


def load_kernel(mixing_far, cells_far, pattern_far, mixing, cells, pattern, arrivals):
    pairs = ((mixing_far, mixing), (cells_far, cells), (pattern_far, pattern))
    fetches = [
        pltpu.make_async_copy(far, near, arrivals.at[i]) for i, (far, near) in enumerate(pairs)
    ]
    for fetch in fetches:
        fetch.start()
    for fetch in fetches:
        fetch.wait()


def pack_kernel(factor, pieces, length, cots, mixing, own, near, across):
    messages = (near, across.at[pl.ds(0, length)], across.at[pl.ds(length, length)])
    my_early, my_late = own_bits()
    for piece in range(pieces):
        base = piece * QUARTERS
        own[piece] = cots[base + my_early * 2 + my_late]
        for flip, message in enumerate(messages, 1):
            early, late = my_early ^ (flip & 1), my_late ^ (flip >> 1)
            message[piece] = cots[base + early * 2 + late]
            for which in range(2):
                number = which * pieces + piece
                if flip == 1:
                    for other in range(2):
                        packed(message, pieces, number * 2 + other)[...] = mixing[
                            factor + which, base + early * 2 + (late ^ other)
                        ]
                else:
                    packed(message, pieces, number)[...] = mixing[
                        factor + which, base + early * 2 + late
                    ]


def forward_kernel(message, out):
    out[...] = message[out.shape[0] :]


def stack_kernel(pieces, *rest):
    quarters, outs = rest[:QUARTERS], rest[QUARTERS:]
    for piece, out in enumerate(outs):
        for quarter, values in enumerate(quarters):
            out[quarter * BLOCK : (quarter + 1) * BLOCK] = values[piece]


def mixing_of(factor, which, pieces, piece, mixing, messages, quarter, other=0):
    if quarter == 0:
        early, late = own_bits()
        return mixing[factor + which, piece * QUARTERS + early * 2 + (late ^ other)]
    number = which * pieces + piece
    if quarter == 1:
        number = number * 2 + other
    return packed(messages[quarter - 1], pieces, number)[...]


def early_kernel(factor, pieces, piece, keep, recv, mixing, message, keep_out, send_out):
    weights = functools.partial(mixing_of, factor, 0, pieces, piece, mixing, [message])
    for other, out in enumerate((keep_out, send_out)):
        mine, theirs = keep[other], recv[other]
        pair = weights(0, other)
        out[0] = (times(pair[:, :BLOCK], mine) + times(pair[:, BLOCK:], theirs)).astype(
            jnp.bfloat16
        )
        pair = weights(1, other)
        out[1] = (times(pair[:, :BLOCK], theirs) + times(pair[:, BLOCK:], mine)).astype(
            jnp.bfloat16
        )


def hold_kernel(received, out):
    out[...] = received[...]


def late_kernel(factor, pieces, piece, keep, recv, mixing, *rest):
    messages, outs = rest[:-2], rest[-2:]
    values = [keep[0], keep[1], recv[0], recv[1]]
    for quarter in range(QUARTERS):
        pair = mixing_of(factor, 1, pieces, piece, mixing, messages, quarter)
        rows = slice(quarter % 2 * BLOCK, (quarter % 2 + 1) * BLOCK)
        outs[quarter // 2][rows] = (
            times(pair[:, :BLOCK], values[quarter]) + times(pair[:, BLOCK:], values[quarter ^ 2])
        ).astype(jnp.bfloat16)


def back_kernel(factor, pieces, piece, cores, cots, total, *rest):
    count = (cores - 1) * 2
    parts, (mixing, message1, message2, message3, *outs) = rest[:count], rest[count:]
    messages = (message1, message2, message3)
    grads = []
    for quarter in range(QUARTERS):
        rows = slice(quarter * BLOCK, (quarter + 1) * BLOCK)
        grad = cots[rows].astype(jnp.float32) + total[rows]
        inner = slice(quarter % 2 * BLOCK, (quarter % 2 + 1) * BLOCK)
        for part in parts[quarter // 2 :: 2]:
            grad = grad + part[inner].astype(jnp.float32)
        grads.append(grad.astype(jnp.bfloat16))
    for which, flip in ((1, 2), (0, 1)):
        both = [
            times_transposed(
                mixing_of(factor, which, pieces, piece, mixing, messages, quarter),
                grads[quarter],
            )
            for quarter in range(QUARTERS)
        ]
        grads = [
            (both[quarter][:BLOCK] + both[quarter ^ flip][BLOCK:]).astype(jnp.bfloat16)
            for quarter in range(QUARTERS)
        ]
    for grad, out in zip(grads, outs):
        out[...] = grad


def regroup_kernel(factor, units, *rest):
    quarters, mixing, outs = rest[:QUARTERS], rest[QUARTERS], rest[QUARTERS + 1 :]
    for number, unit in enumerate(units):
        own, cross = outs[2 * number : 2 * number + 2]
        for spot, block in enumerate(chosen_blocks(unit)):
            grad = quarters[1 - unit[spot // 2] % 2 + spot % 2 * 2][...]
            both = times_transposed(mixing[factor, block], grad)
            own[spot] = both[:BLOCK]
            cross[spot] = both[BLOCK:].astype(jnp.bfloat16)


def plain_back_kernel(factor, unit, mine, theirs, mixing, own, cross):
    for spot, block in enumerate(chosen_blocks(unit)):
        grad = (mine[spot] + theirs[spot].astype(jnp.float32)).astype(jnp.bfloat16)
        both = times_transposed(mixing[factor, block], grad)
        own[spot] = both[:BLOCK]
        cross[spot] = both[BLOCK:].astype(cross.dtype)


def exit_kernel(units, pattern_far, *rest):
    count = len(units)
    mine, theirs = rest[:count], rest[count : 2 * count]
    mixing, out, edges, own, cross, pattern, arrival = rest[2 * count :]
    fetch = pltpu.make_async_copy(pattern_far, pattern, arrival)
    fetch.start()
    blocks = own.shape[0]
    for number, unit in enumerate(units):
        for spot, block in enumerate(chosen_blocks(unit)):
            own[block] = mine[number][spot]
            cross[block] = theirs[number][spot]
    fetch.wait()
    for factor in reversed(range(LOCAL)):
        for block in range(blocks):
            own[block] += cross[pattern[factor, block]]
        for block in range(blocks):
            grad = own[block].astype(jnp.bfloat16)
            if factor == 0:
                out[block * BLOCK : (block + 1) * BLOCK] = grad
                if block == 0:
                    edges[0:1] = grad[:1]
                if block == blocks - 1:
                    edges[1:2] = grad[-1:]
            else:
                both = times_transposed(mixing[factor - 1, block], grad)
                own[block] = both[:BLOCK]
                cross[block] = both[BLOCK:]


def conv_back_kernel(cells, far, near, taps, out, ready):
    ready[...] = jnp.zeros_like(ready)
    values = cells[...].astype(jnp.float32)
    scale = taps[2:5].astype(jnp.float32)
    up, down = shifted(values, near[...], far[...])
    out[...] = (scale[0:1] * down + scale[1:2] * values + scale[2:3] * up).astype(jnp.bfloat16)


def channel_spots(count, chans):
    core = lax.axis_index("ch")
    return [
        pl.ds(pl.multiple_of(lax.rem(core + i, count) * chans, chans), chans)
        for i in range(count)
    ]


def grad_act_kernel(count, *rest):
    cots, (w_out, grad_act, c_all) = rest[:count], rest[count:]
    for spot, cot in zip(channel_spots(count, cots[0].shape[1]), cots):
        c_all[:, spot] = cot[...]
    hidden = w_out.shape[0]
    tile = min(TILE, hidden)
    for start in range(0, hidden, tile):
        grad_act[:, start : start + tile] = lax.dot_general(
            c_all[...], w_out[start : start + tile], ACROSS, preferred_element_type=jnp.float32
        ).astype(grad_act.dtype)


def hidden_kernel(count, *rest):
    mixed, (grad_act, w_in, activation, own) = rest[: 2 * count], rest[2 * count : 2 * count + 4]
    backs, (x_all, back_sum) = rest[2 * count + 4 : -2], rest[-2:]
    rows, chans = mixed[0].shape
    spots = channel_spots(count, chans)
    for i, spot in enumerate(spots):
        x_all[:rows, spot] = mixed[2 * i][...]
        x_all[rows:, spot] = mixed[2 * i + 1][...]
    size = w_in.shape[1]
    tile = min(TILE, size)
    every = [slice(start, start + tile) for start in range(0, size, tile)]
    hidden = times(x_all[...], w_in[:, every[0]])
    for number, tiles in enumerate(every):
        following = None
        if number + 1 < len(every):
            following = times(x_all[...], w_in[:, every[number + 1]])
        square = hidden * hidden
        tanh_val = jnp.tanh(hidden * (root_two_pi + root_two_pi * 0.044715 * square))
        half = 0.5 + 0.5 * tanh_val
        gelu = hidden * half
        activation[:, tiles] = gelu.astype(jnp.bfloat16)
        slope = 2.0 * root_two_pi + 6.0 * root_two_pi * 0.044715 * square
        derivative = half + gelu * (1.0 - half) * slope
        grad_hidden = (grad_act[:, tiles].astype(jnp.float32) * derivative).astype(jnp.bfloat16)
        back = lax.dot_general(
            grad_hidden, w_in[:, tiles], ACROSS, preferred_element_type=jnp.float32
        )
        if number == 0:
            back_sum[...] = back
        else:
            back_sum[...] += back
        hidden = following
    own[...] = back_sum[:, spots[0]]
    for i, spot in enumerate(spots[1:]):
        backs[2 * i][...] = back_sum[:rows, spot].astype(jnp.bfloat16)
        backs[2 * i + 1][...] = back_sum[rows:, spot].astype(jnp.bfloat16)


def out_kernel(count, activation, top, bottom, w_out, own, *others):
    rows, chans = top.shape
    for i, spot in enumerate(channel_spots(count, chans)):
        product = times(activation[...], w_out[:, spot])
        if i == 0:
            own[:rows] = top[...].astype(jnp.float32) + product[:rows]
            own[rows:] = bottom[...].astype(jnp.float32) + product[rows:]
        else:
            cuts = len(others) // (count - 1)
            for cut in range(cuts):
                size = 2 * rows // cuts
                part = product[cut * size : (cut + 1) * size]
                others[(i - 1) * cuts + cut][...] = part.astype(jnp.bfloat16)


def combine_kernel(pieces, counts, *rest):
    owns, parts, outs = rest[:pieces], rest[pieces:-QUARTERS], rest[-QUARTERS:]
    for piece in range(pieces):
        per_piece = counts[piece]
        mine, parts = parts[:per_piece], parts[per_piece:]
        for quarter, out in enumerate(outs):
            total = owns[piece][quarter * BLOCK : (quarter + 1) * BLOCK]
            cuts = total.shape[0] * QUARTERS // mine[0].shape[0]
            start = quarter * BLOCK % mine[0].shape[0]
            for part in mine[quarter * cuts // QUARTERS :: cuts]:
                total = total + part[start : start + BLOCK].astype(jnp.float32)
            out[piece] = total.astype(jnp.bfloat16)


def assemble_kernel(*rest):
    quarters, out = rest[:-1], rest[-1]
    my_early, my_late = own_bits()
    for quarter, values in enumerate(quarters):
        spot = (my_early ^ (quarter & 1)) * 2 + (my_late ^ (quarter >> 1))
        for piece in range(values.shape[0]):
            start = pl.multiple_of((piece * QUARTERS + spot) * BLOCK, BLOCK)
            out[pl.ds(start, BLOCK)] = values[piece]


def on_device(inputs, conv_weight, mixing, pattern, w_in, w_out, cotangent):
    row_count, chan_count = inputs.shape
    blocks = row_count // BLOCK
    pieces = blocks // QUARTERS
    width, hidden = w_in.shape
    cores = lax.axis_size("ch")
    levels = lax.axis_size("seq").bit_length() - 1
    plain = list(range(LOCAL, LOCAL + levels - 2))
    last = LOCAL + levels - 2
    early_bit, late_bit = 1 << (levels - 2), 1 << (levels - 1)
    masks = [0, early_bit, late_bit, early_bit | late_bit]

    def blocks_of(size, kind=jnp.bfloat16):
        return ((size, BLOCK, chan_count), kind)

    half = blocks_of(2)
    whole = ((row_count, chan_count), jnp.bfloat16)
    piece_rows = QUARTERS * BLOCK
    flat = (piece_rows, chan_count)
    block = ((BLOCK, chan_count), jnp.bfloat16)
    half_flat = ((2 * BLOCK, chan_count), jnp.bfloat16)
    flat_piece = (flat, jnp.bfloat16)
    flops = 2 * piece_rows * width * hidden

    latest = []

    def run(kernel, name, outs, arrays, *args, **kwargs):
        results = call(kernel, name, outs, arrays, *args, order=tuple(latest), **kwargs)
        latest[:] = results[-1:]
        return results

    near, far = neighbours(jnp.concatenate([inputs[:1], inputs[-1:], conv_weight]), "seq")
    per_block = chan_count // (2 * BLOCK)
    lengths = [pieces + -(-pieces * 2 * (1 + (flip == 1)) // per_block) for flip in (1, 2, 3)]
    length = lengths[1]
    mixing, cells, pattern = run(
        load_kernel,
        "load",
        [(array.shape, array.dtype) for array in (mixing, inputs, pattern)],
        [],
        [mixing, inputs, pattern],
        [pltpu.SemaphoreType.DMA((3,))],
        limit=ALL,
    )
    units = [(s,) for s in range(2 * pieces)]
    convolved, *states = run(
        functools.partial(entry_kernel, units),
        "conv_and_local_factors",
        [whole] + [blocks_of(2 * len(unit)) for unit in units],
        [cells, far, near, mixing],
        [pattern],
        [pltpu.VMEM((blocks, BLOCK, chan_count), jnp.bfloat16)] * 2
        + [pltpu.SMEM(pattern.shape, jnp.int32), pltpu.SemaphoreType.DMA],
    )
    own_cots, *messages = run(
        functools.partial(pack_kernel, last, pieces, length),
        "pack",
        [((pieces, BLOCK, chan_count), jnp.bfloat16)]
        + [blocks_of(lengths[0]), blocks_of(2 * length)],
        [cotangent.reshape(blocks, BLOCK, chan_count), mixing],
    )
    messages = [from_flipped(m, "seq", mask) for m, mask in zip(messages, masks[1:])]

    def forward():
        (message,) = run(forward_kernel, "forward", [blocks_of(length)], [messages[1]])
        messages.append(from_flipped(message, "seq", early_bit))

    all_cots = []
    halves = {}
    transposed = [None] * pieces
    grad_acts = [None] * pieces
    parts = [None] * pieces
    mixeds = [None] * pieces
    activations = [None] * pieces
    owns = [None] * pieces
    out_owns = [None] * pieces
    out_parts = [None] * pieces

    def stack():
        stacked = run(
            functools.partial(stack_kernel, pieces),
            "stack",
            [flat_piece] * pieces,
            [own_cots, *messages],
        )
        for piece in stacked:
            all_cots.append([piece] + [from_offset(piece, "ch", i) for i in range(1, cores)])

    def grad_act(p):
        (grad_acts[p],) = run(
            functools.partial(grad_act_kernel, cores),
            "grad_act",
            [((piece_rows, hidden), jnp.bfloat16)],
            [*all_cots[p], w_out],
            scratch=[pltpu.VMEM((piece_rows, width), jnp.bfloat16)],
            limit=LARGE,
        )

    def plain_factor(factor, u):
        unit = units[u]
        mates = from_flipped(states[u], "seq", 1 << (factor - LOCAL))
        split = factor == plain[-1] and len(unit) == 2
        results = run(
            functools.partial(plain_kernel, factor, unit),
            "factor",
            [half, half] if split else [blocks_of(2 * len(unit))],
            [states[u], mates, mixing],
        )
        if factor == plain[-1]:
            halves.update(zip(unit, results))
        else:
            states[u] = results[0]

    def early_factor(p):
        send, keep = halves[2 * p], halves[2 * p + 1]
        transposed[p] = run(
            functools.partial(early_kernel, last, pieces, p),
            "early_factor",
            [half, half],
            [keep, from_flipped(send, "seq", early_bit), mixing, messages[0]],
        )

    def arrive(p):
        keep, send = transposed[p]
        (received,) = run(hold_kernel, "hold", [half], [from_flipped(send, "seq", late_bit)])
        transposed[p] = keep, received

    def late_factor(p):
        keep, received = transposed[p]
        if p > 0:
            received = from_flipped(received, "seq", late_bit)
        mixeds[p] = run(
            functools.partial(late_kernel, last, pieces, p),
            "late_factor",
            [half_flat] * 2,
            [keep, received, mixing, *messages],
        )

    def hidden_and_grad(p):
        gathered = [
            from_offset(mixed, "ch", i) if i else mixed for i in range(cores) for mixed in mixeds[p]
        ]
        activations[p], owns[p], *backs = run(
            functools.partial(hidden_kernel, cores),
            "mlp_hidden_and_grad",
            [((piece_rows, hidden), jnp.bfloat16), (flat, jnp.float32)]
            + [half_flat] * ((cores - 1) * 2),
            [*gathered, grad_acts[p], w_in],
            scratch=[
                pltpu.VMEM((piece_rows, width), jnp.bfloat16),
                pltpu.VMEM((piece_rows, width), jnp.float32),
            ],
            limit=LARGE,
        )
        parts[p] = [
            from_offset(back, "ch", cores - 1 - i // 2) for i, back in enumerate(backs)
        ]

    def transposed_back(p):
        quarters = run(
            functools.partial(back_kernel, last, pieces, p, cores),
            "late_and_early_back",
            [block] * QUARTERS,
            [all_cots[p][0], owns[p], *parts[p], mixing, *messages],
        )
        transposed[p] = [
            from_flipped(grad, "seq", mask) if mask else grad
            for grad, mask in zip(quarters, masks)
        ]

    def regroup(p):
        chosen = [u for u, unit in enumerate(back_units) if unit[0] // 2 == p]
        sizes = [2 * len(back_units[u]) for u in chosen]
        results = run(
            functools.partial(regroup_kernel, plain[-1], [back_units[u] for u in chosen]),
            "regroup_and_factor_back",
            [blocks_of(size, kind) for size in sizes for kind in (jnp.float32, jnp.bfloat16)],
            [*transposed[p], mixing],
        )
        for number, u in enumerate(chosen):
            states[u] = results[2 * number : 2 * number + 2]

    def out_product(p):
        cuts = 1 if p + 1 < pieces else 2
        out_owns[p], *others = run(
            functools.partial(out_kernel, cores),
            "mlp_out",
            [(flat, jnp.float32)] + [flat_piece if cuts == 1 else half_flat] * (cuts * (cores - 1)),
            [activations[p], *mixeds[p], w_out],
            limit=LARGE,
        )
        out_parts[p] = [
            from_offset(other, "ch", cores - 1 - i // cuts) for i, other in enumerate(others)
        ]

    def plain_back(factor, u):
        mine, cross = states[u]
        theirs = from_flipped(cross, "seq", 1 << (factor - LOCAL))
        kind = jnp.bfloat16 if factor != plain[0] else jnp.float32
        size = 2 * len(back_units[u])
        states[u] = run(
            functools.partial(plain_back_kernel, factor - 1, back_units[u]),
            "factor_back",
            [blocks_of(size, jnp.float32), blocks_of(size, kind)],
            [mine, theirs, mixing],
        )

    waves = sorted((u + 2 * i, -i, u) for i in range(len(plain)) for u in range(len(units)))
    for _, i, u in waves:
        plain_factor(plain[-i], u)
        if plain[-i] == plain[-1] and u == len(units) - 2:
            arrive(0)
        if plain[-i] == plain[-1] and u == 1:
            early_factor(0)
            forward()
    late_factor(0)
    for p in range(1, pieces):
        early_factor(p)
    stack()
    grad_act(0)
    back_units = [(2 * p, 2 * p + 1) for p in range(pieces - 1)]
    back_units.append((2 * pieces - 1, 2 * pieces - 2))
    states = [None] * len(back_units)
    for p in range(pieces):
        hidden_and_grad(p)
        if p + 1 < pieces:
            grad_act(p + 1)
            out_product(p)
            late_factor(p + 1)
        if p > 0:
            regroup(p - 1)
        if p == pieces - 1:
            out_product(p)
        transposed_back(p)
    early_units = range(pieces - 1)
    late_units = range(pieces - 1, pieces)
    def combine():
        return run(
            functools.partial(combine_kernel, pieces, [len(piece) for piece in out_parts]),
            "combine",
            [((pieces, BLOCK, chan_count), jnp.bfloat16)] * QUARTERS,
            [*out_owns, *[part for piece in out_parts for part in piece]],
        )

    outs = combine()
    regroup(pieces - 1)
    for factor in reversed(plain):
        for u in (*early_units, *late_units):
            plain_back(factor, u)
    arrived = [from_flipped(out, "seq", mask) if mask else out for out, mask in zip(outs, masks)]
    grad_conv, edges = run(
        functools.partial(exit_kernel, back_units),
        "local_factors_back",
        [whole, ((2, chan_count), jnp.bfloat16)],
        [g[0] for g in states] + [g[1] for g in states] + [mixing],
        [pattern],
        [pltpu.VMEM((blocks, BLOCK, chan_count), jnp.float32)] * 2
        + [pltpu.SMEM(pattern.shape, jnp.int32), pltpu.SemaphoreType.DMA],
        limit=LARGE,
    )
    near_grad, far_grad = neighbours(edges, "seq")
    grad_input, _ = run(
        conv_back_kernel,
        "conv_back",
        [whole, ((8, 128), jnp.float32)],
        [grad_conv, far_grad, near_grad, near],
    )
    (layer_out,) = run(assemble_kernel, "assemble", [whole], arrived)
    return (layer_out, convolved, grad_input)


def solution(mesh):
    return jax.shard_map(
        on_device,
        mesh=mesh,
        in_specs=(
            P("seq", "ch"),
            P(None, "ch"),
            P(None, "seq", None, None),
            P(None, "seq"),
            P(None, "ch"),
            P("ch", None),
            P("seq", "ch"),
        ),
        out_specs=(P("seq", "ch"), P("seq", "ch"), P("seq", "ch")),
        check_vma=False,
    )
```

```python
import functools

import jax
import jax.numpy as jnp
from jax import lax
from jax.experimental import pallas as pl
from jax.experimental.pallas import tpu as pltpu
from jax.sharding import PartitionSpec as P

BLOCK = 64
LOCAL = 2
QUARTERS = 4
TILE = 512
SMALL = 8 * 1024 * 1024
LARGE = 20 * 1024 * 1024
ALL = 44 * 1024 * 1024

root_two_pi = 0.7978845608028654

IN_HBM = pl.BlockSpec(memory_space=pltpu.HBM)
IN_VMEM = pl.BlockSpec(memory_space=pltpu.VMEM)
ANYWHERE = pl.BlockSpec(memory_space=pl.ANY)
ACROSS = (((1,), (1,)), ((), ()))
OVER_ROWS = (((0,), (0,)), ((), ()))


def times(weights, value):
    return jnp.dot(weights, value, preferred_element_type=jnp.float32)


def times_transposed(weights, value):
    return lax.dot_general(weights, value, OVER_ROWS, preferred_element_type=jnp.float32)


def neighbours(edges, axis):
    count = lax.axis_size(axis)
    near = lax.ppermute(edges, axis, [(i, i ^ 1) for i in range(count)])
    route = []
    for low in range(1, count - 1, 2):
        route += [(low, low + 1), (low + 1, low)]
    return near, lax.ppermute(edges, axis, route)


def from_flipped(block, axis, mask):
    count = lax.axis_size(axis)
    return lax.ppermute(block, axis, [(i, i ^ mask) for i in range(count)])


def from_offset(block, axis, offset):
    count = lax.axis_size(axis)
    return lax.ppermute(block, axis, [((i + offset) % count, i) for i in range(count)])


def call(kernel, name, outs, arrays, distant=(), scratch=(), order=(), limit=SMALL):
    count = len(distant) + len(arrays)

    def body(*refs):
        kernel(*refs[:count], *refs[count + len(order) :])

    return pl.pallas_call(
        body,
        out_shape=[jax.ShapeDtypeStruct(shape, kind) for shape, kind in outs],
        in_specs=[ANYWHERE] * len(distant) + [IN_VMEM] * len(arrays) + [ANYWHERE] * len(order),
        out_specs=[IN_VMEM] * len(outs),
        scratch_shapes=list(scratch),
        compiler_params=pltpu.CompilerParams(vmem_limit_bytes=limit),
        cost_estimate=pl.CostEstimate(flops=0, bytes_accessed=0, transcendentals=0),
        name=name,
    )(*distant, *arrays, *order)


def own_bits():
    seat = lax.axis_index("seq")
    levels = lax.axis_size("seq").bit_length() - 1
    return (seat >> (levels - 2)) & 1, (seat >> (levels - 1)) & 1


def shifted(cells, near, far):
    rows = cells.shape[0]
    even = lax.axis_index("seq") % 2 == 0
    near, far = near.astype(jnp.float32), far.astype(jnp.float32)
    before = jnp.where(even, far[1:2], near[1:2])
    after = jnp.where(even, near[0:1], far[0:1])
    spot = lax.broadcasted_iota(jnp.int32, cells.shape, 0)
    up = jnp.where(spot == 0, before, pltpu.roll(cells, 1, 0))
    down = jnp.where(spot == rows - 1, after, pltpu.roll(cells, rows - 1, 0))
    return up, down


def chosen_blocks(subs):
    early, late = own_bits()
    return [
        sub // 2 * QUARTERS + (early ^ (1 - sub % 2)) * 2 + (late ^ other)
        for sub in subs
        for other in range(2)
    ]


def local_factor(factor, pattern, source, mixing, target, chosen):
    for spot, block in enumerate(chosen):
        pair = mixing[factor, block]
        target[spot] = (
            times(pair[:, :BLOCK], source[block])
            + times(pair[:, BLOCK:], source[pattern[factor, block]])
        ).astype(jnp.bfloat16)


def entry_kernel(units, pattern_far, cells, far, near, mixing, conv_ref, *rest):
    outs, (first, between, pattern, arrival) = rest[:-4], rest[-4:]
    fetch = pltpu.make_async_copy(pattern_far, pattern, arrival)
    fetch.start()
    values = cells[...].astype(jnp.float32)
    scale = near[2:5].astype(jnp.float32)
    up, down = shifted(values, near[...], far[...])
    convolved = (scale[0:1] * up + scale[1:2] * values + scale[2:3] * down).astype(jnp.bfloat16)
    conv_ref[...] = convolved
    first[...] = convolved.reshape(first.shape)
    fetch.wait()
    every = range(first.shape[0])
    refs = (first, between)
    for factor in range(LOCAL - 1):
        local_factor(factor, pattern, refs[factor % 2], mixing, refs[1 - factor % 2], every)
    source = refs[(LOCAL - 1) % 2]
    for unit, out in zip(units, outs):
        local_factor(LOCAL - 1, pattern, source, mixing, out, chosen_blocks(unit))


def plain_kernel(factor, unit, state, mates, mixing, *outs):
    for spot, block in enumerate(chosen_blocks(unit)):
        pair = mixing[factor, block]
        per_out = state.shape[0] // len(outs)
        outs[spot // per_out][spot % per_out] = (
            times(pair[:, :BLOCK], state[spot]) + times(pair[:, BLOCK:], mates[spot])
        ).astype(jnp.bfloat16)


def packed(message, pieces, number):
    across = message.shape[-1] // (2 * BLOCK)
    lanes = pl.ds(number % across * 2 * BLOCK, 2 * BLOCK)
    return message.at[pieces + number // across, :, lanes]


def load_kernel(mixing_far, cells_far, pattern_far, mixing, cells, pattern, arrivals):
    pairs = ((mixing_far, mixing), (cells_far, cells), (pattern_far, pattern))
    fetches = [
        pltpu.make_async_copy(far, near, arrivals.at[i]) for i, (far, near) in enumerate(pairs)
    ]
    for fetch in fetches:
        fetch.start()
    for fetch in fetches:
        fetch.wait()


def pack_kernel(factor, pieces, length, cots, mixing, own, near, across):
    messages = (near, across.at[pl.ds(0, length)], across.at[pl.ds(length, length)])
    my_early, my_late = own_bits()
    for piece in range(pieces):
        base = piece * QUARTERS
        own[piece] = cots[base + my_early * 2 + my_late]
        for flip, message in enumerate(messages, 1):
            early, late = my_early ^ (flip & 1), my_late ^ (flip >> 1)
            message[piece] = cots[base + early * 2 + late]
            for which in range(2):
                number = which * pieces + piece
                if flip == 1:
                    for other in range(2):
                        packed(message, pieces, number * 2 + other)[...] = mixing[
                            factor + which, base + early * 2 + (late ^ other)
                        ]
                else:
                    packed(message, pieces, number)[...] = mixing[
                        factor + which, base + early * 2 + late
                    ]


def forward_kernel(message, out):
    out[...] = message[out.shape[0] :]


def stack_kernel(pieces, *rest):
    quarters, outs = rest[:QUARTERS], rest[QUARTERS:]
    for piece, out in enumerate(outs):
        for quarter, values in enumerate(quarters):
            out[quarter * BLOCK : (quarter + 1) * BLOCK] = values[piece]


def mixing_of(factor, which, pieces, piece, mixing, messages, quarter, other=0):
    if quarter == 0:
        early, late = own_bits()
        return mixing[factor + which, piece * QUARTERS + early * 2 + (late ^ other)]
    number = which * pieces + piece
    if quarter == 1:
        number = number * 2 + other
    return packed(messages[quarter - 1], pieces, number)[...]


def early_kernel(factor, pieces, piece, keep, recv, mixing, message, keep_out, send_out):
    weights = functools.partial(mixing_of, factor, 0, pieces, piece, mixing, [message])
    for other, out in enumerate((keep_out, send_out)):
        mine, theirs = keep[other], recv[other]
        pair = weights(0, other)
        out[0] = (times(pair[:, :BLOCK], mine) + times(pair[:, BLOCK:], theirs)).astype(
            jnp.bfloat16
        )
        pair = weights(1, other)
        out[1] = (times(pair[:, :BLOCK], theirs) + times(pair[:, BLOCK:], mine)).astype(
            jnp.bfloat16
        )


def hold_kernel(received, out):
    out[...] = received[...]


def late_kernel(factor, pieces, piece, keep, recv, mixing, *rest):
    messages, outs = rest[:-2], rest[-2:]
    values = [keep[0], keep[1], recv[0], recv[1]]
    for quarter in range(QUARTERS):
        pair = mixing_of(factor, 1, pieces, piece, mixing, messages, quarter)
        rows = slice(quarter % 2 * BLOCK, (quarter % 2 + 1) * BLOCK)
        outs[quarter // 2][rows] = (
            times(pair[:, :BLOCK], values[quarter]) + times(pair[:, BLOCK:], values[quarter ^ 2])
        ).astype(jnp.bfloat16)


def back_kernel(factor, pieces, piece, cores, cots, total, *rest):
    count = (cores - 1) * 2
    parts, (mixing, message1, message2, message3, *outs) = rest[:count], rest[count:]
    messages = (message1, message2, message3)
    grads = []
    for quarter in range(QUARTERS):
        rows = slice(quarter * BLOCK, (quarter + 1) * BLOCK)
        grad = cots[rows].astype(jnp.float32) + total[rows]
        inner = slice(quarter % 2 * BLOCK, (quarter % 2 + 1) * BLOCK)
        for part in parts[quarter // 2 :: 2]:
            grad = grad + part[inner].astype(jnp.float32)
        grads.append(grad.astype(jnp.bfloat16))
    for which, flip in ((1, 2), (0, 1)):
        both = [
            times_transposed(
                mixing_of(factor, which, pieces, piece, mixing, messages, quarter),
                grads[quarter],
            )
            for quarter in range(QUARTERS)
        ]
        grads = [
            (both[quarter][:BLOCK] + both[quarter ^ flip][BLOCK:]).astype(jnp.bfloat16)
            for quarter in range(QUARTERS)
        ]
    for grad, out in zip(grads, outs):
        out[...] = grad


def regroup_kernel(factor, units, *rest):
    quarters, mixing, outs = rest[:QUARTERS], rest[QUARTERS], rest[QUARTERS + 1 :]
    for number, unit in enumerate(units):
        own, cross = outs[2 * number : 2 * number + 2]
        for spot, block in enumerate(chosen_blocks(unit)):
            grad = quarters[1 - unit[spot // 2] % 2 + spot % 2 * 2][...]
            both = times_transposed(mixing[factor, block], grad)
            own[spot] = both[:BLOCK]
            cross[spot] = both[BLOCK:].astype(jnp.bfloat16)


def plain_back_kernel(factor, unit, mine, theirs, mixing, own, cross):
    for spot, block in enumerate(chosen_blocks(unit)):
        grad = (mine[spot] + theirs[spot].astype(jnp.float32)).astype(jnp.bfloat16)
        both = times_transposed(mixing[factor, block], grad)
        own[spot] = both[:BLOCK]
        cross[spot] = both[BLOCK:].astype(cross.dtype)


def exit_kernel(units, pattern_far, *rest):
    count = len(units)
    mine, theirs = rest[:count], rest[count : 2 * count]
    mixing, out, edges, own, cross, pattern, arrival = rest[2 * count :]
    fetch = pltpu.make_async_copy(pattern_far, pattern, arrival)
    fetch.start()
    blocks = own.shape[0]
    for number, unit in enumerate(units):
        for spot, block in enumerate(chosen_blocks(unit)):
            own[block] = mine[number][spot]
            cross[block] = theirs[number][spot]
    fetch.wait()
    for factor in reversed(range(LOCAL)):
        for block in range(blocks):
            own[block] += cross[pattern[factor, block]]
        for block in range(blocks):
            grad = own[block].astype(jnp.bfloat16)
            if factor == 0:
                out[block * BLOCK : (block + 1) * BLOCK] = grad
                if block == 0:
                    edges[0:1] = grad[:1]
                if block == blocks - 1:
                    edges[1:2] = grad[-1:]
            else:
                both = times_transposed(mixing[factor - 1, block], grad)
                own[block] = both[:BLOCK]
                cross[block] = both[BLOCK:]


def conv_back_kernel(cells, far, near, taps, out, ready):
    ready[...] = jnp.zeros_like(ready)
    values = cells[...].astype(jnp.float32)
    scale = taps[2:5].astype(jnp.float32)
    up, down = shifted(values, near[...], far[...])
    out[...] = (scale[0:1] * down + scale[1:2] * values + scale[2:3] * up).astype(jnp.bfloat16)


def channel_spots(count, chans):
    core = lax.axis_index("ch")
    return [
        pl.ds(pl.multiple_of(lax.rem(core + i, count) * chans, chans), chans)
        for i in range(count)
    ]


def grad_act_kernel(count, *rest):
    cots, (w_out, grad_act, c_all) = rest[:count], rest[count:]
    for spot, cot in zip(channel_spots(count, cots[0].shape[1]), cots):
        c_all[:, spot] = cot[...]
    hidden = w_out.shape[0]
    tile = min(TILE, hidden)
    for start in range(0, hidden, tile):
        grad_act[:, start : start + tile] = lax.dot_general(
            c_all[...], w_out[start : start + tile], ACROSS, preferred_element_type=jnp.float32
        ).astype(grad_act.dtype)


def hidden_kernel(count, *rest):
    mixed, (grad_act, w_in, activation, own) = rest[: 2 * count], rest[2 * count : 2 * count + 4]
    backs, (x_all, back_sum) = rest[2 * count + 4 : -2], rest[-2:]
    rows, chans = mixed[0].shape
    spots = channel_spots(count, chans)
    for i, spot in enumerate(spots):
        x_all[:rows, spot] = mixed[2 * i][...]
        x_all[rows:, spot] = mixed[2 * i + 1][...]
    size = w_in.shape[1]
    tile = min(TILE, size)
    every = [slice(start, start + tile) for start in range(0, size, tile)]
    hidden = times(x_all[...], w_in[:, every[0]])
    for number, tiles in enumerate(every):
        following = None
        if number + 1 < len(every):
            following = times(x_all[...], w_in[:, every[number + 1]])
        square = hidden * hidden
        tanh_val = jnp.tanh(hidden * (root_two_pi + root_two_pi * 0.044715 * square))
        half = 0.5 + 0.5 * tanh_val
        gelu = hidden * half
        activation[:, tiles] = gelu.astype(jnp.bfloat16)
        slope = 2.0 * root_two_pi + 6.0 * root_two_pi * 0.044715 * square
        derivative = half + gelu * (1.0 - half) * slope
        grad_hidden = (grad_act[:, tiles].astype(jnp.float32) * derivative).astype(jnp.bfloat16)
        back = lax.dot_general(
            grad_hidden, w_in[:, tiles], ACROSS, preferred_element_type=jnp.float32
        )
        if number == 0:
            back_sum[...] = back
        else:
            back_sum[...] += back
        hidden = following
    own[...] = back_sum[:, spots[0]]
    for i, spot in enumerate(spots[1:]):
        backs[2 * i][...] = back_sum[:rows, spot].astype(jnp.bfloat16)
        backs[2 * i + 1][...] = back_sum[rows:, spot].astype(jnp.bfloat16)


def out_kernel(count, activation, top, bottom, w_out, own, *others):
    rows, chans = top.shape
    for i, spot in enumerate(channel_spots(count, chans)):
        product = times(activation[...], w_out[:, spot])
        if i == 0:
            own[:rows] = top[...].astype(jnp.float32) + product[:rows]
            own[rows:] = bottom[...].astype(jnp.float32) + product[rows:]
        else:
            cuts = len(others) // (count - 1)
            for cut in range(cuts):
                size = 2 * rows // cuts
                part = product[cut * size : (cut + 1) * size]
                others[(i - 1) * cuts + cut][...] = part.astype(jnp.bfloat16)


def combine_kernel(pieces, counts, *rest):
    owns, parts, outs = rest[:pieces], rest[pieces:-QUARTERS], rest[-QUARTERS:]
    for piece in range(pieces):
        per_piece = counts[piece]
        mine, parts = parts[:per_piece], parts[per_piece:]
        for quarter, out in enumerate(outs):
            total = owns[piece][quarter * BLOCK : (quarter + 1) * BLOCK]
            cuts = total.shape[0] * QUARTERS // mine[0].shape[0]
            start = quarter * BLOCK % mine[0].shape[0]
            for part in mine[quarter * cuts // QUARTERS :: cuts]:
                total = total + part[start : start + BLOCK].astype(jnp.float32)
            out[piece] = total.astype(jnp.bfloat16)


def assemble_kernel(*rest):
    quarters, out = rest[:-1], rest[-1]
    my_early, my_late = own_bits()
    for quarter, values in enumerate(quarters):
        spot = (my_early ^ (quarter & 1)) * 2 + (my_late ^ (quarter >> 1))
        for piece in range(values.shape[0]):
            start = pl.multiple_of((piece * QUARTERS + spot) * BLOCK, BLOCK)
            out[pl.ds(start, BLOCK)] = values[piece]


def on_device(inputs, conv_weight, mixing, pattern, w_in, w_out, cotangent):
    row_count, chan_count = inputs.shape
    blocks = row_count // BLOCK
    pieces = blocks // QUARTERS
    width, hidden = w_in.shape
    cores = lax.axis_size("ch")
    levels = lax.axis_size("seq").bit_length() - 1
    plain = list(range(LOCAL, LOCAL + levels - 2))
    last = LOCAL + levels - 2
    early_bit, late_bit = 1 << (levels - 2), 1 << (levels - 1)
    masks = [0, early_bit, late_bit, early_bit | late_bit]

    def blocks_of(size, kind=jnp.bfloat16):
        return ((size, BLOCK, chan_count), kind)

    half = blocks_of(2)
    whole = ((row_count, chan_count), jnp.bfloat16)
    piece_rows = QUARTERS * BLOCK
    flat = (piece_rows, chan_count)
    block = ((BLOCK, chan_count), jnp.bfloat16)
    half_flat = ((2 * BLOCK, chan_count), jnp.bfloat16)
    flat_piece = (flat, jnp.bfloat16)
    flops = 2 * piece_rows * width * hidden

    latest = []

    def run(kernel, name, outs, arrays, *args, **kwargs):
        results = call(kernel, name, outs, arrays, *args, order=tuple(latest), **kwargs)
        latest[:] = results[-1:]
        return results

    near, far = neighbours(jnp.concatenate([inputs[:1], inputs[-1:], conv_weight]), "seq")
    per_block = chan_count // (2 * BLOCK)
    lengths = [pieces + -(-pieces * 2 * (1 + (flip == 1)) // per_block) for flip in (1, 2, 3)]
    length = lengths[1]
    mixing, cells, pattern = run(
        load_kernel,
        "load",
        [(array.shape, array.dtype) for array in (mixing, inputs, pattern)],
        [],
        [mixing, inputs, pattern],
        [pltpu.SemaphoreType.DMA((3,))],
        limit=ALL,
    )
    units = [(s,) for s in range(2 * pieces)]
    convolved, *states = run(
        functools.partial(entry_kernel, units),
        "conv_and_local_factors",
        [whole] + [blocks_of(2 * len(unit)) for unit in units],
        [cells, far, near, mixing],
        [pattern],
        [pltpu.VMEM((blocks, BLOCK, chan_count), jnp.bfloat16)] * 2
        + [pltpu.SMEM(pattern.shape, jnp.int32), pltpu.SemaphoreType.DMA],
    )
    own_cots, *messages = run(
        functools.partial(pack_kernel, last, pieces, length),
        "pack",
        [((pieces, BLOCK, chan_count), jnp.bfloat16)]
        + [blocks_of(lengths[0]), blocks_of(2 * length)],
        [cotangent.reshape(blocks, BLOCK, chan_count), mixing],
    )
    messages = [from_flipped(m, "seq", mask) for m, mask in zip(messages, masks[1:])]

    def forward():
        (message,) = run(forward_kernel, "forward", [blocks_of(length)], [messages[1]])
        messages.append(from_flipped(message, "seq", early_bit))

    all_cots = []
    halves = {}
    transposed = [None] * pieces
    grad_acts = [None] * pieces
    parts = [None] * pieces
    mixeds = [None] * pieces
    activations = [None] * pieces
    owns = [None] * pieces
    out_owns = [None] * pieces
    out_parts = [None] * pieces

    def stack():
        stacked = run(
            functools.partial(stack_kernel, pieces),
            "stack",
            [flat_piece] * pieces,
            [own_cots, *messages],
        )
        for piece in stacked:
            all_cots.append([piece] + [from_offset(piece, "ch", i) for i in range(1, cores)])

    def grad_act(p):
        (grad_acts[p],) = run(
            functools.partial(grad_act_kernel, cores),
            "grad_act",
            [((piece_rows, hidden), jnp.bfloat16)],
            [*all_cots[p], w_out],
            scratch=[pltpu.VMEM((piece_rows, width), jnp.bfloat16)],
            limit=LARGE,
        )

    def plain_factor(factor, u):
        unit = units[u]
        mates = from_flipped(states[u], "seq", 1 << (factor - LOCAL))
        split = factor == plain[-1] and len(unit) == 2
        results = run(
            functools.partial(plain_kernel, factor, unit),
            "factor",
            [half, half] if split else [blocks_of(2 * len(unit))],
            [states[u], mates, mixing],
        )
        if factor == plain[-1]:
            halves.update(zip(unit, results))
        else:
            states[u] = results[0]

    def early_factor(p):
        send, keep = halves[2 * p], halves[2 * p + 1]
        transposed[p] = run(
            functools.partial(early_kernel, last, pieces, p),
            "early_factor",
            [half, half],
            [keep, from_flipped(send, "seq", early_bit), mixing, messages[0]],
        )

    def arrive(p):
        keep, send = transposed[p]
        (received,) = run(hold_kernel, "hold", [half], [from_flipped(send, "seq", late_bit)])
        transposed[p] = keep, received

    def late_factor(p):
        keep, received = transposed[p]
        if p > 0:
            received = from_flipped(received, "seq", late_bit)
        mixeds[p] = run(
            functools.partial(late_kernel, last, pieces, p),
            "late_factor",
            [half_flat] * 2,
            [keep, received, mixing, *messages],
        )

    def hidden_and_grad(p):
        gathered = [
            from_offset(mixed, "ch", i) if i else mixed for i in range(cores) for mixed in mixeds[p]
        ]
        activations[p], owns[p], *backs = run(
            functools.partial(hidden_kernel, cores),
            "mlp_hidden_and_grad",
            [((piece_rows, hidden), jnp.bfloat16), (flat, jnp.float32)]
            + [half_flat] * ((cores - 1) * 2),
            [*gathered, grad_acts[p], w_in],
            scratch=[
                pltpu.VMEM((piece_rows, width), jnp.bfloat16),
                pltpu.VMEM((piece_rows, width), jnp.float32),
            ],
            limit=LARGE,
        )
        parts[p] = [
            from_offset(back, "ch", cores - 1 - i // 2) for i, back in enumerate(backs)
        ]

    def transposed_back(p):
        quarters = run(
            functools.partial(back_kernel, last, pieces, p, cores),
            "late_and_early_back",
            [block] * QUARTERS,
            [all_cots[p][0], owns[p], *parts[p], mixing, *messages],
        )
        transposed[p] = [
            from_flipped(grad, "seq", mask) if mask else grad
            for grad, mask in zip(quarters, masks)
        ]

    def regroup(p):
        chosen = [u for u, unit in enumerate(back_units) if unit[0] // 2 == p]
        sizes = [2 * len(back_units[u]) for u in chosen]
        results = run(
            functools.partial(regroup_kernel, plain[-1], [back_units[u] for u in chosen]),
            "regroup_and_factor_back",
            [blocks_of(size, kind) for size in sizes for kind in (jnp.float32, jnp.bfloat16)],
            [*transposed[p], mixing],
        )
        for number, u in enumerate(chosen):
            states[u] = results[2 * number : 2 * number + 2]

    def out_product(p):
        cuts = 1 if p + 1 < pieces else 2
        out_owns[p], *others = run(
            functools.partial(out_kernel, cores),
            "mlp_out",
            [(flat, jnp.float32)] + [flat_piece if cuts == 1 else half_flat] * (cuts * (cores - 1)),
            [activations[p], *mixeds[p], w_out],
            limit=LARGE,
        )
        out_parts[p] = [
            from_offset(other, "ch", cores - 1 - i // cuts) for i, other in enumerate(others)
        ]

    def plain_back(factor, u):
        mine, cross = states[u]
        theirs = from_flipped(cross, "seq", 1 << (factor - LOCAL))
        kind = jnp.bfloat16 if factor != plain[0] else jnp.float32
        size = 2 * len(back_units[u])
        states[u] = run(
            functools.partial(plain_back_kernel, factor - 1, back_units[u]),
            "factor_back",
            [blocks_of(size, jnp.float32), blocks_of(size, kind)],
            [mine, theirs, mixing],
        )

    waves = sorted((u + 2 * i, -i, u) for i in range(len(plain)) for u in range(len(units)))
    for _, i, u in waves:
        plain_factor(plain[-i], u)
        if plain[-i] == plain[-1] and u == len(units) - 2:
            arrive(0)
        if plain[-i] == plain[-1] and u == 1:
            early_factor(0)
            forward()
    late_factor(0)
    for p in range(1, pieces):
        early_factor(p)
    stack()
    grad_act(0)
    back_units = [(2 * p, 2 * p + 1) for p in range(pieces - 1)]
    back_units.append((2 * pieces - 1, 2 * pieces - 2))
    states = [None] * len(back_units)
    for p in range(pieces):
        hidden_and_grad(p)
        if p + 1 < pieces:
            grad_act(p + 1)
            out_product(p)
            late_factor(p + 1)
        if p == pieces - 1:
            out_product(p)
        if p > 0:
            regroup(p - 1)
        transposed_back(p)
    early_units = range(pieces - 1)
    late_units = range(pieces - 1, pieces)
    def combine():
        return run(
            functools.partial(combine_kernel, pieces, [len(piece) for piece in out_parts]),
            "combine",
            [((pieces, BLOCK, chan_count), jnp.bfloat16)] * QUARTERS,
            [*out_owns, *[part for piece in out_parts for part in piece]],
        )

    outs = combine()
    regroup(pieces - 1)
    for factor in reversed(plain):
        for u in (*early_units, *late_units):
            plain_back(factor, u)
    arrived = [from_flipped(out, "seq", mask) if mask else out for out, mask in zip(outs, masks)]
    grad_conv, edges = run(
        functools.partial(exit_kernel, back_units),
        "local_factors_back",
        [whole, ((2, chan_count), jnp.bfloat16)],
        [g[0] for g in states] + [g[1] for g in states] + [mixing],
        [pattern],
        [pltpu.VMEM((blocks, BLOCK, chan_count), jnp.float32)] * 2
        + [pltpu.SMEM(pattern.shape, jnp.int32), pltpu.SemaphoreType.DMA],
        limit=LARGE,
    )
    near_grad, far_grad = neighbours(edges, "seq")
    grad_input, _ = run(
        conv_back_kernel,
        "conv_back",
        [whole, ((8, 128), jnp.float32)],
        [grad_conv, far_grad, near_grad, near],
    )
    (layer_out,) = run(assemble_kernel, "assemble", [whole], arrived)
    return (layer_out, convolved, grad_input)


def solution(mesh):
    return jax.shard_map(
        on_device,
        mesh=mesh,
        in_specs=(
            P("seq", "ch"),
            P(None, "ch"),
            P(None, "seq", None, None),
            P(None, "seq"),
            P(None, "ch"),
            P("ch", None),
            P("seq", "ch"),
        ),
        out_specs=(P("seq", "ch"), P("seq", "ch"), P("seq", "ch")),
        check_vma=False,
    )
```

```python
import functools

import jax
import jax.numpy as jnp
from jax import lax
from jax.experimental import pallas as pl
from jax.experimental.pallas import tpu as pltpu
from jax.sharding import PartitionSpec as P

BLOCK = 64
LOCAL = 2
QUARTERS = 4
TILE = 512
SMALL = 8 * 1024 * 1024
LARGE = 20 * 1024 * 1024
ALL = 44 * 1024 * 1024

root_two_pi = 0.7978845608028654

IN_HBM = pl.BlockSpec(memory_space=pltpu.HBM)
IN_VMEM = pl.BlockSpec(memory_space=pltpu.VMEM)
ANYWHERE = pl.BlockSpec(memory_space=pl.ANY)
ACROSS = (((1,), (1,)), ((), ()))
OVER_ROWS = (((0,), (0,)), ((), ()))


def times(weights, value):
    return jnp.dot(weights, value, preferred_element_type=jnp.float32)


def times_transposed(weights, value):
    return lax.dot_general(weights, value, OVER_ROWS, preferred_element_type=jnp.float32)


def neighbours(edges, axis):
    count = lax.axis_size(axis)
    near = lax.ppermute(edges, axis, [(i, i ^ 1) for i in range(count)])
    route = []
    for low in range(1, count - 1, 2):
        route += [(low, low + 1), (low + 1, low)]
    return near, lax.ppermute(edges, axis, route)


def from_flipped(block, axis, mask):
    count = lax.axis_size(axis)
    return lax.ppermute(block, axis, [(i, i ^ mask) for i in range(count)])


def from_offset(block, axis, offset):
    count = lax.axis_size(axis)
    return lax.ppermute(block, axis, [((i + offset) % count, i) for i in range(count)])


def call(kernel, name, outs, arrays, distant=(), scratch=(), order=(), limit=SMALL):
    count = len(distant) + len(arrays)

    def body(*refs):
        kernel(*refs[:count], *refs[count + len(order) :])

    return pl.pallas_call(
        body,
        out_shape=[jax.ShapeDtypeStruct(shape, kind) for shape, kind in outs],
        in_specs=[ANYWHERE] * len(distant) + [IN_VMEM] * len(arrays) + [ANYWHERE] * len(order),
        out_specs=[IN_VMEM] * len(outs),
        scratch_shapes=list(scratch),
        compiler_params=pltpu.CompilerParams(vmem_limit_bytes=limit),
        cost_estimate=pl.CostEstimate(flops=0, bytes_accessed=0, transcendentals=0),
        name=name,
    )(*distant, *arrays, *order)


def own_bits():
    seat = lax.axis_index("seq")
    levels = lax.axis_size("seq").bit_length() - 1
    return (seat >> (levels - 2)) & 1, (seat >> (levels - 1)) & 1


def shifted(cells, near, far):
    rows = cells.shape[0]
    even = lax.axis_index("seq") % 2 == 0
    near, far = near.astype(jnp.float32), far.astype(jnp.float32)
    before = jnp.where(even, far[1:2], near[1:2])
    after = jnp.where(even, near[0:1], far[0:1])
    spot = lax.broadcasted_iota(jnp.int32, cells.shape, 0)
    up = jnp.where(spot == 0, before, pltpu.roll(cells, 1, 0))
    down = jnp.where(spot == rows - 1, after, pltpu.roll(cells, rows - 1, 0))
    return up, down


def chosen_blocks(subs):
    early, late = own_bits()
    return [
        sub // 2 * QUARTERS + (early ^ (1 - sub % 2)) * 2 + (late ^ other)
        for sub in subs
        for other in range(2)
    ]


def local_factor(factor, pattern, source, mixing, target, chosen):
    for spot, block in enumerate(chosen):
        pair = mixing[factor, block]
        target[spot] = (
            times(pair[:, :BLOCK], source[block])
            + times(pair[:, BLOCK:], source[pattern[factor, block]])
        ).astype(jnp.bfloat16)


def entry_kernel(units, pattern_far, cells, far, near, mixing, conv_ref, *rest):
    outs, (first, between, pattern, arrival) = rest[:-4], rest[-4:]
    fetch = pltpu.make_async_copy(pattern_far, pattern, arrival)
    fetch.start()
    values = cells[...].astype(jnp.float32)
    scale = near[2:5].astype(jnp.float32)
    up, down = shifted(values, near[...], far[...])
    convolved = (scale[0:1] * up + scale[1:2] * values + scale[2:3] * down).astype(jnp.bfloat16)
    conv_ref[...] = convolved
    first[...] = convolved.reshape(first.shape)
    fetch.wait()
    every = range(first.shape[0])
    refs = (first, between)
    for factor in range(LOCAL - 1):
        local_factor(factor, pattern, refs[factor % 2], mixing, refs[1 - factor % 2], every)
    source = refs[(LOCAL - 1) % 2]
    for unit, out in zip(units, outs):
        local_factor(LOCAL - 1, pattern, source, mixing, out, chosen_blocks(unit))


def plain_kernel(factor, unit, state, mates, mixing, *outs):
    for spot, block in enumerate(chosen_blocks(unit)):
        pair = mixing[factor, block]
        per_out = state.shape[0] // len(outs)
        outs[spot // per_out][spot % per_out] = (
            times(pair[:, :BLOCK], state[spot]) + times(pair[:, BLOCK:], mates[spot])
        ).astype(jnp.bfloat16)


def packed(message, pieces, number):
    across = message.shape[-1] // (2 * BLOCK)
    lanes = pl.ds(number % across * 2 * BLOCK, 2 * BLOCK)
    return message.at[pieces + number // across, :, lanes]


def load_kernel(count, *rest):
    fars, nears, arrivals = rest[:count], rest[count : 2 * count], rest[2 * count]
    fetches = [
        pltpu.make_async_copy(far, near, arrivals.at[i])
        for i, (far, near) in enumerate(zip(fars, nears))
    ]
    for fetch in fetches:
        fetch.start()
    for fetch in fetches:
        fetch.wait()


def pack_kernel(factor, pieces, length, cots, mixing, own, near, across):
    messages = (near, across.at[pl.ds(0, length)], across.at[pl.ds(length, length)])
    my_early, my_late = own_bits()
    for piece in range(pieces):
        base = piece * QUARTERS
        own[piece] = cots[base + my_early * 2 + my_late]
        for flip, message in enumerate(messages, 1):
            early, late = my_early ^ (flip & 1), my_late ^ (flip >> 1)
            message[piece] = cots[base + early * 2 + late]
            for which in range(2):
                number = which * pieces + piece
                if flip == 1:
                    for other in range(2):
                        packed(message, pieces, number * 2 + other)[...] = mixing[
                            factor + which, base + early * 2 + (late ^ other)
                        ]
                else:
                    packed(message, pieces, number)[...] = mixing[
                        factor + which, base + early * 2 + late
                    ]


def forward_kernel(message, out):
    out[...] = message[out.shape[0] :]


def stack_kernel(pieces, *rest):
    quarters, outs = rest[:QUARTERS], rest[QUARTERS:]
    for piece, out in enumerate(outs):
        for quarter, values in enumerate(quarters):
            out[quarter * BLOCK : (quarter + 1) * BLOCK] = values[piece]


def mixing_of(factor, which, pieces, piece, mixing, messages, quarter, other=0):
    if quarter == 0:
        early, late = own_bits()
        return mixing[factor + which, piece * QUARTERS + early * 2 + (late ^ other)]
    number = which * pieces + piece
    if quarter == 1:
        number = number * 2 + other
    return packed(messages[quarter - 1], pieces, number)[...]


def early_kernel(factor, pieces, piece, keep, recv, mixing, message, keep_out, send_out):
    weights = functools.partial(mixing_of, factor, 0, pieces, piece, mixing, [message])
    for other, out in enumerate((keep_out, send_out)):
        mine, theirs = keep[other], recv[other]
        pair = weights(0, other)
        out[0] = (times(pair[:, :BLOCK], mine) + times(pair[:, BLOCK:], theirs)).astype(
            jnp.bfloat16
        )
        pair = weights(1, other)
        out[1] = (times(pair[:, :BLOCK], theirs) + times(pair[:, BLOCK:], mine)).astype(
            jnp.bfloat16
        )


def hold_kernel(received, out):
    out[...] = received[...]


def late_kernel(factor, pieces, piece, keep, recv, mixing, *rest):
    messages, outs = rest[:-2], rest[-2:]
    values = [keep[0], keep[1], recv[0], recv[1]]
    for quarter in range(QUARTERS):
        pair = mixing_of(factor, 1, pieces, piece, mixing, messages, quarter)
        rows = slice(quarter % 2 * BLOCK, (quarter % 2 + 1) * BLOCK)
        outs[quarter // 2][rows] = (
            times(pair[:, :BLOCK], values[quarter]) + times(pair[:, BLOCK:], values[quarter ^ 2])
        ).astype(jnp.bfloat16)


def back_kernel(factor, pieces, piece, cores, cots, total, *rest):
    count = (cores - 1) * 2
    parts, (mixing, message1, message2, message3, *outs) = rest[:count], rest[count:]
    messages = (message1, message2, message3)
    grads = []
    for quarter in range(QUARTERS):
        rows = slice(quarter * BLOCK, (quarter + 1) * BLOCK)
        grad = cots[rows].astype(jnp.float32) + total[rows]
        inner = slice(quarter % 2 * BLOCK, (quarter % 2 + 1) * BLOCK)
        for part in parts[quarter // 2 :: 2]:
            grad = grad + part[inner].astype(jnp.float32)
        grads.append(grad.astype(jnp.bfloat16))
    for which, flip in ((1, 2), (0, 1)):
        both = [
            times_transposed(
                mixing_of(factor, which, pieces, piece, mixing, messages, quarter),
                grads[quarter],
            )
            for quarter in range(QUARTERS)
        ]
        grads = [
            (both[quarter][:BLOCK] + both[quarter ^ flip][BLOCK:]).astype(jnp.bfloat16)
            for quarter in range(QUARTERS)
        ]
    for grad, out in zip(grads, outs):
        out[...] = grad


def regroup_kernel(factor, units, *rest):
    quarters, mixing, outs = rest[:QUARTERS], rest[QUARTERS], rest[QUARTERS + 1 :]
    for number, unit in enumerate(units):
        own, cross = outs[2 * number : 2 * number + 2]
        for spot, block in enumerate(chosen_blocks(unit)):
            grad = quarters[1 - unit[spot // 2] % 2 + spot % 2 * 2][...]
            both = times_transposed(mixing[factor, block], grad)
            own[spot] = both[:BLOCK]
            cross[spot] = both[BLOCK:].astype(jnp.bfloat16)


def plain_back_kernel(factor, unit, mine, theirs, mixing, own, cross):
    for spot, block in enumerate(chosen_blocks(unit)):
        grad = (mine[spot] + theirs[spot].astype(jnp.float32)).astype(jnp.bfloat16)
        both = times_transposed(mixing[factor, block], grad)
        own[spot] = both[:BLOCK]
        cross[spot] = both[BLOCK:].astype(cross.dtype)


def exit_kernel(units, pattern_far, *rest):
    count = len(units)
    mine, theirs = rest[:count], rest[count : 2 * count]
    mixing, out, edges, own, cross, pattern, arrival = rest[2 * count :]
    fetch = pltpu.make_async_copy(pattern_far, pattern, arrival)
    fetch.start()
    blocks = own.shape[0]
    for number, unit in enumerate(units):
        for spot, block in enumerate(chosen_blocks(unit)):
            own[block] = mine[number][spot]
            cross[block] = theirs[number][spot]
    fetch.wait()
    for factor in reversed(range(LOCAL)):
        for block in range(blocks):
            own[block] += cross[pattern[factor, block]]
        for block in range(blocks):
            grad = own[block].astype(jnp.bfloat16)
            if factor == 0:
                out[block * BLOCK : (block + 1) * BLOCK] = grad
                if block == 0:
                    edges[0:1] = grad[:1]
                if block == blocks - 1:
                    edges[1:2] = grad[-1:]
            else:
                both = times_transposed(mixing[factor - 1, block], grad)
                own[block] = both[:BLOCK]
                cross[block] = both[BLOCK:]


def conv_back_kernel(cells, far, near, taps, out, ready):
    ready[...] = jnp.zeros_like(ready)
    values = cells[...].astype(jnp.float32)
    scale = taps[2:5].astype(jnp.float32)
    up, down = shifted(values, near[...], far[...])
    out[...] = (scale[0:1] * down + scale[1:2] * values + scale[2:3] * up).astype(jnp.bfloat16)


def channel_spots(count, chans):
    core = lax.axis_index("ch")
    return [
        pl.ds(pl.multiple_of(lax.rem(core + i, count) * chans, chans), chans)
        for i in range(count)
    ]


def grad_act_kernel(count, *rest):
    cots, (w_out, grad_act, c_all) = rest[:count], rest[count:]
    for spot, cot in zip(channel_spots(count, cots[0].shape[1]), cots):
        c_all[:, spot] = cot[...]
    hidden = w_out.shape[0]
    tile = min(TILE, hidden)
    for start in range(0, hidden, tile):
        grad_act[:, start : start + tile] = lax.dot_general(
            c_all[...], w_out[start : start + tile], ACROSS, preferred_element_type=jnp.float32
        ).astype(grad_act.dtype)


def hidden_kernel(count, *rest):
    mixed, (grad_act, w_in, activation, own) = rest[: 2 * count], rest[2 * count : 2 * count + 4]
    backs, (x_all, back_sum) = rest[2 * count + 4 : -2], rest[-2:]
    rows, chans = mixed[0].shape
    spots = channel_spots(count, chans)
    for i, spot in enumerate(spots):
        x_all[:rows, spot] = mixed[2 * i][...]
        x_all[rows:, spot] = mixed[2 * i + 1][...]
    size = w_in.shape[1]
    tile = min(TILE, size)
    every = [slice(start, start + tile) for start in range(0, size, tile)]
    hidden = times(x_all[...], w_in[:, every[0]])
    for number, tiles in enumerate(every):
        following = None
        if number + 1 < len(every):
            following = times(x_all[...], w_in[:, every[number + 1]])
        square = hidden * hidden
        tanh_val = jnp.tanh(hidden * (root_two_pi + root_two_pi * 0.044715 * square))
        half = 0.5 + 0.5 * tanh_val
        gelu = hidden * half
        activation[:, tiles] = gelu.astype(jnp.bfloat16)
        slope = 2.0 * root_two_pi + 6.0 * root_two_pi * 0.044715 * square
        derivative = half + gelu * (1.0 - half) * slope
        grad_hidden = (grad_act[:, tiles].astype(jnp.float32) * derivative).astype(jnp.bfloat16)
        back = lax.dot_general(
            grad_hidden, w_in[:, tiles], ACROSS, preferred_element_type=jnp.float32
        )
        if number == 0:
            back_sum[...] = back
        else:
            back_sum[...] += back
        hidden = following
    own[...] = back_sum[:, spots[0]]
    for i, spot in enumerate(spots[1:]):
        backs[2 * i][...] = back_sum[:rows, spot].astype(jnp.bfloat16)
        backs[2 * i + 1][...] = back_sum[rows:, spot].astype(jnp.bfloat16)


def out_kernel(count, activation, top, bottom, w_out, own, *others):
    rows, chans = top.shape
    for i, spot in enumerate(channel_spots(count, chans)):
        product = times(activation[...], w_out[:, spot])
        if i == 0:
            own[:rows] = top[...].astype(jnp.float32) + product[:rows]
            own[rows:] = bottom[...].astype(jnp.float32) + product[rows:]
        else:
            cuts = len(others) // (count - 1)
            for cut in range(cuts):
                size = 2 * rows // cuts
                part = product[cut * size : (cut + 1) * size]
                others[(i - 1) * cuts + cut][...] = part.astype(jnp.bfloat16)


def combine_kernel(pieces, counts, *rest):
    owns, parts, outs = rest[:pieces], rest[pieces:-QUARTERS], rest[-QUARTERS:]
    for piece in range(pieces):
        per_piece = counts[piece]
        mine, parts = parts[:per_piece], parts[per_piece:]
        for quarter, out in enumerate(outs):
            total = owns[piece][quarter * BLOCK : (quarter + 1) * BLOCK]
            cuts = total.shape[0] * QUARTERS // mine[0].shape[0]
            start = quarter * BLOCK % mine[0].shape[0]
            for part in mine[quarter * cuts // QUARTERS :: cuts]:
                total = total + part[start : start + BLOCK].astype(jnp.float32)
            out[piece] = total.astype(jnp.bfloat16)


def assemble_kernel(*rest):
    quarters, out = rest[:-1], rest[-1]
    my_early, my_late = own_bits()
    for quarter, values in enumerate(quarters):
        spot = (my_early ^ (quarter & 1)) * 2 + (my_late ^ (quarter >> 1))
        for piece in range(values.shape[0]):
            start = pl.multiple_of((piece * QUARTERS + spot) * BLOCK, BLOCK)
            out[pl.ds(start, BLOCK)] = values[piece]


def on_device(inputs, conv_weight, mixing, pattern, w_in, w_out, cotangent):
    row_count, chan_count = inputs.shape
    blocks = row_count // BLOCK
    pieces = blocks // QUARTERS
    width, hidden = w_in.shape
    cores = lax.axis_size("ch")
    levels = lax.axis_size("seq").bit_length() - 1
    plain = list(range(LOCAL, LOCAL + levels - 2))
    last = LOCAL + levels - 2
    early_bit, late_bit = 1 << (levels - 2), 1 << (levels - 1)
    masks = [0, early_bit, late_bit, early_bit | late_bit]

    def blocks_of(size, kind=jnp.bfloat16):
        return ((size, BLOCK, chan_count), kind)

    half = blocks_of(2)
    whole = ((row_count, chan_count), jnp.bfloat16)
    piece_rows = QUARTERS * BLOCK
    flat = (piece_rows, chan_count)
    block = ((BLOCK, chan_count), jnp.bfloat16)
    half_flat = ((2 * BLOCK, chan_count), jnp.bfloat16)
    flat_piece = (flat, jnp.bfloat16)
    flops = 2 * piece_rows * width * hidden

    latest = []

    def run(kernel, name, outs, arrays, *args, **kwargs):
        results = call(kernel, name, outs, arrays, *args, order=tuple(latest), **kwargs)
        latest[:] = results[-1:]
        return results

    near, far = neighbours(jnp.concatenate([inputs[:1], inputs[-1:], conv_weight]), "seq")
    per_block = chan_count // (2 * BLOCK)
    lengths = [pieces + -(-pieces * 2 * (1 + (flip == 1)) // per_block) for flip in (1, 2, 3)]
    length = lengths[1]
    distant = [cotangent.reshape(blocks, BLOCK, chan_count), mixing, inputs, pattern]
    cots, mixing, cells, pattern = run(
        functools.partial(load_kernel, len(distant)),
        "load",
        [(array.shape, array.dtype) for array in distant],
        [],
        distant,
        [pltpu.SemaphoreType.DMA((len(distant),))],
        limit=ALL,
    )
    latest += [far, near]
    own_cots, soon_message, across = run(
        functools.partial(pack_kernel, last, pieces, length),
        "pack",
        [blocks_of(pieces), blocks_of(lengths[0]), blocks_of(2 * length)],
        [cots, mixing],
    )
    units = [(s,) for s in range(2 * pieces)]
    convolved, *states = run(
        functools.partial(entry_kernel, units),
        "conv_and_local_factors",
        [whole] + [blocks_of(2 * len(unit)) for unit in units],
        [cells, far, near, mixing],
        [pattern],
        [pltpu.VMEM((blocks, BLOCK, chan_count), jnp.bfloat16)] * 2
        + [pltpu.SMEM(pattern.shape, jnp.int32), pltpu.SemaphoreType.DMA],
    )
    messages = [soon_message, across]
    messages = [from_flipped(m, "seq", mask) for m, mask in zip(messages, masks[1:])]

    def forward():
        (message,) = run(forward_kernel, "forward", [blocks_of(length)], [messages[1]])
        messages.append(from_flipped(message, "seq", early_bit))

    all_cots = []
    halves = {}
    transposed = [None] * pieces
    grad_acts = [None] * pieces
    parts = [None] * pieces
    mixeds = [None] * pieces
    activations = [None] * pieces
    owns = [None] * pieces
    out_owns = [None] * pieces
    out_parts = [None] * pieces

    def stack():
        stacked = run(
            functools.partial(stack_kernel, pieces),
            "stack",
            [flat_piece] * pieces,
            [own_cots, *messages],
        )
        for piece in stacked:
            all_cots.append([piece] + [from_offset(piece, "ch", i) for i in range(1, cores)])

    def grad_act(p):
        (grad_acts[p],) = run(
            functools.partial(grad_act_kernel, cores),
            "grad_act",
            [((piece_rows, hidden), jnp.bfloat16)],
            [*all_cots[p], w_out],
            scratch=[pltpu.VMEM((piece_rows, width), jnp.bfloat16)],
            limit=LARGE,
        )

    def plain_factor(factor, u):
        unit = units[u]
        mates = from_flipped(states[u], "seq", 1 << (factor - LOCAL))
        split = factor == plain[-1] and len(unit) == 2
        results = run(
            functools.partial(plain_kernel, factor, unit),
            "factor",
            [half, half] if split else [blocks_of(2 * len(unit))],
            [states[u], mates, mixing],
        )
        if factor == plain[-1]:
            halves.update(zip(unit, results))
        else:
            states[u] = results[0]

    def early_factor(p):
        send, keep = halves[2 * p], halves[2 * p + 1]
        transposed[p] = run(
            functools.partial(early_kernel, last, pieces, p),
            "early_factor",
            [half, half],
            [keep, from_flipped(send, "seq", early_bit), mixing, messages[0]],
        )

    def arrive(p):
        keep, send = transposed[p]
        (received,) = run(hold_kernel, "hold", [half], [from_flipped(send, "seq", late_bit)])
        transposed[p] = keep, received

    def late_factor(p):
        keep, received = transposed[p]
        if p > 0:
            received = from_flipped(received, "seq", late_bit)
        mixeds[p] = run(
            functools.partial(late_kernel, last, pieces, p),
            "late_factor",
            [half_flat] * 2,
            [keep, received, mixing, *messages],
        )

    def hidden_and_grad(p):
        gathered = [
            from_offset(mixed, "ch", i) if i else mixed for i in range(cores) for mixed in mixeds[p]
        ]
        activations[p], owns[p], *backs = run(
            functools.partial(hidden_kernel, cores),
            "mlp_hidden_and_grad",
            [((piece_rows, hidden), jnp.bfloat16), (flat, jnp.float32)]
            + [half_flat] * ((cores - 1) * 2),
            [*gathered, grad_acts[p], w_in],
            scratch=[
                pltpu.VMEM((piece_rows, width), jnp.bfloat16),
                pltpu.VMEM((piece_rows, width), jnp.float32),
            ],
            limit=LARGE,
        )
        parts[p] = [
            from_offset(back, "ch", cores - 1 - i // 2) for i, back in enumerate(backs)
        ]

    def transposed_back(p):
        quarters = run(
            functools.partial(back_kernel, last, pieces, p, cores),
            "late_and_early_back",
            [block] * QUARTERS,
            [all_cots[p][0], owns[p], *parts[p], mixing, *messages],
        )
        transposed[p] = [
            from_flipped(grad, "seq", mask) if mask else grad
            for grad, mask in zip(quarters, masks)
        ]

    def regroup(p):
        chosen = [u for u, unit in enumerate(back_units) if unit[0] // 2 == p]
        sizes = [2 * len(back_units[u]) for u in chosen]
        results = run(
            functools.partial(regroup_kernel, plain[-1], [back_units[u] for u in chosen]),
            "regroup_and_factor_back",
            [blocks_of(size, kind) for size in sizes for kind in (jnp.float32, jnp.bfloat16)],
            [*transposed[p], mixing],
        )
        for number, u in enumerate(chosen):
            states[u] = results[2 * number : 2 * number + 2]

    def out_product(p):
        cuts = 1 if p + 1 < pieces else 2
        out_owns[p], *others = run(
            functools.partial(out_kernel, cores),
            "mlp_out",
            [(flat, jnp.float32)] + [flat_piece if cuts == 1 else half_flat] * (cuts * (cores - 1)),
            [activations[p], *mixeds[p], w_out],
            limit=LARGE,
        )
        out_parts[p] = [
            from_offset(other, "ch", cores - 1 - i // cuts) for i, other in enumerate(others)
        ]

    def plain_back(factor, u):
        mine, cross = states[u]
        theirs = from_flipped(cross, "seq", 1 << (factor - LOCAL))
        kind = jnp.bfloat16 if factor != plain[0] else jnp.float32
        size = 2 * len(back_units[u])
        states[u] = run(
            functools.partial(plain_back_kernel, factor - 1, back_units[u]),
            "factor_back",
            [blocks_of(size, jnp.float32), blocks_of(size, kind)],
            [mine, theirs, mixing],
        )

    waves = sorted((u + 2 * i, -i, u) for i in range(len(plain)) for u in range(len(units)))
    for _, i, u in waves:
        plain_factor(plain[-i], u)
        if plain[-i] == plain[-1] and u == len(units) - 2:
            arrive(0)
        if plain[-i] == plain[-1] and u == 1:
            forward()
            early_factor(0)
    late_factor(0)
    for p in range(1, pieces):
        early_factor(p)
    stack()
    grad_act(0)
    back_units = [(2 * p, 2 * p + 1) for p in range(pieces - 1)]
    back_units.append((2 * pieces - 1, 2 * pieces - 2))
    states = [None] * len(back_units)
    for p in range(pieces):
        hidden_and_grad(p)
        if p + 1 < pieces:
            grad_act(p + 1)
            out_product(p)
            late_factor(p + 1)
        if p == pieces - 1:
            out_product(p)
        if p > 0:
            regroup(p - 1)
        transposed_back(p)
    early_units = range(pieces - 1)
    late_units = range(pieces - 1, pieces)
    def combine():
        return run(
            functools.partial(combine_kernel, pieces, [len(piece) for piece in out_parts]),
            "combine",
            [((pieces, BLOCK, chan_count), jnp.bfloat16)] * QUARTERS,
            [*out_owns, *[part for piece in out_parts for part in piece]],
        )

    outs = combine()
    regroup(pieces - 1)
    for factor in reversed(plain):
        for u in (*early_units, *late_units):
            plain_back(factor, u)
    arrived = [from_flipped(out, "seq", mask) if mask else out for out, mask in zip(outs, masks)]
    grad_conv, edges = run(
        functools.partial(exit_kernel, back_units),
        "local_factors_back",
        [whole, ((2, chan_count), jnp.bfloat16)],
        [g[0] for g in states] + [g[1] for g in states] + [mixing],
        [pattern],
        [pltpu.VMEM((blocks, BLOCK, chan_count), jnp.float32)] * 2
        + [pltpu.SMEM(pattern.shape, jnp.int32), pltpu.SemaphoreType.DMA],
        limit=LARGE,
    )
    near_grad, far_grad = neighbours(edges, "seq")
    grad_input, _ = run(
        conv_back_kernel,
        "conv_back",
        [whole, ((8, 128), jnp.float32)],
        [grad_conv, far_grad, near_grad, near],
    )
    (layer_out,) = run(assemble_kernel, "assemble", [whole], arrived)
    return (layer_out, convolved, grad_input)


def solution(mesh):
    return jax.shard_map(
        on_device,
        mesh=mesh,
        in_specs=(
            P("seq", "ch"),
            P(None, "ch"),
            P(None, "seq", None, None),
            P(None, "seq"),
            P(None, "ch"),
            P("ch", None),
            P("seq", "ch"),
        ),
        out_specs=(P("seq", "ch"), P("seq", "ch"), P("seq", "ch")),
        check_vma=False,
    )
```

```python
import functools

import jax
import jax.numpy as jnp
from jax import lax
from jax.experimental import pallas as pl
from jax.experimental.pallas import tpu as pltpu
from jax.sharding import PartitionSpec as P

BLOCK = 64
LOCAL = 2
QUARTERS = 4
TILE = 512
SMALL = 8 * 1024 * 1024
LARGE = 20 * 1024 * 1024
ALL = 44 * 1024 * 1024

root_two_pi = 0.7978845608028654

IN_HBM = pl.BlockSpec(memory_space=pltpu.HBM)
IN_VMEM = pl.BlockSpec(memory_space=pltpu.VMEM)
ANYWHERE = pl.BlockSpec(memory_space=pl.ANY)
ACROSS = (((1,), (1,)), ((), ()))
OVER_ROWS = (((0,), (0,)), ((), ()))


def times(weights, value):
    return jnp.dot(weights, value, preferred_element_type=jnp.float32)


def times_transposed(weights, value):
    return lax.dot_general(weights, value, OVER_ROWS, preferred_element_type=jnp.float32)


def neighbours(edges, axis):
    count = lax.axis_size(axis)
    near = lax.ppermute(edges, axis, [(i, i ^ 1) for i in range(count)])
    route = []
    for low in range(1, count - 1, 2):
        route += [(low, low + 1), (low + 1, low)]
    return near, lax.ppermute(edges, axis, route)


def from_flipped(block, axis, mask):
    count = lax.axis_size(axis)
    return lax.ppermute(block, axis, [(i, i ^ mask) for i in range(count)])


def from_offset(block, axis, offset):
    count = lax.axis_size(axis)
    return lax.ppermute(block, axis, [((i + offset) % count, i) for i in range(count)])


def call(kernel, name, outs, arrays, distant=(), scratch=(), order=(), limit=SMALL):
    count = len(distant) + len(arrays)

    def body(*refs):
        kernel(*refs[:count], *refs[count + len(order) :])

    return pl.pallas_call(
        body,
        out_shape=[jax.ShapeDtypeStruct(shape, kind) for shape, kind in outs],
        in_specs=[ANYWHERE] * len(distant) + [IN_VMEM] * len(arrays) + [ANYWHERE] * len(order),
        out_specs=[IN_VMEM] * len(outs),
        scratch_shapes=list(scratch),
        compiler_params=pltpu.CompilerParams(vmem_limit_bytes=limit),
        cost_estimate=pl.CostEstimate(flops=0, bytes_accessed=0, transcendentals=0),
        name=name,
    )(*distant, *arrays, *order)


def own_bits():
    seat = lax.axis_index("seq")
    levels = lax.axis_size("seq").bit_length() - 1
    return (seat >> (levels - 2)) & 1, (seat >> (levels - 1)) & 1


def shifted(cells, near, far):
    rows = cells.shape[0]
    even = lax.axis_index("seq") % 2 == 0
    near, far = near.astype(jnp.float32), far.astype(jnp.float32)
    before = jnp.where(even, far[1:2], near[1:2])
    after = jnp.where(even, near[0:1], far[0:1])
    spot = lax.broadcasted_iota(jnp.int32, cells.shape, 0)
    up = jnp.where(spot == 0, before, pltpu.roll(cells, 1, 0))
    down = jnp.where(spot == rows - 1, after, pltpu.roll(cells, rows - 1, 0))
    return up, down


def chosen_blocks(subs):
    early, late = own_bits()
    return [
        sub // 2 * QUARTERS + (early ^ (1 - sub % 2)) * 2 + (late ^ other)
        for sub in subs
        for other in range(2)
    ]


def local_factor(factor, pattern, source, mixing, target, chosen):
    for spot, block in enumerate(chosen):
        pair = mixing[factor, block]
        target[spot] = (
            times(pair[:, :BLOCK], source[block])
            + times(pair[:, BLOCK:], source[pattern[factor, block]])
        ).astype(jnp.bfloat16)


def entry_kernel(units, pattern_far, cells, far, near, mixing, conv_ref, *rest):
    outs, (first, between, pattern, arrival) = rest[:-4], rest[-4:]
    fetch = pltpu.make_async_copy(pattern_far, pattern, arrival)
    fetch.start()
    values = cells[...].astype(jnp.float32)
    scale = near[2:5].astype(jnp.float32)
    up, down = shifted(values, near[...], far[...])
    convolved = (scale[0:1] * up + scale[1:2] * values + scale[2:3] * down).astype(jnp.bfloat16)
    conv_ref[...] = convolved
    first[...] = convolved.reshape(first.shape)
    fetch.wait()
    every = range(first.shape[0])
    refs = (first, between)
    for factor in range(LOCAL - 1):
        local_factor(factor, pattern, refs[factor % 2], mixing, refs[1 - factor % 2], every)
    source = refs[(LOCAL - 1) % 2]
    for unit, out in zip(units, outs):
        local_factor(LOCAL - 1, pattern, source, mixing, out, chosen_blocks(unit))


def plain_kernel(factor, unit, state, mates, mixing, *outs):
    for spot, block in enumerate(chosen_blocks(unit)):
        pair = mixing[factor, block]
        per_out = state.shape[0] // len(outs)
        outs[spot // per_out][spot % per_out] = (
            times(pair[:, :BLOCK], state[spot]) + times(pair[:, BLOCK:], mates[spot])
        ).astype(jnp.bfloat16)


def packed(message, pieces, number):
    across = message.shape[-1] // (2 * BLOCK)
    lanes = pl.ds(number % across * 2 * BLOCK, 2 * BLOCK)
    return message.at[pieces + number // across, :, lanes]


def load_kernel(mixing_far, cells_far, pattern_far, mixing, cells, pattern, arrivals):
    pairs = ((mixing_far, mixing), (cells_far, cells), (pattern_far, pattern))
    fetches = [
        pltpu.make_async_copy(far, near, arrivals.at[i]) for i, (far, near) in enumerate(pairs)
    ]
    for fetch in fetches:
        fetch.start()
    for fetch in fetches:
        fetch.wait()


def pack_kernel(factor, pieces, length, cots, mixing, own, near, across):
    messages = (near, across.at[pl.ds(0, length)], across.at[pl.ds(length, length)])
    my_early, my_late = own_bits()
    for piece in range(pieces):
        base = piece * QUARTERS
        own[piece] = cots[base + my_early * 2 + my_late]
        for flip, message in enumerate(messages, 1):
            early, late = my_early ^ (flip & 1), my_late ^ (flip >> 1)
            message[piece] = cots[base + early * 2 + late]
            for which in range(2):
                number = which * pieces + piece
                if flip == 1:
                    for other in range(2):
                        packed(message, pieces, number * 2 + other)[...] = mixing[
                            factor + which, base + early * 2 + (late ^ other)
                        ]
                else:
                    packed(message, pieces, number)[...] = mixing[
                        factor + which, base + early * 2 + late
                    ]


def forward_kernel(message, out):
    out[...] = message[out.shape[0] :]


def stack_kernel(pieces, *rest):
    quarters, outs = rest[:QUARTERS], rest[QUARTERS:]
    for piece, out in enumerate(outs):
        for quarter, values in enumerate(quarters):
            out[quarter * BLOCK : (quarter + 1) * BLOCK] = values[piece]


def mixing_of(factor, which, pieces, piece, mixing, messages, quarter, other=0):
    if quarter == 0:
        early, late = own_bits()
        return mixing[factor + which, piece * QUARTERS + early * 2 + (late ^ other)]
    number = which * pieces + piece
    if quarter == 1:
        number = number * 2 + other
    return packed(messages[quarter - 1], pieces, number)[...]


def early_kernel(factor, pieces, piece, keep, recv, mixing, message, keep_out, send_out):
    weights = functools.partial(mixing_of, factor, 0, pieces, piece, mixing, [message])
    for other, out in enumerate((keep_out, send_out)):
        mine, theirs = keep[other], recv[other]
        pair = weights(0, other)
        out[0] = (times(pair[:, :BLOCK], mine) + times(pair[:, BLOCK:], theirs)).astype(
            jnp.bfloat16
        )
        pair = weights(1, other)
        out[1] = (times(pair[:, :BLOCK], theirs) + times(pair[:, BLOCK:], mine)).astype(
            jnp.bfloat16
        )


def hold_kernel(received, out):
    out[...] = received[...]


def late_kernel(factor, pieces, piece, keep, recv, mixing, *rest):
    messages, outs = rest[:-2], rest[-2:]
    values = [keep[0], keep[1], recv[0], recv[1]]
    for quarter in range(QUARTERS):
        pair = mixing_of(factor, 1, pieces, piece, mixing, messages, quarter)
        rows = slice(quarter % 2 * BLOCK, (quarter % 2 + 1) * BLOCK)
        outs[quarter // 2][rows] = (
            times(pair[:, :BLOCK], values[quarter]) + times(pair[:, BLOCK:], values[quarter ^ 2])
        ).astype(jnp.bfloat16)


def back_kernel(factor, pieces, piece, cores, cots, total, *rest):
    count = (cores - 1) * 2
    parts, (mixing, message1, message2, message3, *outs) = rest[:count], rest[count:]
    messages = (message1, message2, message3)
    grads = []
    for quarter in range(QUARTERS):
        rows = slice(quarter * BLOCK, (quarter + 1) * BLOCK)
        grad = cots[rows].astype(jnp.float32) + total[rows]
        inner = slice(quarter % 2 * BLOCK, (quarter % 2 + 1) * BLOCK)
        for part in parts[quarter // 2 :: 2]:
            grad = grad + part[inner].astype(jnp.float32)
        grads.append(grad.astype(jnp.bfloat16))
    for which, flip in ((1, 2), (0, 1)):
        both = [
            times_transposed(
                mixing_of(factor, which, pieces, piece, mixing, messages, quarter),
                grads[quarter],
            )
            for quarter in range(QUARTERS)
        ]
        grads = [
            (both[quarter][:BLOCK] + both[quarter ^ flip][BLOCK:]).astype(jnp.bfloat16)
            for quarter in range(QUARTERS)
        ]
    for grad, out in zip(grads, outs):
        out[...] = grad


def regroup_kernel(factor, units, *rest):
    quarters, mixing, outs = rest[:QUARTERS], rest[QUARTERS], rest[QUARTERS + 1 :]
    for number, unit in enumerate(units):
        own, cross = outs[2 * number : 2 * number + 2]
        for spot, block in enumerate(chosen_blocks(unit)):
            grad = quarters[1 - unit[spot // 2] % 2 + spot % 2 * 2][...]
            both = times_transposed(mixing[factor, block], grad)
            own[spot] = both[:BLOCK]
            cross[spot] = both[BLOCK:].astype(jnp.bfloat16)


def plain_back_kernel(factor, unit, mine, theirs, mixing, own, cross):
    for spot, block in enumerate(chosen_blocks(unit)):
        grad = (mine[spot] + theirs[spot].astype(jnp.float32)).astype(jnp.bfloat16)
        both = times_transposed(mixing[factor, block], grad)
        own[spot] = both[:BLOCK]
        cross[spot] = both[BLOCK:].astype(cross.dtype)


def exit_kernel(units, pattern_far, *rest):
    count = len(units)
    mine, theirs = rest[:count], rest[count : 2 * count]
    mixing, out, edges, own, cross, pattern, arrival = rest[2 * count :]
    fetch = pltpu.make_async_copy(pattern_far, pattern, arrival)
    fetch.start()
    blocks = own.shape[0]
    for number, unit in enumerate(units):
        for spot, block in enumerate(chosen_blocks(unit)):
            own[block] = mine[number][spot]
            cross[block] = theirs[number][spot]
    fetch.wait()
    for factor in reversed(range(LOCAL)):
        for block in range(blocks):
            own[block] += cross[pattern[factor, block]]
        for block in range(blocks):
            grad = own[block].astype(jnp.bfloat16)
            if factor == 0:
                out[block * BLOCK : (block + 1) * BLOCK] = grad
                if block == 0:
                    edges[0:1] = grad[:1]
                if block == blocks - 1:
                    edges[1:2] = grad[-1:]
            else:
                both = times_transposed(mixing[factor - 1, block], grad)
                own[block] = both[:BLOCK]
                cross[block] = both[BLOCK:]


def conv_back_kernel(cells, far, near, taps, out, ready):
    ready[...] = jnp.zeros_like(ready)
    values = cells[...].astype(jnp.float32)
    scale = taps[2:5].astype(jnp.float32)
    up, down = shifted(values, near[...], far[...])
    out[...] = (scale[0:1] * down + scale[1:2] * values + scale[2:3] * up).astype(jnp.bfloat16)


def channel_spots(count, chans):
    core = lax.axis_index("ch")
    return [
        pl.ds(pl.multiple_of(lax.rem(core + i, count) * chans, chans), chans)
        for i in range(count)
    ]


def grad_act_kernel(count, *rest):
    cots, (w_out, grad_act, c_all) = rest[:count], rest[count:]
    for spot, cot in zip(channel_spots(count, cots[0].shape[1]), cots):
        c_all[:, spot] = cot[...]
    hidden = w_out.shape[0]
    tile = min(TILE, hidden)
    for start in range(0, hidden, tile):
        grad_act[:, start : start + tile] = lax.dot_general(
            c_all[...], w_out[start : start + tile], ACROSS, preferred_element_type=jnp.float32
        ).astype(grad_act.dtype)


def hidden_kernel(count, *rest):
    mixed, (grad_act, w_in, activation, own) = rest[: 2 * count], rest[2 * count : 2 * count + 4]
    backs, (x_all, back_sum) = rest[2 * count + 4 : -2], rest[-2:]
    rows, chans = mixed[0].shape
    spots = channel_spots(count, chans)
    for i, spot in enumerate(spots):
        x_all[:rows, spot] = mixed[2 * i][...]
        x_all[rows:, spot] = mixed[2 * i + 1][...]
    size = w_in.shape[1]
    tile = min(TILE, size)
    every = [slice(start, start + tile) for start in range(0, size, tile)]
    hidden = times(x_all[...], w_in[:, every[0]])
    for number, tiles in enumerate(every):
        following = None
        if number + 1 < len(every):
            following = times(x_all[...], w_in[:, every[number + 1]])
        square = hidden * hidden
        tanh_val = jnp.tanh(hidden * (root_two_pi + root_two_pi * 0.044715 * square))
        half = 0.5 + 0.5 * tanh_val
        gelu = hidden * half
        activation[:, tiles] = gelu.astype(jnp.bfloat16)
        slope = 2.0 * root_two_pi + 6.0 * root_two_pi * 0.044715 * square
        derivative = half + gelu * (1.0 - half) * slope
        grad_hidden = (grad_act[:, tiles].astype(jnp.float32) * derivative).astype(jnp.bfloat16)
        back = lax.dot_general(
            grad_hidden, w_in[:, tiles], ACROSS, preferred_element_type=jnp.float32
        )
        if number == 0:
            back_sum[...] = back
        else:
            back_sum[...] += back
        hidden = following
    own[...] = back_sum[:, spots[0]]
    for i, spot in enumerate(spots[1:]):
        backs[2 * i][...] = back_sum[:rows, spot].astype(jnp.bfloat16)
        backs[2 * i + 1][...] = back_sum[rows:, spot].astype(jnp.bfloat16)


def out_kernel(count, activation, top, bottom, w_out, own, *others):
    rows, chans = top.shape
    for i, spot in enumerate(channel_spots(count, chans)):
        product = times(activation[...], w_out[:, spot])
        if i == 0:
            own[:rows] = top[...].astype(jnp.float32) + product[:rows]
            own[rows:] = bottom[...].astype(jnp.float32) + product[rows:]
        else:
            cuts = len(others) // (count - 1)
            for cut in range(cuts):
                size = 2 * rows // cuts
                part = product[cut * size : (cut + 1) * size]
                others[(i - 1) * cuts + cut][...] = part.astype(jnp.bfloat16)


def combine_kernel(pieces, counts, *rest):
    owns, parts, outs = rest[:pieces], rest[pieces:-QUARTERS], rest[-QUARTERS:]
    for piece in range(pieces):
        per_piece = counts[piece]
        mine, parts = parts[:per_piece], parts[per_piece:]
        for quarter, out in enumerate(outs):
            total = owns[piece][quarter * BLOCK : (quarter + 1) * BLOCK]
            cuts = total.shape[0] * QUARTERS // mine[0].shape[0]
            start = quarter * BLOCK % mine[0].shape[0]
            for part in mine[quarter * cuts // QUARTERS :: cuts]:
                total = total + part[start : start + BLOCK].astype(jnp.float32)
            out[piece] = total.astype(jnp.bfloat16)


def assemble_kernel(*rest):
    quarters, out = rest[:-1], rest[-1]
    my_early, my_late = own_bits()
    for quarter, values in enumerate(quarters):
        spot = (my_early ^ (quarter & 1)) * 2 + (my_late ^ (quarter >> 1))
        for piece in range(values.shape[0]):
            start = pl.multiple_of((piece * QUARTERS + spot) * BLOCK, BLOCK)
            out[pl.ds(start, BLOCK)] = values[piece]


def on_device(inputs, conv_weight, mixing, pattern, w_in, w_out, cotangent):
    row_count, chan_count = inputs.shape
    blocks = row_count // BLOCK
    pieces = blocks // QUARTERS
    width, hidden = w_in.shape
    cores = lax.axis_size("ch")
    levels = lax.axis_size("seq").bit_length() - 1
    plain = list(range(LOCAL, LOCAL + levels - 2))
    last = LOCAL + levels - 2
    early_bit, late_bit = 1 << (levels - 2), 1 << (levels - 1)
    masks = [0, early_bit, late_bit, early_bit | late_bit]

    def blocks_of(size, kind=jnp.bfloat16):
        return ((size, BLOCK, chan_count), kind)

    half = blocks_of(2)
    whole = ((row_count, chan_count), jnp.bfloat16)
    piece_rows = QUARTERS * BLOCK
    flat = (piece_rows, chan_count)
    block = ((BLOCK, chan_count), jnp.bfloat16)
    half_flat = ((2 * BLOCK, chan_count), jnp.bfloat16)
    flat_piece = (flat, jnp.bfloat16)
    flops = 2 * piece_rows * width * hidden

    latest = []

    def run(kernel, name, outs, arrays, *args, **kwargs):
        results = call(kernel, name, outs, arrays, *args, order=tuple(latest), **kwargs)
        latest[:] = results[-1:]
        return results

    near, far = neighbours(jnp.concatenate([inputs[:1], inputs[-1:], conv_weight]), "seq")
    per_block = chan_count // (2 * BLOCK)
    lengths = [pieces + -(-pieces * 2 * (1 + (flip == 1)) // per_block) for flip in (1, 2, 3)]
    length = lengths[1]
    mixing, cells, pattern = run(
        load_kernel,
        "load",
        [(array.shape, array.dtype) for array in (mixing, inputs, pattern)],
        [],
        [mixing, inputs, pattern],
        [pltpu.SemaphoreType.DMA((3,))],
        limit=ALL,
    )
    units = [(s,) for s in range(2 * pieces)]
    convolved, *states = run(
        functools.partial(entry_kernel, units),
        "conv_and_local_factors",
        [whole] + [blocks_of(2 * len(unit)) for unit in units],
        [cells, far, near, mixing],
        [pattern],
        [pltpu.VMEM((blocks, BLOCK, chan_count), jnp.bfloat16)] * 2
        + [pltpu.SMEM(pattern.shape, jnp.int32), pltpu.SemaphoreType.DMA],
    )
    own_cots, *messages = run(
        functools.partial(pack_kernel, last, pieces, length),
        "pack",
        [((pieces, BLOCK, chan_count), jnp.bfloat16)]
        + [blocks_of(lengths[0]), blocks_of(2 * length)],
        [cotangent.reshape(blocks, BLOCK, chan_count), mixing],
    )
    messages = [from_flipped(m, "seq", mask) for m, mask in zip(messages, masks[1:])]

    def forward():
        (message,) = run(forward_kernel, "forward", [blocks_of(length)], [messages[1]])
        messages.append(from_flipped(message, "seq", early_bit))

    all_cots = []
    halves = {}
    transposed = [None] * pieces
    grad_acts = [None] * pieces
    parts = [None] * pieces
    mixeds = [None] * pieces
    activations = [None] * pieces
    owns = [None] * pieces
    out_owns = [None] * pieces
    out_parts = [None] * pieces

    def stack():
        stacked = run(
            functools.partial(stack_kernel, pieces),
            "stack",
            [flat_piece] * pieces,
            [own_cots, *messages],
        )
        for piece in stacked:
            all_cots.append([piece] + [from_offset(piece, "ch", i) for i in range(1, cores)])

    def grad_act(p):
        (grad_acts[p],) = run(
            functools.partial(grad_act_kernel, cores),
            "grad_act",
            [((piece_rows, hidden), jnp.bfloat16)],
            [*all_cots[p], w_out],
            scratch=[pltpu.VMEM((piece_rows, width), jnp.bfloat16)],
            limit=LARGE,
        )

    def plain_factor(factor, u):
        unit = units[u]
        mates = from_flipped(states[u], "seq", 1 << (factor - LOCAL))
        split = factor == plain[-1] and len(unit) == 2
        results = run(
            functools.partial(plain_kernel, factor, unit),
            "factor",
            [half, half] if split else [blocks_of(2 * len(unit))],
            [states[u], mates, mixing],
        )
        if factor == plain[-1]:
            halves.update(zip(unit, results))
        else:
            states[u] = results[0]

    def early_factor(p):
        send, keep = halves[2 * p], halves[2 * p + 1]
        transposed[p] = run(
            functools.partial(early_kernel, last, pieces, p),
            "early_factor",
            [half, half],
            [keep, from_flipped(send, "seq", early_bit), mixing, messages[0]],
        )

    def arrive(p):
        keep, send = transposed[p]
        (received,) = run(hold_kernel, "hold", [half], [from_flipped(send, "seq", late_bit)])
        transposed[p] = keep, received

    def late_factor(p):
        keep, received = transposed[p]
        if p > 0:
            received = from_flipped(received, "seq", late_bit)
        mixeds[p] = run(
            functools.partial(late_kernel, last, pieces, p),
            "late_factor",
            [half_flat] * 2,
            [keep, received, mixing, *messages],
        )

    def hidden_and_grad(p):
        gathered = [
            from_offset(mixed, "ch", i) if i else mixed for i in range(cores) for mixed in mixeds[p]
        ]
        activations[p], owns[p], *backs = run(
            functools.partial(hidden_kernel, cores),
            "mlp_hidden_and_grad",
            [((piece_rows, hidden), jnp.bfloat16), (flat, jnp.float32)]
            + [half_flat] * ((cores - 1) * 2),
            [*gathered, grad_acts[p], w_in],
            scratch=[
                pltpu.VMEM((piece_rows, width), jnp.bfloat16),
                pltpu.VMEM((piece_rows, width), jnp.float32),
            ],
            limit=LARGE,
        )
        parts[p] = [
            from_offset(back, "ch", cores - 1 - i // 2) for i, back in enumerate(backs)
        ]

    def transposed_back(p):
        quarters = run(
            functools.partial(back_kernel, last, pieces, p, cores),
            "late_and_early_back",
            [block] * QUARTERS,
            [all_cots[p][0], owns[p], *parts[p], mixing, *messages],
        )
        transposed[p] = [
            from_flipped(grad, "seq", mask) if mask else grad
            for grad, mask in zip(quarters, masks)
        ]

    def regroup(p):
        chosen = [u for u, unit in enumerate(back_units) if unit[0] // 2 == p]
        sizes = [2 * len(back_units[u]) for u in chosen]
        results = run(
            functools.partial(regroup_kernel, plain[-1], [back_units[u] for u in chosen]),
            "regroup_and_factor_back",
            [blocks_of(size, kind) for size in sizes for kind in (jnp.float32, jnp.bfloat16)],
            [*transposed[p], mixing],
        )
        for number, u in enumerate(chosen):
            states[u] = results[2 * number : 2 * number + 2]

    def out_product(p):
        cuts = 1 if p + 1 < pieces else 2
        out_owns[p], *others = run(
            functools.partial(out_kernel, cores),
            "mlp_out",
            [(flat, jnp.float32)] + [flat_piece if cuts == 1 else half_flat] * (cuts * (cores - 1)),
            [activations[p], *mixeds[p], w_out],
            limit=LARGE,
        )
        out_parts[p] = [
            from_offset(other, "ch", cores - 1 - i // cuts) for i, other in enumerate(others)
        ]

    def plain_back(factor, u):
        mine, cross = states[u]
        theirs = from_flipped(cross, "seq", 1 << (factor - LOCAL))
        kind = jnp.bfloat16 if factor != plain[0] else jnp.float32
        size = 2 * len(back_units[u])
        states[u] = run(
            functools.partial(plain_back_kernel, factor - 1, back_units[u]),
            "factor_back",
            [blocks_of(size, jnp.float32), blocks_of(size, kind)],
            [mine, theirs, mixing],
        )

    waves = sorted((u + 2 * i, -i, u) for i in range(len(plain)) for u in range(len(units)))
    for _, i, u in waves:
        plain_factor(plain[-i], u)
        if plain[-i] == plain[-1] and u == len(units) - 2:
            arrive(0)
        if plain[-i] == plain[-1] and u == 1:
            early_factor(0)
            forward()
    late_factor(0)
    for p in range(1, pieces):
        early_factor(p)
    stack()
    grad_act(0)
    back_units = [(2 * p, 2 * p + 1) for p in range(pieces - 1)]
    back_units += [(2 * pieces - 1,), (2 * pieces - 2,)]
    states = [None] * len(back_units)
    for p in range(pieces):
        hidden_and_grad(p)
        if p + 1 < pieces:
            grad_act(p + 1)
            out_product(p)
            late_factor(p + 1)
        if p == pieces - 1:
            out_product(p)
        if p > 0:
            regroup(p - 1)
        transposed_back(p)
    early_units = range(pieces - 1)
    late_units = range(pieces - 1, pieces + 1)
    def combine():
        return run(
            functools.partial(combine_kernel, pieces, [len(piece) for piece in out_parts]),
            "combine",
            [((pieces, BLOCK, chan_count), jnp.bfloat16)] * QUARTERS,
            [*out_owns, *[part for piece in out_parts for part in piece]],
        )

    outs = combine()
    regroup(pieces - 1)
    for factor in reversed(plain):
        for u in (*early_units, *late_units):
            plain_back(factor, u)
    arrived = [from_flipped(out, "seq", mask) if mask else out for out, mask in zip(outs, masks)]
    grad_conv, edges = run(
        functools.partial(exit_kernel, back_units),
        "local_factors_back",
        [whole, ((2, chan_count), jnp.bfloat16)],
        [g[0] for g in states] + [g[1] for g in states] + [mixing],
        [pattern],
        [pltpu.VMEM((blocks, BLOCK, chan_count), jnp.float32)] * 2
        + [pltpu.SMEM(pattern.shape, jnp.int32), pltpu.SemaphoreType.DMA],
        limit=LARGE,
    )
    near_grad, far_grad = neighbours(edges, "seq")
    grad_input, _ = run(
        conv_back_kernel,
        "conv_back",
        [whole, ((8, 128), jnp.float32)],
        [grad_conv, far_grad, near_grad, near],
    )
    (layer_out,) = run(assemble_kernel, "assemble", [whole], arrived)
    return (layer_out, convolved, grad_input)


def solution(mesh):
    return jax.shard_map(
        on_device,
        mesh=mesh,
        in_specs=(
            P("seq", "ch"),
            P(None, "ch"),
            P(None, "seq", None, None),
            P(None, "seq"),
            P(None, "ch"),
            P("ch", None),
            P("seq", "ch"),
        ),
        out_specs=(P("seq", "ch"), P("seq", "ch"), P("seq", "ch")),
        check_vma=False,
    )
```

```python
import functools

import jax
import jax.numpy as jnp
from jax import lax
from jax.experimental import pallas as pl
from jax.experimental.pallas import tpu as pltpu
from jax.sharding import PartitionSpec as P

BLOCK = 64
LOCAL = 2
QUARTERS = 4
TILE = 256
SMALL = 8 * 1024 * 1024
LARGE = 20 * 1024 * 1024
ALL = 44 * 1024 * 1024

root_two_pi = 0.7978845608028654

IN_HBM = pl.BlockSpec(memory_space=pltpu.HBM)
IN_VMEM = pl.BlockSpec(memory_space=pltpu.VMEM)
ANYWHERE = pl.BlockSpec(memory_space=pl.ANY)
ACROSS = (((1,), (1,)), ((), ()))
OVER_ROWS = (((0,), (0,)), ((), ()))


def times(weights, value):
    return jnp.dot(weights, value, preferred_element_type=jnp.float32)


def times_transposed(weights, value):
    return lax.dot_general(weights, value, OVER_ROWS, preferred_element_type=jnp.float32)


def neighbours(edges, axis):
    count = lax.axis_size(axis)
    near = lax.ppermute(edges, axis, [(i, i ^ 1) for i in range(count)])
    route = []
    for low in range(1, count - 1, 2):
        route += [(low, low + 1), (low + 1, low)]
    return near, lax.ppermute(edges, axis, route)


def from_flipped(block, axis, mask):
    count = lax.axis_size(axis)
    return lax.ppermute(block, axis, [(i, i ^ mask) for i in range(count)])


def from_offset(block, axis, offset):
    count = lax.axis_size(axis)
    return lax.ppermute(block, axis, [((i + offset) % count, i) for i in range(count)])


def call(kernel, name, outs, arrays, distant=(), scratch=(), order=(), limit=SMALL):
    count = len(distant) + len(arrays)

    def body(*refs):
        kernel(*refs[:count], *refs[count + len(order) :])

    return pl.pallas_call(
        body,
        out_shape=[jax.ShapeDtypeStruct(shape, kind) for shape, kind in outs],
        in_specs=[ANYWHERE] * len(distant) + [IN_VMEM] * len(arrays) + [ANYWHERE] * len(order),
        out_specs=[IN_VMEM] * len(outs),
        scratch_shapes=list(scratch),
        compiler_params=pltpu.CompilerParams(vmem_limit_bytes=limit),
        cost_estimate=pl.CostEstimate(flops=0, bytes_accessed=0, transcendentals=0),
        name=name,
    )(*distant, *arrays, *order)


def own_bits():
    seat = lax.axis_index("seq")
    levels = lax.axis_size("seq").bit_length() - 1
    return (seat >> (levels - 2)) & 1, (seat >> (levels - 1)) & 1


def shifted(cells, near, far):
    rows = cells.shape[0]
    even = lax.axis_index("seq") % 2 == 0
    near, far = near.astype(jnp.float32), far.astype(jnp.float32)
    before = jnp.where(even, far[1:2], near[1:2])
    after = jnp.where(even, near[0:1], far[0:1])
    spot = lax.broadcasted_iota(jnp.int32, cells.shape, 0)
    up = jnp.where(spot == 0, before, pltpu.roll(cells, 1, 0))
    down = jnp.where(spot == rows - 1, after, pltpu.roll(cells, rows - 1, 0))
    return up, down


def chosen_blocks(subs):
    early, late = own_bits()
    return [
        sub // 2 * QUARTERS + (early ^ (1 - sub % 2)) * 2 + (late ^ other)
        for sub in subs
        for other in range(2)
    ]


def local_factor(factor, pattern, source, mixing, target, chosen):
    for spot, block in enumerate(chosen):
        pair = mixing[factor, block]
        target[spot] = (
            times(pair[:, :BLOCK], source[block])
            + times(pair[:, BLOCK:], source[pattern[factor, block]])
        ).astype(jnp.bfloat16)


def entry_kernel(units, pattern_far, cells, far, near, mixing, conv_ref, *rest):
    outs, (first, between, pattern, arrival) = rest[:-4], rest[-4:]
    fetch = pltpu.make_async_copy(pattern_far, pattern, arrival)
    fetch.start()
    values = cells[...].astype(jnp.float32)
    scale = near[2:5].astype(jnp.float32)
    up, down = shifted(values, near[...], far[...])
    convolved = (scale[0:1] * up + scale[1:2] * values + scale[2:3] * down).astype(jnp.bfloat16)
    conv_ref[...] = convolved
    first[...] = convolved.reshape(first.shape)
    fetch.wait()
    every = range(first.shape[0])
    refs = (first, between)
    for factor in range(LOCAL - 1):
        local_factor(factor, pattern, refs[factor % 2], mixing, refs[1 - factor % 2], every)
    source = refs[(LOCAL - 1) % 2]
    for unit, out in zip(units, outs):
        local_factor(LOCAL - 1, pattern, source, mixing, out, chosen_blocks(unit))


def plain_kernel(factor, unit, state, mates, mixing, *outs):
    for spot, block in enumerate(chosen_blocks(unit)):
        pair = mixing[factor, block]
        per_out = state.shape[0] // len(outs)
        outs[spot // per_out][spot % per_out] = (
            times(pair[:, :BLOCK], state[spot]) + times(pair[:, BLOCK:], mates[spot])
        ).astype(jnp.bfloat16)


def packed(message, pieces, number):
    across = message.shape[-1] // (2 * BLOCK)
    lanes = pl.ds(number % across * 2 * BLOCK, 2 * BLOCK)
    return message.at[pieces + number // across, :, lanes]


def load_kernel(mixing_far, cells_far, pattern_far, mixing, cells, pattern, arrivals):
    pairs = ((mixing_far, mixing), (cells_far, cells), (pattern_far, pattern))
    fetches = [
        pltpu.make_async_copy(far, near, arrivals.at[i]) for i, (far, near) in enumerate(pairs)
    ]
    for fetch in fetches:
        fetch.start()
    for fetch in fetches:
        fetch.wait()


def pack_kernel(factor, pieces, length, cots, mixing, own, near, across):
    messages = (near, across.at[pl.ds(0, length)], across.at[pl.ds(length, length)])
    my_early, my_late = own_bits()
    for piece in range(pieces):
        base = piece * QUARTERS
        own[piece] = cots[base + my_early * 2 + my_late]
        for flip, message in enumerate(messages, 1):
            early, late = my_early ^ (flip & 1), my_late ^ (flip >> 1)
            message[piece] = cots[base + early * 2 + late]
            for which in range(2):
                number = which * pieces + piece
                if flip == 1:
                    for other in range(2):
                        packed(message, pieces, number * 2 + other)[...] = mixing[
                            factor + which, base + early * 2 + (late ^ other)
                        ]
                else:
                    packed(message, pieces, number)[...] = mixing[
                        factor + which, base + early * 2 + late
                    ]


def forward_kernel(message, out):
    out[...] = message[out.shape[0] :]


def stack_kernel(pieces, *rest):
    quarters, outs = rest[:QUARTERS], rest[QUARTERS:]
    for piece, out in enumerate(outs):
        for quarter, values in enumerate(quarters):
            out[quarter * BLOCK : (quarter + 1) * BLOCK] = values[piece]


def mixing_of(factor, which, pieces, piece, mixing, messages, quarter, other=0):
    if quarter == 0:
        early, late = own_bits()
        return mixing[factor + which, piece * QUARTERS + early * 2 + (late ^ other)]
    number = which * pieces + piece
    if quarter == 1:
        number = number * 2 + other
    return packed(messages[quarter - 1], pieces, number)[...]


def early_kernel(factor, pieces, piece, keep, recv, mixing, message, keep_out, send_out):
    weights = functools.partial(mixing_of, factor, 0, pieces, piece, mixing, [message])
    for other, out in enumerate((keep_out, send_out)):
        mine, theirs = keep[other], recv[other]
        pair = weights(0, other)
        out[0] = (times(pair[:, :BLOCK], mine) + times(pair[:, BLOCK:], theirs)).astype(
            jnp.bfloat16
        )
        pair = weights(1, other)
        out[1] = (times(pair[:, :BLOCK], theirs) + times(pair[:, BLOCK:], mine)).astype(
            jnp.bfloat16
        )


def hold_kernel(received, out):
    out[...] = received[...]


def late_kernel(factor, pieces, piece, keep, recv, mixing, *rest):
    messages, outs = rest[:-2], rest[-2:]
    values = [keep[0], keep[1], recv[0], recv[1]]
    for quarter in range(QUARTERS):
        pair = mixing_of(factor, 1, pieces, piece, mixing, messages, quarter)
        rows = slice(quarter % 2 * BLOCK, (quarter % 2 + 1) * BLOCK)
        outs[quarter // 2][rows] = (
            times(pair[:, :BLOCK], values[quarter]) + times(pair[:, BLOCK:], values[quarter ^ 2])
        ).astype(jnp.bfloat16)


def back_kernel(factor, pieces, piece, cores, cots, total, *rest):
    count = (cores - 1) * 2
    parts, (mixing, message1, message2, message3, *outs) = rest[:count], rest[count:]
    messages = (message1, message2, message3)
    grads = []
    for quarter in range(QUARTERS):
        rows = slice(quarter * BLOCK, (quarter + 1) * BLOCK)
        grad = cots[rows].astype(jnp.float32) + total[rows]
        inner = slice(quarter % 2 * BLOCK, (quarter % 2 + 1) * BLOCK)
        for part in parts[quarter // 2 :: 2]:
            grad = grad + part[inner].astype(jnp.float32)
        grads.append(grad.astype(jnp.bfloat16))
    for which, flip in ((1, 2), (0, 1)):
        both = [
            times_transposed(
                mixing_of(factor, which, pieces, piece, mixing, messages, quarter),
                grads[quarter],
            )
            for quarter in range(QUARTERS)
        ]
        grads = [
            (both[quarter][:BLOCK] + both[quarter ^ flip][BLOCK:]).astype(jnp.bfloat16)
            for quarter in range(QUARTERS)
        ]
    for grad, out in zip(grads, outs):
        out[...] = grad


def regroup_kernel(factor, units, *rest):
    quarters, mixing, outs = rest[:QUARTERS], rest[QUARTERS], rest[QUARTERS + 1 :]
    for number, unit in enumerate(units):
        own, cross = outs[2 * number : 2 * number + 2]
        for spot, block in enumerate(chosen_blocks(unit)):
            grad = quarters[1 - unit[spot // 2] % 2 + spot % 2 * 2][...]
            both = times_transposed(mixing[factor, block], grad)
            own[spot] = both[:BLOCK]
            cross[spot] = both[BLOCK:].astype(jnp.bfloat16)


def plain_back_kernel(factor, unit, mine, theirs, mixing, own, cross):
    for spot, block in enumerate(chosen_blocks(unit)):
        grad = (mine[spot] + theirs[spot].astype(jnp.float32)).astype(jnp.bfloat16)
        both = times_transposed(mixing[factor, block], grad)
        own[spot] = both[:BLOCK]
        cross[spot] = both[BLOCK:].astype(cross.dtype)


def exit_kernel(units, pattern_far, *rest):
    count = len(units)
    mine, theirs = rest[:count], rest[count : 2 * count]
    mixing, out, edges, own, cross, pattern, arrival = rest[2 * count :]
    fetch = pltpu.make_async_copy(pattern_far, pattern, arrival)
    fetch.start()
    blocks = own.shape[0]
    for number, unit in enumerate(units):
        for spot, block in enumerate(chosen_blocks(unit)):
            own[block] = mine[number][spot]
            cross[block] = theirs[number][spot]
    fetch.wait()
    for factor in reversed(range(LOCAL)):
        for block in range(blocks):
            own[block] += cross[pattern[factor, block]]
        for block in range(blocks):
            grad = own[block].astype(jnp.bfloat16)
            if factor == 0:
                out[block * BLOCK : (block + 1) * BLOCK] = grad
                if block == 0:
                    edges[0:1] = grad[:1]
                if block == blocks - 1:
                    edges[1:2] = grad[-1:]
            else:
                both = times_transposed(mixing[factor - 1, block], grad)
                own[block] = both[:BLOCK]
                cross[block] = both[BLOCK:]


def conv_back_kernel(cells, far, near, taps, out, ready):
    ready[...] = jnp.zeros_like(ready)
    values = cells[...].astype(jnp.float32)
    scale = taps[2:5].astype(jnp.float32)
    up, down = shifted(values, near[...], far[...])
    out[...] = (scale[0:1] * down + scale[1:2] * values + scale[2:3] * up).astype(jnp.bfloat16)


def channel_spots(count, chans):
    core = lax.axis_index("ch")
    return [
        pl.ds(pl.multiple_of(lax.rem(core + i, count) * chans, chans), chans)
        for i in range(count)
    ]


def grad_act_kernel(count, *rest):
    cots, (w_out, grad_act, c_all) = rest[:count], rest[count:]
    for spot, cot in zip(channel_spots(count, cots[0].shape[1]), cots):
        c_all[:, spot] = cot[...]
    hidden = w_out.shape[0]
    tile = min(TILE, hidden)
    for start in range(0, hidden, tile):
        grad_act[:, start : start + tile] = lax.dot_general(
            c_all[...], w_out[start : start + tile], ACROSS, preferred_element_type=jnp.float32
        ).astype(grad_act.dtype)


def hidden_kernel(count, *rest):
    mixed, (grad_act, w_in, activation, own) = rest[: 2 * count], rest[2 * count : 2 * count + 4]
    backs, (x_all, back_sum) = rest[2 * count + 4 : -2], rest[-2:]
    rows, chans = mixed[0].shape
    spots = channel_spots(count, chans)
    for i, spot in enumerate(spots):
        x_all[:rows, spot] = mixed[2 * i][...]
        x_all[rows:, spot] = mixed[2 * i + 1][...]
    size = w_in.shape[1]
    tile = min(TILE, size)
    every = [slice(start, start + tile) for start in range(0, size, tile)]
    hidden = times(x_all[...], w_in[:, every[0]])
    for number, tiles in enumerate(every):
        following = None
        if number + 1 < len(every):
            following = times(x_all[...], w_in[:, every[number + 1]])
        square = hidden * hidden
        tanh_val = jnp.tanh(hidden * (root_two_pi + root_two_pi * 0.044715 * square))
        half = 0.5 + 0.5 * tanh_val
        gelu = hidden * half
        activation[:, tiles] = gelu.astype(jnp.bfloat16)
        slope = 2.0 * root_two_pi + 6.0 * root_two_pi * 0.044715 * square
        derivative = half + gelu * (1.0 - half) * slope
        grad_hidden = (grad_act[:, tiles].astype(jnp.float32) * derivative).astype(jnp.bfloat16)
        back = lax.dot_general(
            grad_hidden, w_in[:, tiles], ACROSS, preferred_element_type=jnp.float32
        )
        if number == 0:
            back_sum[...] = back
        else:
            back_sum[...] += back
        hidden = following
    own[...] = back_sum[:, spots[0]]
    for i, spot in enumerate(spots[1:]):
        backs[2 * i][...] = back_sum[:rows, spot].astype(jnp.bfloat16)
        backs[2 * i + 1][...] = back_sum[rows:, spot].astype(jnp.bfloat16)


def out_kernel(count, activation, top, bottom, w_out, own, *others):
    rows, chans = top.shape
    for i, spot in enumerate(channel_spots(count, chans)):
        product = times(activation[...], w_out[:, spot])
        if i == 0:
            own[:rows] = top[...].astype(jnp.float32) + product[:rows]
            own[rows:] = bottom[...].astype(jnp.float32) + product[rows:]
        else:
            cuts = len(others) // (count - 1)
            for cut in range(cuts):
                size = 2 * rows // cuts
                part = product[cut * size : (cut + 1) * size]
                others[(i - 1) * cuts + cut][...] = part.astype(jnp.bfloat16)


def combine_kernel(pieces, counts, *rest):
    owns, parts, outs = rest[:pieces], rest[pieces:-QUARTERS], rest[-QUARTERS:]
    for piece in range(pieces):
        per_piece = counts[piece]
        mine, parts = parts[:per_piece], parts[per_piece:]
        for quarter, out in enumerate(outs):
            total = owns[piece][quarter * BLOCK : (quarter + 1) * BLOCK]
            cuts = total.shape[0] * QUARTERS // mine[0].shape[0]
            start = quarter * BLOCK % mine[0].shape[0]
            for part in mine[quarter * cuts // QUARTERS :: cuts]:
                total = total + part[start : start + BLOCK].astype(jnp.float32)
            out[piece] = total.astype(jnp.bfloat16)


def assemble_kernel(*rest):
    quarters, out = rest[:-1], rest[-1]
    my_early, my_late = own_bits()
    for quarter, values in enumerate(quarters):
        spot = (my_early ^ (quarter & 1)) * 2 + (my_late ^ (quarter >> 1))
        for piece in range(values.shape[0]):
            start = pl.multiple_of((piece * QUARTERS + spot) * BLOCK, BLOCK)
            out[pl.ds(start, BLOCK)] = values[piece]


def on_device(inputs, conv_weight, mixing, pattern, w_in, w_out, cotangent):
    row_count, chan_count = inputs.shape
    blocks = row_count // BLOCK
    pieces = blocks // QUARTERS
    width, hidden = w_in.shape
    cores = lax.axis_size("ch")
    levels = lax.axis_size("seq").bit_length() - 1
    plain = list(range(LOCAL, LOCAL + levels - 2))
    last = LOCAL + levels - 2
    early_bit, late_bit = 1 << (levels - 2), 1 << (levels - 1)
    masks = [0, early_bit, late_bit, early_bit | late_bit]

    def blocks_of(size, kind=jnp.bfloat16):
        return ((size, BLOCK, chan_count), kind)

    half = blocks_of(2)
    whole = ((row_count, chan_count), jnp.bfloat16)
    piece_rows = QUARTERS * BLOCK
    flat = (piece_rows, chan_count)
    block = ((BLOCK, chan_count), jnp.bfloat16)
    half_flat = ((2 * BLOCK, chan_count), jnp.bfloat16)
    flat_piece = (flat, jnp.bfloat16)
    flops = 2 * piece_rows * width * hidden

    latest = []

    def run(kernel, name, outs, arrays, *args, **kwargs):
        results = call(kernel, name, outs, arrays, *args, order=tuple(latest), **kwargs)
        latest[:] = results[-1:]
        return results

    near, far = neighbours(jnp.concatenate([inputs[:1], inputs[-1:], conv_weight]), "seq")
    per_block = chan_count // (2 * BLOCK)
    lengths = [pieces + -(-pieces * 2 * (1 + (flip == 1)) // per_block) for flip in (1, 2, 3)]
    length = lengths[1]
    mixing, cells, pattern = run(
        load_kernel,
        "load",
        [(array.shape, array.dtype) for array in (mixing, inputs, pattern)],
        [],
        [mixing, inputs, pattern],
        [pltpu.SemaphoreType.DMA((3,))],
        limit=ALL,
    )
    units = [(s,) for s in range(2 * pieces)]
    convolved, *states = run(
        functools.partial(entry_kernel, units),
        "conv_and_local_factors",
        [whole] + [blocks_of(2 * len(unit)) for unit in units],
        [cells, far, near, mixing],
        [pattern],
        [pltpu.VMEM((blocks, BLOCK, chan_count), jnp.bfloat16)] * 2
        + [pltpu.SMEM(pattern.shape, jnp.int32), pltpu.SemaphoreType.DMA],
    )
    own_cots, *messages = run(
        functools.partial(pack_kernel, last, pieces, length),
        "pack",
        [((pieces, BLOCK, chan_count), jnp.bfloat16)]
        + [blocks_of(lengths[0]), blocks_of(2 * length)],
        [cotangent.reshape(blocks, BLOCK, chan_count), mixing],
    )
    messages = [from_flipped(m, "seq", mask) for m, mask in zip(messages, masks[1:])]

    def forward():
        (message,) = run(forward_kernel, "forward", [blocks_of(length)], [messages[1]])
        messages.append(from_flipped(message, "seq", early_bit))

    all_cots = []
    halves = {}
    transposed = [None] * pieces
    grad_acts = [None] * pieces
    parts = [None] * pieces
    mixeds = [None] * pieces
    activations = [None] * pieces
    owns = [None] * pieces
    out_owns = [None] * pieces
    out_parts = [None] * pieces

    def stack():
        stacked = run(
            functools.partial(stack_kernel, pieces),
            "stack",
            [flat_piece] * pieces,
            [own_cots, *messages],
        )
        for piece in stacked:
            all_cots.append([piece] + [from_offset(piece, "ch", i) for i in range(1, cores)])

    def grad_act(p):
        (grad_acts[p],) = run(
            functools.partial(grad_act_kernel, cores),
            "grad_act",
            [((piece_rows, hidden), jnp.bfloat16)],
            [*all_cots[p], w_out],
            scratch=[pltpu.VMEM((piece_rows, width), jnp.bfloat16)],
            limit=LARGE,
        )

    def plain_factor(factor, u):
        unit = units[u]
        mates = from_flipped(states[u], "seq", 1 << (factor - LOCAL))
        split = factor == plain[-1] and len(unit) == 2
        results = run(
            functools.partial(plain_kernel, factor, unit),
            "factor",
            [half, half] if split else [blocks_of(2 * len(unit))],
            [states[u], mates, mixing],
        )
        if factor == plain[-1]:
            halves.update(zip(unit, results))
        else:
            states[u] = results[0]

    def early_factor(p):
        send, keep = halves[2 * p], halves[2 * p + 1]
        transposed[p] = run(
            functools.partial(early_kernel, last, pieces, p),
            "early_factor",
            [half, half],
            [keep, from_flipped(send, "seq", early_bit), mixing, messages[0]],
        )

    def arrive(p):
        keep, send = transposed[p]
        (received,) = run(hold_kernel, "hold", [half], [from_flipped(send, "seq", late_bit)])
        transposed[p] = keep, received

    def late_factor(p):
        keep, received = transposed[p]
        if p > 0:
            received = from_flipped(received, "seq", late_bit)
        mixeds[p] = run(
            functools.partial(late_kernel, last, pieces, p),
            "late_factor",
            [half_flat] * 2,
            [keep, received, mixing, *messages],
        )

    def hidden_and_grad(p):
        gathered = [
            from_offset(mixed, "ch", i) if i else mixed for i in range(cores) for mixed in mixeds[p]
        ]
        activations[p], owns[p], *backs = run(
            functools.partial(hidden_kernel, cores),
            "mlp_hidden_and_grad",
            [((piece_rows, hidden), jnp.bfloat16), (flat, jnp.float32)]
            + [half_flat] * ((cores - 1) * 2),
            [*gathered, grad_acts[p], w_in],
            scratch=[
                pltpu.VMEM((piece_rows, width), jnp.bfloat16),
                pltpu.VMEM((piece_rows, width), jnp.float32),
            ],
            limit=LARGE,
        )
        parts[p] = [
            from_offset(back, "ch", cores - 1 - i // 2) for i, back in enumerate(backs)
        ]

    def transposed_back(p):
        quarters = run(
            functools.partial(back_kernel, last, pieces, p, cores),
            "late_and_early_back",
            [block] * QUARTERS,
            [all_cots[p][0], owns[p], *parts[p], mixing, *messages],
        )
        transposed[p] = [
            from_flipped(grad, "seq", mask) if mask else grad
            for grad, mask in zip(quarters, masks)
        ]

    def regroup(p):
        chosen = [u for u, unit in enumerate(back_units) if unit[0] // 2 == p]
        sizes = [2 * len(back_units[u]) for u in chosen]
        results = run(
            functools.partial(regroup_kernel, plain[-1], [back_units[u] for u in chosen]),
            "regroup_and_factor_back",
            [blocks_of(size, kind) for size in sizes for kind in (jnp.float32, jnp.bfloat16)],
            [*transposed[p], mixing],
        )
        for number, u in enumerate(chosen):
            states[u] = results[2 * number : 2 * number + 2]

    def out_product(p):
        cuts = 1 if p + 1 < pieces else 2
        out_owns[p], *others = run(
            functools.partial(out_kernel, cores),
            "mlp_out",
            [(flat, jnp.float32)] + [flat_piece if cuts == 1 else half_flat] * (cuts * (cores - 1)),
            [activations[p], *mixeds[p], w_out],
            limit=LARGE,
        )
        out_parts[p] = [
            from_offset(other, "ch", cores - 1 - i // cuts) for i, other in enumerate(others)
        ]

    def plain_back(factor, u):
        mine, cross = states[u]
        theirs = from_flipped(cross, "seq", 1 << (factor - LOCAL))
        kind = jnp.bfloat16 if factor != plain[0] else jnp.float32
        size = 2 * len(back_units[u])
        states[u] = run(
            functools.partial(plain_back_kernel, factor - 1, back_units[u]),
            "factor_back",
            [blocks_of(size, jnp.float32), blocks_of(size, kind)],
            [mine, theirs, mixing],
        )

    waves = sorted((u + 2 * i, -i, u) for i in range(len(plain)) for u in range(len(units)))
    for _, i, u in waves:
        plain_factor(plain[-i], u)
        if plain[-i] == plain[-1] and u == len(units) - 2:
            arrive(0)
        if plain[-i] == plain[-1] and u == 1:
            early_factor(0)
            forward()
    late_factor(0)
    for p in range(1, pieces):
        early_factor(p)
    stack()
    grad_act(0)
    back_units = [(2 * p, 2 * p + 1) for p in range(pieces - 1)]
    back_units.append((2 * pieces - 1, 2 * pieces - 2))
    states = [None] * len(back_units)
    for p in range(pieces):
        hidden_and_grad(p)
        if p + 1 < pieces:
            grad_act(p + 1)
            out_product(p)
            late_factor(p + 1)
        if p == pieces - 1:
            out_product(p)
        if p > 0:
            regroup(p - 1)
        transposed_back(p)
    early_units = range(pieces - 1)
    late_units = range(pieces - 1, pieces)
    def combine():
        return run(
            functools.partial(combine_kernel, pieces, [len(piece) for piece in out_parts]),
            "combine",
            [((pieces, BLOCK, chan_count), jnp.bfloat16)] * QUARTERS,
            [*out_owns, *[part for piece in out_parts for part in piece]],
        )

    outs = combine()
    regroup(pieces - 1)
    for factor in reversed(plain):
        for u in (*early_units, *late_units):
            plain_back(factor, u)
    arrived = [from_flipped(out, "seq", mask) if mask else out for out, mask in zip(outs, masks)]
    grad_conv, edges = run(
        functools.partial(exit_kernel, back_units),
        "local_factors_back",
        [whole, ((2, chan_count), jnp.bfloat16)],
        [g[0] for g in states] + [g[1] for g in states] + [mixing],
        [pattern],
        [pltpu.VMEM((blocks, BLOCK, chan_count), jnp.float32)] * 2
        + [pltpu.SMEM(pattern.shape, jnp.int32), pltpu.SemaphoreType.DMA],
        limit=LARGE,
    )
    near_grad, far_grad = neighbours(edges, "seq")
    grad_input, _ = run(
        conv_back_kernel,
        "conv_back",
        [whole, ((8, 128), jnp.float32)],
        [grad_conv, far_grad, near_grad, near],
    )
    (layer_out,) = run(assemble_kernel, "assemble", [whole], arrived)
    return (layer_out, convolved, grad_input)


def solution(mesh):
    return jax.shard_map(
        on_device,
        mesh=mesh,
        in_specs=(
            P("seq", "ch"),
            P(None, "ch"),
            P(None, "seq", None, None),
            P(None, "seq"),
            P(None, "ch"),
            P("ch", None),
            P("seq", "ch"),
        ),
        out_specs=(P("seq", "ch"), P("seq", "ch"), P("seq", "ch")),
        check_vma=False,
    )
```
